32 devices in a mesh: groups: 2 (over y), req: 4 (over x, core), tp: 4 (over z).
Axes of the slice: x: 2, y: 2, z: 4, core: 2. Of those that a mesh axis runs over, the one named last changes fastest.
Arguments:
- tokens: bfloat16 [4096, 8192], P(('groups', 'req'), 'tp'), parts along dimension 0, may hold values from -6 to 6
- norm_gain: bfloat16 [8192], replicated, may hold values from 0.25 to 1.75
- w_query: bfloat16 [8192, 4096], P(None, 'tp'), may hold values from -0.0625 to 0.0625
- key_weight: bfloat16 [8192, 1024], P(None, 'tp'), may hold values from -0.0625 to 0.0625
- value_weight: bfloat16 [8192, 1024], P(None, 'tp'), may hold values from -0.0625 to 0.0625
- lengths: int32 [8], P('groups'), parts along dimension 0, may hold values from 1 to 512, 1024 in all
- plan: int32 [32], P('groups'), parts along dimension 0, may hold values from 0 to 15, as said below
Outputs:
- attended: bfloat16 [4096, 4096], P(('groups', 'req'), 'tp'), parts along dimension 0
- cache: bfloat16 [2, 4096, 1024], P(None, ('groups', 'req'), 'tp'), parts along dimension 1
The draws below stay inside these ranges and needn't reach their ends.
There are 2 independent parts, one for each index of `groups`. The reference program is written for one: setup_inputs(seed, part) draws one part's arguments, and reference() takes and returns one part's arrays. A program takes and returns all parts, laid end to end along the dimension named above; an argument that names none is the same for every part. Nothing has to cross between parts.
Inputs may be any that keep to these rules, and one draw needn't show every extreme that they name: lengths: the longest request is exactly 512. plan is a permutation of the spans 0 to 15; span g is request g // 4 at positions (g % 4) * 128 onward; slot k belongs to worker k // 4; the 4 spans of one request go to 4 different workers.
All inputs are finite; a program needn't handle non-finite values.
Results may differ from the reference program's by a relative error of at most 0.008.
Values may be sent and summed in bfloat16 or wider, within the bound.
No kernel may reach another device: no remote copies, remote signals or barrier semaphores. Data moves between devices by JAX's collectives and lax.ppermute only.
A program may use at most 128 MiB of HBM per device.

```python
import math
import jax
import jax.numpy as jnp
import numpy as np
from jax import lax

MODEL_WIDTH = 8192
HQ = 32
KEY_VALUE_HEADS = 8
HEAD_SIZE = 128
TOK_DEV = 512
SPAN = 128
CPD = 4
REQS = 4


def draw_plan(key, part):
    key = jax.random.fold_in(key, 7)
    first_key, second_key, third_key = jax.random.split(key, 3)
    first = jax.random.permutation(first_key, jnp.arange(REQS, dtype=jnp.int32))
    offsets = jax.random.permutation(second_key, jnp.arange(REQS, dtype=jnp.int32))[:CPD]
    turn = jax.random.randint(third_key, (REQS,), 0, CPD).astype(jnp.int32)
    home = (first[:, None] + offsets[None, :]) % REQS
    span_index = (jnp.arange(CPD, dtype=jnp.int32)[None, :] + turn[home]) % CPD
    return (home * CPD + span_index).reshape(-1).astype(jnp.int32)


def block_levels(own_key, dims, cuts, least, largest):
    factor_of = 1.0
    for position, blocks in cuts:
        draws = jax.random.uniform(jax.random.fold_in(jax.random.fold_in(own_key, 6), position), (blocks,), jnp.float32, least / len(cuts), largest / len(cuts))
        factor_of = factor_of * jnp.repeat(jnp.exp(draws), dims[position] // blocks).reshape((-1,) + (1,) * (len(dims) - 1 - position))
    return factor_of


def split_up(amount, total, most, slope):
    weights = [(1 << 20) // math.isqrt(standing ** slope) + 1 for standing in range(2, amount + 1)]
    spare, given = total - most - (amount - 1), [1] * (amount - 1)
    while spare > 0:
        movable = [i for i in range(amount - 1) if given[i] < most]
        mass, remaining = sum([weights[i] for i in movable]), spare
        for i in movable:
            more = min(most - given[i], max(1, remaining * weights[i] // mass), spare)
            given[i] = given[i] + more
            spare = spare - more
    return np.array([most] + given)


def uneven_parts(key, count, total, limit, skew):
    if count == 2:
        one = jax.random.randint(key, (), max(1, total - limit), min(limit, total - 1) + 1)
        return jnp.stack([one, total - one])
    sizes = jnp.asarray(split_up(count, total, limit, skew), jnp.int32)
    twos = (count - 1) // 2
    donor, receiver = sizes[1:1 + 2 * twos:2], sizes[2:2 + 2 * twos:2]
    margin = jnp.minimum(donor - 1, limit - receiver)
    shifted = jax.random.randint(jax.random.fold_in(key, 1), (twos,), 0, 1 << 20) % (margin + 1)
    sizes = sizes.at[1:1 + 2 * twos:2].set(donor - shifted).at[2:2 + 2 * twos:2].set(receiver + shifted)
    return sizes[jax.random.permutation(jax.random.fold_in(key, 2), count)]


def gaussian(stream_key, extent, scale, reach, cuts=(), held_as=jnp.bfloat16):
    loudness = block_levels(stream_key, extent, cuts, -0.22, 0.18) if cuts else 1.0
    array = jax.random.normal(stream_key, extent, jnp.float32) * scale * loudness
    return jnp.minimum(jnp.maximum(array, -reach), reach).astype(held_as)


def setup_inputs(seed: int = 0, part: int = 0) -> dict:
    key_of = jax.random.split(jax.random.key(seed), 8)
    part_splits = jax.random.split(jax.random.fold_in(key_of[7], part), 8)
    return {
        "tokens": gaussian(part_splits[0], (REQS * TOK_DEV, MODEL_WIDTH), 1.0, 6.0, ((0, 4), (1, 4))),
        "norm_gain": jnp.clip(1.0 + 0.15 * jax.random.normal(key_of[1], (MODEL_WIDTH,), jnp.float32), 0.25, 1.75).astype(jnp.bfloat16),
        "w_query": gaussian(key_of[2], (MODEL_WIDTH, HQ * HEAD_SIZE), MODEL_WIDTH ** -0.5, 0.0625, ((1, 4),)),
        "key_weight": gaussian(key_of[3], (MODEL_WIDTH, KEY_VALUE_HEADS * HEAD_SIZE), MODEL_WIDTH ** -0.5, 0.0625, ((1, 4),)),
        "value_weight": gaussian(key_of[4], (MODEL_WIDTH, KEY_VALUE_HEADS * HEAD_SIZE), MODEL_WIDTH ** -0.5, 0.0625, ((1, 4),)),
        "lengths": uneven_parts(part_splits[5], REQS, REQS * TOK_DEV // 2, TOK_DEV, 2).astype(jnp.int32),
        "plan": draw_plan(jax.random.fold_in(jax.random.fold_in(key_of[7], part), 71), part),
    }


def rotate(values, positions, width):
    shaped = values.reshape(values.shape[0], -1, width)
    halfway = width // 2
    frequency = jnp.exp(-(jnp.arange(halfway).astype(jnp.float32) * 2.0 / width) * math.log(500000.0))
    angles = positions.astype(jnp.float32)[:, None] * frequency[None, :]
    cosines = jnp.cos(angles)[:, None, :]
    sinusoid = jnp.sin(angles)[:, None, :]
    lower_half = shaped[..., :halfway]
    upper_half = shaped[..., halfway:]
    turned = jnp.concatenate([lower_half * cosines - upper_half * sinusoid, upper_half * cosines + lower_half * sinusoid], -1)
    return turned.reshape(values.shape)

def attend_span(queries, key_rows, value_rows, first_pos, length):
    count = queries.shape[0]
    key_value_heads = key_rows.shape[1] // HEAD_SIZE
    per_group = queries.shape[1] // HEAD_SIZE // key_value_heads
    query_view = queries.astype(jnp.float32).reshape(count, key_value_heads, per_group, HEAD_SIZE)
    key_view = key_rows.astype(jnp.float32).reshape(-1, key_value_heads, HEAD_SIZE)
    value_view = value_rows.astype(jnp.float32).reshape(-1, key_value_heads, HEAD_SIZE)
    scores = jnp.einsum('ckgd,lkd->kgcl', query_view, key_view) / math.sqrt(HEAD_SIZE)
    query_pos = first_pos + jnp.arange(count).astype(jnp.int32)
    key_pos = jnp.arange(key_view.shape[0]).astype(jnp.int32)
    allowed = (key_pos[None, :] <= query_pos[:, None]) & (key_pos[None, :] < length)
    scores = jnp.where(allowed, scores, -1e+30)
    weights = jax.nn.softmax(scores, axis=-1).astype(jnp.bfloat16)
    mixed = jnp.einsum('kgcl,lkd->ckgd', weights.astype(jnp.float32), value_view)
    mixed = jnp.where((query_pos < length)[:, None, None, None], mixed, 0.0)
    return mixed.reshape(count, -1).astype(jnp.bfloat16)

def one_request(tokens_block, length, norm_gain, w_query, key_weight, value_weight):
    wide = tokens_block.astype(jnp.float32)
    scale = lax.rsqrt(lax.optimization_barrier(jnp.mean(wide * wide, axis=-1, keepdims=True)) + 1e-05)
    normed = (wide * scale * norm_gain.astype(jnp.float32)).astype(jnp.bfloat16)
    positions = jnp.arange(TOK_DEV).astype(jnp.int32)
    live = (positions < length)[:, None]
    queries = rotate(jnp.dot(normed, w_query, preferred_element_type=jnp.float32), positions, HEAD_SIZE).astype(jnp.bfloat16)
    key_rows = jnp.where(live, rotate(jnp.dot(normed, key_weight, preferred_element_type=jnp.float32), positions, HEAD_SIZE), 0.0).astype(jnp.bfloat16)
    value_rows = jnp.where(live, jnp.dot(normed, value_weight, preferred_element_type=jnp.float32), 0.0).astype(jnp.bfloat16)
    output = attend_span(queries, key_rows, value_rows, 0, length)
    return (output, key_rows, value_rows)

def reference(tokens, norm_gain, w_query, key_weight, value_weight, lengths, plan):
    blocks = tokens.reshape(REQS, TOK_DEV, MODEL_WIDTH)

    def apply_one(item):
        return one_request(item[0], item[1], norm_gain, w_query, key_weight, value_weight)
    output, key_rows, value_rows = lax.map(apply_one, (blocks, lengths))
    cache = jnp.stack([key_rows.reshape(REQS * TOK_DEV, -1), value_rows.reshape(REQS * TOK_DEV, -1)])
    span_rows = output.reshape(REQS * CPD, SPAN, HQ * HEAD_SIZE)
    attended = jnp.take(span_rows, plan, axis=0).reshape(REQS * TOK_DEV, HQ * HEAD_SIZE)
    return (attended, cache)
```

```python
import math

import jax
import jax.numpy as jnp
from jax import lax
from jax.sharding import PartitionSpec as P

HEAD_SIZE = 128
SPAN = 128
CHUNKS = 1


def rotate(values, positions, width):
    shaped = values.reshape(values.shape[0], -1, width)
    halfway = width // 2
    frequency = jnp.exp(
        -(jnp.arange(halfway).astype(jnp.float32) * 2.0 / width) * math.log(500000.0)
    )
    angles = positions.astype(jnp.float32)[:, None] * frequency[None, :]
    cosines = jnp.cos(angles)[:, None, :]
    sinusoid = jnp.sin(angles)[:, None, :]
    lower_half = shaped[..., :halfway]
    upper_half = shaped[..., halfway:]
    turned = jnp.concatenate(
        [
            lower_half * cosines - upper_half * sinusoid,
            upper_half * cosines + lower_half * sinusoid,
        ],
        -1,
    )
    return turned.reshape(values.shape)


def attend_span(queries, key_rows, value_rows, first_pos, length):
    count = queries.shape[0]
    key_value_heads = key_rows.shape[1] // HEAD_SIZE
    per_group = queries.shape[1] // HEAD_SIZE // key_value_heads
    query_view = queries.reshape(count, key_value_heads, per_group, HEAD_SIZE)
    key_view = key_rows.reshape(-1, key_value_heads, HEAD_SIZE)
    value_view = value_rows.reshape(-1, key_value_heads, HEAD_SIZE)
    scores = jnp.einsum(
        "ckgd,lkd->kgcl", query_view, key_view, preferred_element_type=jnp.float32
    ) / math.sqrt(HEAD_SIZE)
    query_pos = first_pos + jnp.arange(count)
    key_pos = jnp.arange(key_view.shape[0])
    allowed = (key_pos[None, :] <= query_pos[:, None]) & (key_pos[None, :] < length)
    scores = jnp.where(allowed, scores, -1e30)
    weights = jax.nn.softmax(scores, axis=-1).astype(jnp.bfloat16)
    mixed = jnp.einsum("kgcl,lkd->ckgd", weights, value_view, preferred_element_type=jnp.float32)
    mixed = jnp.where((query_pos < length)[:, None, None, None], mixed, 0.0)
    return mixed.reshape(count, -1).astype(jnp.bfloat16)


def pick(one_hot, rows):
    return jnp.dot(
        one_hot.astype(jnp.bfloat16), rows, preferred_element_type=jnp.float32
    ).astype(jnp.bfloat16)


def shift_chips(value, hop, chips):
    pairs = [(2 * x + c, 2 * ((x + hop) % chips) + c) for x in range(chips) for c in range(2)]
    return lax.ppermute(value, "req", pairs)


def swap_cores(value, chips):
    return lax.ppermute(value, "req", [(d, d ^ 1) for d in range(2 * chips)])


def local(chips, tokens, norm_gain, w_query, key_weight, value_weight, lengths, plan):
    workers = 2 * chips
    slots = tokens.shape[0]
    per_home = slots // SPAN
    live_rows = workers * slots // 2
    rows = live_rows // workers // CHUNKS
    query_width, key_width = w_query.shape[1], key_weight.shape[1]
    me = lax.axis_index("req")
    chip, core = me // 2, me % 2
    ends = jnp.cumsum(lengths)
    starts = ends - lengths
    slot_pos = jnp.arange(slots)

    own_row = jnp.where(slot_pos < lengths[me], starts[me] + slot_pos, -1)
    sent = []
    for chunk in range(CHUNKS):
        number = chunk * workers * rows + jnp.arange(workers * rows)
        mine = pick(number[:, None] == own_row[None, :], tokens)
        mine = mine.reshape(chips, 2, rows, tokens.shape[1])
        other = lax.dynamic_index_in_dim(mine, 1 - core, 1, keepdims=False)
        both = lax.dynamic_index_in_dim(mine, core, 1, keepdims=False) + swap_cores(other, chips)
        block = lax.dynamic_index_in_dim(both, chip, 0, keepdims=False)
        for hop in range(1, chips):
            away = lax.dynamic_index_in_dim(both, (chip + hop) % chips, 0, keepdims=False)
            block = block + shift_chips(away, hop, chips)
        sent.append(block)

    gathered_rows, gathered_numbers = [], []
    for chunk in range(CHUNKS):
        base = chunk * workers * rows
        gathered = lax.all_gather(sent[chunk], "tp", axis=1, tiled=True)
        wide = gathered.astype(jnp.float32)
        scale = lax.rsqrt(jnp.mean(wide * wide, axis=-1, keepdims=True) + 1e-05)
        normed = (wide * scale * norm_gain.astype(jnp.float32)).astype(jnp.bfloat16)
        number = base + me * rows + jnp.arange(rows)
        owner = jnp.sum((ends[None, :] <= number[:, None]).astype(jnp.int32), axis=1)
        positions = number - starts[owner]
        queries = rotate(
            jnp.dot(normed, w_query, preferred_element_type=jnp.float32), positions, HEAD_SIZE
        )
        key_rows = rotate(
            jnp.dot(normed, key_weight, preferred_element_type=jnp.float32), positions, HEAD_SIZE
        )
        value_rows = jnp.dot(normed, value_weight, preferred_element_type=jnp.float32)
        block = jnp.concatenate([queries, key_rows, value_rows], axis=1).astype(jnp.bfloat16)
        held = [block] + [shift_chips(block, hop, chips) for hop in range(1, chips)]
        swapped = [swap_cores(piece, chips) for piece in held]
        for hop in range(chips):
            source = (chip - hop) % chips
            for piece, owner_core in ((held[hop], core), (swapped[hop], 1 - core)):
                gathered_rows.append(piece)
                gathered_numbers.append(
                    base + (2 * source + owner_core) * rows + jnp.arange(rows)
                )
    all_rows = jnp.concatenate(gathered_rows, axis=0)
    all_numbers = jnp.concatenate(gathered_numbers, axis=0)
    keys_values = all_rows[:, query_width:]

    own = pick(own_row[:, None] == all_numbers[None, :], keys_values)
    cache = jnp.stack([own[:, :key_width], own[:, key_width:]])
    pieces = []
    for slot_index in range(per_home):
        span_id = plan[me * per_home + slot_index]
        source = span_id // per_home
        offset = span_id % per_home * SPAN
        length = lengths[source]
        request_row = jnp.where(slot_pos < length, starts[source] + slot_pos, -1)
        span_row = lax.dynamic_slice_in_dim(request_row, offset, SPAN, 0)
        span_queries = pick(
            span_row[:, None] == all_numbers[None, :], all_rows[:, :query_width]
        )
        prefix = pick(request_row[:, None] == all_numbers[None, :], keys_values)
        pieces.append(
            attend_span(span_queries, prefix[:, :key_width], prefix[:, key_width:], offset, length)
        )
    return (jnp.concatenate(pieces, axis=0), cache)


def solution(mesh):
    placed = (
        P(("groups", "req"), "tp"),
        P(),
        P(None, "tp"),
        P(None, "tp"),
        P(None, "tp"),
        P("groups"),
        P("groups"),
    )

    def block(*arrays):
        return local(mesh.shape["req"] // 2, *arrays)

    return jax.shard_map(
        block,
        mesh=mesh,
        in_specs=placed,
        out_specs=(P(("groups", "req"), "tp"), P(None, ("groups", "req"), "tp")),
        check_vma=False,
    )
```

```python
import functools
import math

import jax
import jax.numpy as jnp
import numpy as np
from jax import lax
from jax.experimental import pallas as pl
from jax.experimental.pallas import tpu as pltpu
from jax.sharding import PartitionSpec as P

HEAD_SIZE = 128
SPAN = 128
ALIGN = 16
SHARES = (4, 8, 4)
DEPTH = 512
VMEM_LIMIT = 40 * 1024 * 1024
F32, BF16 = jnp.float32, jnp.bfloat16


def run_of(lengths_ref, request, count):
    start = jnp.int32(0)
    length = jnp.int32(0)
    for other in range(count):
        amount = lengths_ref[other]
        start = start + jnp.where(other < request, amount, 0)
        length = jnp.where(other == request, amount, length)
    return start, length


def iota(shape, dimension):
    return lax.broadcasted_iota(jnp.int32, shape, dimension)


def deal_kernel(chips, base, rows, lengths_ref, own_ref, twin_ref, home_ref, away_ref):
    me = lax.axis_index("req")
    chip, core = lax.div(me, 2), lax.rem(me, 2)
    runs = [
        run_of(lengths_ref, request, 2 * chips) for request in (me, me + 1 - 2 * core)
    ]
    slots = own_ref.shape[0]
    for hop in range(chips):
        target = lax.rem(chip + hop, chips) * 2 + core
        number = base + target * rows + iota((rows, slots), 0)
        slot = iota((rows, slots), 1)
        total = None
        for (start, length), source in zip(runs, (own_ref, twin_ref)):
            hot = ((number - start == slot) & (slot < length)).astype(BF16)
            part = jnp.dot(hot, source[...], preferred_element_type=F32)
            total = part if total is None else total + part
        if hop == 0:
            home_ref[...] = total.astype(BF16)
        else:
            away_ref[hop - 1] = total.astype(BF16)


def deal(chips, base, rows, lengths, own, twin):
    slots, width = own.shape
    block = min(512, width)
    return pl.pallas_call(
        functools.partial(deal_kernel, chips, base, rows),
        grid=(width // block,),
        in_specs=[
            pl.BlockSpec(memory_space=pltpu.SMEM),
            pl.BlockSpec((slots, block), lambda i: (0, i)),
            pl.BlockSpec((slots, block), lambda i: (0, i)),
        ],
        out_specs=[
            pl.BlockSpec((rows, block), lambda i: (0, i)),
            pl.BlockSpec((chips - 1, rows, block), lambda i: (0, 0, i)),
        ],
        out_shape=[
            jax.ShapeDtypeStruct((rows, width), BF16),
            jax.ShapeDtypeStruct((chips - 1, rows, width), BF16),
        ],
        compiler_params=pltpu.CompilerParams(vmem_limit_bytes=VMEM_LIMIT),
        cost_estimate=pl.CostEstimate(
            flops=4 * chips * rows * slots * width,
            bytes_accessed=4 * slots * width + 2 * chips * rows * width,
            transcendentals=0,
        ),
        name="deal",
    )(lengths, own, twin)


def project_kernel(offsets, shards, steps, base, members, *refs):
    first, final = offsets == (0,), 0 not in offsets and abs(offsets[0]) == shards - 1
    place_ref, lengths_ref = refs[:2]
    refs = refs[2:]
    pieces, refs = refs[: len(offsets)], refs[len(offsets) :]
    gain_ref, query_ref, key_ref, value_ref = refs[:4]
    refs = refs[4:]
    if not first:
        sums_in, squares_in = refs[:2]
        refs = refs[2:]
    if final:
        cosine_ref, sine_ref, frequency_ref, out_ref, sums, squares = (*refs[:2], None, *refs[2:])
    elif first:
        frequency_ref, sums, squares, cosine_ref, sine_ref = refs
    else:
        sums, squares = refs
    piece, step = pl.program_id(0), pl.program_id(1)
    rows = sums.shape[0]

    @pl.when((piece == 0) & (step == 0))
    def _():
        if first:
            sums[...] = jnp.zeros_like(sums)
            squares[...] = jnp.zeros_like(squares)
            number = base + place_ref[1] * rows + iota((rows, HEAD_SIZE), 0)
            start = jnp.zeros((rows, HEAD_SIZE), jnp.int32)
            before = jnp.int32(0)
            for other in range(members):
                before = before + lengths_ref[other]
                start = jnp.where(number >= before, before, start)
            angle = (number - start).astype(F32) * frequency_ref[...]
            lower = iota((rows, HEAD_SIZE), 1) < HEAD_SIZE // 2
            sine = jnp.sin(angle)
            cosine_ref[...] = jnp.cos(angle)
            sine_ref[...] = jnp.where(lower, -sine, sine)
        else:
            sums[...] = sums_in[...]
            squares[...] = squares_in[...]

    for index, offset in enumerate(offsets):
        shard = place_ref[0] + offset

        @pl.when((piece == index) & (shard >= 0) & (shard < shards))
        def _():
            wide = pieces[index][...].astype(F32)
            square = wide * wide
            part = square[:, :128]
            for at in range(128, square.shape[1], 128):
                part = part + square[:, at : at + 128]
            squares[...] += part
            scaled = (wide * gain_ref[...]).astype(BF16)
            at = 0
            for weight in (query_ref, key_ref, value_ref):
                columns = slice(at, at + weight.shape[1])
                sums[:, columns] += jnp.dot(scaled, weight[...], preferred_element_type=F32)
                at += weight.shape[1]

    if final:

        @pl.when((piece == len(offsets) - 1) & (step == steps - 1))
        def _():
            mean = jnp.sum(squares[...], axis=1, keepdims=True) / (
                shards * steps * pieces[0].shape[1]
            )
            scale = lax.rsqrt(mean + 1e-05)
            turned = query_ref.shape[1] + key_ref.shape[1]
            for at in range(0, sums.shape[1], HEAD_SIZE):
                columns = slice(at, at + HEAD_SIZE)
                head = sums[:, columns] * scale
                if at < turned:
                    head = head * cosine_ref[...] + pltpu.roll(
                        head, HEAD_SIZE // 2, 1
                    ) * sine_ref[...]
                out_ref[:, columns] = head.astype(BF16)


def project(offsets, shards, base, place, lengths, pieces, gain, weights, carried, frequency):
    rows, width = pieces[0].shape
    depth = min(DEPTH, width)
    steps = width // depth
    columns = sum(weight.shape[1] for weight in weights)
    first = offsets == (0,)
    final = not first and abs(offsets[0]) == shards - 1

    def block_of(piece, step, place_ref):
        if len(offsets) == 1:
            return place_ref[0] * steps + step
        left, right = place_ref[0] + offsets[0], place_ref[0] + offsets[1]
        has_left, has_right = left >= 0, right < shards
        on_left = jnp.where(
            has_left, left * steps + step, jnp.where(has_right, right * steps, 0)
        )
        on_right = jnp.where(
            has_right, right * steps + step, jnp.where(has_left, left * steps + steps - 1, 0)
        )
        return jnp.where(piece == 0, on_left, on_right)

    def piece_spec(index):
        def where(piece, step, place_ref, lengths_ref):
            edge = 0 if index else steps - 1
            return (0, jnp.where(piece == index, step, edge))

        return pl.BlockSpec((rows, depth), where)

    def whole(shape):
        return pl.BlockSpec(shape, lambda piece, step, place_ref, lengths_ref: (0, 0))

    def deep(block, dimension):
        def where(piece, step, place_ref, lengths_ref):
            at = block_of(piece, step, place_ref)
            return (at, 0) if dimension == 0 else (0, at)

        return pl.BlockSpec(block, where)

    in_specs = [piece_spec(index) for index in range(len(offsets))]
    in_specs += [deep((1, depth), 1)]
    in_specs += [deep((depth, weight.shape[1]), 0) for weight in weights]
    operands = [*pieces, gain, *weights]
    sums = jax.ShapeDtypeStruct((rows, columns), F32)
    lanes = jax.ShapeDtypeStruct((rows, 128), F32)
    table = jax.ShapeDtypeStruct((rows, HEAD_SIZE), F32)
    aliases, scratch = {}, []
    if first:
        in_specs += [whole((1, HEAD_SIZE))]
        operands += [frequency]
        out_shape = [sums, lanes, table, table]
    else:
        in_specs += [whole((rows, columns)), whole((rows, 128))]
        operands += carried[:2]
        if final:
            in_specs += [whole((rows, HEAD_SIZE))] * 2
            operands += carried[2:]
            out_shape = [jax.ShapeDtypeStruct((rows, columns), BF16)]
            scratch = [pltpu.VMEM((rows, columns), F32), pltpu.VMEM((rows, 128), F32)]
        else:
            out_shape = [sums, lanes]
    return pl.pallas_call(
        functools.partial(project_kernel, offsets, shards, steps, base, lengths.shape[0]),
        grid_spec=pltpu.PrefetchScalarGridSpec(
            num_scalar_prefetch=2,
            grid=(len(offsets), steps),
            in_specs=in_specs,
            out_specs=[whole(leaf.shape) for leaf in out_shape],
            scratch_shapes=scratch,
        ),
        out_shape=out_shape,
        compiler_params=pltpu.CompilerParams(vmem_limit_bytes=VMEM_LIMIT),
        cost_estimate=pl.CostEstimate(
            flops=2 * rows * width * columns * len(offsets),
            bytes_accessed=2 * width * columns * len(offsets) + 8 * rows * columns,
            transcendentals=0,
        ),
        name="project",
    )(place, lengths, *operands)


def attend_kernel(chips, bases, sizes, query_width, key_width, lengths_ref, plan_ref, *refs):
    blocks, (attended_ref, cache_ref, rows_ref, sems) = refs[:-4], refs[-4:]
    workers = 2 * chips
    me = lax.axis_index("req")
    chip, core = lax.div(me, 2), lax.rem(me, 2)
    slots = cache_ref.shape[1]
    spans = slots // SPAN
    total = workers * sum(sizes)
    copies = []
    for chunk, (base, rows) in enumerate(zip(bases, sizes)):
        for hop in range(chips):
            source = lax.rem(chip - hop + chips, chips) * 2
            for twin in range(2):
                owner = source + (core if twin == 0 else 1 - core)
                index = (chunk * chips + hop) * 2 + twin
                at = pl.multiple_of(base + owner * rows, ALIGN)
                copies.append(
                    pltpu.make_async_copy(
                        blocks[index], rows_ref.at[pl.ds(at, rows), :], sems.at[index]
                    )
                )
    for copy in copies:
        copy.start()
    pad = rows_ref.shape[0] - total
    rows_ref[total:, :] = jnp.zeros((pad, rows_ref.shape[1]), BF16)
    for copy in copies:
        copy.wait()

    def aligned(row):
        first = pl.multiple_of(lax.div(row, ALIGN) * ALIGN, ALIGN)
        return first, row - first

    start, length = run_of(lengths_ref, me, workers)
    first, shift = aligned(start)
    reach = slots + SPAN
    row, column = iota((slots, reach), 0), iota((slots, reach), 1)
    hot = ((column == row + shift) & (row < length)).astype(BF16)
    for half in range(2):
        window = rows_ref[
            pl.ds(first, reach),
            query_width + half * key_width : query_width + (half + 1) * key_width,
        ]
        cache_ref[half] = jnp.dot(hot, window, preferred_element_type=F32).astype(BF16)

    heads, key_heads = query_width // HEAD_SIZE, key_width // HEAD_SIZE
    group = heads // key_heads
    factor = math.log2(math.e) / math.sqrt(HEAD_SIZE)
    for slot in range(spans):
        span = plan_ref[me * spans + slot]
        source = lax.div(span, spans)
        part = lax.rem(span, spans)
        start, length = run_of(lengths_ref, source, workers)
        offset = part * SPAN
        out_rows = slice(slot * SPAN, (slot + 1) * SPAN)
        dead = offset >= length

        @pl.when(dead)
        def _():
            attended_ref[out_rows, :] = jnp.zeros((SPAN, query_width), BF16)

        for count in range(1, spans + 1):

            @pl.when(jnp.logical_not(dead) & (part == count - 1))
            def _():
                first, shift = aligned(start + offset)
                hot = iota((SPAN, 2 * SPAN), 1) == iota((SPAN, 2 * SPAN), 0) + shift
                queries = jnp.dot(
                    hot.astype(BF16),
                    rows_ref[pl.ds(first, 2 * SPAN), :query_width],
                    preferred_element_type=F32,
                ).astype(BF16)
                reach = (count + 1) * SPAN
                first, shift = aligned(start)
                key_pos = iota((SPAN, reach), 1) - shift
                query_pos = (count - 1) * SPAN + iota((SPAN, reach), 0)
                allowed = (key_pos >= 0) & (key_pos <= query_pos) & (key_pos < length)
                bias = jnp.where(allowed, 0.0, -1e30)
                bias = jnp.concatenate([bias] * group, axis=0)
                live = (count - 1) * SPAN + iota((SPAN, HEAD_SIZE), 0) < length
                for head in range(key_heads):
                    stacked = jnp.concatenate(
                        [
                            queries[:, at * HEAD_SIZE : (at + 1) * HEAD_SIZE]
                            for at in range(head * group, (head + 1) * group)
                        ],
                        axis=0,
                    )
                    left = query_width + head * HEAD_SIZE
                    keys = rows_ref[pl.ds(first, reach), left : left + HEAD_SIZE]
                    left += key_width
                    values = rows_ref[pl.ds(first, reach), left : left + HEAD_SIZE]
                    scores = lax.dot_general(
                        stacked, keys, (((1,), (1,)), ((), ())), preferred_element_type=F32
                    )
                    scores = scores + bias
                    top = jnp.max(scores, axis=1, keepdims=True)
                    weights = jnp.exp2((scores - top) * factor)
                    norm = jnp.sum(weights, axis=1, keepdims=True)
                    mixed = jnp.dot(weights.astype(BF16), values, preferred_element_type=F32)
                    mixed = mixed / norm
                    for at in range(group):
                        left = (head * group + at) * HEAD_SIZE
                        attended_ref[out_rows, left : left + HEAD_SIZE] = jnp.where(
                            live, mixed[at * SPAN : (at + 1) * SPAN], 0.0
                        ).astype(BF16)


def attend(chips, bases, sizes, query_width, key_width, slots, lengths, plan, blocks):
    width = query_width + 2 * key_width
    total = 2 * chips * sum(sizes)
    return pl.pallas_call(
        functools.partial(attend_kernel, chips, bases, sizes, query_width, key_width),
        in_specs=[pl.BlockSpec(memory_space=pltpu.SMEM)] * 2
        + [pl.BlockSpec(memory_space=pl.ANY)] * len(blocks),
        out_specs=[pl.BlockSpec(memory_space=pltpu.VMEM)] * 2,
        out_shape=[
            jax.ShapeDtypeStruct((slots, query_width), BF16),
            jax.ShapeDtypeStruct((2, slots, key_width), BF16),
        ],
        scratch_shapes=[
            pltpu.VMEM((total + slots + SPAN, width), BF16),
            pltpu.SemaphoreType.DMA((len(blocks),)),
        ],
        compiler_params=pltpu.CompilerParams(vmem_limit_bytes=VMEM_LIMIT),
        name="attend",
    )(lengths, plan, *blocks)


def shift_chips(value, hop, chips):
    pairs = [(2 * x + c, 2 * ((x + hop) % chips) + c) for x in range(chips) for c in range(2)]
    return lax.ppermute(value, "req", pairs)


def swap_cores(value, chips):
    return lax.ppermute(value, "req", [(d, d ^ 1) for d in range(2 * chips)])


def local(
    chips, shards, tokens, norm_gain, w_query, key_weight, value_weight, lengths, plan
):
    workers = 2 * chips
    slots = tokens.shape[0]
    live = slots // 2
    sizes = [live * share // sum(SHARES) // ALIGN * ALIGN for share in SHARES]
    sizes[-1] = live - sum(sizes[:-1])
    bases = [workers * sum(sizes[:chunk]) for chunk in range(len(sizes))]
    weights = (w_query, key_weight, value_weight)
    place = jnp.stack([lax.axis_index("tp"), lax.axis_index("req")]).astype(jnp.int32)
    gain = norm_gain.astype(F32).reshape(1, -1)
    halfway = HEAD_SIZE // 2
    frequency = np.exp(-np.arange(halfway) * 2.0 / HEAD_SIZE * math.log(500000.0))
    frequency = jnp.asarray(np.tile(frequency, 2)[None, :], F32)

    twin = swap_cores(tokens, chips)
    held = []
    for base, rows in zip(bases, sizes):
        block, away = deal(chips, base, rows, lengths, tokens, twin)
        for hop in range(1, chips):
            block = block + shift_chips(away[hop - 1], hop, chips)
        held.append(block)

    onward = [[(block, block)] for block in held]
    for step in range(1, shards):
        right = [(at, at + 1) for at in range(step - 1, shards - 1)]
        left = [(at, at - 1) for at in range(1, shards - step + 1)]
        for line in onward:
            line.append(
                (lax.ppermute(line[-1][0], "tp", right), lax.ppermute(line[-1][1], "tp", left))
            )

    blocks = []
    for base, line in zip(bases, onward):
        carried = project(
            (0,), shards, base, place, lengths, line[0][:1], gain, weights, (), frequency
        )
        tables = carried[2:]
        for step in range(1, shards):
            last = step == shards - 1
            carried = project(
                (-step, step),
                shards,
                base,
                place,
                lengths,
                line[step],
                gain,
                weights,
                [*carried[:2], *tables] if last else carried[:2],
                frequency,
            )
        block = carried[0]
        here = [block] + [shift_chips(block, hop, chips) for hop in range(1, chips)]
        for piece in here:
            blocks += [piece, swap_cores(piece, chips)]
    return tuple(
        attend(
            chips,
            bases,
            sizes,
            w_query.shape[1],
            key_weight.shape[1],
            slots,
            lengths,
            plan,
            blocks,
        )
    )


def solution(mesh):
    placed = (
        P(("groups", "req"), "tp"),
        P(),
        P(None, "tp"),
        P(None, "tp"),
        P(None, "tp"),
        P("groups"),
        P("groups"),
    )
    return jax.shard_map(
        functools.partial(local, mesh.shape["req"] // 2, mesh.shape["tp"]),
        mesh=mesh,
        in_specs=placed,
        out_specs=(P(("groups", "req"), "tp"), P(None, ("groups", "req"), "tp")),
        check_vma=False,
    )
```

```python
import functools
import math

import jax
import jax.numpy as jnp
import numpy as np
from jax import lax
from jax.experimental import pallas as pl
from jax.experimental.pallas import tpu as pltpu
from jax.sharding import PartitionSpec as P

HEAD_SIZE = 128
SPAN = 128
ALIGN = 16
SHARES = (4, 8, 4)
DEPTH = 1024
VMEM_LIMIT = 56 * 1024 * 1024
F32, BF16 = jnp.float32, jnp.bfloat16


def run_of(lengths_ref, request, count):
    start = jnp.int32(0)
    length = jnp.int32(0)
    for other in range(count):
        amount = lengths_ref[other]
        start = start + jnp.where(other < request, amount, 0)
        length = jnp.where(other == request, amount, length)
    return start, length


def iota(shape, dimension):
    return lax.broadcasted_iota(jnp.int32, shape, dimension)


def deal_kernel(chips, bases, sizes, lengths_ref, own_ref, twin_ref, *out_refs):
    me = lax.axis_index("req")
    chip, core = lax.div(me, 2), lax.rem(me, 2)
    runs = [
        run_of(lengths_ref, request, 2 * chips) for request in (me, me + 1 - 2 * core)
    ]
    slots = own_ref.shape[0]
    for chunk, (base, rows) in enumerate(zip(bases, sizes)):
        home_ref, away_ref = out_refs[2 * chunk : 2 * chunk + 2]
        for hop in range(chips):
            target = lax.rem(chip + hop, chips) * 2 + core
            number = base + target * rows + iota((rows, slots), 0)
            slot = iota((rows, slots), 1)
            total = None
            for (start, length), source in zip(runs, (own_ref, twin_ref)):
                hot = ((number - start == slot) & (slot < length)).astype(BF16)
                part = jnp.dot(hot, source[...], preferred_element_type=F32)
                total = part if total is None else total + part
            if hop == 0:
                home_ref[...] = total.astype(BF16)
            else:
                away_ref[hop - 1] = total.astype(BF16)


def deal(chips, bases, sizes, lengths, own, twin):
    slots, width = own.shape
    block = min(512, width)
    out_specs, out_shape = [], []
    for rows in sizes:
        out_specs += [
            pl.BlockSpec((rows, block), lambda i: (0, i)),
            pl.BlockSpec((chips - 1, rows, block), lambda i: (0, 0, i)),
        ]
        out_shape += [
            jax.ShapeDtypeStruct((rows, width), BF16),
            jax.ShapeDtypeStruct((chips - 1, rows, width), BF16),
        ]
    return pl.pallas_call(
        functools.partial(deal_kernel, chips, bases, sizes),
        grid=(width // block,),
        in_specs=[
            pl.BlockSpec(memory_space=pltpu.SMEM),
            pl.BlockSpec((slots, block), lambda i: (0, i)),
            pl.BlockSpec((slots, block), lambda i: (0, i)),
        ],
        out_specs=out_specs,
        out_shape=out_shape,
        compiler_params=pltpu.CompilerParams(vmem_limit_bytes=VMEM_LIMIT),
        cost_estimate=pl.CostEstimate(
            flops=4 * chips * sum(sizes) * slots * width,
            bytes_accessed=4 * slots * width + 2 * chips * sum(sizes) * width,
            transcendentals=0,
        ),
        name="deal",
    )(lengths, own, twin)


def merge_kernel(count, home_ref, *refs):
    total = home_ref[...]
    for ref in refs[:count]:
        total = total + ref[...]
    refs[-1 if len(refs) == count + 1 else -2][...] = total


def merge(home, arrived, later):
    count = len(arrived)
    vmem, anywhere = pl.BlockSpec(memory_space=pltpu.VMEM), pl.BlockSpec(memory_space=pl.ANY)
    operands, in_specs = [home, *arrived], [vmem] * (count + 1)
    out_shape, out_specs = [jax.ShapeDtypeStruct(home.shape, home.dtype)], [vmem]
    aliases = {}
    if later is not None:
        operands.append(later)
        in_specs.append(anywhere)
        out_shape.append(jax.ShapeDtypeStruct(later.shape, later.dtype))
        out_specs.append(anywhere)
        aliases = {count + 1: 1}
    results = pl.pallas_call(
        functools.partial(merge_kernel, count),
        in_specs=in_specs,
        out_specs=out_specs,
        out_shape=out_shape,
        input_output_aliases=aliases,
        compiler_params=pltpu.CompilerParams(vmem_limit_bytes=VMEM_LIMIT),
        cost_estimate=pl.CostEstimate(
            flops=home.size, bytes_accessed=2 * home.size * (count + 2), transcendentals=0
        ),
        name="merge",
    )(*operands)
    return results if later is not None else (results[0], None)


def routes_of(shards):
    if shards == 4:
        routes = [
            (-1, [(0, 1), (1, 0), (2, 3), (3, 2)]),
            (-1, [(1, 2), (2, 1)]),
            (-1, [(0, 2), (1, 3), (2, 0), (3, 1)]),
            (2, [(2, 3), (1, 0)]),
        ]
    else:
        routes = []
        for step in range(1, shards):
            source = len(routes) - 2 if step > 1 else -1
            routes.append((source, [(at, at + 1) for at in range(step - 1, shards - 1)]))
            source = len(routes) - 2 if step > 1 else -1
            routes.append((source, [(at, at - 1) for at in range(1, shards - step + 1)]))
    held, depth = [list(range(shards))], [0]
    for source, pairs in routes:
        now = [-1] * shards
        for start, end in pairs:
            now[end] = held[source + 1][start]
        held.append(now)
        depth.append(depth[source + 1] + 1)
    return routes, held, depth


def visits_of(held, shards):
    visits = [
        [(piece, now[at]) for piece, now in enumerate(held) if now[at] >= 0]
        for at in range(shards)
    ]
    count = max(len(line) for line in visits)
    table = []
    for line in visits:
        pad = (-1, line[-1][1] if line else 0)
        line = line + [pad] * (count - len(line))
        table.append([piece for piece, _ in line] + [shard for _, shard in line])
    return np.array(table, np.int32), count


def project_kernel(
    count, carries, final, shards, steps, base, members, place_ref, lengths_ref, *refs
):
    pieces, refs = refs[:count], refs[count:]
    gain_ref, query_ref, key_ref, value_ref = refs[:4]
    refs = refs[4:]
    if carries:
        sums_in, squares_in = refs[:2]
        refs = refs[2:]
    frequency_ref, refs = refs[0], refs[1:]
    if final:
        out_ref, refs = refs[0], refs[1:]
    sums, squares, chosen = refs
    visit, step = pl.program_id(0), pl.program_id(1)
    visits = pl.num_programs(0)
    rows, depth = chosen.shape
    piece = place_ref[visit]

    @pl.when((visit == 0) & (step == 0))
    def _():
        sums[...] = sums_in[...] if carries else jnp.zeros_like(sums)
        squares[...] = squares_in[...] if carries else jnp.zeros_like(squares)

    for index in range(count):

        @pl.when(piece == index)
        def _():
            columns = pl.ds(pl.multiple_of(step * depth, depth), depth)
            chosen[...] = pieces[index][:, columns]

    @pl.when(piece >= 0)
    def _():
        wide = chosen[...].astype(F32)
        square = wide * wide
        part = square[:, :128]
        for at in range(128, depth, 128):
            part = part + square[:, at : at + 128]
        squares[...] += part
        scaled = (wide * gain_ref[...]).astype(BF16)
        at = 0
        for weight in (query_ref, key_ref, value_ref):
            columns = slice(at, at + weight.shape[1])
            sums[:, columns] += jnp.dot(scaled, weight[...], preferred_element_type=F32)
            at += weight.shape[1]

    if final:

        @pl.when((visit == visits - 1) & (step == steps - 1))
        def _():
            me = lax.axis_index("req")
            number = base + me * rows + iota((rows, HEAD_SIZE), 0)
            start = jnp.zeros((rows, HEAD_SIZE), jnp.int32)
            before = jnp.int32(0)
            for other in range(members):
                before = before + lengths_ref[other]
                start = jnp.where(number >= before, before, start)
            angle = (number - start).astype(F32) * frequency_ref[...]
            cosine, sine = jnp.cos(angle), jnp.sin(angle)
            sine = jnp.where(iota((rows, HEAD_SIZE), 1) < HEAD_SIZE // 2, -sine, sine)
            mean = jnp.sum(squares[...], axis=1, keepdims=True) / (shards * steps * depth)
            scale = lax.rsqrt(mean + 1e-05)
            turned = query_ref.shape[1] + key_ref.shape[1]
            for at in range(0, sums.shape[1], HEAD_SIZE):
                columns = slice(at, at + HEAD_SIZE)
                head = sums[:, columns] * scale
                if at < turned:
                    head = head * cosine + pltpu.roll(head, HEAD_SIZE // 2, 1) * sine
                out_ref[:, columns] = head.astype(BF16)


def project(final, shards, base, place, visits, lengths, pieces, gain, weights, carried, frequency):
    rows, width = pieces[0].shape
    depth = min(DEPTH, width)
    steps = width // depth
    columns = sum(weight.shape[1] for weight in weights)

    def block_of(visit, step, place_ref):
        step = jnp.where(place_ref[visit] < 0, steps - 1, step)
        return place_ref[visits + visit] * steps + step

    def whole(shape):
        return pl.BlockSpec(shape, lambda visit, step, place_ref, lengths_ref: (0, 0))

    def deep(block, dimension):
        def where(visit, step, place_ref, lengths_ref):
            at = block_of(visit, step, place_ref)
            return (at, 0) if dimension == 0 else (0, at)

        return pl.BlockSpec(block, where)

    operands = [*pieces, gain, *weights, *carried, frequency]
    in_specs = [whole((rows, width)) for _ in pieces]
    in_specs += [deep((1, depth), 1)]
    in_specs += [deep((depth, weight.shape[1]), 0) for weight in weights]
    in_specs += [whole(leaf.shape) for leaf in carried]
    in_specs += [whole((1, HEAD_SIZE))]
    scratch = [pltpu.VMEM((rows, depth), BF16)]
    if final:
        out_shape = [jax.ShapeDtypeStruct((rows, columns), BF16)]
        scratch = [pltpu.VMEM((rows, columns), F32), pltpu.VMEM((rows, 128), F32), *scratch]
    else:
        out_shape = [
            jax.ShapeDtypeStruct((rows, columns), F32),
            jax.ShapeDtypeStruct((rows, 128), F32),
        ]
    return pl.pallas_call(
        functools.partial(
            project_kernel,
            len(pieces),
            bool(carried),
            final,
            shards,
            steps,
            base,
            lengths.shape[0],
        ),
        grid_spec=pltpu.PrefetchScalarGridSpec(
            num_scalar_prefetch=2,
            grid=(visits, steps),
            in_specs=in_specs,
            out_specs=[whole(leaf.shape) for leaf in out_shape],
            scratch_shapes=scratch,
        ),
        out_shape=out_shape,
        compiler_params=pltpu.CompilerParams(vmem_limit_bytes=VMEM_LIMIT),
        cost_estimate=pl.CostEstimate(
            flops=2 * rows * width * columns * visits,
            bytes_accessed=2 * width * columns * visits + 8 * rows * columns,
            transcendentals=0,
        ),
        name="project",
    )(place, lengths, *operands)


def attend_kernel(chips, bases, sizes, query_width, key_width, lengths_ref, plan_ref, *refs):
    blocks, (attended_ref, cache_ref, rows_ref, sems) = refs[:-4], refs[-4:]
    workers = 2 * chips
    me = lax.axis_index("req")
    chip, core = lax.div(me, 2), lax.rem(me, 2)
    slots = cache_ref.shape[1]
    spans = slots // SPAN
    total = workers * sum(sizes)
    copies = []
    for chunk, (base, rows) in enumerate(zip(bases, sizes)):
        for hop in range(chips):
            source = lax.rem(chip - hop + chips, chips) * 2
            for twin in range(2):
                owner = source + (core if twin == 0 else 1 - core)
                index = (chunk * chips + hop) * 2 + twin
                at = pl.multiple_of(base + owner * rows, ALIGN)
                copies.append(
                    pltpu.make_async_copy(
                        blocks[index], rows_ref.at[pl.ds(at, rows), :], sems.at[index]
                    )
                )
    for copy in copies:
        copy.start()
    pad = rows_ref.shape[0] - total
    rows_ref[total:, :] = jnp.zeros((pad, rows_ref.shape[1]), BF16)
    for copy in copies:
        copy.wait()

    def aligned(row):
        first = pl.multiple_of(lax.div(row, ALIGN) * ALIGN, ALIGN)
        return first, row - first

    start, length = run_of(lengths_ref, me, workers)
    first, shift = aligned(start)
    reach = slots + SPAN
    row, column = iota((slots, reach), 0), iota((slots, reach), 1)
    hot = ((column == row + shift) & (row < length)).astype(BF16)
    for half in range(2):
        window = rows_ref[
            pl.ds(first, reach),
            query_width + half * key_width : query_width + (half + 1) * key_width,
        ]
        cache_ref[half] = jnp.dot(hot, window, preferred_element_type=F32).astype(BF16)

    heads, key_heads = query_width // HEAD_SIZE, key_width // HEAD_SIZE
    group = heads // key_heads
    factor = math.log2(math.e) / math.sqrt(HEAD_SIZE)
    for slot in range(spans):
        span = plan_ref[me * spans + slot]
        source = lax.div(span, spans)
        part = lax.rem(span, spans)
        start, length = run_of(lengths_ref, source, workers)
        offset = part * SPAN
        out_rows = slice(slot * SPAN, (slot + 1) * SPAN)
        dead = offset >= length

        @pl.when(dead)
        def _():
            attended_ref[out_rows, :] = jnp.zeros((SPAN, query_width), BF16)

        for count in range(1, spans + 1):

            @pl.when(jnp.logical_not(dead) & (part == count - 1))
            def _():
                first, shift = aligned(start + offset)
                hot = iota((SPAN, 2 * SPAN), 1) == iota((SPAN, 2 * SPAN), 0) + shift
                queries = jnp.dot(
                    hot.astype(BF16),
                    rows_ref[pl.ds(first, 2 * SPAN), :query_width],
                    preferred_element_type=F32,
                ).astype(BF16)
                reach = (count + 1) * SPAN
                first, shift = aligned(start)
                key_pos = iota((SPAN, reach), 1) - shift
                query_pos = (count - 1) * SPAN + iota((SPAN, reach), 0)
                allowed = (key_pos >= 0) & (key_pos <= query_pos) & (key_pos < length)
                bias = jnp.where(allowed, 0.0, -1e30)
                bias = jnp.concatenate([bias] * group, axis=0)
                live = (count - 1) * SPAN + iota((SPAN, HEAD_SIZE), 0) < length
                for head in range(key_heads):
                    stacked = jnp.concatenate(
                        [
                            queries[:, at * HEAD_SIZE : (at + 1) * HEAD_SIZE]
                            for at in range(head * group, (head + 1) * group)
                        ],
                        axis=0,
                    )
                    left = query_width + head * HEAD_SIZE
                    keys = rows_ref[pl.ds(first, reach), left : left + HEAD_SIZE]
                    left += key_width
                    values = rows_ref[pl.ds(first, reach), left : left + HEAD_SIZE]
                    scores = lax.dot_general(
                        stacked, keys, (((1,), (1,)), ((), ())), preferred_element_type=F32
                    )
                    scores = scores + bias
                    top = jnp.max(scores, axis=1, keepdims=True)
                    weights = jnp.exp2((scores - top) * factor)
                    norm = jnp.sum(weights, axis=1, keepdims=True)
                    mixed = jnp.dot(weights.astype(BF16), values, preferred_element_type=F32)
                    mixed = mixed / norm
                    for at in range(group):
                        left = (head * group + at) * HEAD_SIZE
                        attended_ref[out_rows, left : left + HEAD_SIZE] = jnp.where(
                            live, mixed[at * SPAN : (at + 1) * SPAN], 0.0
                        ).astype(BF16)


def attend(chips, bases, sizes, query_width, key_width, slots, lengths, plan, blocks):
    width = query_width + 2 * key_width
    total = 2 * chips * sum(sizes)
    return pl.pallas_call(
        functools.partial(attend_kernel, chips, bases, sizes, query_width, key_width),
        in_specs=[pl.BlockSpec(memory_space=pltpu.SMEM)] * 2
        + [pl.BlockSpec(memory_space=pl.ANY)] * len(blocks),
        out_specs=[pl.BlockSpec(memory_space=pltpu.VMEM)] * 2,
        out_shape=[
            jax.ShapeDtypeStruct((slots, query_width), BF16),
            jax.ShapeDtypeStruct((2, slots, key_width), BF16),
        ],
        scratch_shapes=[
            pltpu.VMEM((total + slots + SPAN, width), BF16),
            pltpu.SemaphoreType.DMA((len(blocks),)),
        ],
        compiler_params=pltpu.CompilerParams(vmem_limit_bytes=VMEM_LIMIT),
        name="attend",
    )(lengths, plan, *blocks)


def shift_chips(value, hop, chips):
    pairs = [(2 * x + c, 2 * ((x + hop) % chips) + c) for x in range(chips) for c in range(2)]
    return lax.ppermute(value, "req", pairs)


def swap_cores(value, chips):
    return lax.ppermute(value, "req", [(d, d ^ 1) for d in range(2 * chips)])


def local(
    chips, shards, tokens, norm_gain, w_query, key_weight, value_weight, lengths, plan
):
    workers = 2 * chips
    slots = tokens.shape[0]
    live = slots // 2
    sizes = [live * share // sum(SHARES) // ALIGN * ALIGN for share in SHARES]
    sizes[-1] = live - sum(sizes[:-1])
    bases = [workers * sum(sizes[:chunk]) for chunk in range(len(sizes))]
    weights = (w_query, key_weight, value_weight)
    gain = norm_gain.astype(F32).reshape(1, -1)
    halfway = HEAD_SIZE // 2
    frequency = np.exp(-np.arange(halfway) * 2.0 / HEAD_SIZE * math.log(500000.0))
    frequency = jnp.asarray(np.tile(frequency, 2)[None, :], F32)

    twin = swap_cores(tokens, chips)
    dealt = [
        *deal(chips, bases[:1], sizes[:1], lengths, tokens, twin),
        *deal(chips, bases[1:], sizes[1:], lengths, tokens, twin),
    ]
    homes, aways = dealt[::2], dealt[1::2]
    held = []
    for chunk in range(len(sizes)):
        arrived = [shift_chips(aways[chunk][hop - 1], hop, chips) for hop in range(1, chips)]
        later = aways[chunk + 1] if chunk + 1 < len(sizes) else None
        block, later = merge(homes[chunk], arrived, later)
        if later is not None:
            aways[chunk + 1] = later
        held.append(block)

    routes, owned, depth = routes_of(shards)
    lines = []
    for block in held:
        line = [block]
        for source, pairs in routes:
            line.append(lax.ppermute(line[source + 1], "tp", pairs))
        lines.append(line)

    early = [piece for piece in range(len(owned)) if depth[piece] < max(depth)]
    late = [piece for piece in range(len(owned)) if depth[piece] == max(depth)]
    tables, counts = zip(
        *(
            visits_of([owned[piece] for piece in group], shards)
            for group in (range(len(owned)), early, late)
        )
    )
    table = jnp.asarray(np.concatenate(tables, axis=1))
    table = lax.dynamic_index_in_dim(table, lax.axis_index("tp"), 0, keepdims=False)
    places = [
        table[2 * sum(counts[:at]) : 2 * sum(counts[: at + 1])] for at in range(3)
    ]

    blocks = []
    for chunk, (base, line) in enumerate(zip(bases, lines)):
        common = (gain, weights)
        if chunk + 1 < len(sizes):
            (block,) = project(
                True, shards, base, places[0], counts[0], lengths, line, *common, (), frequency
            )
        else:
            pieces = [line[piece] for piece in early]
            carried = project(
                False, shards, base, places[1], counts[1], lengths, pieces, *common, (), frequency
            )
            pieces = [line[piece] for piece in late]
            (block,) = project(
                True,
                shards,
                base,
                places[2],
                counts[2],
                lengths,
                pieces,
                *common,
                carried,
                frequency,
            )
        here = [block] + [shift_chips(block, hop, chips) for hop in range(1, chips)]
        for piece in here:
            blocks += [piece, swap_cores(piece, chips)]
    return tuple(
        attend(
            chips,
            bases,
            sizes,
            w_query.shape[1],
            key_weight.shape[1],
            slots,
            lengths,
            plan,
            blocks,
        )
    )


def solution(mesh):
    placed = (
        P(("groups", "req"), "tp"),
        P(),
        P(None, "tp"),
        P(None, "tp"),
        P(None, "tp"),
        P("groups"),
        P("groups"),
    )
    return jax.shard_map(
        functools.partial(local, mesh.shape["req"] // 2, mesh.shape["tp"]),
        mesh=mesh,
        in_specs=placed,
        out_specs=(P(("groups", "req"), "tp"), P(None, ("groups", "req"), "tp")),
        check_vma=False,
    )
```

```python
import functools
import math

import jax
import jax.numpy as jnp
import numpy as np
from jax import lax
from jax.experimental import pallas as pl
from jax.experimental.pallas import tpu as pltpu
from jax.sharding import PartitionSpec as P

HEAD_SIZE = 128
SPAN = 128
ALIGN = 16
SHARES = (4, 4, 8)
GROUPS = ((0, 1), (2,))
DEPTH = 1024
MEBI = 1024 * 1024
F32, BF16 = jnp.float32, jnp.bfloat16


def run_of(lengths_ref, request, count):
    start = jnp.int32(0)
    length = jnp.int32(0)
    for other in range(count):
        amount = lengths_ref[other]
        start = start + jnp.where(other < request, amount, 0)
        length = jnp.where(other == request, amount, length)
    return start, length


def iota(shape, dimension):
    return lax.broadcasted_iota(jnp.int32, shape, dimension)


def deal_kernel(chips, bases, sizes, twins, lengths_ref, *refs):
    me = lax.axis_index("req")
    chip, core = lax.div(me, 2), lax.rem(me, 2)
    sources, refs = refs[: len(twins)], refs[len(twins) :]
    count = 2 * len(sizes)
    priors, out_refs = refs[:-count], refs[-count:]
    requests = [me + 1 - 2 * core if twin else me for twin in twins]
    runs = [run_of(lengths_ref, request, 2 * chips) for request in requests]
    slots = sources[0].shape[0]
    for chunk, (base, rows) in enumerate(zip(bases, sizes)):
        home_ref, away_ref = out_refs[2 * chunk : 2 * chunk + 2]
        for hop in range(chips):
            target = lax.rem(chip + hop, chips) * 2 + core
            number = base + target * rows + iota((rows, slots), 0)
            slot = iota((rows, slots), 1)
            total = None
            for (start, length), source in zip(runs, sources):
                hot = ((number - start == slot) & (slot < length)).astype(BF16)
                part = jnp.dot(hot, source[...], preferred_element_type=F32)
                total = part if total is None else total + part
            total = total.astype(BF16)
            if hop == 0:
                home_ref[...] = total + priors[2 * chunk][...] if priors else total
            elif priors:
                away_ref[hop - 1] = total + priors[2 * chunk + 1][hop - 1]
            else:
                away_ref[hop - 1] = total


def deal(chips, bases, sizes, lengths, sources, twins, priors=()):
    slots, width = sources[0].shape
    block = min(1024, width)
    out_specs, out_shape = [], []
    for rows in sizes:
        out_specs += [
            pl.BlockSpec((rows, block), lambda i: (0, i)),
            pl.BlockSpec((chips - 1, rows, block), lambda i: (0, 0, i)),
        ]
        out_shape += [
            jax.ShapeDtypeStruct((rows, width), BF16),
            jax.ShapeDtypeStruct((chips - 1, rows, width), BF16),
        ]
    return pl.pallas_call(
        functools.partial(deal_kernel, chips, bases, sizes, twins),
        grid=(width // block,),
        in_specs=[pl.BlockSpec(memory_space=pltpu.SMEM)]
        + [pl.BlockSpec((slots, block), lambda i: (0, i)) for _ in sources]
        + (out_specs if priors else []),
        out_specs=out_specs,
        out_shape=out_shape,
        compiler_params=pltpu.CompilerParams(vmem_limit_bytes=24 * MEBI),
        cost_estimate=pl.CostEstimate(
            flops=2 * len(sources) * chips * sum(sizes) * slots * width,
            bytes_accessed=2 * len(sources) * slots * width + 2 * chips * sum(sizes) * width,
            transcendentals=0,
        ),
        name="deal",
    )(lengths, *sources, *priors)


def merge_kernel(count, home_ref, *refs):
    total = home_ref[...]
    for ref in refs[:count]:
        total = total + ref[...]
    passed = (len(refs) - count - 1) // 2
    refs[count + passed][...] = total


def merge(home, arrived, later):
    count = len(arrived)
    vmem, anywhere = pl.BlockSpec(memory_space=pltpu.VMEM), pl.BlockSpec(memory_space=pl.ANY)
    block, *later = pl.pallas_call(
        functools.partial(merge_kernel, count),
        in_specs=[vmem] * (count + 1) + [anywhere] * len(later),
        out_specs=[vmem] + [anywhere] * len(later),
        out_shape=[jax.ShapeDtypeStruct(leaf.shape, leaf.dtype) for leaf in (home, *later)],
        input_output_aliases={count + 1 + at: 1 + at for at in range(len(later))},
        compiler_params=pltpu.CompilerParams(vmem_limit_bytes=8 * MEBI),
        cost_estimate=pl.CostEstimate(
            flops=home.size, bytes_accessed=2 * home.size * (count + 2), transcendentals=0
        ),
        name="merge",
    )(home, *arrived, *later)
    return block, later


def routes_of(shards):
    if shards == 4:
        routes = [
            (-1, [(0, 1), (1, 0), (2, 3), (3, 2)]),
            (-1, [(1, 2), (2, 1)]),
            (-1, [(0, 2), (1, 3), (2, 0), (3, 1)]),
            (2, [(2, 3), (1, 0)]),
        ]
    else:
        routes = []
        for step in range(1, shards):
            source = len(routes) - 2 if step > 1 else -1
            routes.append((source, [(at, at + 1) for at in range(step - 1, shards - 1)]))
            source = len(routes) - 2 if step > 1 else -1
            routes.append((source, [(at, at - 1) for at in range(1, shards - step + 1)]))
    held, depth = [list(range(shards))], [0]
    for source, pairs in routes:
        now = [-1] * shards
        for start, end in pairs:
            now[end] = held[source + 1][start]
        held.append(now)
        depth.append(depth[source + 1] + 1)
    return routes, held, depth


def visits_of(held, shards):
    visits = [
        [(piece, now[at]) for piece, now in enumerate(held) if now[at] >= 0]
        for at in range(shards)
    ]
    count = max(len(line) for line in visits)
    table = []
    for line in visits:
        pad = (-1, line[-1][1] if line else 0)
        line = line + [pad] * (count - len(line))
        table.append([piece for piece, _ in line] + [shard for _, shard in line])
    return np.array(table, np.int32), count


def project_kernel(
    count, carries, final, shards, steps, bases, sizes, members, place_ref, lengths_ref, *refs
):
    pieces, refs = refs[: count * len(sizes)], refs[count * len(sizes) :]
    gain_ref, query_ref, key_ref, value_ref = refs[:4]
    refs = refs[4:]
    if carries:
        sums_in, squares_in = refs[:2]
        refs = refs[2:]
    frequency_ref, refs = refs[0], refs[1:]
    if final:
        out_ref, refs = refs[0], refs[1:]
    sums, squares, chosen = refs
    visit, step = pl.program_id(0), pl.program_id(1)
    visits = pl.num_programs(0)
    rows, depth = chosen.shape
    piece = place_ref[visit]

    @pl.when((visit == 0) & (step == 0))
    def _():
        sums[...] = sums_in[...] if carries else jnp.zeros_like(sums)
        squares[...] = squares_in[...] if carries else jnp.zeros_like(squares)

    for index in range(count):

        @pl.when(piece == index)
        def _():
            columns = pl.ds(pl.multiple_of(step * depth, depth), depth)
            at = 0
            for chunk, size in enumerate(sizes):
                chosen[at : at + size, :] = pieces[chunk * count + index][:, columns]
                at += size

    @pl.when(piece >= 0)
    def _():
        wide = chosen[...].astype(F32)
        square = wide * wide
        part = square[:, :128]
        for at in range(128, depth, 128):
            part = part + square[:, at : at + 128]
        squares[...] += part
        scaled = (wide * gain_ref[...]).astype(BF16)
        at = 0
        for weight in (query_ref, key_ref, value_ref):
            columns = slice(at, at + weight.shape[1])
            sums[:, columns] += jnp.dot(scaled, weight[...], preferred_element_type=F32)
            at += weight.shape[1]

    if final:

        @pl.when((visit == visits - 1) & (step == steps - 1))
        def _():
            me = lax.axis_index("req")
            number = jnp.concatenate(
                [
                    base + me * size + iota((size, HEAD_SIZE), 0)
                    for base, size in zip(bases, sizes)
                ],
                axis=0,
            )
            start = jnp.zeros((rows, HEAD_SIZE), jnp.int32)
            before = jnp.int32(0)
            for other in range(members):
                before = before + lengths_ref[other]
                start = jnp.where(number >= before, before, start)
            angle = (number - start).astype(F32) * frequency_ref[...]
            cosine, sine = jnp.cos(angle), jnp.sin(angle)
            sine = jnp.where(iota((rows, HEAD_SIZE), 1) < HEAD_SIZE // 2, -sine, sine)
            mean = jnp.sum(squares[...], axis=1, keepdims=True) / (shards * steps * depth)
            scale = lax.rsqrt(mean + 1e-05)
            turned = query_ref.shape[1] + key_ref.shape[1]
            for at in range(0, sums.shape[1], HEAD_SIZE):
                columns = slice(at, at + HEAD_SIZE)
                head = sums[:, columns] * scale
                if at < turned:
                    head = head * cosine + pltpu.roll(head, HEAD_SIZE // 2, 1) * sine
                out_ref[:, columns] = head.astype(BF16)


def project(
    final, shards, bases, sizes, place, visits, lengths, lines, gain, weights, carried, frequency
):
    pieces = [piece for line in lines for piece in line]
    rows, width = sum(sizes), pieces[0].shape[1]
    depth = min(DEPTH, width)
    steps = width // depth
    columns = sum(weight.shape[1] for weight in weights)

    def block_of(visit, step, place_ref):
        step = jnp.where(place_ref[visit] < 0, steps - 1, step)
        return place_ref[visits + visit] * steps + step

    def whole(shape):
        return pl.BlockSpec(shape, lambda visit, step, place_ref, lengths_ref: (0, 0))

    def deep(block, dimension):
        def where(visit, step, place_ref, lengths_ref):
            at = block_of(visit, step, place_ref)
            return (at, 0) if dimension == 0 else (0, at)

        return pl.BlockSpec(block, where)

    operands = [*pieces, gain, *weights, *carried, frequency]
    in_specs = [whole(piece.shape) for piece in pieces]
    in_specs += [deep((1, depth), 1)]
    in_specs += [deep((depth, weight.shape[1]), 0) for weight in weights]
    in_specs += [whole(leaf.shape) for leaf in carried]
    in_specs += [whole((1, HEAD_SIZE))]
    scratch = [pltpu.VMEM((rows, depth), BF16)]
    if final:
        out_shape = [jax.ShapeDtypeStruct((rows, columns), BF16)]
        scratch = [pltpu.VMEM((rows, columns), F32), pltpu.VMEM((rows, 128), F32), *scratch]
    else:
        out_shape = [
            jax.ShapeDtypeStruct((rows, columns), F32),
            jax.ShapeDtypeStruct((rows, 128), F32),
        ]
    return pl.pallas_call(
        functools.partial(
            project_kernel,
            len(lines[0]),
            bool(carried),
            final,
            shards,
            steps,
            bases,
            sizes,
            lengths.shape[0],
        ),
        grid_spec=pltpu.PrefetchScalarGridSpec(
            num_scalar_prefetch=2,
            grid=(visits, steps),
            in_specs=in_specs,
            out_specs=[whole(leaf.shape) for leaf in out_shape],
            scratch_shapes=scratch,
        ),
        out_shape=out_shape,
        compiler_params=pltpu.CompilerParams(vmem_limit_bytes=32 * MEBI),
        cost_estimate=pl.CostEstimate(
            flops=2 * rows * width * columns * visits,
            bytes_accessed=2 * width * columns * visits + 8 * rows * columns,
            transcendentals=0,
        ),
        name="project",
    )(place, lengths, *operands)


def attend_kernel(chips, groups, query_width, key_width, lengths_ref, plan_ref, *refs):
    blocks, (attended_ref, cache_ref, rows_ref, sems) = refs[:-4], refs[-4:]
    workers = 2 * chips
    me = lax.axis_index("req")
    chip, core = lax.div(me, 2), lax.rem(me, 2)
    slots = cache_ref.shape[1]
    spans = slots // SPAN
    total = workers * sum(sum(sizes) for _, sizes in groups)
    copies = []
    for group, (bases, sizes) in enumerate(groups):
        for hop in range(chips):
            source = lax.rem(chip - hop + chips, chips) * 2
            for twin in range(2):
                owner = source + (core if twin == 0 else 1 - core)
                block = blocks[(group * chips + hop) * 2 + twin]
                first = 0
                for base, rows in zip(bases, sizes):
                    at = pl.multiple_of(base + owner * rows, ALIGN)
                    copies.append(
                        pltpu.make_async_copy(
                            block.at[pl.ds(first, rows), :],
                            rows_ref.at[pl.ds(at, rows), :],
                            sems.at[len(copies)],
                        )
                    )
                    first += rows
    for copy in copies:
        copy.start()
    pad = rows_ref.shape[0] - total
    rows_ref[total:, :] = jnp.zeros((pad, rows_ref.shape[1]), BF16)
    for copy in copies:
        copy.wait()

    def aligned(row):
        first = pl.multiple_of(lax.div(row, ALIGN) * ALIGN, ALIGN)
        return first, row - first

    start, length = run_of(lengths_ref, me, workers)
    first, shift = aligned(start)
    reach = slots + SPAN
    row, column = iota((slots, reach), 0), iota((slots, reach), 1)
    hot = ((column == row + shift) & (row < length)).astype(BF16)
    for half in range(2):
        window = rows_ref[
            pl.ds(first, reach),
            query_width + half * key_width : query_width + (half + 1) * key_width,
        ]
        cache_ref[half] = jnp.dot(hot, window, preferred_element_type=F32).astype(BF16)

    heads, key_heads = query_width // HEAD_SIZE, key_width // HEAD_SIZE
    group = heads // key_heads
    factor = math.log2(math.e) / math.sqrt(HEAD_SIZE)
    for slot in range(spans):
        span = plan_ref[me * spans + slot]
        source = lax.div(span, spans)
        part = lax.rem(span, spans)
        start, length = run_of(lengths_ref, source, workers)
        offset = part * SPAN
        out_rows = slice(slot * SPAN, (slot + 1) * SPAN)
        dead = offset >= length

        @pl.when(dead)
        def _():
            attended_ref[out_rows, :] = jnp.zeros((SPAN, query_width), BF16)

        for count in range(1, spans + 1):

            @pl.when(jnp.logical_not(dead) & (part == count - 1))
            def _():
                first, shift = aligned(start + offset)
                hot = iota((SPAN, 2 * SPAN), 1) == iota((SPAN, 2 * SPAN), 0) + shift
                queries = jnp.dot(
                    hot.astype(BF16),
                    rows_ref[pl.ds(first, 2 * SPAN), :query_width],
                    preferred_element_type=F32,
                ).astype(BF16)
                reach = (count + 1) * SPAN
                first, shift = aligned(start)
                key_pos = iota((SPAN, reach), 1) - shift
                query_pos = (count - 1) * SPAN + iota((SPAN, reach), 0)
                allowed = (key_pos >= 0) & (key_pos <= query_pos) & (key_pos < length)
                bias = jnp.where(allowed, 0.0, -1e30)
                bias = jnp.concatenate([bias] * group, axis=0)
                live = (count - 1) * SPAN + iota((SPAN, HEAD_SIZE), 0) < length
                for head in range(key_heads):
                    stacked = jnp.concatenate(
                        [
                            queries[:, at * HEAD_SIZE : (at + 1) * HEAD_SIZE]
                            for at in range(head * group, (head + 1) * group)
                        ],
                        axis=0,
                    )
                    left = query_width + head * HEAD_SIZE
                    keys = rows_ref[pl.ds(first, reach), left : left + HEAD_SIZE]
                    left += key_width
                    values = rows_ref[pl.ds(first, reach), left : left + HEAD_SIZE]
                    scores = lax.dot_general(
                        stacked, keys, (((1,), (1,)), ((), ())), preferred_element_type=F32
                    )
                    scores = scores + bias
                    top = jnp.max(scores, axis=1, keepdims=True)
                    weights = jnp.exp2((scores - top) * factor)
                    norm = jnp.sum(weights, axis=1, keepdims=True)
                    mixed = jnp.dot(weights.astype(BF16), values, preferred_element_type=F32)
                    mixed = mixed / norm
                    for at in range(group):
                        left = (head * group + at) * HEAD_SIZE
                        attended_ref[out_rows, left : left + HEAD_SIZE] = jnp.where(
                            live, mixed[at * SPAN : (at + 1) * SPAN], 0.0
                        ).astype(BF16)


def attend(chips, groups, query_width, key_width, slots, lengths, plan, blocks):
    width = query_width + 2 * key_width
    total = 2 * chips * sum(sum(sizes) for _, sizes in groups)
    copies = 2 * chips * sum(len(sizes) for _, sizes in groups)
    return pl.pallas_call(
        functools.partial(attend_kernel, chips, groups, query_width, key_width),
        in_specs=[pl.BlockSpec(memory_space=pltpu.SMEM)] * 2
        + [pl.BlockSpec(memory_space=pl.ANY)] * len(blocks),
        out_specs=[pl.BlockSpec(memory_space=pltpu.VMEM)] * 2,
        out_shape=[
            jax.ShapeDtypeStruct((slots, query_width), BF16),
            jax.ShapeDtypeStruct((2, slots, key_width), BF16),
        ],
        scratch_shapes=[
            pltpu.VMEM((total + slots + SPAN, width), BF16),
            pltpu.SemaphoreType.DMA((copies,)),
        ],
        compiler_params=pltpu.CompilerParams(vmem_limit_bytes=32 * MEBI),
        name="attend",
    )(lengths, plan, *blocks)


def shift_chips(value, hop, chips):
    pairs = [(2 * x + c, 2 * ((x + hop) % chips) + c) for x in range(chips) for c in range(2)]
    return lax.ppermute(value, "req", pairs)


def swap_cores(value, chips):
    return lax.ppermute(value, "req", [(d, d ^ 1) for d in range(2 * chips)])


def local(
    chips, shards, tokens, norm_gain, w_query, key_weight, value_weight, lengths, plan
):
    workers = 2 * chips
    slots = tokens.shape[0]
    live = slots // 2
    sizes = [live * share // sum(SHARES) // ALIGN * ALIGN for share in SHARES]
    sizes[-1] = live - sum(sizes[:-1])
    bases = [workers * sum(sizes[:chunk]) for chunk in range(len(sizes))]
    weights = (w_query, key_weight, value_weight)
    gain = norm_gain.astype(F32).reshape(1, -1)
    halfway = HEAD_SIZE // 2
    frequency = np.exp(-np.arange(halfway) * 2.0 / HEAD_SIZE * math.log(500000.0))
    frequency = jnp.asarray(np.tile(frequency, 2)[None, :], F32)

    twin = swap_cores(tokens, chips)
    first = deal(chips, bases[:1], sizes[:1], lengths, [tokens], [False])
    dealt = [
        *deal(chips, bases[:1], sizes[:1], lengths, [twin], [True], first),
        *deal(chips, bases[1:], sizes[1:], lengths, [tokens, twin], [False, True]),
    ]
    homes, aways = dealt[::2], dealt[1::2]
    routes, owned, depth = routes_of(shards)
    early = [piece for piece in range(len(owned)) if depth[piece] < max(depth)]
    late = [piece for piece in range(len(owned)) if depth[piece] == max(depth)]
    direct = [piece for piece in range(len(owned)) if depth[piece] == 1]
    relayed = {source + 1 for source, _ in routes} - {0}

    lines = []
    for chunk in range(len(sizes)):
        arrived = [shift_chips(aways[chunk][hop - 1], hop, chips) for hop in range(1, chips)]
        places = [(chunk - 1, piece) for piece in direct if piece not in relayed]
        places += [(chunk - 2, piece) for piece in direct if piece in relayed]
        places = [(at, piece) for at, piece in places if at >= 0]
        later = aways[chunk + 1 : chunk + 2] + [lines[at][piece] for at, piece in places]
        block, later = merge(homes[chunk], arrived, later)
        if chunk + 1 < len(sizes):
            aways[chunk + 1] = later.pop(0)
        for (at, piece), leaf in zip(places, later):
            lines[at][piece] = leaf
        line = {0: block}
        for index, (source, pairs) in enumerate(routes):
            if index + 1 in direct:
                line[index + 1] = lax.ppermute(block, "tp", pairs)
        lines.append(line)
    for line in lines:
        for index, (source, pairs) in enumerate(routes):
            if index + 1 not in direct:
                line[index + 1] = lax.ppermute(line[source + 1], "tp", pairs)

    tables, counts = zip(
        *(visits_of([owned[piece] for piece in group], shards) for group in (early, late))
    )
    table = jnp.asarray(np.concatenate(tables, axis=1))
    table = lax.dynamic_index_in_dim(table, lax.axis_index("tp"), 0, keepdims=False)
    places = table[: 2 * counts[0]], table[2 * counts[0] :]

    blocks, groups = [], []
    for chunks in GROUPS:
        span = [bases[chunk] for chunk in chunks], [sizes[chunk] for chunk in chunks]
        groups.append(span)
        carried = ()
        for place, count, chosen in zip(places, counts, (early, late)):
            carried = project(
                chosen is late,
                shards,
                *span,
                place,
                count,
                lengths,
                [[lines[chunk][piece] for piece in chosen] for chunk in chunks],
                gain,
                weights,
                carried,
                frequency,
            )
        block = carried[0]
        here = [block] + [shift_chips(block, hop, chips) for hop in range(1, chips)]
        for piece in here:
            blocks += [piece, swap_cores(piece, chips)]
    return tuple(
        attend(
            chips,
            groups,
            w_query.shape[1],
            key_weight.shape[1],
            slots,
            lengths,
            plan,
            blocks,
        )
    )


def solution(mesh):
    placed = (
        P(("groups", "req"), "tp"),
        P(),
        P(None, "tp"),
        P(None, "tp"),
        P(None, "tp"),
        P("groups"),
        P("groups"),
    )
    return jax.shard_map(
        functools.partial(local, mesh.shape["req"] // 2, mesh.shape["tp"]),
        mesh=mesh,
        in_specs=placed,
        out_specs=(P(("groups", "req"), "tp"), P(None, ("groups", "req"), "tp")),
        check_vma=False,
    )
```

```python
import functools
import math

import jax
import jax.numpy as jnp
import numpy as np
from jax import lax
from jax.experimental import pallas as pl
from jax.experimental.pallas import tpu as pltpu
from jax.sharding import PartitionSpec as P

HEAD_SIZE = 128
SPAN = 128
ALIGN = 16
SHARES = (4, 6, 6)
GROUPS = ((0, 1), (2,))
DEPTH = 1024
MEBI = 1024 * 1024
F32, BF16 = jnp.float32, jnp.bfloat16


def run_of(lengths_ref, request, count):
    start = jnp.int32(0)
    length = jnp.int32(0)
    for other in range(count):
        amount = lengths_ref[other]
        start = start + jnp.where(other < request, amount, 0)
        length = jnp.where(other == request, amount, length)
    return start, length


def iota(shape, dimension):
    return lax.broadcasted_iota(jnp.int32, shape, dimension)


def deal_kernel(chips, bases, sizes, twins, lengths_ref, *refs):
    me = lax.axis_index("req")
    chip, core = lax.div(me, 2), lax.rem(me, 2)
    sources, refs = refs[: len(twins)], refs[len(twins) :]
    count = 2 * len(sizes)
    priors, out_refs = refs[:-count], refs[-count:]
    requests = [me + 1 - 2 * core if twin else me for twin in twins]
    runs = [run_of(lengths_ref, request, 2 * chips) for request in requests]
    slots = sources[0].shape[0]
    for chunk, (base, rows) in enumerate(zip(bases, sizes)):
        home_ref, away_ref = out_refs[2 * chunk : 2 * chunk + 2]
        for hop in range(chips):
            target = lax.rem(chip + hop, chips) * 2 + core
            number = base + target * rows + iota((rows, slots), 0)
            slot = iota((rows, slots), 1)
            total = None
            for (start, length), source in zip(runs, sources):
                hot = ((number - start == slot) & (slot < length)).astype(BF16)
                part = jnp.dot(hot, source[...], preferred_element_type=F32)
                total = part if total is None else total + part
            total = total.astype(BF16)
            if hop == 0:
                home_ref[...] = total + priors[2 * chunk][...] if priors else total
            elif priors:
                away_ref[hop - 1] = total + priors[2 * chunk + 1][hop - 1]
            else:
                away_ref[hop - 1] = total


def deal(chips, bases, sizes, lengths, sources, twins, priors=()):
    slots, width = sources[0].shape
    block = min(1024, width)
    out_specs, out_shape = [], []
    for rows in sizes:
        out_specs += [
            pl.BlockSpec((rows, block), lambda i: (0, i)),
            pl.BlockSpec((chips - 1, rows, block), lambda i: (0, 0, i)),
        ]
        out_shape += [
            jax.ShapeDtypeStruct((rows, width), BF16),
            jax.ShapeDtypeStruct((chips - 1, rows, width), BF16),
        ]
    return pl.pallas_call(
        functools.partial(deal_kernel, chips, bases, sizes, twins),
        grid=(width // block,),
        in_specs=[pl.BlockSpec(memory_space=pltpu.SMEM)]
        + [pl.BlockSpec((slots, block), lambda i: (0, i)) for _ in sources]
        + (out_specs if priors else []),
        out_specs=out_specs,
        out_shape=out_shape,
        compiler_params=pltpu.CompilerParams(vmem_limit_bytes=24 * MEBI),
        cost_estimate=pl.CostEstimate(
            flops=2 * len(sources) * chips * sum(sizes) * slots * width,
            bytes_accessed=2 * len(sources) * slots * width + 2 * chips * sum(sizes) * width,
            transcendentals=0,
        ),
        name="deal",
    )(lengths, *sources, *priors)


def merge_kernel(count, home_ref, *refs):
    total = home_ref[...]
    for ref in refs[:count]:
        total = total + ref[...]
    passed = (len(refs) - count - 1) // 2
    refs[count + passed][...] = total


def merge(home, arrived, later):
    count = len(arrived)
    vmem, anywhere = pl.BlockSpec(memory_space=pltpu.VMEM), pl.BlockSpec(memory_space=pl.ANY)
    block, *later = pl.pallas_call(
        functools.partial(merge_kernel, count),
        in_specs=[vmem] * (count + 1) + [anywhere] * len(later),
        out_specs=[vmem] + [anywhere] * len(later),
        out_shape=[jax.ShapeDtypeStruct(leaf.shape, leaf.dtype) for leaf in (home, *later)],
        input_output_aliases={count + 1 + at: 1 + at for at in range(len(later))},
        compiler_params=pltpu.CompilerParams(vmem_limit_bytes=8 * MEBI),
        cost_estimate=pl.CostEstimate(
            flops=home.size, bytes_accessed=2 * home.size * (count + 2), transcendentals=0
        ),
        name="merge",
    )(home, *arrived, *later)
    return block, later


def routes_of(shards):
    if shards == 4:
        routes = [
            (-1, [(1, 2), (2, 1)]),
            (-1, [(0, 1), (1, 0), (2, 3), (3, 2)]),
            (-1, [(0, 2), (1, 3), (2, 0), (3, 1)]),
            (2, [(2, 3), (1, 0)]),
        ]
    else:
        routes = []
        for step in range(1, shards):
            source = len(routes) - 2 if step > 1 else -1
            routes.append((source, [(at, at + 1) for at in range(step - 1, shards - 1)]))
            source = len(routes) - 2 if step > 1 else -1
            routes.append((source, [(at, at - 1) for at in range(1, shards - step + 1)]))
    held, depth = [list(range(shards))], [0]
    for source, pairs in routes:
        now = [-1] * shards
        for start, end in pairs:
            now[end] = held[source + 1][start]
        held.append(now)
        depth.append(depth[source + 1] + 1)
    return routes, held, depth


def visits_of(held, shards):
    visits = [
        [(piece, now[at]) for piece, now in enumerate(held) if now[at] >= 0]
        for at in range(shards)
    ]
    count = max(len(line) for line in visits)
    table = []
    for line in visits:
        pad = (-1, line[-1][1] if line else 0)
        line = line + [pad] * (count - len(line))
        table.append([piece for piece, _ in line] + [shard for _, shard in line])
    return np.array(table, np.int32), count


def project_kernel(
    count, carries, final, shards, steps, bases, sizes, members, place_ref, lengths_ref, *refs
):
    pieces, refs = refs[: count * len(sizes)], refs[count * len(sizes) :]
    gain_ref, query_ref, key_ref, value_ref = refs[:4]
    refs = refs[4:]
    if carries:
        sums_in, squares_in = refs[:2]
        refs = refs[2:]
    frequency_ref, refs = refs[0], refs[1:]
    if final:
        out_ref, refs = refs[0], refs[1:]
    sums, squares, chosen = refs
    visit, step = pl.program_id(0), pl.program_id(1)
    visits = pl.num_programs(0)
    rows, depth = chosen.shape
    piece = place_ref[visit]

    @pl.when((visit == 0) & (step == 0))
    def _():
        sums[...] = sums_in[...] if carries else jnp.zeros_like(sums)
        squares[...] = squares_in[...] if carries else jnp.zeros_like(squares)

    for index in range(count):

        @pl.when(piece == index)
        def _():
            columns = pl.ds(pl.multiple_of(step * depth, depth), depth)
            at = 0
            for chunk, size in enumerate(sizes):
                chosen[at : at + size, :] = pieces[chunk * count + index][:, columns]
                at += size

    @pl.when(piece >= 0)
    def _():
        wide = chosen[...].astype(F32)
        square = wide * wide
        part = square[:, :128]
        for at in range(128, depth, 128):
            part = part + square[:, at : at + 128]
        squares[...] += part
        scaled = (wide * gain_ref[...]).astype(BF16)
        at = 0
        for weight in (query_ref, key_ref, value_ref):
            columns = slice(at, at + weight.shape[1])
            sums[:, columns] += jnp.dot(scaled, weight[...], preferred_element_type=F32)
            at += weight.shape[1]

    if final:

        @pl.when((visit == visits - 1) & (step == steps - 1))
        def _():
            me = lax.axis_index("req")
            number = jnp.concatenate(
                [
                    base + me * size + iota((size, HEAD_SIZE), 0)
                    for base, size in zip(bases, sizes)
                ],
                axis=0,
            )
            start = jnp.zeros((rows, HEAD_SIZE), jnp.int32)
            before = jnp.int32(0)
            for other in range(members):
                before = before + lengths_ref[other]
                start = jnp.where(number >= before, before, start)
            angle = (number - start).astype(F32) * frequency_ref[...]
            cosine, sine = jnp.cos(angle), jnp.sin(angle)
            sine = jnp.where(iota((rows, HEAD_SIZE), 1) < HEAD_SIZE // 2, -sine, sine)
            mean = jnp.sum(squares[...], axis=1, keepdims=True) / (shards * steps * depth)
            scale = lax.rsqrt(mean + 1e-05)
            turned = query_ref.shape[1] + key_ref.shape[1]
            for at in range(0, sums.shape[1], HEAD_SIZE):
                columns = slice(at, at + HEAD_SIZE)
                head = sums[:, columns] * scale
                if at < turned:
                    head = head * cosine + pltpu.roll(head, HEAD_SIZE // 2, 1) * sine
                out_ref[:, columns] = head.astype(BF16)


def project(
    final, shards, bases, sizes, place, visits, lengths, lines, gain, weights, carried, frequency
):
    pieces = [piece for line in lines for piece in line]
    rows, width = sum(sizes), pieces[0].shape[1]
    depth = min(DEPTH, width)
    steps = width // depth
    columns = sum(weight.shape[1] for weight in weights)

    def block_of(visit, step, place_ref):
        step = jnp.where(place_ref[visit] < 0, steps - 1, step)
        return place_ref[visits + visit] * steps + step

    def whole(shape):
        return pl.BlockSpec(shape, lambda visit, step, place_ref, lengths_ref: (0, 0))

    def deep(block, dimension):
        def where(visit, step, place_ref, lengths_ref):
            at = block_of(visit, step, place_ref)
            return (at, 0) if dimension == 0 else (0, at)

        return pl.BlockSpec(block, where)

    operands = [*pieces, gain, *weights, *carried, frequency]
    in_specs = [whole(piece.shape) for piece in pieces]
    in_specs += [deep((1, depth), 1)]
    in_specs += [deep((depth, weight.shape[1]), 0) for weight in weights]
    in_specs += [whole(leaf.shape) for leaf in carried]
    in_specs += [whole((1, HEAD_SIZE))]
    scratch = [pltpu.VMEM((rows, depth), BF16)]
    if final:
        out_shape = [jax.ShapeDtypeStruct((rows, columns), BF16)]
        scratch = [pltpu.VMEM((rows, columns), F32), pltpu.VMEM((rows, 128), F32), *scratch]
    else:
        out_shape = [
            jax.ShapeDtypeStruct((rows, columns), F32),
            jax.ShapeDtypeStruct((rows, 128), F32),
        ]
    return pl.pallas_call(
        functools.partial(
            project_kernel,
            len(lines[0]),
            bool(carried),
            final,
            shards,
            steps,
            bases,
            sizes,
            lengths.shape[0],
        ),
        grid_spec=pltpu.PrefetchScalarGridSpec(
            num_scalar_prefetch=2,
            grid=(visits, steps),
            in_specs=in_specs,
            out_specs=[whole(leaf.shape) for leaf in out_shape],
            scratch_shapes=scratch,
        ),
        out_shape=out_shape,
        compiler_params=pltpu.CompilerParams(vmem_limit_bytes=32 * MEBI),
        cost_estimate=pl.CostEstimate(
            flops=2 * rows * width * columns * visits,
            bytes_accessed=2 * width * columns * visits + 8 * rows * columns,
            transcendentals=0,
        ),
        name="project",
    )(place, lengths, *operands)


def attend_kernel(
    chips, groups, known, prior, query_width, key_width, lengths_ref, plan_ref, *refs
):
    blocks, refs = refs[: -9 if prior else -7], refs[-7:]
    attended_out, cache_out, attended_ref, cache_ref, rows_ref, sems, out_sems = refs
    workers = 2 * chips
    me = lax.axis_index("req")
    chip, core = lax.div(me, 2), lax.rem(me, 2)
    slots = cache_ref.shape[1]
    spans = slots // SPAN
    total = workers * sum(sum(sizes) for _, sizes in groups)
    copies = []
    for group, (bases, sizes) in enumerate(groups):
        for hop in range(chips):
            source = lax.rem(chip - hop + chips, chips) * 2
            for twin in range(2):
                owner = source + (core if twin == 0 else 1 - core)
                block = blocks[(group * chips + hop) * 2 + twin]
                first = 0
                for base, rows in zip(bases, sizes):
                    at = pl.multiple_of(base + owner * rows, ALIGN)
                    copies.append(
                        pltpu.make_async_copy(
                            block.at[pl.ds(first, rows), :],
                            rows_ref.at[pl.ds(at, rows), :],
                            sems.at[len(copies)],
                        )
                    )
                    first += rows
    for copy in copies:
        copy.start()
    pad = rows_ref.shape[0] - total
    rows_ref[total:, :] = jnp.zeros((pad, rows_ref.shape[1]), BF16)
    for copy in copies:
        copy.wait()

    def aligned(row):
        first = pl.multiple_of(lax.div(row, ALIGN) * ALIGN, ALIGN)
        return first, row - first

    start, length = run_of(lengths_ref, me, workers)

    mine = (start + length <= known) & (start + length > prior)
    results = [(mine, pltpu.make_async_copy(cache_ref, cache_out, out_sems.at[spans]))]

    @pl.when(mine)
    def _():
        first, shift = aligned(start)
        reach = slots + SPAN
        row, column = iota((slots, reach), 0), iota((slots, reach), 1)
        hot = ((column == row + shift) & (row < length)).astype(BF16)
        for half in range(2):
            window = rows_ref[
                pl.ds(first, reach),
                query_width + half * key_width : query_width + (half + 1) * key_width,
            ]
            cache_ref[half] = jnp.dot(hot, window, preferred_element_type=F32).astype(BF16)
        results[0][1].start()

    heads, key_heads = query_width // HEAD_SIZE, key_width // HEAD_SIZE
    group = heads // key_heads
    factor = math.log2(math.e) / math.sqrt(HEAD_SIZE)
    for slot in range(spans):
        span = plan_ref[me * spans + slot]
        source = lax.div(span, spans)
        part = lax.rem(span, spans)
        start, length = run_of(lengths_ref, source, workers)
        offset = part * SPAN
        out_rows = slice(slot * SPAN, (slot + 1) * SPAN)
        dead = offset >= length
        needed = start + jnp.minimum(offset + SPAN, length)
        due = jnp.logical_not(dead) & (needed <= known) & (needed > prior)

        copy = pltpu.make_async_copy(
            attended_ref.at[out_rows, :], attended_out.at[out_rows, :], out_sems.at[slot]
        )
        results.append((due if prior else due | dead, copy))

        if not prior:

            @pl.when(dead)
            def _():
                attended_ref[out_rows, :] = jnp.zeros((SPAN, query_width), BF16)

        for count in range(1, spans + 1):

            @pl.when(due & (part == count - 1))
            def _():
                first, shift = aligned(start + offset)
                hot = iota((SPAN, 2 * SPAN), 1) == iota((SPAN, 2 * SPAN), 0) + shift
                queries = jnp.dot(
                    hot.astype(BF16),
                    rows_ref[pl.ds(first, 2 * SPAN), :query_width],
                    preferred_element_type=F32,
                ).astype(BF16)
                reach = (count + 1) * SPAN
                first, shift = aligned(start)
                key_pos = iota((SPAN, reach), 1) - shift
                query_pos = (count - 1) * SPAN + iota((SPAN, reach), 0)
                allowed = (key_pos >= 0) & (key_pos <= query_pos) & (key_pos < length)
                bias = jnp.where(allowed, 0.0, -1e30)
                bias = jnp.concatenate([bias] * group, axis=0)
                live = (count - 1) * SPAN + iota((SPAN, HEAD_SIZE), 0) < length
                for head in range(key_heads):
                    stacked = jnp.concatenate(
                        [
                            queries[:, at * HEAD_SIZE : (at + 1) * HEAD_SIZE]
                            for at in range(head * group, (head + 1) * group)
                        ],
                        axis=0,
                    )
                    left = query_width + head * HEAD_SIZE
                    keys = rows_ref[pl.ds(first, reach), left : left + HEAD_SIZE]
                    left += key_width
                    values = rows_ref[pl.ds(first, reach), left : left + HEAD_SIZE]
                    scores = lax.dot_general(
                        stacked, keys, (((1,), (1,)), ((), ())), preferred_element_type=F32
                    )
                    scores = scores + bias
                    top = jnp.max(scores, axis=1, keepdims=True)
                    weights = jnp.exp2((scores - top) * factor)
                    norm = jnp.sum(weights, axis=1, keepdims=True)
                    mixed = jnp.dot(weights.astype(BF16), values, preferred_element_type=F32)
                    mixed = mixed / norm
                    for at in range(group):
                        left = (head * group + at) * HEAD_SIZE
                        attended_ref[out_rows, left : left + HEAD_SIZE] = jnp.where(
                            live, mixed[at * SPAN : (at + 1) * SPAN], 0.0
                        ).astype(BF16)

        @pl.when(results[-1][0])
        def _():
            results[-1][1].start()

    for done, copy in results:

        @pl.when(done)
        def _():
            copy.wait()


def attend(chips, groups, known, prior, widths, slots, lengths, plan, blocks, outputs):
    query_width, key_width = widths
    width = query_width + 2 * key_width
    total = 2 * chips * sum(sum(sizes) for _, sizes in groups)
    copies = 2 * chips * sum(len(sizes) for _, sizes in groups)
    at = 2 + len(blocks)
    return pl.pallas_call(
        functools.partial(attend_kernel, chips, groups, known, prior, query_width, key_width),
        in_specs=[pl.BlockSpec(memory_space=pltpu.SMEM)] * 2
        + [pl.BlockSpec(memory_space=pl.ANY)] * (len(blocks) + len(outputs)),
        out_specs=[pl.BlockSpec(memory_space=pl.ANY)] * 2,
        out_shape=[
            jax.ShapeDtypeStruct((slots, query_width), BF16),
            jax.ShapeDtypeStruct((2, slots, key_width), BF16),
        ],
        input_output_aliases={at + index: index for index in range(len(outputs))},
        scratch_shapes=[
            pltpu.VMEM((slots, query_width), BF16),
            pltpu.VMEM((2, slots, key_width), BF16),
            pltpu.VMEM((total + slots + SPAN, width), BF16),
            pltpu.SemaphoreType.DMA((copies,)),
            pltpu.SemaphoreType.DMA((slots // SPAN + 1,)),
        ],
        compiler_params=pltpu.CompilerParams(vmem_limit_bytes=32 * MEBI),
        name="attend",
    )(lengths, plan, *blocks, *outputs)


def shift_chips(value, hop, chips):
    pairs = [(2 * x + c, 2 * ((x + hop) % chips) + c) for x in range(chips) for c in range(2)]
    return lax.ppermute(value, "req", pairs)


def swap_cores(value, chips):
    return lax.ppermute(value, "req", [(d, d ^ 1) for d in range(2 * chips)])


def local(
    chips, shards, tokens, norm_gain, w_query, key_weight, value_weight, lengths, plan
):
    workers = 2 * chips
    slots = tokens.shape[0]
    live = slots // 2
    sizes = [live * share // sum(SHARES) // ALIGN * ALIGN for share in SHARES]
    sizes[-1] = live - sum(sizes[:-1])
    bases = [workers * sum(sizes[:chunk]) for chunk in range(len(sizes))]
    weights = [
        pltpu.with_memory_space_constraint(weight, pltpu.HBM)
        for weight in (w_query, key_weight, value_weight)
    ]
    gain = norm_gain.astype(F32).reshape(1, -1)
    halfway = HEAD_SIZE // 2
    frequency = np.exp(-np.arange(halfway) * 2.0 / HEAD_SIZE * math.log(500000.0))
    frequency = jnp.asarray(np.tile(frequency, 2)[None, :], F32)

    twin = swap_cores(tokens, chips)
    first = deal(chips, bases[:1], sizes[:1], lengths, [tokens], [False])
    dealt = [
        *deal(chips, bases[:1], sizes[:1], lengths, [twin], [True], first),
        *deal(chips, bases[1:], sizes[1:], lengths, [tokens, twin], [False, True]),
    ]
    homes, aways = dealt[::2], dealt[1::2]
    routes, owned, depth = routes_of(shards)
    early = [piece for piece in range(len(owned)) if depth[piece] < max(depth)]
    late = [piece for piece in range(len(owned)) if depth[piece] == max(depth)]
    direct = [piece for piece in range(len(owned)) if depth[piece] == 1]

    lines = []
    for chunk in range(len(sizes)):
        arrived = [shift_chips(aways[chunk][hop - 1], hop, chips) for hop in range(1, chips)]
        places = [(chunk - 1, piece) for piece in direct if chunk]
        places += [(chunk - 2, piece) for piece in late if chunk > 1]
        later = aways[chunk + 1 : chunk + 2] + [lines[at][piece] for at, piece in places]
        block, later = merge(homes[chunk], arrived, later)
        if chunk + 1 < len(sizes):
            aways[chunk + 1] = later.pop(0)
        for (at, piece), leaf in zip(places, later):
            lines[at][piece] = leaf
        line = {0: block}
        for index, (source, pairs) in enumerate(routes):
            if index + 1 in direct:
                line[index + 1] = lax.ppermute(block, "tp", pairs)
        lines.append(line)
        for line in lines[-2:-1] if chunk + 1 < len(sizes) else lines[-2:]:
            for index, (source, pairs) in enumerate(routes):
                if index + 1 not in direct:
                    line[index + 1] = lax.ppermute(line[source + 1], "tp", pairs)

    tables, counts = zip(
        *(visits_of([owned[piece] for piece in group], shards) for group in (early, late))
    )
    table = jnp.asarray(np.concatenate(tables, axis=1))
    table = lax.dynamic_index_in_dim(table, lax.axis_index("tp"), 0, keepdims=False)
    places = table[: 2 * counts[0]], table[2 * counts[0] :]

    blocks, groups, outputs, known = [], [], (), 0
    widths = w_query.shape[1], key_weight.shape[1]
    for chunks in GROUPS:
        span = [bases[chunk] for chunk in chunks], [sizes[chunk] for chunk in chunks]
        groups.append(span)
        carried = ()
        for place, count, chosen in zip(places, counts, (early, late)):
            carried = project(
                chosen is late,
                shards,
                *span,
                place,
                count,
                lengths,
                [[lines[chunk][piece] for piece in chosen] for chunk in chunks],
                gain,
                weights,
                carried,
                frequency,
            )
        block = carried[0]
        here = [block] + [shift_chips(block, hop, chips) for hop in range(1, chips)]
        for piece in here:
            blocks += [piece, swap_cores(piece, chips)]
        prior, known = known, known + workers * sum(span[1])
        outputs = attend(
            chips, tuple(groups), known, prior, widths, slots, lengths, plan, blocks, outputs
        )
    return tuple(outputs)


def solution(mesh):
    placed = (
        P(("groups", "req"), "tp"),
        P(),
        P(None, "tp"),
        P(None, "tp"),
        P(None, "tp"),
        P("groups"),
        P("groups"),
    )
    return jax.shard_map(
        functools.partial(local, mesh.shape["req"] // 2, mesh.shape["tp"]),
        mesh=mesh,
        in_specs=placed,
        out_specs=(P(("groups", "req"), "tp"), P(None, ("groups", "req"), "tp")),
        check_vma=False,
    )
```

```python
import functools
import math

import jax
import jax.numpy as jnp
import numpy as np
from jax import lax
from jax.experimental import pallas as pl
from jax.experimental.pallas import tpu as pltpu
from jax.sharding import PartitionSpec as P

HEAD_SIZE = 128
SPAN = 128
ALIGN = 16
SHARES = (4, 6, 6)
GROUPS = ((0, 1), (2,))
DEPTH = 1024
MEBI = 1024 * 1024
F32, BF16 = jnp.float32, jnp.bfloat16


def run_of(lengths_ref, request, count):
    start = jnp.int32(0)
    length = jnp.int32(0)
    for other in range(count):
        amount = lengths_ref[other]
        start = start + jnp.where(other < request, amount, 0)
        length = jnp.where(other == request, amount, length)
    return start, length


def iota(shape, dimension):
    return lax.broadcasted_iota(jnp.int32, shape, dimension)


def deal_kernel(chips, bases, sizes, twins, lengths_ref, *refs):
    me = lax.axis_index("req")
    chip, core = lax.div(me, 2), lax.rem(me, 2)
    sources, refs = refs[: len(twins)], refs[len(twins) :]
    count = 2 * len(sizes)
    priors, out_refs = refs[:-count], refs[-count:]
    requests = [me + 1 - 2 * core if twin else me for twin in twins]
    runs = [run_of(lengths_ref, request, 2 * chips) for request in requests]
    slots = sources[0].shape[0]
    for chunk, (base, rows) in enumerate(zip(bases, sizes)):
        home_ref, away_ref = out_refs[2 * chunk : 2 * chunk + 2]
        for hop in range(chips):
            target = lax.rem(chip + hop, chips) * 2 + core
            number = base + target * rows + iota((rows, slots), 0)
            slot = iota((rows, slots), 1)
            total = None
            for (start, length), source in zip(runs, sources):
                hot = ((number - start == slot) & (slot < length)).astype(BF16)
                part = jnp.dot(hot, source[...], preferred_element_type=F32)
                total = part if total is None else total + part
            total = total.astype(BF16)
            if hop == 0:
                home_ref[...] = total + priors[2 * chunk][...] if priors else total
            elif priors:
                away_ref[hop - 1] = total + priors[2 * chunk + 1][hop - 1]
            else:
                away_ref[hop - 1] = total


def deal(chips, bases, sizes, lengths, sources, twins, priors=()):
    slots, width = sources[0].shape
    block = min(1024, width)
    out_specs, out_shape = [], []
    for rows in sizes:
        out_specs += [
            pl.BlockSpec((rows, block), lambda i: (0, i)),
            pl.BlockSpec((chips - 1, rows, block), lambda i: (0, 0, i)),
        ]
        out_shape += [
            jax.ShapeDtypeStruct((rows, width), BF16),
            jax.ShapeDtypeStruct((chips - 1, rows, width), BF16),
        ]
    return pl.pallas_call(
        functools.partial(deal_kernel, chips, bases, sizes, twins),
        grid=(width // block,),
        in_specs=[pl.BlockSpec(memory_space=pltpu.SMEM)]
        + [pl.BlockSpec((slots, block), lambda i: (0, i)) for _ in sources]
        + (out_specs if priors else []),
        out_specs=out_specs,
        out_shape=out_shape,
        compiler_params=pltpu.CompilerParams(vmem_limit_bytes=24 * MEBI),
        cost_estimate=pl.CostEstimate(
            flops=2 * len(sources) * chips * sum(sizes) * slots * width,
            bytes_accessed=2 * len(sources) * slots * width + 2 * chips * sum(sizes) * width,
            transcendentals=0,
        ),
        name="deal",
    )(lengths, *sources, *priors)


def merge_kernel(count, home_ref, *refs):
    total = home_ref[...]
    for ref in refs[:count]:
        total = total + ref[...]
    passed = (len(refs) - count - 1) // 2
    refs[count + passed][...] = total


def merge(home, arrived, later):
    count = len(arrived)
    vmem, anywhere = pl.BlockSpec(memory_space=pltpu.VMEM), pl.BlockSpec(memory_space=pl.ANY)
    block, *later = pl.pallas_call(
        functools.partial(merge_kernel, count),
        in_specs=[vmem] * (count + 1) + [anywhere] * len(later),
        out_specs=[vmem] + [anywhere] * len(later),
        out_shape=[jax.ShapeDtypeStruct(leaf.shape, leaf.dtype) for leaf in (home, *later)],
        input_output_aliases={count + 1 + at: 1 + at for at in range(len(later))},
        compiler_params=pltpu.CompilerParams(vmem_limit_bytes=8 * MEBI),
        cost_estimate=pl.CostEstimate(
            flops=home.size, bytes_accessed=2 * home.size * (count + 2), transcendentals=0
        ),
        name="merge",
    )(home, *arrived, *later)
    return block, later


def after(array, anchors):
    def kernel(*refs):
        pass

    anywhere = pl.BlockSpec(memory_space=pl.ANY)
    return pl.pallas_call(
        kernel,
        in_specs=[anywhere] * (1 + len(anchors)),
        out_specs=anywhere,
        out_shape=jax.ShapeDtypeStruct(array.shape, array.dtype),
        input_output_aliases={0: 0},
        compiler_params=pltpu.CompilerParams(vmem_limit_bytes=MEBI),
        name="after",
    )(array, *anchors)


def routes_of(shards):
    if shards == 4:
        routes = [
            (-1, [(1, 2), (2, 1)]),
            (-1, [(0, 1), (1, 0), (2, 3), (3, 2)]),
            (-1, [(0, 2), (1, 3), (2, 0), (3, 1)]),
            (2, [(2, 3), (1, 0)]),
        ]
    else:
        routes = []
        for step in range(1, shards):
            source = len(routes) - 2 if step > 1 else -1
            routes.append((source, [(at, at + 1) for at in range(step - 1, shards - 1)]))
            source = len(routes) - 2 if step > 1 else -1
            routes.append((source, [(at, at - 1) for at in range(1, shards - step + 1)]))
    held, depth = [list(range(shards))], [0]
    for source, pairs in routes:
        now = [-1] * shards
        for start, end in pairs:
            now[end] = held[source + 1][start]
        held.append(now)
        depth.append(depth[source + 1] + 1)
    return routes, held, depth


def visits_of(held, shards):
    visits = [
        [(piece, now[at]) for piece, now in enumerate(held) if now[at] >= 0]
        for at in range(shards)
    ]
    count = max(len(line) for line in visits)
    table = []
    for line in visits:
        pad = (-1, line[-1][1] if line else 0)
        line = line + [pad] * (count - len(line))
        table.append([piece for piece, _ in line] + [shard for _, shard in line])
    return np.array(table, np.int32), count


def project_kernel(
    count, carries, final, shards, steps, bases, sizes, members, place_ref, lengths_ref, *refs
):
    pieces, refs = refs[: count * len(sizes)], refs[count * len(sizes) :]
    gain_ref, query_ref, key_ref, value_ref = refs[:4]
    refs = refs[4:]
    if carries:
        sums_in, squares_in = refs[:2]
        refs = refs[2:]
    frequency_ref, refs = refs[0], refs[1:]
    if final:
        out_ref, refs = refs[0], refs[1:]
    sums, squares, chosen = refs
    visit, step = pl.program_id(0), pl.program_id(1)
    visits = pl.num_programs(0)
    rows, depth = chosen.shape
    piece = place_ref[visit]

    @pl.when((visit == 0) & (step == 0))
    def _():
        sums[...] = sums_in[...] if carries else jnp.zeros_like(sums)
        squares[...] = squares_in[...] if carries else jnp.zeros_like(squares)

    for index in range(count):

        @pl.when(piece == index)
        def _():
            columns = pl.ds(pl.multiple_of(step * depth, depth), depth)
            at = 0
            for chunk, size in enumerate(sizes):
                chosen[at : at + size, :] = pieces[chunk * count + index][:, columns]
                at += size

    @pl.when(piece >= 0)
    def _():
        wide = chosen[...].astype(F32)
        square = wide * wide
        part = square[:, :128]
        for at in range(128, depth, 128):
            part = part + square[:, at : at + 128]
        squares[...] += part
        scaled = (wide * gain_ref[...]).astype(BF16)
        at = 0
        for weight in (query_ref, key_ref, value_ref):
            columns = slice(at, at + weight.shape[1])
            sums[:, columns] += jnp.dot(scaled, weight[...], preferred_element_type=F32)
            at += weight.shape[1]

    if final:

        @pl.when((visit == visits - 1) & (step == steps - 1))
        def _():
            me = lax.axis_index("req")
            number = jnp.concatenate(
                [
                    base + me * size + iota((size, HEAD_SIZE), 0)
                    for base, size in zip(bases, sizes)
                ],
                axis=0,
            )
            start = jnp.zeros((rows, HEAD_SIZE), jnp.int32)
            before = jnp.int32(0)
            for other in range(members):
                before = before + lengths_ref[other]
                start = jnp.where(number >= before, before, start)
            angle = (number - start).astype(F32) * frequency_ref[...]
            cosine, sine = jnp.cos(angle), jnp.sin(angle)
            sine = jnp.where(iota((rows, HEAD_SIZE), 1) < HEAD_SIZE // 2, -sine, sine)
            mean = jnp.sum(squares[...], axis=1, keepdims=True) / (shards * steps * depth)
            scale = lax.rsqrt(mean + 1e-05)
            turned = query_ref.shape[1] + key_ref.shape[1]
            for at in range(0, sums.shape[1], HEAD_SIZE):
                columns = slice(at, at + HEAD_SIZE)
                head = sums[:, columns] * scale
                if at < turned:
                    head = head * cosine + pltpu.roll(head, HEAD_SIZE // 2, 1) * sine
                out_ref[:, columns] = head.astype(BF16)


def project(
    final, shards, bases, sizes, place, visits, lengths, lines, gain, weights, carried, frequency
):
    pieces = [piece for line in lines for piece in line]
    rows, width = sum(sizes), pieces[0].shape[1]
    depth = min(DEPTH, width)
    steps = width // depth
    columns = sum(weight.shape[1] for weight in weights)

    def block_of(visit, step, place_ref):
        step = jnp.where(place_ref[visit] < 0, steps - 1, step)
        return place_ref[visits + visit] * steps + step

    def whole(shape):
        return pl.BlockSpec(shape, lambda visit, step, place_ref, lengths_ref: (0, 0))

    def deep(block, dimension):
        def where(visit, step, place_ref, lengths_ref):
            at = block_of(visit, step, place_ref)
            return (at, 0) if dimension == 0 else (0, at)

        return pl.BlockSpec(block, where)

    operands = [*pieces, gain, *weights, *carried, frequency]
    in_specs = [whole(piece.shape) for piece in pieces]
    in_specs += [deep((1, depth), 1)]
    in_specs += [deep((depth, weight.shape[1]), 0) for weight in weights]
    in_specs += [whole(leaf.shape) for leaf in carried]
    in_specs += [whole((1, HEAD_SIZE))]
    scratch = [pltpu.VMEM((rows, depth), BF16)]
    if final:
        out_shape = [jax.ShapeDtypeStruct((rows, columns), BF16)]
        scratch = [pltpu.VMEM((rows, columns), F32), pltpu.VMEM((rows, 128), F32), *scratch]
    else:
        out_shape = [
            jax.ShapeDtypeStruct((rows, columns), F32),
            jax.ShapeDtypeStruct((rows, 128), F32),
        ]
    return pl.pallas_call(
        functools.partial(
            project_kernel,
            len(lines[0]),
            bool(carried),
            final,
            shards,
            steps,
            bases,
            sizes,
            lengths.shape[0],
        ),
        grid_spec=pltpu.PrefetchScalarGridSpec(
            num_scalar_prefetch=2,
            grid=(visits, steps),
            in_specs=in_specs,
            out_specs=[whole(leaf.shape) for leaf in out_shape],
            scratch_shapes=scratch,
        ),
        out_shape=out_shape,
        compiler_params=pltpu.CompilerParams(vmem_limit_bytes=32 * MEBI),
        cost_estimate=pl.CostEstimate(
            flops=2 * rows * width * columns * visits,
            bytes_accessed=2 * width * columns * visits + 8 * rows * columns,
            transcendentals=0,
        ),
        name="project",
    )(place, lengths, *operands)


def attend_kernel(
    chips, groups, known, prior, query_width, key_width, lengths_ref, plan_ref, *refs
):
    blocks, refs = refs[: -12 if prior else -10], refs[-10:]
    attended_out, cache_out, attended_ref, cache_ref, rows_ref, queries_ref = refs[:6]
    scores_ref, top_ref, sems, out_sems = refs[6:]
    workers = 2 * chips
    me = lax.axis_index("req")
    chip, core = lax.div(me, 2), lax.rem(me, 2)
    slots = cache_ref.shape[1]
    spans = slots // SPAN
    total = workers * sum(sum(sizes) for _, sizes in groups)
    copies = []
    for group, (bases, sizes) in enumerate(groups):
        for hop in range(chips):
            source = lax.rem(chip - hop + chips, chips) * 2
            for twin in range(2):
                owner = source + (core if twin == 0 else 1 - core)
                block = blocks[(group * chips + hop) * 2 + twin]
                first = 0
                for base, rows in zip(bases, sizes):
                    at = pl.multiple_of(base + owner * rows, ALIGN)
                    copies.append(
                        pltpu.make_async_copy(
                            block.at[pl.ds(first, rows), :],
                            rows_ref.at[pl.ds(at, rows), :],
                            sems.at[len(copies)],
                        )
                    )
                    first += rows
    for copy in copies:
        copy.start()
    rows_ref[total:, :] = jnp.zeros((rows_ref.shape[0] - total, rows_ref.shape[1]), BF16)
    for copy in copies:
        copy.wait()

    def window(row, columns):
        first = pl.multiple_of(lax.div(row, ALIGN) * ALIGN, ALIGN)
        shape = (SPAN, 2 * SPAN)
        hot = (iota(shape, 1) == iota(shape, 0) + (row - first)).astype(BF16)
        return jnp.dot(
            hot, rows_ref[pl.ds(first, 2 * SPAN), columns], preferred_element_type=F32
        )

    own_start, own_length = run_of(lengths_ref, me, workers)
    mine = (own_start + own_length <= known) & (own_start + own_length > prior)
    cache_copy = pltpu.make_async_copy(cache_ref, cache_out, out_sems.at[spans])

    @pl.when(mine)
    def _():
        def step(part, carry):
            at = pl.multiple_of(part * SPAN, SPAN)

            @pl.when(at < own_length)
            def _():
                picked = window(own_start + at, slice(query_width, query_width + 2 * key_width))
                live = at + iota(picked.shape, 0) < own_length
                picked = jnp.where(live, picked, 0.0).astype(BF16)
                cache_ref[0, pl.ds(at, SPAN), :] = picked[:, :key_width]
                cache_ref[1, pl.ds(at, SPAN), :] = picked[:, key_width:]

            @pl.when(at >= own_length)
            def _():
                empty = jnp.zeros((SPAN, key_width), BF16)
                cache_ref[0, pl.ds(at, SPAN), :] = empty
                cache_ref[1, pl.ds(at, SPAN), :] = empty

            return carry

        lax.fori_loop(0, spans, step, 0)
        cache_copy.start()

    heads, key_heads = query_width // HEAD_SIZE, key_width // HEAD_SIZE
    group = heads // key_heads
    factor = math.log2(math.e) / math.sqrt(HEAD_SIZE)
    tall = group * SPAN

    def span_of(slot):
        span = plan_ref[me * spans + slot]
        start, length = run_of(lengths_ref, lax.div(span, spans), workers)
        offset = lax.rem(span, spans) * SPAN
        dead = offset >= length
        needed = start + jnp.minimum(offset + SPAN, length)
        due = jnp.logical_not(dead) & (needed <= known) & (needed > prior)
        return start, length, offset, dead, due

    def result(slot):
        rows = pl.ds(pl.multiple_of(slot * SPAN, SPAN), SPAN)
        return pltpu.make_async_copy(
            attended_ref.at[rows, :], attended_out.at[rows, :], out_sems.at[slot]
        )

    def attend_slot(slot, carry):
        start, length, offset, dead, due = span_of(slot)
        out_rows = pl.ds(pl.multiple_of(slot * SPAN, SPAN), SPAN)

        if not prior:

            @pl.when(dead)
            def _():
                attended_ref[out_rows, :] = jnp.zeros((SPAN, query_width), BF16)
                result(slot).start()

        @pl.when(due)
        def _():
            queries = window(start + offset, slice(0, query_width)).astype(BF16)
            for head in range(heads):
                at = head % group * SPAN
                queries_ref[head // group, at : at + SPAN, :] = queries[
                    :, head * HEAD_SIZE : (head + 1) * HEAD_SIZE
                ]
            first = pl.multiple_of(lax.div(start, ALIGN) * ALIGN, ALIGN)
            shift = start - first
            reach = shift + jnp.minimum(offset + SPAN, length)
            tiles = lax.div(reach + SPAN - 1, SPAN)

            def attend_head(head, carry):
                def columns(at):
                    return pl.ds(pl.multiple_of(at + head * HEAD_SIZE, HEAD_SIZE), HEAD_SIZE)

                def tile_rows(tile):
                    return pl.ds(pl.multiple_of(first + tile * SPAN, ALIGN), SPAN)

                top_ref[...] = jnp.full((tall, SPAN), -1e30, F32)

                def score(tile, carry):
                    keys = rows_ref[tile_rows(tile), columns(query_width)]
                    scores = lax.dot_general(
                        queries_ref[head],
                        keys,
                        (((1,), (1,)), ((), ())),
                        preferred_element_type=F32,
                    )
                    key_pos = tile * SPAN + iota((SPAN, SPAN), 1) - shift
                    query_pos = offset + iota((SPAN, SPAN), 0)
                    allowed = (key_pos >= 0) & (key_pos <= query_pos) & (key_pos < length)
                    bias = jnp.where(allowed, 0.0, -1e30)
                    scores = scores + jnp.concatenate([bias] * group, axis=0)
                    scores_ref[tile] = scores
                    top_ref[...] = jnp.maximum(top_ref[...], scores)
                    return carry

                lax.fori_loop(0, tiles, score, 0)
                top = jnp.max(top_ref[...], axis=1, keepdims=True)

                def mix(tile, carry):
                    weights = jnp.exp2((scores_ref[tile] - top) * factor).astype(BF16)
                    values = rows_ref[tile_rows(tile), columns(query_width + key_width)]
                    values = jnp.concatenate([values, jnp.ones((SPAN, HEAD_SIZE), BF16)], axis=1)
                    return carry + jnp.dot(weights, values, preferred_element_type=F32)

                mixed = lax.fori_loop(0, tiles, mix, jnp.zeros((tall, 2 * HEAD_SIZE), F32))
                mixed = mixed[:, :HEAD_SIZE] / mixed[:, HEAD_SIZE:]
                live = offset + iota((SPAN, HEAD_SIZE), 0) < length
                for at in range(group):
                    left = pl.multiple_of((head * group + at) * HEAD_SIZE, HEAD_SIZE)
                    attended_ref[out_rows, pl.ds(left, HEAD_SIZE)] = jnp.where(
                        live, mixed[at * SPAN : (at + 1) * SPAN], 0.0
                    ).astype(BF16)
                return carry

            lax.fori_loop(0, key_heads, attend_head, 0)
            result(slot).start()

        return carry

    lax.fori_loop(0, spans, attend_slot, 0)

    def finish(slot, carry):
        _, _, _, dead, due = span_of(slot)

        @pl.when(due if prior else due | dead)
        def _():
            result(slot).wait()

        return carry

    lax.fori_loop(0, spans, finish, 0)

    @pl.when(mine)
    def _():
        cache_copy.wait()


def attend(chips, groups, known, prior, widths, slots, lengths, plan, blocks, outputs):
    query_width, key_width = widths
    width = query_width + 2 * key_width
    total = 2 * chips * sum(sum(sizes) for _, sizes in groups)
    copies = 2 * chips * sum(len(sizes) for _, sizes in groups)
    key_heads, tall = key_width // HEAD_SIZE, query_width // key_width * SPAN
    at = 2 + len(blocks)
    return pl.pallas_call(
        functools.partial(attend_kernel, chips, groups, known, prior, query_width, key_width),
        in_specs=[pl.BlockSpec(memory_space=pltpu.SMEM)] * 2
        + [pl.BlockSpec(memory_space=pl.ANY)] * (len(blocks) + len(outputs)),
        out_specs=[pl.BlockSpec(memory_space=pl.ANY)] * 2,
        out_shape=[
            jax.ShapeDtypeStruct((slots, query_width), BF16),
            jax.ShapeDtypeStruct((2, slots, key_width), BF16),
        ],
        input_output_aliases={at + index: index for index in range(len(outputs))},
        scratch_shapes=[
            pltpu.VMEM((slots, query_width), BF16),
            pltpu.VMEM((2, slots, key_width), BF16),
            pltpu.VMEM((total + 2 * SPAN, width), BF16),
            pltpu.VMEM((key_heads, tall, HEAD_SIZE), BF16),
            pltpu.VMEM((slots // SPAN + 1, tall, SPAN), F32),
            pltpu.VMEM((tall, SPAN), F32),
            pltpu.SemaphoreType.DMA((copies,)),
            pltpu.SemaphoreType.DMA((slots // SPAN + 1,)),
        ],
        compiler_params=pltpu.CompilerParams(vmem_limit_bytes=32 * MEBI),
        name="attend",
    )(lengths, plan, *blocks, *outputs)


def shift_chips(value, hop, chips):
    pairs = [(2 * x + c, 2 * ((x + hop) % chips) + c) for x in range(chips) for c in range(2)]
    return lax.ppermute(value, "req", pairs)


def swap_cores(value, chips):
    return lax.ppermute(value, "req", [(d, d ^ 1) for d in range(2 * chips)])


def local(
    chips, shards, tokens, norm_gain, w_query, key_weight, value_weight, lengths, plan
):
    workers = 2 * chips
    slots = tokens.shape[0]
    live = slots // 2
    sizes = [live * share // sum(SHARES) // ALIGN * ALIGN for share in SHARES]
    sizes[-1] = live - sum(sizes[:-1])
    bases = [workers * sum(sizes[:chunk]) for chunk in range(len(sizes))]
    weights = [
        pltpu.with_memory_space_constraint(weight, pltpu.HBM)
        for weight in (w_query, key_weight, value_weight)
    ]
    gain = norm_gain.astype(F32).reshape(1, -1)
    halfway = HEAD_SIZE // 2
    frequency = np.exp(-np.arange(halfway) * 2.0 / HEAD_SIZE * math.log(500000.0))
    frequency = jnp.asarray(np.tile(frequency, 2)[None, :], F32)

    twin = swap_cores(tokens, chips)
    first = deal(chips, bases[:1], sizes[:1], lengths, [tokens], [False])
    dealt = [
        *deal(chips, bases[:1], sizes[:1], lengths, [twin], [True], first),
        *deal(chips, bases[1:], sizes[1:], lengths, [tokens, twin], [False, True]),
    ]
    homes, aways = dealt[::2], dealt[1::2]
    routes, owned, depth = routes_of(shards)
    early = [piece for piece in range(len(owned)) if depth[piece] < max(depth)]
    late = [piece for piece in range(len(owned)) if depth[piece] == max(depth)]
    direct = [piece for piece in range(len(owned)) if depth[piece] == 1]

    def relay(line):
        for index, (source, pairs) in enumerate(routes):
            if index + 1 not in direct:
                line[index + 1] = lax.ppermute(line[source + 1], "tp", pairs)

    lines = []
    for chunk in range(len(sizes)):
        arrived = [shift_chips(aways[chunk][hop - 1], hop, chips) for hop in range(1, chips)]
        places = [(chunk - 1, piece) for piece in direct if chunk]
        places += [(chunk - 2, piece) for piece in late if chunk > 1]
        later = aways[chunk + 1 : chunk + 2] + [lines[at][piece] for at, piece in places]
        block, later = merge(homes[chunk], arrived, later)
        if chunk + 1 < len(sizes):
            aways[chunk + 1] = later.pop(0)
        for (at, piece), leaf in zip(places, later):
            lines[at][piece] = leaf
        line = {0: block}
        for index, (source, pairs) in enumerate(routes):
            if index + 1 in direct:
                line[index + 1] = lax.ppermute(block, "tp", pairs)
        lines.append(line)
        for line in lines[-2:-1]:
            relay(line)

    tables, counts = zip(
        *(visits_of([owned[piece] for piece in group], shards) for group in (early, late))
    )
    table = jnp.asarray(np.concatenate(tables, axis=1))
    table = lax.dynamic_index_in_dim(table, lax.axis_index("tp"), 0, keepdims=False)
    places = table[: 2 * counts[0]], table[2 * counts[0] :]

    blocks, groups, outputs, known = [], [], (), 0
    widths = w_query.shape[1], key_weight.shape[1]
    for chunks in GROUPS:
        if len(sizes) - 1 in chunks:
            for source in {source + 1 for source, _ in routes} - {0}:
                if depth[source] == 1:
                    lines[-1][source] = after(lines[-1][source], blocks[:1])
            relay(lines[-1])
        span = [bases[chunk] for chunk in chunks], [sizes[chunk] for chunk in chunks]
        groups.append(span)
        carried = ()
        for place, count, chosen in zip(places, counts, (early, late)):
            carried = project(
                chosen is late,
                shards,
                *span,
                place,
                count,
                lengths,
                [[lines[chunk][piece] for piece in chosen] for chunk in chunks],
                gain,
                weights,
                carried,
                frequency,
            )
        block = carried[0]
        here = [block] + [shift_chips(block, hop, chips) for hop in range(1, chips)]
        for piece in here:
            blocks += [piece, swap_cores(piece, chips)]
        prior, known = known, known + workers * sum(span[1])
        outputs = attend(
            chips, tuple(groups), known, prior, widths, slots, lengths, plan, blocks, outputs
        )
    return tuple(outputs)


def solution(mesh):
    placed = (
        P(("groups", "req"), "tp"),
        P(),
        P(None, "tp"),
        P(None, "tp"),
        P(None, "tp"),
        P("groups"),
        P("groups"),
    )
    return jax.shard_map(
        functools.partial(local, mesh.shape["req"] // 2, mesh.shape["tp"]),
        mesh=mesh,
        in_specs=placed,
        out_specs=(P(("groups", "req"), "tp"), P(None, ("groups", "req"), "tp")),
        check_vma=False,
    )
```

```python
import functools
import math

import jax
import jax.numpy as jnp
import numpy as np
from jax import lax
from jax.experimental import pallas as pl
from jax.experimental.pallas import tpu as pltpu
from jax.sharding import PartitionSpec as P

HEAD_SIZE = 128
SPAN = 128
ALIGN = 16
TILE = 2 * SPAN
SHARES = (4, 6, 6)
GROUPS = ((0, 1), (2,))
DEPTH = 1024
MEBI = 1024 * 1024
F32, BF16 = jnp.float32, jnp.bfloat16


def run_of(lengths_ref, request, count):
    start = jnp.int32(0)
    length = jnp.int32(0)
    for other in range(count):
        amount = lengths_ref[other]
        start = start + jnp.where(other < request, amount, 0)
        length = jnp.where(other == request, amount, length)
    return start, length


def iota(shape, dimension):
    return lax.broadcasted_iota(jnp.int32, shape, dimension)


def deal_kernel(chips, bases, sizes, twins, lengths_ref, *refs):
    me = lax.axis_index("req")
    chip, core = lax.div(me, 2), lax.rem(me, 2)
    sources, refs = refs[: len(twins)], refs[len(twins) :]
    count = 2 * len(sizes)
    priors, out_refs = refs[:-count], refs[-count:]
    requests = [me + 1 - 2 * core if twin else me for twin in twins]
    runs = [run_of(lengths_ref, request, 2 * chips) for request in requests]
    slots = sources[0].shape[0]
    for chunk, (base, rows) in enumerate(zip(bases, sizes)):
        home_ref, away_ref = out_refs[2 * chunk : 2 * chunk + 2]
        for hop in range(chips):
            target = lax.rem(chip + hop, chips) * 2 + core
            number = base + target * rows + iota((rows, slots), 0)
            slot = iota((rows, slots), 1)
            total = None
            for (start, length), source in zip(runs, sources):
                hot = ((number - start == slot) & (slot < length)).astype(BF16)
                part = jnp.dot(hot, source[...], preferred_element_type=F32)
                total = part if total is None else total + part
            total = total.astype(BF16)
            if hop == 0:
                home_ref[...] = total + priors[2 * chunk][...] if priors else total
            elif priors:
                away_ref[hop - 1] = total + priors[2 * chunk + 1][hop - 1]
            else:
                away_ref[hop - 1] = total


def deal(chips, bases, sizes, lengths, sources, twins, priors=()):
    slots, width = sources[0].shape
    block = min(1024, width)
    out_specs, out_shape = [], []
    for rows in sizes:
        out_specs += [
            pl.BlockSpec((rows, block), lambda i: (0, i)),
            pl.BlockSpec((chips - 1, rows, block), lambda i: (0, 0, i)),
        ]
        out_shape += [
            jax.ShapeDtypeStruct((rows, width), BF16),
            jax.ShapeDtypeStruct((chips - 1, rows, width), BF16),
        ]
    return pl.pallas_call(
        functools.partial(deal_kernel, chips, bases, sizes, twins),
        grid=(width // block,),
        in_specs=[pl.BlockSpec(memory_space=pltpu.SMEM)]
        + [pl.BlockSpec((slots, block), lambda i: (0, i)) for _ in sources]
        + (out_specs if priors else []),
        out_specs=out_specs,
        out_shape=out_shape,
        compiler_params=pltpu.CompilerParams(vmem_limit_bytes=24 * MEBI),
        cost_estimate=pl.CostEstimate(
            flops=2 * len(sources) * chips * sum(sizes) * slots * width,
            bytes_accessed=2 * len(sources) * slots * width + 2 * chips * sum(sizes) * width,
            transcendentals=0,
        ),
        name="deal",
    )(lengths, *sources, *priors)


def merge_kernel(count, home_ref, *refs):
    total = home_ref[...]
    for ref in refs[:count]:
        total = total + ref[...]
    passed = (len(refs) - count - 1) // 2
    refs[count + passed][...] = total


def merge(home, arrived, later):
    count = len(arrived)
    vmem, anywhere = pl.BlockSpec(memory_space=pltpu.VMEM), pl.BlockSpec(memory_space=pl.ANY)
    block, *later = pl.pallas_call(
        functools.partial(merge_kernel, count),
        in_specs=[vmem] * (count + 1) + [anywhere] * len(later),
        out_specs=[vmem] + [anywhere] * len(later),
        out_shape=[jax.ShapeDtypeStruct(leaf.shape, leaf.dtype) for leaf in (home, *later)],
        input_output_aliases={count + 1 + at: 1 + at for at in range(len(later))},
        compiler_params=pltpu.CompilerParams(vmem_limit_bytes=8 * MEBI),
        cost_estimate=pl.CostEstimate(
            flops=home.size, bytes_accessed=2 * home.size * (count + 2), transcendentals=0
        ),
        name="merge",
    )(home, *arrived, *later)
    return block, later


def routes_of(shards):
    if shards == 4:
        routes = [
            (-1, [(1, 2), (2, 1)]),
            (-1, [(0, 1), (1, 0), (2, 3), (3, 2)]),
            (-1, [(0, 2), (1, 3), (2, 0), (3, 1)]),
            (2, [(2, 3), (1, 0)]),
        ]
    else:
        routes = []
        for step in range(1, shards):
            source = len(routes) - 2 if step > 1 else -1
            routes.append((source, [(at, at + 1) for at in range(step - 1, shards - 1)]))
            source = len(routes) - 2 if step > 1 else -1
            routes.append((source, [(at, at - 1) for at in range(1, shards - step + 1)]))
    held, depth = [list(range(shards))], [0]
    for source, pairs in routes:
        now = [-1] * shards
        for start, end in pairs:
            now[end] = held[source + 1][start]
        held.append(now)
        depth.append(depth[source + 1] + 1)
    return routes, held, depth


def visits_of(held, shards):
    visits = [
        [(piece, now[at]) for piece, now in enumerate(held) if now[at] >= 0]
        for at in range(shards)
    ]
    count = max(len(line) for line in visits)
    table = []
    for line in visits:
        pad = (-1, line[-1][1] if line else 0)
        line = line + [pad] * (count - len(line))
        table.append([piece for piece, _ in line] + [shard for _, shard in line])
    return np.array(table, np.int32), count


def project_kernel(
    count, carries, final, shards, steps, bases, sizes, members, place_ref, lengths_ref, *refs
):
    pieces, refs = refs[: count * len(sizes)], refs[count * len(sizes) :]
    gain_ref, query_ref, key_ref, value_ref = refs[:4]
    refs = refs[4:]
    if carries:
        sums_in, squares_in = refs[:2]
        refs = refs[2:]
    frequency_ref, refs = refs[0], refs[1:]
    if final:
        out_ref, refs = refs[0], refs[1:]
    sums, squares, chosen = refs
    visit, step = pl.program_id(0), pl.program_id(1)
    visits = pl.num_programs(0)
    rows, depth = chosen.shape
    piece = place_ref[visit]

    @pl.when((visit == 0) & (step == 0))
    def _():
        sums[...] = sums_in[...] if carries else jnp.zeros_like(sums)
        squares[...] = squares_in[...] if carries else jnp.zeros_like(squares)

    for index in range(count):

        @pl.when(piece == index)
        def _():
            columns = pl.ds(pl.multiple_of(step * depth, depth), depth)
            at = 0
            for chunk, size in enumerate(sizes):
                chosen[at : at + size, :] = pieces[chunk * count + index][:, columns]
                at += size

    @pl.when(piece >= 0)
    def _():
        wide = chosen[...].astype(F32)
        square = wide * wide
        part = square[:, :128]
        for at in range(128, depth, 128):
            part = part + square[:, at : at + 128]
        squares[...] += part
        scaled = (wide * gain_ref[...]).astype(BF16)
        at = 0
        for weight in (query_ref, key_ref, value_ref):
            columns = slice(at, at + weight.shape[1])
            sums[:, columns] += jnp.dot(scaled, weight[...], preferred_element_type=F32)
            at += weight.shape[1]

    if final:

        @pl.when((visit == visits - 1) & (step == steps - 1))
        def _():
            me = lax.axis_index("req")
            number = jnp.concatenate(
                [
                    base + me * size + iota((size, HEAD_SIZE), 0)
                    for base, size in zip(bases, sizes)
                ],
                axis=0,
            )
            start = jnp.zeros((rows, HEAD_SIZE), jnp.int32)
            before = jnp.int32(0)
            for other in range(members):
                before = before + lengths_ref[other]
                start = jnp.where(number >= before, before, start)
            angle = (number - start).astype(F32) * frequency_ref[...]
            cosine, sine = jnp.cos(angle), jnp.sin(angle)
            sine = jnp.where(iota((rows, HEAD_SIZE), 1) < HEAD_SIZE // 2, -sine, sine)
            mean = jnp.sum(squares[...], axis=1, keepdims=True) / (shards * steps * depth)
            scale = lax.rsqrt(mean + 1e-05)
            turned = query_ref.shape[1] + key_ref.shape[1]
            for at in range(0, sums.shape[1], HEAD_SIZE):
                columns = slice(at, at + HEAD_SIZE)
                head = sums[:, columns] * scale
                if at < turned:
                    head = head * cosine + pltpu.roll(head, HEAD_SIZE // 2, 1) * sine
                out_ref[:, columns] = head.astype(BF16)


def project(
    final, shards, bases, sizes, place, visits, lengths, lines, gain, weights, carried, frequency
):
    pieces = [piece for line in lines for piece in line]
    rows, width = sum(sizes), pieces[0].shape[1]
    depth = min(DEPTH, width)
    steps = width // depth
    columns = sum(weight.shape[1] for weight in weights)

    def block_of(visit, step, place_ref):
        step = jnp.where(place_ref[visit] < 0, steps - 1, step)
        return place_ref[visits + visit] * steps + step

    def whole(shape):
        return pl.BlockSpec(shape, lambda visit, step, place_ref, lengths_ref: (0, 0))

    def deep(block, dimension):
        def where(visit, step, place_ref, lengths_ref):
            at = block_of(visit, step, place_ref)
            return (at, 0) if dimension == 0 else (0, at)

        return pl.BlockSpec(block, where)

    operands = [*pieces, gain, *weights, *carried, frequency]
    in_specs = [whole(piece.shape) for piece in pieces]
    in_specs += [deep((1, depth), 1)]
    in_specs += [deep((depth, weight.shape[1]), 0) for weight in weights]
    in_specs += [whole(leaf.shape) for leaf in carried]
    in_specs += [whole((1, HEAD_SIZE))]
    scratch = [pltpu.VMEM((rows, depth), BF16)]
    if final:
        out_shape = [jax.ShapeDtypeStruct((rows, columns), BF16)]
        scratch = [pltpu.VMEM((rows, columns), F32), pltpu.VMEM((rows, 128), F32), *scratch]
    else:
        out_shape = [
            jax.ShapeDtypeStruct((rows, columns), F32),
            jax.ShapeDtypeStruct((rows, 128), F32),
        ]
    return pl.pallas_call(
        functools.partial(
            project_kernel,
            len(lines[0]),
            bool(carried),
            final,
            shards,
            steps,
            bases,
            sizes,
            lengths.shape[0],
        ),
        grid_spec=pltpu.PrefetchScalarGridSpec(
            num_scalar_prefetch=2,
            grid=(visits, steps),
            in_specs=in_specs,
            out_specs=[whole(leaf.shape) for leaf in out_shape],
            scratch_shapes=scratch,
        ),
        out_shape=out_shape,
        compiler_params=pltpu.CompilerParams(vmem_limit_bytes=32 * MEBI),
        cost_estimate=pl.CostEstimate(
            flops=2 * rows * width * columns * visits,
            bytes_accessed=2 * width * columns * visits + 8 * rows * columns,
            transcendentals=0,
        ),
        name="project",
    )(place, lengths, *operands)


def attend_kernel(
    chips, groups, known, prior, query_width, key_width, lengths_ref, plan_ref, *refs
):
    blocks, refs = refs[: -12 if prior else -10], refs[-10:]
    attended_out, cache_out, attended_ref, cache_ref, rows_ref, queries_ref = refs[:6]
    scores_ref, top_ref, sems, out_sems = refs[6:]
    workers = 2 * chips
    me = lax.axis_index("req")
    chip, core = lax.div(me, 2), lax.rem(me, 2)
    slots = cache_ref.shape[1]
    spans = slots // SPAN
    total = workers * sum(sum(sizes) for _, sizes in groups)
    copies = []
    for group, (bases, sizes) in enumerate(groups):
        for hop in range(chips):
            source = lax.rem(chip - hop + chips, chips) * 2
            for twin in range(2):
                owner = source + (core if twin == 0 else 1 - core)
                block = blocks[(group * chips + hop) * 2 + twin]
                first = 0
                for base, rows in zip(bases, sizes):
                    at = pl.multiple_of(base + owner * rows, ALIGN)
                    copies.append(
                        pltpu.make_async_copy(
                            block.at[pl.ds(first, rows), :],
                            rows_ref.at[pl.ds(at, rows), :],
                            sems.at[len(copies)],
                        )
                    )
                    first += rows
    for copy in copies:
        copy.start()
    rows_ref[total:, :] = jnp.zeros((rows_ref.shape[0] - total, rows_ref.shape[1]), BF16)
    for copy in copies:
        copy.wait()

    def window(row, columns):
        first = pl.multiple_of(lax.div(row, ALIGN) * ALIGN, ALIGN)
        shape = (SPAN, 2 * SPAN)
        hot = (iota(shape, 1) == iota(shape, 0) + (row - first)).astype(BF16)
        return jnp.dot(
            hot, rows_ref[pl.ds(first, 2 * SPAN), columns], preferred_element_type=F32
        )

    own_start, own_length = run_of(lengths_ref, me, workers)
    mine = (own_start + own_length <= known) & (own_start + own_length > prior)
    cache_copy = pltpu.make_async_copy(cache_ref, cache_out, out_sems.at[spans])

    @pl.when(mine)
    def _():
        def step(part, carry):
            at = pl.multiple_of(part * SPAN, SPAN)

            @pl.when(at < own_length)
            def _():
                picked = window(own_start + at, slice(query_width, query_width + 2 * key_width))
                live = at + iota(picked.shape, 0) < own_length
                picked = jnp.where(live, picked, 0.0).astype(BF16)
                cache_ref[0, pl.ds(at, SPAN), :] = picked[:, :key_width]
                cache_ref[1, pl.ds(at, SPAN), :] = picked[:, key_width:]

            @pl.when(at >= own_length)
            def _():
                empty = jnp.zeros((SPAN, key_width), BF16)
                cache_ref[0, pl.ds(at, SPAN), :] = empty
                cache_ref[1, pl.ds(at, SPAN), :] = empty

            return carry

        lax.fori_loop(0, spans, step, 0)
        cache_copy.start()

    heads, key_heads = query_width // HEAD_SIZE, key_width // HEAD_SIZE
    group = heads // key_heads
    factor = math.log2(math.e) / math.sqrt(HEAD_SIZE)
    tall = group * SPAN

    def span_of(slot):
        span = plan_ref[me * spans + slot]
        start, length = run_of(lengths_ref, lax.div(span, spans), workers)
        offset = lax.rem(span, spans) * SPAN
        dead = offset >= length
        needed = start + jnp.minimum(offset + SPAN, length)
        due = jnp.logical_not(dead) & (needed <= known) & (needed > prior)
        return start, length, offset, dead, due

    def result(slot):
        rows = pl.ds(pl.multiple_of(slot * SPAN, SPAN), SPAN)
        return pltpu.make_async_copy(
            attended_ref.at[rows, :], attended_out.at[rows, :], out_sems.at[slot]
        )

    def attend_slot(slot, carry):
        start, length, offset, dead, due = span_of(slot)
        out_rows = pl.ds(pl.multiple_of(slot * SPAN, SPAN), SPAN)

        if not prior:

            @pl.when(dead)
            def _():
                attended_ref[out_rows, :] = jnp.zeros((SPAN, query_width), BF16)
                result(slot).start()

        @pl.when(due)
        def _():
            queries = window(start + offset, slice(0, query_width)).astype(BF16)
            for head in range(heads):
                at = head % group * SPAN
                queries_ref[head // group, at : at + SPAN, :] = queries[
                    :, head * HEAD_SIZE : (head + 1) * HEAD_SIZE
                ]
            first = pl.multiple_of(lax.div(start, ALIGN) * ALIGN, ALIGN)
            shift = start - first
            reach = shift + jnp.minimum(offset + SPAN, length)
            tiles = lax.div(reach + TILE - 1, TILE)

            def columns(at, head):
                return slice(at + head * HEAD_SIZE, at + (head + 1) * HEAD_SIZE)

            def tile_rows(tile):
                return pl.ds(pl.multiple_of(first + tile * TILE, ALIGN), TILE)

            top_ref[...] = jnp.full(top_ref.shape, -1e30, F32)

            def score(tile, carry):
                key_pos = tile * TILE + iota((SPAN, TILE), 1) - shift
                query_pos = offset + iota((SPAN, TILE), 0)
                allowed = (key_pos >= 0) & (key_pos <= query_pos) & (key_pos < length)
                bias = jnp.where(allowed, 0.0, -1e30)
                bias = jnp.concatenate([bias] * group, axis=0)
                for head in range(key_heads):
                    scores = lax.dot_general(
                        queries_ref[head],
                        rows_ref[tile_rows(tile), columns(query_width, head)],
                        (((1,), (1,)), ((), ())),
                        preferred_element_type=F32,
                    )
                    scores = scores + bias
                    scores_ref[head, tile] = scores
                    top_ref[head] = jnp.maximum(top_ref[head], scores)
                return carry

            lax.fori_loop(0, tiles, score, 0)
            tops = [jnp.max(top_ref[head], axis=1, keepdims=True) for head in range(key_heads)]

            def mix(tile, carry):
                ones = jnp.ones((TILE, HEAD_SIZE), BF16)
                totals = []
                for head in range(key_heads):
                    weights = jnp.exp2((scores_ref[head, tile] - tops[head]) * factor)
                    values = rows_ref[tile_rows(tile), columns(query_width + key_width, head)]
                    values = jnp.concatenate([values, ones], axis=1)
                    totals.append(
                        carry[head]
                        + jnp.dot(weights.astype(BF16), values, preferred_element_type=F32)
                    )
                return tuple(totals)

            empty = jnp.zeros((tall, 2 * HEAD_SIZE), F32)
            mixed = lax.fori_loop(0, tiles, mix, (empty,) * key_heads)
            live = offset + iota((SPAN, HEAD_SIZE), 0) < length
            for head in range(heads):
                at = head % group * SPAN
                part = mixed[head // group][at : at + SPAN]
                part = part[:, :HEAD_SIZE] / part[:, HEAD_SIZE:]
                attended_ref[out_rows, columns(0, head)] = jnp.where(live, part, 0.0).astype(BF16)

            result(slot).start()

        return carry

    lax.fori_loop(0, spans, attend_slot, 0)

    def finish(slot, carry):
        _, _, _, dead, due = span_of(slot)

        @pl.when(due if prior else due | dead)
        def _():
            result(slot).wait()

        return carry

    lax.fori_loop(0, spans, finish, 0)

    @pl.when(mine)
    def _():
        cache_copy.wait()


def attend(chips, groups, known, prior, widths, slots, lengths, plan, blocks, outputs):
    query_width, key_width = widths
    width = query_width + 2 * key_width
    total = 2 * chips * sum(sum(sizes) for _, sizes in groups)
    copies = 2 * chips * sum(len(sizes) for _, sizes in groups)
    key_heads, tall = key_width // HEAD_SIZE, query_width // key_width * SPAN
    at = 2 + len(blocks)
    return pl.pallas_call(
        functools.partial(attend_kernel, chips, groups, known, prior, query_width, key_width),
        in_specs=[pl.BlockSpec(memory_space=pltpu.SMEM)] * 2
        + [pl.BlockSpec(memory_space=pl.ANY)] * (len(blocks) + len(outputs)),
        out_specs=[pl.BlockSpec(memory_space=pl.ANY)] * 2,
        out_shape=[
            jax.ShapeDtypeStruct((slots, query_width), BF16),
            jax.ShapeDtypeStruct((2, slots, key_width), BF16),
        ],
        input_output_aliases={at + index: index for index in range(len(outputs))},
        scratch_shapes=[
            pltpu.VMEM((slots, query_width), BF16),
            pltpu.VMEM((2, slots, key_width), BF16),
            pltpu.VMEM((total + TILE + ALIGN, width), BF16),
            pltpu.VMEM((key_heads, tall, HEAD_SIZE), BF16),
            pltpu.VMEM((key_heads, slots // TILE + 1, tall, TILE), F32),
            pltpu.VMEM((key_heads, tall, TILE), F32),
            pltpu.SemaphoreType.DMA((copies,)),
            pltpu.SemaphoreType.DMA((slots // SPAN + 1,)),
        ],
        compiler_params=pltpu.CompilerParams(vmem_limit_bytes=32 * MEBI),
        name="attend",
    )(lengths, plan, *blocks, *outputs)


def shift_chips(value, hop, chips):
    pairs = [(2 * x + c, 2 * ((x + hop) % chips) + c) for x in range(chips) for c in range(2)]
    return lax.ppermute(value, "req", pairs)


def swap_cores(value, chips):
    return lax.ppermute(value, "req", [(d, d ^ 1) for d in range(2 * chips)])


def local(
    chips, shards, tokens, norm_gain, w_query, key_weight, value_weight, lengths, plan
):
    workers = 2 * chips
    slots = tokens.shape[0]
    live = slots // 2
    sizes = [live * share // sum(SHARES) // ALIGN * ALIGN for share in SHARES]
    sizes[-1] = live - sum(sizes[:-1])
    bases = [workers * sum(sizes[:chunk]) for chunk in range(len(sizes))]
    weights = [
        pltpu.with_memory_space_constraint(weight, pltpu.HBM)
        for weight in (w_query, key_weight, value_weight)
    ]
    gain = norm_gain.astype(F32).reshape(1, -1)
    halfway = HEAD_SIZE // 2
    frequency = np.exp(-np.arange(halfway) * 2.0 / HEAD_SIZE * math.log(500000.0))
    frequency = jnp.asarray(np.tile(frequency, 2)[None, :], F32)

    twin = swap_cores(tokens, chips)
    first = deal(chips, bases[:1], sizes[:1], lengths, [tokens], [False])
    dealt = [
        *deal(chips, bases[:1], sizes[:1], lengths, [twin], [True], first),
        *deal(chips, bases[1:], sizes[1:], lengths, [tokens, twin], [False, True]),
    ]
    homes, aways = dealt[::2], dealt[1::2]
    routes, owned, depth = routes_of(shards)
    early = [piece for piece in range(len(owned)) if depth[piece] < max(depth)]
    late = [piece for piece in range(len(owned)) if depth[piece] == max(depth)]
    direct = [piece for piece in range(len(owned)) if depth[piece] == 1]

    sources = {source + 1 for source, _ in routes} - {0}
    awaited = [piece for piece in direct if piece in sources or owned[piece][0] >= 0]

    def relay(line):
        for index, (source, pairs) in enumerate(routes):
            if index + 1 not in direct:
                line[index + 1] = lax.ppermute(line[source + 1], "tp", pairs)

    lines = []
    for chunk in range(len(sizes)):
        arrived = [shift_chips(aways[chunk][hop - 1], hop, chips) for hop in range(1, chips)]
        places = [(chunk - 1, piece) for piece in awaited if chunk]
        places += [(chunk - 2, piece) for piece in late if chunk > 1]
        later = aways[chunk + 1 : chunk + 2] + [lines[at][piece] for at, piece in places]
        block, later = merge(homes[chunk], arrived, later)
        if chunk + 1 < len(sizes):
            aways[chunk + 1] = later.pop(0)
        for (at, piece), leaf in zip(places, later):
            lines[at][piece] = leaf
        line = {0: block}
        for index, (source, pairs) in enumerate(routes):
            if index + 1 in direct:
                line[index + 1] = lax.ppermute(block, "tp", pairs)
        lines.append(line)
        for line in lines[-2:-1]:
            relay(line)

    tables, counts = zip(
        *(visits_of([owned[piece] for piece in group], shards) for group in (early, late))
    )
    table = jnp.asarray(np.concatenate(tables, axis=1))
    table = lax.dynamic_index_in_dim(table, lax.axis_index("tp"), 0, keepdims=False)
    places = table[: 2 * counts[0]], table[2 * counts[0] :]

    blocks, groups, outputs, known = [], [], (), 0
    widths = w_query.shape[1], key_weight.shape[1]
    for chunks in GROUPS:
        if len(sizes) - 1 in chunks:
            relay(lines[-1])
        span = [bases[chunk] for chunk in chunks], [sizes[chunk] for chunk in chunks]
        groups.append(span)
        carried = ()
        for place, count, chosen in zip(places, counts, (early, late)):
            carried = project(
                chosen is late,
                shards,
                *span,
                place,
                count,
                lengths,
                [[lines[chunk][piece] for piece in chosen] for chunk in chunks],
                gain,
                weights,
                carried,
                frequency,
            )
        block = carried[0]
        here = [block] + [shift_chips(block, hop, chips) for hop in range(1, chips)]
        for piece in here:
            blocks += [piece, swap_cores(piece, chips)]
        prior, known = known, known + workers * sum(span[1])
        outputs = attend(
            chips, tuple(groups), known, prior, widths, slots, lengths, plan, blocks, outputs
        )
    return tuple(outputs)


def solution(mesh):
    placed = (
        P(("groups", "req"), "tp"),
        P(),
        P(None, "tp"),
        P(None, "tp"),
        P(None, "tp"),
        P("groups"),
        P("groups"),
    )
    return jax.shard_map(
        functools.partial(local, mesh.shape["req"] // 2, mesh.shape["tp"]),
        mesh=mesh,
        in_specs=placed,
        out_specs=(P(("groups", "req"), "tp"), P(None, ("groups", "req"), "tp")),
        check_vma=False,
    )
```

```python
import functools
import math

import jax
import jax.numpy as jnp
import numpy as np
from jax import lax
from jax.experimental import pallas as pl
from jax.experimental.pallas import tpu as pltpu
from jax.sharding import PartitionSpec as P

HEAD_SIZE = 128
SPAN = 128
ALIGN = 16
TILE = 2 * SPAN
SHARES = (4, 8, 4)
DEPTH = 1024
MEBI = 1024 * 1024
F32, BF16 = jnp.float32, jnp.bfloat16


def run_of(lengths_ref, request, count):
    start = jnp.int32(0)
    length = jnp.int32(0)
    for other in range(count):
        amount = lengths_ref[other]
        start = start + jnp.where(other < request, amount, 0)
        length = jnp.where(other == request, amount, length)
    return start, length


def iota(shape, dimension):
    return lax.broadcasted_iota(jnp.int32, shape, dimension)


def deal_kernel(chips, bases, sizes, twins, lengths_ref, *refs):
    me = lax.axis_index("req")
    chip, core = lax.div(me, 2), lax.rem(me, 2)
    sources, refs = refs[: len(twins)], refs[len(twins) :]
    count = 2 * len(sizes)
    priors, out_refs = refs[:-count], refs[-count:]
    requests = [me + 1 - 2 * core if twin else me for twin in twins]
    runs = [run_of(lengths_ref, request, 2 * chips) for request in requests]
    slots = sources[0].shape[0]
    for chunk, (base, rows) in enumerate(zip(bases, sizes)):
        home_ref, away_ref = out_refs[2 * chunk : 2 * chunk + 2]
        for hop in range(chips):
            target = lax.rem(chip + hop, chips) * 2 + core
            number = base + target * rows + iota((rows, slots), 0)
            slot = iota((rows, slots), 1)
            total = None
            for (start, length), source in zip(runs, sources):
                hot = ((number - start == slot) & (slot < length)).astype(BF16)
                part = jnp.dot(hot, source[...], preferred_element_type=F32)
                total = part if total is None else total + part
            total = total.astype(BF16)
            if hop == 0:
                home_ref[...] = total + priors[2 * chunk][...] if priors else total
            elif priors:
                away_ref[hop - 1] = total + priors[2 * chunk + 1][hop - 1]
            else:
                away_ref[hop - 1] = total


def deal(chips, bases, sizes, lengths, sources, twins, priors=()):
    slots, width = sources[0].shape
    block = min(1024, width)
    out_specs, out_shape = [], []
    for rows in sizes:
        out_specs += [
            pl.BlockSpec((rows, block), lambda i: (0, i)),
            pl.BlockSpec((chips - 1, rows, block), lambda i: (0, 0, i)),
        ]
        out_shape += [
            jax.ShapeDtypeStruct((rows, width), BF16),
            jax.ShapeDtypeStruct((chips - 1, rows, width), BF16),
        ]
    return pl.pallas_call(
        functools.partial(deal_kernel, chips, bases, sizes, twins),
        grid=(width // block,),
        in_specs=[pl.BlockSpec(memory_space=pltpu.SMEM)]
        + [pl.BlockSpec((slots, block), lambda i: (0, i)) for _ in sources]
        + (out_specs if priors else []),
        out_specs=out_specs,
        out_shape=out_shape,
        compiler_params=pltpu.CompilerParams(vmem_limit_bytes=24 * MEBI),
        name="deal",
    )(lengths, *sources, *priors)


def merge_kernel(count, passed, home_ref, *refs):
    total = home_ref[...]
    for ref in refs[:count]:
        total = total + ref[...]
    refs[len(refs) - 1 - passed][...] = total


def merge(home, arrived, later, anchors):
    count = len(arrived)
    vmem, anywhere = pl.BlockSpec(memory_space=pltpu.VMEM), pl.BlockSpec(memory_space=pl.ANY)
    block, *later = pl.pallas_call(
        functools.partial(merge_kernel, count, len(later)),
        in_specs=[vmem] * (count + 1) + [anywhere] * (len(later) + len(anchors)),
        out_specs=[vmem] + [anywhere] * len(later),
        out_shape=[jax.ShapeDtypeStruct(leaf.shape, leaf.dtype) for leaf in (home, *later)],
        input_output_aliases={count + 1 + at: 1 + at for at in range(len(later))},
        compiler_params=pltpu.CompilerParams(vmem_limit_bytes=8 * MEBI),
        name="merge",
    )(home, *arrived, *later, *anchors)
    return block, later


def after(arrays, anchors):
    def kernel(*refs):
        pass

    anywhere = pl.BlockSpec(memory_space=pl.ANY)
    return pl.pallas_call(
        kernel,
        in_specs=[anywhere] * (len(arrays) + len(anchors)),
        out_specs=[anywhere] * len(arrays),
        out_shape=[jax.ShapeDtypeStruct(leaf.shape, leaf.dtype) for leaf in arrays],
        input_output_aliases={at: at for at in range(len(arrays))},
        compiler_params=pltpu.CompilerParams(vmem_limit_bytes=MEBI),
        name="after",
    )(*arrays, *anchors)


def routes_of(shards):
    if shards == 4:
        routes = [
            (-1, [(1, 2), (2, 1)]),
            (-1, [(0, 1), (1, 0), (2, 3), (3, 2)]),
            (-1, [(0, 2), (1, 3), (2, 0), (3, 1)]),
            (2, [(2, 3), (1, 0)]),
        ]
    else:
        routes = []
        for step in range(1, shards):
            source = len(routes) - 2 if step > 1 else -1
            routes.append((source, [(at, at + 1) for at in range(step - 1, shards - 1)]))
            source = len(routes) - 2 if step > 1 else -1
            routes.append((source, [(at, at - 1) for at in range(1, shards - step + 1)]))
    held, depth = [list(range(shards))], [0]
    for source, pairs in routes:
        now = [-1] * shards
        for start, end in pairs:
            now[end] = held[source + 1][start]
        held.append(now)
        depth.append(depth[source + 1] + 1)
    return routes, held, depth


def visits_of(held, shards):
    visits = [
        [(piece, now[at]) for piece, now in enumerate(held) if now[at] >= 0]
        for at in range(shards)
    ]
    count = max(len(line) for line in visits)
    table = []
    for line in visits:
        pad = (-1, line[-1][1] if line else 0)
        line = line + [pad] * (count - len(line))
        table.append([piece for piece, _ in line] + [shard for _, shard in line])
    return np.array(table, np.int32), count


def angles_kernel(groups, members, lengths_ref, frequency_ref, anchor_ref, *out_refs):
    me = lax.axis_index("req")
    for group, (bases, sizes) in enumerate(groups):
        first = 0
        for base, rows in zip(bases, sizes):
            number = base + me * rows + iota((rows, HEAD_SIZE), 0)
            start = jnp.zeros((rows, HEAD_SIZE), jnp.int32)
            before = jnp.int32(0)
            for other in range(members):
                before = before + lengths_ref[other]
                start = jnp.where(number >= before, before, start)
            angle = (number - start).astype(F32) * frequency_ref[...]
            sine = jnp.sin(angle)
            lower = iota((rows, HEAD_SIZE), 1) < HEAD_SIZE // 2
            out_refs[2 * group][first : first + rows, :] = jnp.cos(angle)
            out_refs[2 * group + 1][first : first + rows, :] = jnp.where(lower, -sine, sine)
            first += rows


def angles(groups, lengths, frequency, anchor):
    shapes = [
        jax.ShapeDtypeStruct((sum(sizes), HEAD_SIZE), F32) for _, sizes in groups for _ in range(2)
    ]
    vmem = pl.BlockSpec(memory_space=pltpu.VMEM)
    tables = pl.pallas_call(
        functools.partial(angles_kernel, groups, lengths.shape[0]),
        in_specs=[
            pl.BlockSpec(memory_space=pltpu.SMEM),
            vmem,
            pl.BlockSpec(memory_space=pl.ANY),
        ],
        out_specs=[vmem] * len(shapes),
        out_shape=shapes,
        compiler_params=pltpu.CompilerParams(vmem_limit_bytes=8 * MEBI),
        name="angles",
    )(lengths, frequency, anchor)
    return [tables[at : at + 2] for at in range(0, len(tables), 2)]


def project_kernel(
    count, carries, final, shards, steps, sizes, anchored, place_ref, *refs
):
    refs = refs[anchored:]
    pieces, refs = refs[: count * len(sizes)], refs[count * len(sizes) :]
    gain_ref, query_ref, key_ref, value_ref = refs[:4]
    refs = refs[4:]
    if carries:
        sums_in, squares_in = refs[:2]
        refs = refs[2:]
    if final:
        cosine_ref, sine_ref, out_ref, *refs = refs
    sums, squares, chosen = refs
    visit, step = pl.program_id(0), pl.program_id(1)
    visits = pl.num_programs(0)
    rows, depth = chosen.shape
    piece = place_ref[visit]

    @pl.when((visit == 0) & (step == 0))
    def _():
        sums[...] = sums_in[...] if carries else jnp.zeros_like(sums)
        squares[...] = squares_in[...] if carries else jnp.zeros_like(squares)

    for index in range(count):

        @pl.when(piece == index)
        def _():
            columns = pl.ds(pl.multiple_of(step * depth, depth), depth)
            at = 0
            for chunk, size in enumerate(sizes):
                chosen[at : at + size, :] = pieces[chunk * count + index][:, columns]
                at += size

    @pl.when(piece >= 0)
    def _():
        wide = chosen[...].astype(F32)
        square = wide * wide
        part = square[:, :128]
        for at in range(128, depth, 128):
            part = part + square[:, at : at + 128]
        squares[...] += part
        scaled = (wide * gain_ref[...]).astype(BF16)
        at = 0
        for weight in (query_ref, key_ref, value_ref):
            columns = slice(at, at + weight.shape[1])
            sums[:, columns] += jnp.dot(scaled, weight[...], preferred_element_type=F32)
            at += weight.shape[1]

    if final:

        @pl.when((visit == visits - 1) & (step == steps - 1))
        def _():
            mean = jnp.sum(squares[...], axis=1, keepdims=True) / (shards * steps * depth)
            scale = lax.rsqrt(mean + 1e-05)
            turned = query_ref.shape[1] + key_ref.shape[1]
            for at in range(0, sums.shape[1], HEAD_SIZE):
                columns = slice(at, at + HEAD_SIZE)
                head = sums[:, columns] * scale
                if at < turned:
                    head = head * cosine_ref[...] + pltpu.roll(
                        head, HEAD_SIZE // 2, 1
                    ) * sine_ref[...]
                out_ref[:, columns] = head.astype(BF16)


def project(
    final, shards, sizes, place, visits, lines, gain, weights, carried, tables, anchors
):
    pieces = [piece for line in lines for piece in line]
    rows, width = sum(sizes), pieces[0].shape[1]
    depth = min(DEPTH, width)
    steps = width // depth
    columns = sum(weight.shape[1] for weight in weights)

    def block_of(visit, step, place_ref):
        step = jnp.where(place_ref[visit] < 0, steps - 1, step)
        return place_ref[visits + visit] * steps + step

    def whole(shape):
        return pl.BlockSpec(shape, lambda visit, step, place_ref: (0, 0))

    def deep(block, dimension):
        def where(visit, step, place_ref):
            at = block_of(visit, step, place_ref)
            return (at, 0) if dimension == 0 else (0, at)

        return pl.BlockSpec(block, where)

    extra = [*carried, *tables] if final else carried
    operands = [*anchors, *pieces, gain, *weights, *extra]
    in_specs = [pl.BlockSpec(memory_space=pl.ANY)] * len(anchors)
    in_specs += [whole(piece.shape) for piece in pieces]
    in_specs += [deep((1, depth), 1)]
    in_specs += [deep((depth, weight.shape[1]), 0) for weight in weights]
    in_specs += [whole(leaf.shape) for leaf in extra]
    scratch = [pltpu.VMEM((rows, depth), BF16)]
    if final:
        out_shape = [jax.ShapeDtypeStruct((rows, columns), BF16)]
        scratch = [pltpu.VMEM((rows, columns), F32), pltpu.VMEM((rows, 128), F32), *scratch]
    else:
        out_shape = [
            jax.ShapeDtypeStruct((rows, columns), F32),
            jax.ShapeDtypeStruct((rows, 128), F32),
        ]
    return pl.pallas_call(
        functools.partial(
            project_kernel,
            len(lines[0]),
            bool(carried),
            final,
            shards,
            steps,
            sizes,
            len(anchors),
        ),
        grid_spec=pltpu.PrefetchScalarGridSpec(
            num_scalar_prefetch=1,
            grid=(visits, steps),
            in_specs=in_specs,
            out_specs=[whole(leaf.shape) for leaf in out_shape],
            scratch_shapes=scratch,
        ),
        out_shape=out_shape,
        compiler_params=pltpu.CompilerParams(vmem_limit_bytes=32 * MEBI),
        name="project",
    )(place, *operands)


def attend_kernel(
    chips, groups, known, prior, query_width, key_width, lengths_ref, plan_ref, *refs
):
    blocks, refs = refs[: -12 if prior else -10], refs[-10:]
    attended_out, cache_out, attended_ref, cache_ref, rows_ref, queries_ref = refs[:6]
    scores_ref, top_ref, sems, out_sems = refs[6:]
    workers = 2 * chips
    me = lax.axis_index("req")
    chip, core = lax.div(me, 2), lax.rem(me, 2)
    slots = cache_ref.shape[1]
    spans = slots // SPAN
    total = workers * sum(sum(sizes) for _, sizes in groups)
    copies = []
    for group, (bases, sizes) in enumerate(groups):
        for hop in range(chips):
            source = lax.rem(chip - hop + chips, chips) * 2
            for twin in range(2):
                owner = source + (core if twin == 0 else 1 - core)
                block = blocks[(group * chips + hop) * 2 + twin]
                first = 0
                for base, rows in zip(bases, sizes):
                    at = pl.multiple_of(base + owner * rows, ALIGN)
                    copies.append(
                        pltpu.make_async_copy(
                            block.at[pl.ds(first, rows), :],
                            rows_ref.at[pl.ds(at, rows), :],
                            sems.at[len(copies)],
                        )
                    )
                    first += rows
    for copy in copies:
        copy.start()
    rows_ref[total:, :] = jnp.zeros((rows_ref.shape[0] - total, rows_ref.shape[1]), BF16)
    for copy in copies:
        copy.wait()

    def window(row, columns):
        first = pl.multiple_of(lax.div(row, ALIGN) * ALIGN, ALIGN)
        shape = (SPAN, 2 * SPAN)
        hot = (iota(shape, 1) == iota(shape, 0) + (row - first)).astype(BF16)
        return jnp.dot(
            hot, rows_ref[pl.ds(first, 2 * SPAN), columns], preferred_element_type=F32
        )

    own_start, own_length = run_of(lengths_ref, me, workers)
    mine = (own_start + own_length <= known) & (own_start + own_length > prior)
    cache_copy = pltpu.make_async_copy(cache_ref, cache_out, out_sems.at[spans])

    @pl.when(mine)
    def _():
        def step(part, carry):
            at = pl.multiple_of(part * SPAN, SPAN)

            @pl.when(at < own_length)
            def _():
                picked = window(own_start + at, slice(query_width, query_width + 2 * key_width))
                live = at + iota(picked.shape, 0) < own_length
                picked = jnp.where(live, picked, 0.0).astype(BF16)
                cache_ref[0, pl.ds(at, SPAN), :] = picked[:, :key_width]
                cache_ref[1, pl.ds(at, SPAN), :] = picked[:, key_width:]

            @pl.when(at >= own_length)
            def _():
                empty = jnp.zeros((SPAN, key_width), BF16)
                cache_ref[0, pl.ds(at, SPAN), :] = empty
                cache_ref[1, pl.ds(at, SPAN), :] = empty

            return carry

        lax.fori_loop(0, spans, step, 0)
        cache_copy.start()

    heads, key_heads = query_width // HEAD_SIZE, key_width // HEAD_SIZE
    group = heads // key_heads
    factor = math.log2(math.e) / math.sqrt(HEAD_SIZE)
    tall = group * SPAN

    def span_of(slot):
        span = plan_ref[me * spans + slot]
        start, length = run_of(lengths_ref, lax.div(span, spans), workers)
        offset = lax.rem(span, spans) * SPAN
        dead = offset >= length
        needed = start + jnp.minimum(offset + SPAN, length)
        due = jnp.logical_not(dead) & (needed <= known) & (needed > prior)
        return start, length, offset, dead, due

    def result(slot):
        rows = pl.ds(pl.multiple_of(slot * SPAN, SPAN), SPAN)
        return pltpu.make_async_copy(
            attended_ref.at[rows, :], attended_out.at[rows, :], out_sems.at[slot]
        )

    def attend_slot(slot, carry):
        start, length, offset, dead, due = span_of(slot)
        out_rows = pl.ds(pl.multiple_of(slot * SPAN, SPAN), SPAN)

        if not prior:

            @pl.when(dead)
            def _():
                attended_ref[out_rows, :] = jnp.zeros((SPAN, query_width), BF16)
                result(slot).start()

        @pl.when(due)
        def _():
            queries = window(start + offset, slice(0, query_width)).astype(BF16)
            for head in range(heads):
                at = head % group * SPAN
                queries_ref[head // group, at : at + SPAN, :] = queries[
                    :, head * HEAD_SIZE : (head + 1) * HEAD_SIZE
                ]
            first = pl.multiple_of(lax.div(start, ALIGN) * ALIGN, ALIGN)
            shift = start - first
            reach = shift + jnp.minimum(offset + SPAN, length)
            tiles = lax.div(reach + TILE - 1, TILE)

            def columns(at, head):
                return slice(at + head * HEAD_SIZE, at + (head + 1) * HEAD_SIZE)

            def tile_rows(tile):
                return pl.ds(pl.multiple_of(first + tile * TILE, ALIGN), TILE)

            top_ref[...] = jnp.full(top_ref.shape, -1e30, F32)

            def score(tile, carry):
                key_pos = tile * TILE + iota((SPAN, TILE), 1) - shift
                query_pos = offset + iota((SPAN, TILE), 0)
                allowed = (key_pos >= 0) & (key_pos <= query_pos) & (key_pos < length)
                bias = jnp.where(allowed, 0.0, -1e30)
                bias = jnp.concatenate([bias] * group, axis=0)
                for head in range(key_heads):
                    scores = lax.dot_general(
                        queries_ref[head],
                        rows_ref[tile_rows(tile), columns(query_width, head)],
                        (((1,), (1,)), ((), ())),
                        preferred_element_type=F32,
                    )
                    scores = scores + bias
                    scores_ref[head, tile] = scores
                    top_ref[head] = jnp.maximum(top_ref[head], scores)
                return carry

            lax.fori_loop(0, tiles, score, 0)
            tops = [jnp.max(top_ref[head], axis=1, keepdims=True) for head in range(key_heads)]

            def mix(tile, carry):
                ones = jnp.ones((TILE, HEAD_SIZE), BF16)
                totals = []
                for head in range(key_heads):
                    weights = jnp.exp2((scores_ref[head, tile] - tops[head]) * factor)
                    values = rows_ref[tile_rows(tile), columns(query_width + key_width, head)]
                    values = jnp.concatenate([values, ones], axis=1)
                    totals.append(
                        carry[head]
                        + jnp.dot(weights.astype(BF16), values, preferred_element_type=F32)
                    )
                return tuple(totals)

            empty = jnp.zeros((tall, 2 * HEAD_SIZE), F32)
            mixed = lax.fori_loop(0, tiles, mix, (empty,) * key_heads)
            live = offset + iota((SPAN, HEAD_SIZE), 0) < length
            for head in range(heads):
                at = head % group * SPAN
                part = mixed[head // group][at : at + SPAN]
                part = part[:, :HEAD_SIZE] / part[:, HEAD_SIZE:]
                attended_ref[out_rows, columns(0, head)] = jnp.where(live, part, 0.0).astype(BF16)

            result(slot).start()

        return carry

    lax.fori_loop(0, spans, attend_slot, 0)

    def finish(slot, carry):
        _, _, _, dead, due = span_of(slot)

        @pl.when(due if prior else due | dead)
        def _():
            result(slot).wait()

        return carry

    lax.fori_loop(0, spans, finish, 0)

    @pl.when(mine)
    def _():
        cache_copy.wait()


def attend(chips, groups, known, prior, widths, slots, lengths, plan, blocks, outputs):
    query_width, key_width = widths
    width = query_width + 2 * key_width
    total = 2 * chips * sum(sum(sizes) for _, sizes in groups)
    copies = 2 * chips * sum(len(sizes) for _, sizes in groups)
    key_heads, tall = key_width // HEAD_SIZE, query_width // key_width * SPAN
    at = 2 + len(blocks)
    return pl.pallas_call(
        functools.partial(attend_kernel, chips, groups, known, prior, query_width, key_width),
        in_specs=[pl.BlockSpec(memory_space=pltpu.SMEM)] * 2
        + [pl.BlockSpec(memory_space=pl.ANY)] * (len(blocks) + len(outputs)),
        out_specs=[pl.BlockSpec(memory_space=pl.ANY)] * 2,
        out_shape=[
            jax.ShapeDtypeStruct((slots, query_width), BF16),
            jax.ShapeDtypeStruct((2, slots, key_width), BF16),
        ],
        input_output_aliases={at + index: index for index in range(len(outputs))},
        scratch_shapes=[
            pltpu.VMEM((slots, query_width), BF16),
            pltpu.VMEM((2, slots, key_width), BF16),
            pltpu.VMEM((total + TILE + ALIGN, width), BF16),
            pltpu.VMEM((key_heads, tall, HEAD_SIZE), BF16),
            pltpu.VMEM((key_heads, slots // TILE + 1, tall, TILE), F32),
            pltpu.VMEM((key_heads, tall, TILE), F32),
            pltpu.SemaphoreType.DMA((copies,)),
            pltpu.SemaphoreType.DMA((slots // SPAN + 1,)),
        ],
        compiler_params=pltpu.CompilerParams(vmem_limit_bytes=32 * MEBI),
        name="attend",
    )(lengths, plan, *blocks, *outputs)


def shift_chips(value, hop, chips):
    pairs = [(2 * x + c, 2 * ((x + hop) % chips) + c) for x in range(chips) for c in range(2)]
    return lax.ppermute(value, "req", pairs)


def swap_cores(value, chips):
    return lax.ppermute(value, "req", [(d, d ^ 1) for d in range(2 * chips)])


def local(
    chips, shards, tokens, norm_gain, w_query, key_weight, value_weight, lengths, plan
):
    workers = 2 * chips
    slots = tokens.shape[0]
    live = slots // 2
    sizes = [live * share // sum(SHARES) // ALIGN * ALIGN for share in SHARES]
    sizes[-1] = live - sum(sizes[:-1])
    bases = [workers * sum(sizes[:chunk]) for chunk in range(len(sizes))]
    weights = [
        pltpu.with_memory_space_constraint(weight, pltpu.HBM)
        for weight in (w_query, key_weight, value_weight)
    ]
    gain = norm_gain.astype(F32).reshape(1, -1)
    halfway = HEAD_SIZE // 2
    frequency = np.exp(-np.arange(halfway) * 2.0 / HEAD_SIZE * math.log(500000.0))
    frequency = jnp.asarray(np.tile(frequency, 2)[None, :], F32)

    twin = swap_cores(tokens, chips)
    first = deal(chips, bases[:1], sizes[:1], lengths, [tokens], [False])
    dealt = [
        *deal(chips, bases[:1], sizes[:1], lengths, [twin], [True], first),
        *deal(chips, bases[1:], sizes[1:], lengths, [tokens, twin], [False, True]),
    ]
    homes, aways = dealt[::2], dealt[1::2]
    routes, owned, depth = routes_of(shards)
    direct = [piece for piece in range(len(owned)) if depth[piece] == 1]

    sources = {source + 1 for source, _ in routes} - {0}
    awaited = [piece for piece in direct if piece in sources or owned[piece][0] >= 0]
    early = [0, *awaited]
    late = [piece for piece in range(len(owned)) if piece not in early]

    tables, counts = zip(
        *(visits_of([owned[piece] for piece in group], shards) for group in (early, late))
    )
    table = jnp.asarray(np.concatenate(tables, axis=1))
    table = lax.dynamic_index_in_dim(table, lax.axis_index("tp"), 0, keepdims=False)
    places = table[: 2 * counts[0]], table[2 * counts[0] :]

    groups = [([base], [rows]) for base, rows in zip(bases, sizes)]
    widths = w_query.shape[1], key_weight.shape[1]

    def first_sums(at):
        lists = [[lines[at][piece] for piece in early]]
        shape = shards, sizes[at : at + 1], places[0], counts[0]
        return project(False, *shape, lists, gain, weights, (), (), ())

    def finished(at, sums, anchors):
        lists = [[lines[at][piece] for piece in late]]
        shape = shards, sizes[at : at + 1], places[1], counts[1]
        return project(True, *shape, lists, gain, weights, sums, turns[at], anchors)[0]

    def from_chips(block):
        return [shift_chips(block, hop, chips) for hop in range(1, chips)]

    def all_blocks(block, arrived):
        return [leaf for piece in (block, *arrived) for leaf in (piece, swap_cores(piece, chips))]

    lines, own, sent = [], [], []
    last = len(sizes) - 1
    for chunk in range(len(sizes) + 1):
        passed = [0, *(piece for piece in awaited if piece in sources)] if chunk else []
        later = [lines[-1][piece] for piece in passed] + aways[chunk + 1 : chunk + 2]
        anchors = [lines[-1][piece] for piece in awaited if piece not in passed] if chunk else []
        if chunk > 1:
            own.append(finished(chunk - 2, first_sums(chunk - 2), ()))
            sent.append(from_chips(own[-1]))
            anchors.append(own[-1])
        if chunk <= last:
            arrived = [shift_chips(aways[chunk][hop - 1], hop, chips) for hop in range(1, chips)]
            block, later = merge(homes[chunk], arrived, later, anchors)
        else:
            later = after(later, [*anchors, *sent[-2]])
        aways[chunk + 1 : chunk + 2] = later[len(passed) :]
        if chunk:
            lines[-1].update(zip(passed, later))
            for index, (source, pairs) in enumerate(routes):
                if index + 1 in late:
                    lines[-1][index + 1] = lax.ppermute(lines[-1][source + 1], "tp", pairs)
        if chunk <= last:
            line = {0: block}
            for index, (source, pairs) in enumerate(routes):
                if index + 1 in awaited:
                    line[index + 1] = lax.ppermute(block, "tp", pairs)
            lines.append(line)
        if chunk == 1:
            turns = angles(groups, lengths, frequency, block)
    own.append(finished(last, first_sums(last), sent[-1]))
    blocks = []
    for at in range(last):
        blocks += all_blocks(own[at], after(sent[at], own[at + 1 : at + 2]))
    sent.append(from_chips(own[last]))
    known = workers * sum(sizes[:-1])
    common = widths, slots, lengths, plan
    outputs = attend(chips, groups[:-1], known, 0, *common, blocks, ())
    blocks += all_blocks(own[last], after(sent[last], outputs[:1]))
    return tuple(attend(chips, groups, workers * live, known, *common, blocks, outputs))


def solution(mesh):
    placed = (
        P(("groups", "req"), "tp"),
        P(),
        P(None, "tp"),
        P(None, "tp"),
        P(None, "tp"),
        P("groups"),
        P("groups"),
    )
    return jax.shard_map(
        functools.partial(local, mesh.shape["req"] // 2, mesh.shape["tp"]),
        mesh=mesh,
        in_specs=placed,
        out_specs=(P(("groups", "req"), "tp"), P(None, ("groups", "req"), "tp")),
        check_vma=False,
    )
```

```python
import functools
import math

import jax
import jax.numpy as jnp
import numpy as np
from jax import lax
from jax.experimental import pallas as pl
from jax.experimental.pallas import tpu as pltpu
from jax.sharding import PartitionSpec as P

HEAD_SIZE = 128
SPAN = 128
ALIGN = 16
TILE = 2 * SPAN
SHARES = (4, 8, 4)
DEPTH = 1024
MEBI = 1024 * 1024
F32, BF16 = jnp.float32, jnp.bfloat16


def run_of(lengths_ref, request, count):
    start = jnp.int32(0)
    length = jnp.int32(0)
    for other in range(count):
        amount = lengths_ref[other]
        start = start + jnp.where(other < request, amount, 0)
        length = jnp.where(other == request, amount, length)
    return start, length


def iota(shape, dimension):
    return lax.broadcasted_iota(jnp.int32, shape, dimension)


def deal_kernel(chips, bases, sizes, twins, lengths_ref, *refs):
    me = lax.axis_index("req")
    chip, core = lax.div(me, 2), lax.rem(me, 2)
    sources, refs = refs[: len(twins)], refs[len(twins) :]
    count = 2 * len(sizes)
    priors, out_refs = refs[:-count], refs[-count:]
    requests = [me + 1 - 2 * core if twin else me for twin in twins]
    runs = [run_of(lengths_ref, request, 2 * chips) for request in requests]
    slots = sources[0].shape[0]
    for chunk, (base, rows) in enumerate(zip(bases, sizes)):
        home_ref, away_ref = out_refs[2 * chunk : 2 * chunk + 2]
        for hop in range(chips):
            target = lax.rem(chip + hop, chips) * 2 + core
            number = base + target * rows + iota((rows, slots), 0)
            slot = iota((rows, slots), 1)
            total = None
            for (start, length), source in zip(runs, sources):
                hot = ((number - start == slot) & (slot < length)).astype(BF16)
                part = jnp.dot(hot, source[...], preferred_element_type=F32)
                total = part if total is None else total + part
            total = total.astype(BF16)
            if hop == 0:
                home_ref[...] = total + priors[2 * chunk][...] if priors else total
            elif priors:
                away_ref[hop - 1] = total + priors[2 * chunk + 1][hop - 1]
            else:
                away_ref[hop - 1] = total


def deal(chips, bases, sizes, lengths, sources, twins, priors=()):
    slots, width = sources[0].shape
    block = min(1024, width)
    out_specs, out_shape = [], []
    for rows in sizes:
        out_specs += [
            pl.BlockSpec((rows, block), lambda i: (0, i)),
            pl.BlockSpec((chips - 1, rows, block), lambda i: (0, 0, i)),
        ]
        out_shape += [
            jax.ShapeDtypeStruct((rows, width), BF16),
            jax.ShapeDtypeStruct((chips - 1, rows, width), BF16),
        ]
    return pl.pallas_call(
        functools.partial(deal_kernel, chips, bases, sizes, twins),
        grid=(width // block,),
        in_specs=[pl.BlockSpec(memory_space=pltpu.SMEM)]
        + [pl.BlockSpec((slots, block), lambda i: (0, i)) for _ in sources]
        + (out_specs if priors else []),
        out_specs=out_specs,
        out_shape=out_shape,
        compiler_params=pltpu.CompilerParams(vmem_limit_bytes=24 * MEBI),
        name="deal",
    )(lengths, *sources, *priors)


def merge_kernel(count, passed, home_ref, *refs):
    total = home_ref[...]
    for ref in refs[:count]:
        total = total + ref[...]
    refs[len(refs) - 1 - passed][...] = total


def merge(home, arrived, later, anchors):
    count = len(arrived)
    vmem, anywhere = pl.BlockSpec(memory_space=pltpu.VMEM), pl.BlockSpec(memory_space=pl.ANY)
    block, *later = pl.pallas_call(
        functools.partial(merge_kernel, count, len(later)),
        in_specs=[vmem] * (count + 1) + [anywhere] * (len(later) + len(anchors)),
        out_specs=[vmem] + [anywhere] * len(later),
        out_shape=[jax.ShapeDtypeStruct(leaf.shape, leaf.dtype) for leaf in (home, *later)],
        input_output_aliases={count + 1 + at: 1 + at for at in range(len(later))},
        compiler_params=pltpu.CompilerParams(vmem_limit_bytes=8 * MEBI),
        name="merge",
    )(home, *arrived, *later, *anchors)
    return block, later


def after(arrays, anchors):
    def kernel(*refs):
        pass

    anywhere = pl.BlockSpec(memory_space=pl.ANY)
    return pl.pallas_call(
        kernel,
        in_specs=[anywhere] * (len(arrays) + len(anchors)),
        out_specs=[anywhere] * len(arrays),
        out_shape=[jax.ShapeDtypeStruct(leaf.shape, leaf.dtype) for leaf in arrays],
        input_output_aliases={at: at for at in range(len(arrays))},
        compiler_params=pltpu.CompilerParams(vmem_limit_bytes=MEBI),
        name="after",
    )(*arrays, *anchors)


def routes_of(shards):
    if shards == 4:
        routes = [
            (-1, [(1, 2), (2, 1)]),
            (-1, [(0, 1), (1, 0), (2, 3), (3, 2)]),
            (-1, [(0, 2), (1, 3), (2, 0), (3, 1)]),
            (2, [(2, 3), (1, 0)]),
        ]
    else:
        routes = []
        for step in range(1, shards):
            source = len(routes) - 2 if step > 1 else -1
            routes.append((source, [(at, at + 1) for at in range(step - 1, shards - 1)]))
            source = len(routes) - 2 if step > 1 else -1
            routes.append((source, [(at, at - 1) for at in range(1, shards - step + 1)]))
    held, depth = [list(range(shards))], [0]
    for source, pairs in routes:
        now = [-1] * shards
        for start, end in pairs:
            now[end] = held[source + 1][start]
        held.append(now)
        depth.append(depth[source + 1] + 1)
    return routes, held, depth


def visits_of(held, shards):
    visits = [
        [(piece, now[at]) for piece, now in enumerate(held) if now[at] >= 0]
        for at in range(shards)
    ]
    count = max(len(line) for line in visits)
    table = []
    for line in visits:
        pad = (-1, line[-1][1] if line else 0)
        line = line + [pad] * (count - len(line))
        table.append([piece for piece, _ in line] + [shard for _, shard in line])
    return np.array(table, np.int32), count


def angles_kernel(groups, members, lengths_ref, frequency_ref, anchor_ref, *out_refs):
    me = lax.axis_index("req")
    for group, (bases, sizes) in enumerate(groups):
        first = 0
        for base, rows in zip(bases, sizes):
            number = base + me * rows + iota((rows, HEAD_SIZE), 0)
            start = jnp.zeros((rows, HEAD_SIZE), jnp.int32)
            before = jnp.int32(0)
            for other in range(members):
                before = before + lengths_ref[other]
                start = jnp.where(number >= before, before, start)
            angle = (number - start).astype(F32) * frequency_ref[...]
            sine = jnp.sin(angle)
            lower = iota((rows, HEAD_SIZE), 1) < HEAD_SIZE // 2
            out_refs[2 * group][first : first + rows, :] = jnp.cos(angle)
            out_refs[2 * group + 1][first : first + rows, :] = jnp.where(lower, -sine, sine)
            first += rows


def angles(groups, lengths, frequency, anchor):
    shapes = [
        jax.ShapeDtypeStruct((sum(sizes), HEAD_SIZE), F32) for _, sizes in groups for _ in range(2)
    ]
    vmem = pl.BlockSpec(memory_space=pltpu.VMEM)
    tables = pl.pallas_call(
        functools.partial(angles_kernel, groups, lengths.shape[0]),
        in_specs=[
            pl.BlockSpec(memory_space=pltpu.SMEM),
            vmem,
            pl.BlockSpec(memory_space=pl.ANY),
        ],
        out_specs=[vmem] * len(shapes),
        out_shape=shapes,
        compiler_params=pltpu.CompilerParams(vmem_limit_bytes=8 * MEBI),
        name="angles",
    )(lengths, frequency, anchor)
    return [tables[at : at + 2] for at in range(0, len(tables), 2)]


def project_kernel(
    count, carries, final, shards, steps, sizes, anchored, streams, place_ref, *refs
):
    refs = refs[anchored:]
    pieces, refs = refs[: count * len(sizes)], refs[count * len(sizes) :]
    gain_ref, refs = refs[0], refs[1:]
    weights = []
    for parts in streams:
        weights.append(refs[:parts])
        refs = refs[parts:]
    if carries:
        sums_in, squares_in = refs[:2]
        refs = refs[2:]
    if final:
        cosine_ref, sine_ref, out_ref, *refs = refs
    sums, squares, chosen = refs
    visit, step = pl.program_id(0), pl.program_id(1)
    visits = pl.num_programs(0)
    rows, depth = chosen.shape
    piece = place_ref[visit]

    @pl.when((visit == 0) & (step == 0))
    def _():
        sums[...] = sums_in[...] if carries else jnp.zeros_like(sums)
        squares[...] = squares_in[...] if carries else jnp.zeros_like(squares)

    for index in range(count):

        @pl.when(piece == index)
        def _():
            columns = pl.ds(pl.multiple_of(step * depth, depth), depth)
            at = 0
            for chunk, size in enumerate(sizes):
                chosen[at : at + size, :] = pieces[chunk * count + index][:, columns]
                at += size

    @pl.when(piece >= 0)
    def _():
        wide = chosen[...].astype(F32)
        square = wide * wide
        part = square[:, :128]
        for at in range(128, depth, 128):
            part = part + square[:, at : at + 128]
        squares[...] += part
        scaled = (wide * gain_ref[...]).astype(BF16)
        at = 0
        for weight in weights:
            columns = slice(at, at + weight[0].shape[1])
            share = depth // len(weight)
            total = sums[:, columns]
            for part, ref in enumerate(weight):
                deep = scaled[:, part * share : (part + 1) * share]
                total += jnp.dot(deep, ref[...], preferred_element_type=F32)
            sums[:, columns] = total
            at += weight[0].shape[1]

    if final:

        @pl.when((visit == visits - 1) & (step == steps - 1))
        def _():
            mean = jnp.sum(squares[...], axis=1, keepdims=True) / (shards * steps * depth)
            scale = lax.rsqrt(mean + 1e-05)
            turned = sums.shape[1] - weights[-1][0].shape[1]
            for at in range(0, sums.shape[1], HEAD_SIZE):
                columns = slice(at, at + HEAD_SIZE)
                head = sums[:, columns] * scale
                if at < turned:
                    head = head * cosine_ref[...] + pltpu.roll(
                        head, HEAD_SIZE // 2, 1
                    ) * sine_ref[...]
                out_ref[:, columns] = head.astype(BF16)


def project(
    final, shards, sizes, place, visits, lines, gain, weights, carried, tables, anchors
):
    pieces = [piece for line in lines for piece in line]
    rows, width = sum(sizes), pieces[0].shape[1]
    depth = min(DEPTH, width)
    steps = width // depth
    columns = sum(weight.shape[1] for weight in weights)

    def block_of(visit, step, place_ref):
        step = jnp.where(place_ref[visit] < 0, steps - 1, step)
        return place_ref[visits + visit] * steps + step

    def whole(shape):
        return pl.BlockSpec(shape, lambda visit, step, place_ref: (0, 0))

    def deep(block, dimension, part=0, parts=1):
        def where(visit, step, place_ref):
            at = block_of(visit, step, place_ref) * parts + part
            return (at, 0) if dimension == 0 else (0, at)

        return pl.BlockSpec(block, where)

    extra = [*carried, *tables] if final else carried
    streams = [weight.shape[1] // weights[-1].shape[1] for weight in weights]
    cut = [weight for weight, parts in zip(weights, streams) for _ in range(parts)]
    operands = [*anchors, *pieces, gain, *cut, *extra]
    in_specs = [pl.BlockSpec(memory_space=pl.ANY)] * len(anchors)
    in_specs += [whole(piece.shape) for piece in pieces]
    in_specs += [deep((1, depth), 1)]
    in_specs += [
        deep((depth // parts, weight.shape[1]), 0, part, parts)
        for weight, parts in zip(weights, streams)
        for part in range(parts)
    ]
    in_specs += [whole(leaf.shape) for leaf in extra]
    scratch = [pltpu.VMEM((rows, depth), BF16)]
    if final:
        out_shape = [jax.ShapeDtypeStruct((rows, columns), BF16)]
        scratch = [pltpu.VMEM((rows, columns), F32), pltpu.VMEM((rows, 128), F32), *scratch]
    else:
        out_shape = [
            jax.ShapeDtypeStruct((rows, columns), F32),
            jax.ShapeDtypeStruct((rows, 128), F32),
        ]
    return pl.pallas_call(
        functools.partial(
            project_kernel,
            len(lines[0]),
            bool(carried),
            final,
            shards,
            steps,
            sizes,
            len(anchors),
            streams,
        ),
        grid_spec=pltpu.PrefetchScalarGridSpec(
            num_scalar_prefetch=1,
            grid=(visits, steps),
            in_specs=in_specs,
            out_specs=[whole(leaf.shape) for leaf in out_shape],
            scratch_shapes=scratch,
        ),
        out_shape=out_shape,
        compiler_params=pltpu.CompilerParams(vmem_limit_bytes=32 * MEBI),
        name="project",
    )(place, *operands)


def attend_kernel(
    chips, groups, known, prior, query_width, key_width, lengths_ref, plan_ref, *refs
):
    blocks, refs = refs[: -13 if prior else -11], refs[-11:]
    attended_out, cache_out, token_ref, attended_ref, cache_ref, rows_ref, queries_ref = refs[:7]
    scores_ref, top_ref, sems, out_sems = refs[7:]
    token_ref[...] = jnp.zeros_like(token_ref)
    workers = 2 * chips
    me = lax.axis_index("req")
    chip, core = lax.div(me, 2), lax.rem(me, 2)
    slots = cache_ref.shape[1]
    spans = slots // SPAN
    total = workers * sum(sum(sizes) for _, sizes in groups)
    end = needed = jnp.int32(0)
    for other in range(workers):
        end = end + lengths_ref[other]
        needed = jnp.where(end <= prior, end, needed)
    copies = []
    for group, (bases, sizes) in enumerate(groups):
        for hop in range(chips):
            source = lax.rem(chip - hop + chips, chips) * 2
            for twin in range(2):
                owner = source + (core if twin == 0 else 1 - core)
                block = blocks[(group * chips + hop) * 2 + twin]
                first = 0
                for base, rows in zip(bases, sizes):
                    at = pl.multiple_of(base + owner * rows, ALIGN)
                    copy = pltpu.make_async_copy(
                        block.at[pl.ds(first, rows), :],
                        rows_ref.at[pl.ds(at, rows), :],
                        sems.at[len(copies)],
                    )
                    copies.append((at + rows > needed, copy))
                    first += rows
    for wanted, copy in copies:

        @pl.when(wanted)
        def _():
            copy.start()

    rows_ref[total:, :] = jnp.zeros((rows_ref.shape[0] - total, rows_ref.shape[1]), BF16)
    for wanted, copy in copies:

        @pl.when(wanted)
        def _():
            copy.wait()

    def window(row, columns):
        first = pl.multiple_of(lax.div(row, ALIGN) * ALIGN, ALIGN)
        shape = (SPAN, 2 * SPAN)
        hot = (iota(shape, 1) == iota(shape, 0) + (row - first)).astype(BF16)
        return jnp.dot(
            hot, rows_ref[pl.ds(first, 2 * SPAN), columns], preferred_element_type=F32
        )

    own_start, own_length = run_of(lengths_ref, me, workers)
    mine = (own_start + own_length <= known) & (own_start + own_length > prior)
    cache_copy = pltpu.make_async_copy(cache_ref, cache_out, out_sems.at[spans])

    @pl.when(mine)
    def _():
        def step(part, carry):
            at = pl.multiple_of(part * SPAN, SPAN)

            @pl.when(at < own_length)
            def _():
                picked = window(own_start + at, slice(query_width, query_width + 2 * key_width))
                live = at + iota(picked.shape, 0) < own_length
                picked = jnp.where(live, picked, 0.0).astype(BF16)
                cache_ref[0, pl.ds(at, SPAN), :] = picked[:, :key_width]
                cache_ref[1, pl.ds(at, SPAN), :] = picked[:, key_width:]

            @pl.when(at >= own_length)
            def _():
                empty = jnp.zeros((SPAN, key_width), BF16)
                cache_ref[0, pl.ds(at, SPAN), :] = empty
                cache_ref[1, pl.ds(at, SPAN), :] = empty

            return carry

        lax.fori_loop(0, spans, step, 0)
        cache_copy.start()

    heads, key_heads = query_width // HEAD_SIZE, key_width // HEAD_SIZE
    group = heads // key_heads
    factor = math.log2(math.e) / math.sqrt(HEAD_SIZE)
    tall = group * SPAN

    def span_of(slot):
        span = plan_ref[me * spans + slot]
        start, length = run_of(lengths_ref, lax.div(span, spans), workers)
        offset = lax.rem(span, spans) * SPAN
        dead = offset >= length
        needed = start + jnp.minimum(offset + SPAN, length)
        due = jnp.logical_not(dead) & (needed <= known) & (needed > prior)
        return start, length, offset, dead, due

    def result(slot):
        rows = pl.ds(pl.multiple_of(slot * SPAN, SPAN), SPAN)
        return pltpu.make_async_copy(
            attended_ref.at[rows, :], attended_out.at[rows, :], out_sems.at[slot]
        )

    def attend_slot(slot, carry):
        start, length, offset, dead, due = span_of(slot)
        out_rows = pl.ds(pl.multiple_of(slot * SPAN, SPAN), SPAN)

        if not prior:

            @pl.when(dead)
            def _():
                attended_ref[out_rows, :] = jnp.zeros((SPAN, query_width), BF16)
                result(slot).start()

        @pl.when(due)
        def _():
            queries = window(start + offset, slice(0, query_width)).astype(BF16)
            for head in range(heads):
                at = head % group * SPAN
                queries_ref[head // group, at : at + SPAN, :] = queries[
                    :, head * HEAD_SIZE : (head + 1) * HEAD_SIZE
                ]
            first = pl.multiple_of(lax.div(start, ALIGN) * ALIGN, ALIGN)
            shift = start - first
            reach = shift + jnp.minimum(offset + SPAN, length)
            tiles = lax.div(reach + TILE - 1, TILE)

            def columns(at, head):
                return slice(at + head * HEAD_SIZE, at + (head + 1) * HEAD_SIZE)

            def tile_rows(tile):
                return pl.ds(pl.multiple_of(first + tile * TILE, ALIGN), TILE)

            top_ref[...] = jnp.full(top_ref.shape, -1e30, F32)

            def score(tile, carry):
                key_pos = tile * TILE + iota((SPAN, TILE), 1) - shift
                query_pos = offset + iota((SPAN, TILE), 0)
                allowed = (key_pos >= 0) & (key_pos <= query_pos) & (key_pos < length)
                bias = jnp.where(allowed, 0.0, -1e30)
                bias = jnp.concatenate([bias] * group, axis=0)
                for head in range(key_heads):
                    scores = lax.dot_general(
                        queries_ref[head],
                        rows_ref[tile_rows(tile), columns(query_width, head)],
                        (((1,), (1,)), ((), ())),
                        preferred_element_type=F32,
                    )
                    scores = scores + bias
                    scores_ref[head, tile] = scores
                    top_ref[head] = jnp.maximum(top_ref[head], scores)
                return carry

            lax.fori_loop(0, tiles, score, 0)
            tops = [jnp.max(top_ref[head], axis=1, keepdims=True) for head in range(key_heads)]

            def mix(tile, carry):
                ones = jnp.ones((TILE, HEAD_SIZE), BF16)
                totals = []
                for head in range(key_heads):
                    weights = jnp.exp2((scores_ref[head, tile] - tops[head]) * factor)
                    values = rows_ref[tile_rows(tile), columns(query_width + key_width, head)]
                    values = jnp.concatenate([values, ones], axis=1)
                    totals.append(
                        carry[head]
                        + jnp.dot(weights.astype(BF16), values, preferred_element_type=F32)
                    )
                return tuple(totals)

            empty = jnp.zeros((tall, 2 * HEAD_SIZE), F32)
            mixed = lax.fori_loop(0, tiles, mix, (empty,) * key_heads)
            live = offset + iota((SPAN, HEAD_SIZE), 0) < length
            for head in range(heads):
                at = head % group * SPAN
                part = mixed[head // group][at : at + SPAN]
                part = part[:, :HEAD_SIZE] / part[:, HEAD_SIZE:]
                attended_ref[out_rows, columns(0, head)] = jnp.where(live, part, 0.0).astype(BF16)

            result(slot).start()

        return carry

    lax.fori_loop(0, spans, attend_slot, 0)

    def finish(slot, carry):
        _, _, _, dead, due = span_of(slot)

        @pl.when(due if prior else due | dead)
        def _():
            result(slot).wait()

        return carry

    lax.fori_loop(0, spans, finish, 0)

    @pl.when(mine)
    def _():
        cache_copy.wait()


def attend(chips, groups, known, prior, widths, slots, lengths, plan, blocks, outputs):
    query_width, key_width = widths
    width = query_width + 2 * key_width
    total = 2 * chips * sum(sum(sizes) for _, sizes in groups)
    copies = 2 * chips * sum(len(sizes) for _, sizes in groups)
    key_heads, tall = key_width // HEAD_SIZE, query_width // key_width * SPAN
    at = 2 + len(blocks)
    return pl.pallas_call(
        functools.partial(attend_kernel, chips, groups, known, prior, query_width, key_width),
        in_specs=[pl.BlockSpec(memory_space=pltpu.SMEM)] * 2
        + [pl.BlockSpec(memory_space=pl.ANY)] * (len(blocks) + len(outputs)),
        out_specs=[pl.BlockSpec(memory_space=pl.ANY)] * 2
        + [pl.BlockSpec(memory_space=pltpu.VMEM)],
        out_shape=[
            jax.ShapeDtypeStruct((slots, query_width), BF16),
            jax.ShapeDtypeStruct((2, slots, key_width), BF16),
            jax.ShapeDtypeStruct((8, 128), F32),
        ],
        input_output_aliases={at + index: index for index in range(len(outputs))},
        scratch_shapes=[
            pltpu.VMEM((slots, query_width), BF16),
            pltpu.VMEM((2, slots, key_width), BF16),
            pltpu.VMEM((total + TILE + ALIGN, width), BF16),
            pltpu.VMEM((key_heads, tall, HEAD_SIZE), BF16),
            pltpu.VMEM((key_heads, slots // TILE + 1, tall, TILE), F32),
            pltpu.VMEM((key_heads, tall, TILE), F32),
            pltpu.SemaphoreType.DMA((copies,)),
            pltpu.SemaphoreType.DMA((slots // SPAN + 1,)),
        ],
        compiler_params=pltpu.CompilerParams(vmem_limit_bytes=32 * MEBI),
        name="attend",
    )(lengths, plan, *blocks, *outputs)


def shift_chips(value, hop, chips):
    pairs = [(2 * x + c, 2 * ((x + hop) % chips) + c) for x in range(chips) for c in range(2)]
    return lax.ppermute(value, "req", pairs)


def swap_cores(value, chips):
    return lax.ppermute(value, "req", [(d, d ^ 1) for d in range(2 * chips)])


def local(
    chips, shards, tokens, norm_gain, w_query, key_weight, value_weight, lengths, plan
):
    workers = 2 * chips
    slots = tokens.shape[0]
    live = slots // 2
    sizes = [live * share // sum(SHARES) // ALIGN * ALIGN for share in SHARES]
    sizes[-1] = live - sum(sizes[:-1])
    bases = [workers * sum(sizes[:chunk]) for chunk in range(len(sizes))]
    weights = [
        pltpu.with_memory_space_constraint(weight, pltpu.HBM)
        for weight in (w_query, key_weight, value_weight)
    ]
    gain = norm_gain.astype(F32).reshape(1, -1)
    halfway = HEAD_SIZE // 2
    frequency = np.exp(-np.arange(halfway) * 2.0 / HEAD_SIZE * math.log(500000.0))
    frequency = jnp.asarray(np.tile(frequency, 2)[None, :], F32)

    twin = swap_cores(tokens, chips)
    first = deal(chips, bases[:1], sizes[:1], lengths, [tokens], [False])
    dealt = [
        *deal(chips, bases[:1], sizes[:1], lengths, [twin], [True], first),
        *deal(chips, bases[1:], sizes[1:], lengths, [tokens, twin], [False, True]),
    ]
    homes, aways = dealt[::2], dealt[1::2]
    routes, owned, depth = routes_of(shards)
    direct = [piece for piece in range(len(owned)) if depth[piece] == 1]

    sources = {source + 1 for source, _ in routes} - {0}
    awaited = [piece for piece in direct if piece in sources or owned[piece][0] >= 0]
    early = [0, *awaited]
    late = [piece for piece in range(len(owned)) if piece not in early]

    tables, counts = zip(
        *(visits_of([owned[piece] for piece in group], shards) for group in (early, late))
    )
    table = jnp.asarray(np.concatenate(tables, axis=1))
    table = lax.dynamic_index_in_dim(table, lax.axis_index("tp"), 0, keepdims=False)
    places = table[: 2 * counts[0]], table[2 * counts[0] :]

    groups = [([base], [rows]) for base, rows in zip(bases, sizes)]
    widths = w_query.shape[1], key_weight.shape[1]

    def first_sums(at):
        lists = [[lines[at][piece] for piece in early]]
        shape = shards, sizes[at : at + 1], places[0], counts[0]
        return project(False, *shape, lists, gain, weights, (), (), ())

    def finished(at, sums, anchors):
        lists = [[lines[at][piece] for piece in late]]
        shape = shards, sizes[at : at + 1], places[1], counts[1]
        return project(True, *shape, lists, gain, weights, sums, turns[at], anchors)[0]

    def from_chips(block):
        return [shift_chips(block, hop, chips) for hop in range(1, chips)]

    def all_blocks(block, arrived):
        return [leaf for piece in (block, *arrived) for leaf in (piece, swap_cores(piece, chips))]

    lines, own, sent = [], [], []
    last = len(sizes) - 1
    for chunk in range(len(sizes) + 1):
        passed = [0, *(piece for piece in awaited if piece in sources)] if chunk else []
        later = [lines[-1][piece] for piece in passed] + aways[chunk + 1 : chunk + 2]
        anchors = [lines[-1][piece] for piece in awaited if piece not in passed] if chunk else []
        if chunk > 1:
            sums = first_sums(chunk - 2)
            anchors += [sums[1], *(lines[-2][piece] for piece in late)]
        if chunk <= last:
            arrived = [shift_chips(aways[chunk][hop - 1], hop, chips) for hop in range(1, chips)]
            block, later = merge(homes[chunk], arrived, later, anchors)
        else:
            later = after(later, [*anchors, *sent[-1]])
        aways[chunk + 1 : chunk + 2] = later[len(passed) :]
        if chunk:
            lines[-1].update(zip(passed, later))
            for index, (source, pairs) in enumerate(routes):
                if index + 1 in late:
                    lines[-1][index + 1] = lax.ppermute(lines[-1][source + 1], "tp", pairs)
        if chunk <= last:
            line = {0: block}
            for index, (source, pairs) in enumerate(routes):
                if index + 1 in awaited:
                    line[index + 1] = lax.ppermute(block, "tp", pairs)
            lines.append(line)
        if chunk > 1:
            own.append(finished(chunk - 2, sums, ()))
            sent.append(from_chips(own[-1]))
        if chunk == 1:
            turns = angles(groups, lengths, frequency, block)
    own.append(finished(last, first_sums(last), ()))
    blocks = []
    for at in range(last):
        blocks += all_blocks(own[at], after(sent[at], own[at + 1 : at + 2]))
    sent.append(from_chips(own[last]))
    known = workers * sum(sizes[:-1])
    common = widths, slots, lengths, plan
    *outputs, token = attend(chips, groups[:-1], known, 0, *common, blocks, ())
    blocks += all_blocks(own[last], after(sent[last], [token]))
    return tuple(attend(chips, groups, workers * live, known, *common, blocks, outputs)[:2])


def solution(mesh):
    placed = (
        P(("groups", "req"), "tp"),
        P(),
        P(None, "tp"),
        P(None, "tp"),
        P(None, "tp"),
        P("groups"),
        P("groups"),
    )
    return jax.shard_map(
        functools.partial(local, mesh.shape["req"] // 2, mesh.shape["tp"]),
        mesh=mesh,
        in_specs=placed,
        out_specs=(P(("groups", "req"), "tp"), P(None, ("groups", "req"), "tp")),
        check_vma=False,
    )
```

```python
import functools
import math

import jax
import jax.numpy as jnp
import numpy as np
from jax import lax
from jax.experimental import pallas as pl
from jax.experimental.pallas import tpu as pltpu
from jax.sharding import PartitionSpec as P

HEAD_SIZE = 128
SPAN = 128
ALIGN = 16
TILE = 2 * SPAN
SHARES = (4, 8, 4)
DEPTH = 1024
MEBI = 1024 * 1024
F32, BF16 = jnp.float32, jnp.bfloat16


def run_of(lengths_ref, request, count):
    start = jnp.int32(0)
    length = jnp.int32(0)
    for other in range(count):
        amount = lengths_ref[other]
        start = start + jnp.where(other < request, amount, 0)
        length = jnp.where(other == request, amount, length)
    return start, length


def iota(shape, dimension):
    return lax.broadcasted_iota(jnp.int32, shape, dimension)


def deal_kernel(chips, bases, sizes, twins, lengths_ref, *refs):
    me = lax.axis_index("req")
    chip, core = lax.div(me, 2), lax.rem(me, 2)
    sources, refs = refs[: len(twins)], refs[len(twins) :]
    count = 2 * len(sizes)
    priors, out_refs = refs[:-count], refs[-count:]
    requests = [me + 1 - 2 * core if twin else me for twin in twins]
    runs = [run_of(lengths_ref, request, 2 * chips) for request in requests]
    slots = sources[0].shape[0]
    for chunk, (base, rows) in enumerate(zip(bases, sizes)):
        home_ref, away_ref = out_refs[2 * chunk : 2 * chunk + 2]
        for hop in range(chips):
            target = lax.rem(chip + hop, chips) * 2 + core
            number = base + target * rows + iota((rows, slots), 0)
            slot = iota((rows, slots), 1)
            total = None
            for (start, length), source in zip(runs, sources):
                hot = ((number - start == slot) & (slot < length)).astype(BF16)
                part = jnp.dot(hot, source[...], preferred_element_type=F32)
                total = part if total is None else total + part
            total = total.astype(BF16)
            if hop == 0:
                home_ref[...] = total + priors[2 * chunk][...] if priors else total
            elif priors:
                away_ref[hop - 1] = total + priors[2 * chunk + 1][hop - 1]
            else:
                away_ref[hop - 1] = total


def deal(chips, bases, sizes, lengths, sources, twins, priors=()):
    slots, width = sources[0].shape
    block = min(1024, width)
    out_specs, out_shape = [], []
    for rows in sizes:
        out_specs += [
            pl.BlockSpec((rows, block), lambda i: (0, i)),
            pl.BlockSpec((chips - 1, rows, block), lambda i: (0, 0, i)),
        ]
        out_shape += [
            jax.ShapeDtypeStruct((rows, width), BF16),
            jax.ShapeDtypeStruct((chips - 1, rows, width), BF16),
        ]
    return pl.pallas_call(
        functools.partial(deal_kernel, chips, bases, sizes, twins),
        grid=(width // block,),
        in_specs=[pl.BlockSpec(memory_space=pltpu.SMEM)]
        + [pl.BlockSpec((slots, block), lambda i: (0, i)) for _ in sources]
        + (out_specs if priors else []),
        out_specs=out_specs,
        out_shape=out_shape,
        compiler_params=pltpu.CompilerParams(vmem_limit_bytes=24 * MEBI),
        name="deal",
    )(lengths, *sources, *priors)


def merge_kernel(count, passed, home_ref, *refs):
    total = home_ref[...]
    for ref in refs[:count]:
        total = total + ref[...]
    refs[len(refs) - 1 - passed][...] = total


def merge(home, arrived, later):
    count = len(arrived)
    vmem, anywhere = pl.BlockSpec(memory_space=pltpu.VMEM), pl.BlockSpec(memory_space=pl.ANY)
    block, *later = pl.pallas_call(
        functools.partial(merge_kernel, count, len(later)),
        in_specs=[vmem] * (count + 1) + [anywhere] * len(later),
        out_specs=[vmem] + [anywhere] * len(later),
        out_shape=[jax.ShapeDtypeStruct(leaf.shape, leaf.dtype) for leaf in (home, *later)],
        input_output_aliases={count + 1 + at: 1 + at for at in range(len(later))},
        compiler_params=pltpu.CompilerParams(vmem_limit_bytes=8 * MEBI),
        name="merge",
    )(home, *arrived, *later)
    return block, later


def after(arrays, anchors):
    def kernel(*refs):
        pass

    anywhere = pl.BlockSpec(memory_space=pl.ANY)
    return pl.pallas_call(
        kernel,
        in_specs=[anywhere] * (len(arrays) + len(anchors)),
        out_specs=[anywhere] * len(arrays),
        out_shape=[jax.ShapeDtypeStruct(leaf.shape, leaf.dtype) for leaf in arrays],
        input_output_aliases={at: at for at in range(len(arrays))},
        compiler_params=pltpu.CompilerParams(vmem_limit_bytes=MEBI),
        name="after",
    )(*arrays, *anchors)


def routes_of(shards):
    if shards == 4:
        routes = [
            (-1, [(1, 2), (2, 1)]),
            (-1, [(0, 1), (1, 0), (2, 3), (3, 2)]),
            (-1, [(0, 2), (1, 3), (2, 0), (3, 1)]),
            (2, [(2, 3), (1, 0)]),
        ]
    else:
        routes = []
        for step in range(1, shards):
            source = len(routes) - 2 if step > 1 else -1
            routes.append((source, [(at, at + 1) for at in range(step - 1, shards - 1)]))
            source = len(routes) - 2 if step > 1 else -1
            routes.append((source, [(at, at - 1) for at in range(1, shards - step + 1)]))
    held, depth = [list(range(shards))], [0]
    for source, pairs in routes:
        now = [-1] * shards
        for start, end in pairs:
            now[end] = held[source + 1][start]
        held.append(now)
        depth.append(depth[source + 1] + 1)
    return routes, held, depth


def visits_of(held, shards):
    visits = [
        [(piece, now[at]) for piece, now in enumerate(held) if now[at] >= 0]
        for at in range(shards)
    ]
    count = max(len(line) for line in visits)
    table = []
    for line in visits:
        pad = (-1, line[-1][1] if line else 0)
        line = line + [pad] * (count - len(line))
        table.append([piece for piece, _ in line] + [shard for _, shard in line])
    return np.array(table, np.int32), count


def angles_kernel(groups, members, lengths_ref, frequency_ref, anchor_ref, *out_refs):
    me = lax.axis_index("req")
    for group, (bases, sizes) in enumerate(groups):
        first = 0
        for base, rows in zip(bases, sizes):
            number = base + me * rows + iota((rows, HEAD_SIZE), 0)
            start = jnp.zeros((rows, HEAD_SIZE), jnp.int32)
            before = jnp.int32(0)
            for other in range(members):
                before = before + lengths_ref[other]
                start = jnp.where(number >= before, before, start)
            angle = (number - start).astype(F32) * frequency_ref[...]
            sine = jnp.sin(angle)
            lower = iota((rows, HEAD_SIZE), 1) < HEAD_SIZE // 2
            out_refs[2 * group][first : first + rows, :] = jnp.cos(angle)
            out_refs[2 * group + 1][first : first + rows, :] = jnp.where(lower, -sine, sine)
            first += rows


def angles(groups, lengths, frequency, anchor):
    shapes = [
        jax.ShapeDtypeStruct((sum(sizes), HEAD_SIZE), F32) for _, sizes in groups for _ in range(2)
    ]
    vmem = pl.BlockSpec(memory_space=pltpu.VMEM)
    tables = pl.pallas_call(
        functools.partial(angles_kernel, groups, lengths.shape[0]),
        in_specs=[
            pl.BlockSpec(memory_space=pltpu.SMEM),
            vmem,
            pl.BlockSpec(memory_space=pl.ANY),
        ],
        out_specs=[vmem] * len(shapes),
        out_shape=shapes,
        compiler_params=pltpu.CompilerParams(vmem_limit_bytes=8 * MEBI),
        name="angles",
    )(lengths, frequency, anchor)
    return [tables[at : at + 2] for at in range(0, len(tables), 2)]


def project_kernel(count, carries, final, shards, steps, sizes, place_ref, *refs):
    chunks = len(sizes)
    pieces, refs = refs[: count * chunks], refs[count * chunks :]
    (gain_ref, *weights), refs = refs[:4], refs[4:]
    if carries:
        carried, refs = refs[: 2 * chunks], refs[2 * chunks :]
    if final:
        cosine_ref, sine_ref, out_ref, *refs = refs
    sums, squares, chosen = refs[: 2 * chunks : 2], refs[1 : 2 * chunks : 2], refs[-1]
    visit, step = pl.program_id(0), pl.program_id(1)
    visits = pl.num_programs(0)
    depth = chosen.shape[1]
    piece = place_ref[visit]
    spans, first = [], 0
    for size in sizes:
        spans.append(slice(first, first + size))
        first += size

    @pl.when((visit == 0) & (step == 0))
    def _():
        for at in range(chunks):
            sums[at][...] = carried[2 * at][...] if carries else jnp.zeros_like(sums[at])
            squares[at][...] = carried[2 * at + 1][...] if carries else jnp.zeros_like(squares[at])

    for index in range(count):

        @pl.when(piece == index)
        def _():
            columns = pl.ds(pl.multiple_of(step * depth, depth), depth)
            for chunk, span in enumerate(spans):
                chosen[span, :] = pieces[chunk * count + index][:, columns]

    @pl.when(piece >= 0)
    def _():
        wide = chosen[...].astype(F32)
        square = wide * wide
        part = square[:, :128]
        for at in range(128, depth, 128):
            part = part + square[:, at : at + 128]
        for at, span in enumerate(spans):
            squares[at][...] += part[span]
        scaled = (wide * gain_ref[...]).astype(BF16)
        left = 0
        for weight in weights:
            columns = slice(left, left + weight.shape[1])
            product = jnp.dot(scaled, weight[...], preferred_element_type=F32)
            for at, span in enumerate(spans):
                sums[at][:, columns] += product[span]
            left += weight.shape[1]

    if final:

        @pl.when((visit == visits - 1) & (step == steps - 1))
        def _():
            mean = jnp.sum(squares[0][...], axis=1, keepdims=True) / (shards * steps * depth)
            scale = lax.rsqrt(mean + 1e-05)
            turned = sums[0].shape[1] - weights[-1].shape[1]
            for left in range(0, sums[0].shape[1], HEAD_SIZE):
                columns = slice(left, left + HEAD_SIZE)
                head = sums[0][:, columns] * scale
                if left < turned:
                    head = head * cosine_ref[...] + pltpu.roll(
                        head, HEAD_SIZE // 2, 1
                    ) * sine_ref[...]
                out_ref[:, columns] = head.astype(BF16)


def project(final, shards, sizes, place, lines, gain, weights, carried, tables):
    place, visits = place
    pieces = [piece for line in lines for piece in line]
    rows, width = sum(sizes), pieces[0].shape[1]
    depth = min(DEPTH, width)
    steps = width // depth
    columns = sum(weight.shape[1] for weight in weights)

    def block_of(visit, step, place_ref):
        step = jnp.where(place_ref[visit] < 0, steps - 1, step)
        return place_ref[visits + visit] * steps + step

    def whole(shape):
        return pl.BlockSpec(shape, lambda visit, step, place_ref: (0, 0))

    def deep(block, dimension):
        def where(visit, step, place_ref):
            at = block_of(visit, step, place_ref)
            return (at, 0) if dimension == 0 else (0, at)

        return pl.BlockSpec(block, where)

    extra = [*carried, *tables]
    operands = [*pieces, gain, *weights, *extra]
    in_specs = [whole(piece.shape) for piece in pieces]
    in_specs += [deep((1, depth), 1)]
    in_specs += [deep((depth, weight.shape[1]), 0) for weight in weights]
    in_specs += [whole(leaf.shape) for leaf in extra]
    scratch = [pltpu.VMEM((rows, depth), BF16)]
    if final:
        out_shape = [jax.ShapeDtypeStruct((rows, columns), BF16)]
        scratch = [pltpu.VMEM((rows, columns), F32), pltpu.VMEM((rows, 128), F32), *scratch]
    else:
        out_shape = [
            jax.ShapeDtypeStruct((size, wide), F32) for size in sizes for wide in (columns, 128)
        ]
    return pl.pallas_call(
        functools.partial(
            project_kernel, len(lines[0]), bool(carried), final, shards, steps, sizes
        ),
        grid_spec=pltpu.PrefetchScalarGridSpec(
            num_scalar_prefetch=1,
            grid=(visits, steps),
            in_specs=in_specs,
            out_specs=[whole(leaf.shape) for leaf in out_shape],
            scratch_shapes=scratch,
        ),
        out_shape=out_shape,
        compiler_params=pltpu.CompilerParams(vmem_limit_bytes=32 * MEBI),
        name="project",
    )(place, *operands)


def attend_kernel(
    chips, groups, known, prior, query_width, key_width, lengths_ref, plan_ref, *refs
):
    blocks, refs = refs[: -13 if prior else -11], refs[-11:]
    attended_out, cache_out, token_ref, attended_ref, cache_ref, rows_ref, queries_ref = refs[:7]
    scores_ref, top_ref, sems, out_sems = refs[7:]
    token_ref[...] = jnp.zeros_like(token_ref)
    workers = 2 * chips
    me = lax.axis_index("req")
    chip, core = lax.div(me, 2), lax.rem(me, 2)
    slots = cache_ref.shape[1]
    spans = slots // SPAN
    total = workers * sum(sum(sizes) for _, sizes in groups)
    end = needed = jnp.int32(0)
    for other in range(workers):
        end = end + lengths_ref[other]
        needed = jnp.where(end <= prior, end, needed)
    copies = []
    for group, (bases, sizes) in enumerate(groups):
        for hop in range(chips):
            source = lax.rem(chip - hop + chips, chips) * 2
            for twin in range(2):
                owner = source + (core if twin == 0 else 1 - core)
                block = blocks[(group * chips + hop) * 2 + twin]
                first = 0
                for base, rows in zip(bases, sizes):
                    at = pl.multiple_of(base + owner * rows, ALIGN)
                    copy = pltpu.make_async_copy(
                        block.at[pl.ds(first, rows), :],
                        rows_ref.at[pl.ds(at, rows), :],
                        sems.at[len(copies)],
                    )
                    copies.append((at + rows > needed, copy))
                    first += rows
    for wanted, copy in copies:

        @pl.when(wanted)
        def _():
            copy.start()

    rows_ref[total:, :] = jnp.zeros((rows_ref.shape[0] - total, rows_ref.shape[1]), BF16)
    for wanted, copy in copies:

        @pl.when(wanted)
        def _():
            copy.wait()

    def window(row, columns):
        first = pl.multiple_of(lax.div(row, ALIGN) * ALIGN, ALIGN)
        shape = (SPAN, 2 * SPAN)
        hot = (iota(shape, 1) == iota(shape, 0) + (row - first)).astype(BF16)
        return jnp.dot(
            hot, rows_ref[pl.ds(first, 2 * SPAN), columns], preferred_element_type=F32
        )

    own_start, own_length = run_of(lengths_ref, me, workers)
    mine = (own_start + own_length <= known) & (own_start + own_length > prior)
    cache_copy = pltpu.make_async_copy(cache_ref, cache_out, out_sems.at[spans])

    @pl.when(mine)
    def _():
        def step(part, carry):
            at = pl.multiple_of(part * SPAN, SPAN)

            @pl.when(at < own_length)
            def _():
                picked = window(own_start + at, slice(query_width, query_width + 2 * key_width))
                live = at + iota(picked.shape, 0) < own_length
                picked = jnp.where(live, picked, 0.0).astype(BF16)
                cache_ref[0, pl.ds(at, SPAN), :] = picked[:, :key_width]
                cache_ref[1, pl.ds(at, SPAN), :] = picked[:, key_width:]

            @pl.when(at >= own_length)
            def _():
                empty = jnp.zeros((SPAN, key_width), BF16)
                cache_ref[0, pl.ds(at, SPAN), :] = empty
                cache_ref[1, pl.ds(at, SPAN), :] = empty

            return carry

        lax.fori_loop(0, spans, step, 0)
        cache_copy.start()

    heads, key_heads = query_width // HEAD_SIZE, key_width // HEAD_SIZE
    group = heads // key_heads
    factor = math.log2(math.e) / math.sqrt(HEAD_SIZE)
    tall = group * SPAN

    def span_of(slot):
        span = plan_ref[me * spans + slot]
        start, length = run_of(lengths_ref, lax.div(span, spans), workers)
        offset = lax.rem(span, spans) * SPAN
        dead = offset >= length
        needed = start + jnp.minimum(offset + SPAN, length)
        due = jnp.logical_not(dead) & (needed <= known) & (needed > prior)
        return start, length, offset, dead, due

    def result(slot):
        rows = pl.ds(pl.multiple_of(slot * SPAN, SPAN), SPAN)
        return pltpu.make_async_copy(
            attended_ref.at[rows, :], attended_out.at[rows, :], out_sems.at[slot]
        )

    def attend_slot(slot, carry):
        start, length, offset, dead, due = span_of(slot)
        out_rows = pl.ds(pl.multiple_of(slot * SPAN, SPAN), SPAN)

        if not prior:

            @pl.when(dead)
            def _():
                attended_ref[out_rows, :] = jnp.zeros((SPAN, query_width), BF16)
                result(slot).start()

        @pl.when(due)
        def _():
            queries = window(start + offset, slice(0, query_width)).astype(BF16)
            for head in range(heads):
                at = head % group * SPAN
                queries_ref[head // group, at : at + SPAN, :] = queries[
                    :, head * HEAD_SIZE : (head + 1) * HEAD_SIZE
                ]
            first = pl.multiple_of(lax.div(start, ALIGN) * ALIGN, ALIGN)
            shift = start - first
            reach = shift + jnp.minimum(offset + SPAN, length)
            tiles = lax.div(reach + TILE - 1, TILE)

            def columns(at, head):
                return slice(at + head * HEAD_SIZE, at + (head + 1) * HEAD_SIZE)

            def tile_rows(tile):
                return pl.ds(pl.multiple_of(first + tile * TILE, ALIGN), TILE)

            top_ref[...] = jnp.full(top_ref.shape, -1e30, F32)

            def score(tile, carry):
                key_pos = tile * TILE + iota((SPAN, TILE), 1) - shift
                query_pos = offset + iota((SPAN, TILE), 0)
                allowed = (key_pos >= 0) & (key_pos <= query_pos) & (key_pos < length)
                bias = jnp.where(allowed, 0.0, -1e30)
                bias = jnp.concatenate([bias] * group, axis=0)
                for head in range(key_heads):
                    scores = lax.dot_general(
                        queries_ref[head],
                        rows_ref[tile_rows(tile), columns(query_width, head)],
                        (((1,), (1,)), ((), ())),
                        preferred_element_type=F32,
                    )
                    scores = scores + bias
                    scores_ref[head, tile] = scores
                    top_ref[head] = jnp.maximum(top_ref[head], scores)
                return carry

            lax.fori_loop(0, tiles, score, 0)
            tops = [jnp.max(top_ref[head], axis=1, keepdims=True) for head in range(key_heads)]

            def mix(tile, carry):
                ones = jnp.ones((TILE, HEAD_SIZE), BF16)
                totals = []
                for head in range(key_heads):
                    weights = jnp.exp2((scores_ref[head, tile] - tops[head]) * factor)
                    values = rows_ref[tile_rows(tile), columns(query_width + key_width, head)]
                    values = jnp.concatenate([values, ones], axis=1)
                    totals.append(
                        carry[head]
                        + jnp.dot(weights.astype(BF16), values, preferred_element_type=F32)
                    )
                return tuple(totals)

            empty = jnp.zeros((tall, 2 * HEAD_SIZE), F32)
            mixed = lax.fori_loop(0, tiles, mix, (empty,) * key_heads)
            live = offset + iota((SPAN, HEAD_SIZE), 0) < length
            for head in range(heads):
                at = head % group * SPAN
                part = mixed[head // group][at : at + SPAN]
                part = part[:, :HEAD_SIZE] / part[:, HEAD_SIZE:]
                attended_ref[out_rows, columns(0, head)] = jnp.where(live, part, 0.0).astype(BF16)

            result(slot).start()

        return carry

    lax.fori_loop(0, spans, attend_slot, 0)

    def finish(slot, carry):
        _, _, _, dead, due = span_of(slot)

        @pl.when(due if prior else due | dead)
        def _():
            result(slot).wait()

        return carry

    lax.fori_loop(0, spans, finish, 0)

    @pl.when(mine)
    def _():
        cache_copy.wait()


def attend(chips, groups, known, prior, widths, slots, lengths, plan, blocks, outputs):
    query_width, key_width = widths
    width = query_width + 2 * key_width
    total = 2 * chips * sum(sum(sizes) for _, sizes in groups)
    copies = 2 * chips * sum(len(sizes) for _, sizes in groups)
    key_heads, tall = key_width // HEAD_SIZE, query_width // key_width * SPAN
    at = 2 + len(blocks)
    return pl.pallas_call(
        functools.partial(attend_kernel, chips, groups, known, prior, query_width, key_width),
        in_specs=[pl.BlockSpec(memory_space=pltpu.SMEM)] * 2
        + [pl.BlockSpec(memory_space=pl.ANY)] * (len(blocks) + len(outputs)),
        out_specs=[pl.BlockSpec(memory_space=pl.ANY)] * 2
        + [pl.BlockSpec(memory_space=pltpu.VMEM)],
        out_shape=[
            jax.ShapeDtypeStruct((slots, query_width), BF16),
            jax.ShapeDtypeStruct((2, slots, key_width), BF16),
            jax.ShapeDtypeStruct((8, 128), F32),
        ],
        input_output_aliases={at + index: index for index in range(len(outputs))},
        scratch_shapes=[
            pltpu.VMEM((slots, query_width), BF16),
            pltpu.VMEM((2, slots, key_width), BF16),
            pltpu.VMEM((total + TILE + ALIGN, width), BF16),
            pltpu.VMEM((key_heads, tall, HEAD_SIZE), BF16),
            pltpu.VMEM((key_heads, slots // TILE + 1, tall, TILE), F32),
            pltpu.VMEM((key_heads, tall, TILE), F32),
            pltpu.SemaphoreType.DMA((copies,)),
            pltpu.SemaphoreType.DMA((slots // SPAN + 1,)),
        ],
        compiler_params=pltpu.CompilerParams(vmem_limit_bytes=32 * MEBI),
        name="attend",
    )(lengths, plan, *blocks, *outputs)


def shift_chips(value, hop, chips):
    pairs = [(2 * x + c, 2 * ((x + hop) % chips) + c) for x in range(chips) for c in range(2)]
    return lax.ppermute(value, "req", pairs)


def swap_cores(value, chips):
    return lax.ppermute(value, "req", [(d, d ^ 1) for d in range(2 * chips)])


def local(
    chips, shards, tokens, norm_gain, w_query, key_weight, value_weight, lengths, plan
):
    workers = 2 * chips
    slots = tokens.shape[0]
    live = slots // 2
    sizes = [live * share // sum(SHARES) // ALIGN * ALIGN for share in SHARES]
    sizes[-1] = live - sum(sizes[:-1])
    bases = [workers * sum(sizes[:chunk]) for chunk in range(len(sizes))]
    weights = [
        pltpu.with_memory_space_constraint(weight, pltpu.HBM)
        for weight in (w_query, key_weight, value_weight)
    ]
    gain = norm_gain.astype(F32).reshape(1, -1)
    halfway = HEAD_SIZE // 2
    frequency = np.exp(-np.arange(halfway) * 2.0 / HEAD_SIZE * math.log(500000.0))
    frequency = jnp.asarray(np.tile(frequency, 2)[None, :], F32)

    twin = swap_cores(tokens, chips)
    first = deal(chips, bases[:1], sizes[:1], lengths, [tokens], [False])
    dealt = [
        *deal(chips, bases[:1], sizes[:1], lengths, [twin], [True], first),
        *deal(chips, bases[1:], sizes[1:], lengths, [tokens, twin], [False, True]),
    ]
    homes, aways = dealt[::2], dealt[1::2]
    routes, owned, depth = routes_of(shards)
    direct = [piece for piece in range(len(owned)) if depth[piece] == 1]

    sources = {source + 1 for source, _ in routes} - {0}
    awaited = [piece for piece in direct if piece in sources or owned[piece][0] >= 0]
    early = [0, *awaited]
    late = [piece for piece in range(len(owned)) if piece not in early]

    kinds = {"own": [0], "first": early, "direct": awaited, "late": late}
    tables, counts = zip(
        *(visits_of([owned[piece] for piece in kind], shards) for kind in kinds.values())
    )
    table = jnp.asarray(np.concatenate(tables, axis=1))
    table = lax.dynamic_index_in_dim(table, lax.axis_index("tp"), 0, keepdims=False)
    ends = [2 * sum(counts[: at + 1]) for at in range(len(counts))]
    places = {
        kind: (table[end - 2 * count : end], count)
        for kind, count, end in zip(kinds, counts, ends)
    }

    groups = [([base], [rows]) for base, rows in zip(bases, sizes)]
    widths = w_query.shape[1], key_weight.shape[1]

    def add(kind, chunks, carried=()):
        held = [[lines[chunk][piece] for piece in kinds[kind]] for chunk in chunks]
        rows = [sizes[chunk] for chunk in chunks]
        turned = turns[chunks[0]] if kind == "late" else ()
        return project(
            kind == "late", shards, rows, places[kind], held, gain, weights, carried, turned
        )

    def from_chips(block):
        return [shift_chips(block, hop, chips) for hop in range(1, chips)]

    def all_blocks(block, arrived):
        return [leaf for piece in (block, *arrived) for leaf in (piece, swap_cores(piece, chips))]

    def start(line, group):
        for index, (source, pairs) in enumerate(routes):
            if index + 1 in group:
                line[index + 1] = lax.ppermute(line[source + 1], "tp", pairs)

    passed = [0, *(piece for piece in awaited if piece in sources)]
    lines, own, sent = [], [], []
    last = len(sizes) - 1
    sums, open_sums = {}, []
    for chunk in range(last + 2):
        fenced, anchors = [], []
        if chunk:
            fenced = [lines[-1][piece] for piece in passed]
            anchors = [lines[-1][piece] for piece in awaited if piece not in passed]
        if chunk <= last:
            arrived = [shift_chips(aways[chunk][hop - 1], hop, chips) for hop in range(1, chips)]
            later = aways[chunk + 1 : chunk + 2]
            block, aways[chunk + 1 : chunk + 2] = merge(homes[chunk], arrived, later)
            lines.append({0: block})
            fenced.append(block)
        if chunk == 2:
            sums[0] = add("first", [0])
            rest = list(range(1, last + 1))
            shared = add("own", rest)
            sums.update({at: shared[2 * index : 2 * index + 2] for index, at in enumerate(rest)})
            anchors += [sums[0][1], shared[1], *(lines[0][piece] for piece in late)]
        if chunk > 2:
            sums[chunk - 2] = add("direct", [chunk - 2], sums[chunk - 2])
            own.append(add("late", [chunk - 2], sums[chunk - 2])[0])
            sent.append(from_chips(own[-1]))
            anchors += [own[-1], *sent[-2]]
        if chunk:
            fenced = after(fenced, anchors)
            before = lines[chunk - 1]
            before.update(zip(passed, fenced))
            if chunk <= last:
                lines[chunk][0] = fenced[-1]
            start(before, late)
        if chunk <= last:
            start(lines[chunk], awaited)
        if chunk == 1:
            turns = angles(groups, lengths, frequency, lines[1][0])
        if chunk == 2:
            own.append(add("late", [0], sums[0])[0])
            sent.append(from_chips(own[0]))
    sums[last] = add("direct", [last], sums[last])
    own.append(add("late", [last], sums[last])[0])
    blocks = []
    for at in range(last):
        blocks += all_blocks(own[at], after(sent[at], own[at + 1 : at + 2]))
    sent.append(from_chips(own[last]))
    known = workers * sum(sizes[:-1])
    common = widths, slots, lengths, plan
    *outputs, token = attend(chips, groups[:-1], known, 0, *common, blocks, ())
    blocks += all_blocks(own[last], after(sent[last], [token]))
    return tuple(attend(chips, groups, workers * live, known, *common, blocks, outputs)[:2])


def solution(mesh):
    placed = (
        P(("groups", "req"), "tp"),
        P(),
        P(None, "tp"),
        P(None, "tp"),
        P(None, "tp"),
        P("groups"),
        P("groups"),
    )
    return jax.shard_map(
        functools.partial(local, mesh.shape["req"] // 2, mesh.shape["tp"]),
        mesh=mesh,
        in_specs=placed,
        out_specs=(P(("groups", "req"), "tp"), P(None, ("groups", "req"), "tp")),
        check_vma=False,
    )
```

```python
import functools
import math

import jax
import jax.numpy as jnp
import numpy as np
from jax import lax
from jax.experimental import pallas as pl
from jax.experimental.pallas import tpu as pltpu
from jax.sharding import PartitionSpec as P

HEAD_SIZE = 128
SPAN = 128
ALIGN = 16
TILE = 2 * SPAN
SHARES = (4, 8, 4)
DEPTH = 1024
MEBI = 1024 * 1024
F32, BF16 = jnp.float32, jnp.bfloat16


def run_of(lengths_ref, request, count):
    start = jnp.int32(0)
    length = jnp.int32(0)
    for other in range(count):
        amount = lengths_ref[other]
        start = start + jnp.where(other < request, amount, 0)
        length = jnp.where(other == request, amount, length)
    return start, length


def iota(shape, dimension):
    return lax.broadcasted_iota(jnp.int32, shape, dimension)


def deal_kernel(chips, bases, sizes, twins, lengths_ref, *refs):
    me = lax.axis_index("req")
    chip, core = lax.div(me, 2), lax.rem(me, 2)
    sources, refs = refs[: len(twins)], refs[len(twins) :]
    count = 2 * len(sizes)
    priors, out_refs = refs[:-count], refs[-count:]
    requests = [me + 1 - 2 * core if twin else me for twin in twins]
    runs = [run_of(lengths_ref, request, 2 * chips) for request in requests]
    slots = sources[0].shape[0]
    for chunk, (base, rows) in enumerate(zip(bases, sizes)):
        home_ref, away_ref = out_refs[2 * chunk : 2 * chunk + 2]
        for hop in range(chips):
            target = lax.rem(chip + hop, chips) * 2 + core
            number = base + target * rows + iota((rows, slots), 0)
            slot = iota((rows, slots), 1)
            total = None
            for (start, length), source in zip(runs, sources):
                hot = ((number - start == slot) & (slot < length)).astype(BF16)
                part = jnp.dot(hot, source[...], preferred_element_type=F32)
                total = part if total is None else total + part
            total = total.astype(BF16)
            if hop == 0:
                home_ref[...] = total + priors[2 * chunk][...] if priors else total
            elif priors:
                away_ref[hop - 1] = total + priors[2 * chunk + 1][hop - 1]
            else:
                away_ref[hop - 1] = total


def deal(chips, bases, sizes, lengths, sources, twins, priors=()):
    slots, width = sources[0].shape
    block = min(1024, width)
    out_specs, out_shape = [], []
    for rows in sizes:
        out_specs += [
            pl.BlockSpec((rows, block), lambda i: (0, i)),
            pl.BlockSpec((chips - 1, rows, block), lambda i: (0, 0, i)),
        ]
        out_shape += [
            jax.ShapeDtypeStruct((rows, width), BF16),
            jax.ShapeDtypeStruct((chips - 1, rows, width), BF16),
        ]
    return pl.pallas_call(
        functools.partial(deal_kernel, chips, bases, sizes, twins),
        grid=(width // block,),
        in_specs=[pl.BlockSpec(memory_space=pltpu.SMEM)]
        + [pl.BlockSpec((slots, block), lambda i: (0, i)) for _ in sources]
        + (out_specs if priors else []),
        out_specs=out_specs,
        out_shape=out_shape,
        compiler_params=pltpu.CompilerParams(vmem_limit_bytes=10 * MEBI),
        name="deal",
    )(lengths, *sources, *priors)


def merge_kernel(count, passed, home_ref, *refs):
    total = home_ref[...]
    for ref in refs[:count]:
        total = total + ref[...]
    refs[len(refs) - 1 - passed][...] = total


def merge(home, arrived, later):
    count = len(arrived)
    vmem, anywhere = pl.BlockSpec(memory_space=pltpu.VMEM), pl.BlockSpec(memory_space=pl.ANY)
    block, *later = pl.pallas_call(
        functools.partial(merge_kernel, count, len(later)),
        in_specs=[vmem] * (count + 1) + [anywhere] * len(later),
        out_specs=[vmem] + [anywhere] * len(later),
        out_shape=[jax.ShapeDtypeStruct(leaf.shape, leaf.dtype) for leaf in (home, *later)],
        input_output_aliases={count + 1 + at: 1 + at for at in range(len(later))},
        compiler_params=pltpu.CompilerParams(vmem_limit_bytes=4 * MEBI),
        name="merge",
    )(home, *arrived, *later)
    return block, later


def after(arrays, anchors):
    def kernel(*refs):
        pass

    anywhere = pl.BlockSpec(memory_space=pl.ANY)
    return pl.pallas_call(
        kernel,
        in_specs=[anywhere] * (len(arrays) + len(anchors)),
        out_specs=[anywhere] * len(arrays),
        out_shape=[jax.ShapeDtypeStruct(leaf.shape, leaf.dtype) for leaf in arrays],
        input_output_aliases={at: at for at in range(len(arrays))},
        compiler_params=pltpu.CompilerParams(vmem_limit_bytes=MEBI),
        name="after",
    )(*arrays, *anchors)


def routes_of(shards):
    if shards == 4:
        routes = [
            (-1, [(1, 2), (2, 1)]),
            (-1, [(0, 1), (1, 0), (2, 3), (3, 2)]),
            (-1, [(0, 2), (1, 3), (2, 0), (3, 1)]),
            (2, [(2, 3), (1, 0)]),
        ]
    else:
        routes = []
        for step in range(1, shards):
            source = len(routes) - 2 if step > 1 else -1
            routes.append((source, [(at, at + 1) for at in range(step - 1, shards - 1)]))
            source = len(routes) - 2 if step > 1 else -1
            routes.append((source, [(at, at - 1) for at in range(1, shards - step + 1)]))
    held, depth = [list(range(shards))], [0]
    for source, pairs in routes:
        now = [-1] * shards
        for start, end in pairs:
            now[end] = held[source + 1][start]
        held.append(now)
        depth.append(depth[source + 1] + 1)
    return routes, held, depth


def visits_of(held, shards):
    visits = [
        [(piece, now[at]) for piece, now in enumerate(held) if now[at] >= 0]
        for at in range(shards)
    ]
    count = max(len(line) for line in visits)
    table = []
    for line in visits:
        pad = (-1, line[-1][1] if line else 0)
        line = line + [pad] * (count - len(line))
        table.append([piece for piece, _ in line] + [shard for _, shard in line])
    return np.array(table, np.int32), count


def angles_kernel(groups, members, lengths_ref, frequency_ref, anchor_ref, *out_refs):
    me = lax.axis_index("req")
    for group, (bases, sizes) in enumerate(groups):
        first = 0
        for base, rows in zip(bases, sizes):
            number = base + me * rows + iota((rows, HEAD_SIZE), 0)
            start = jnp.zeros((rows, HEAD_SIZE), jnp.int32)
            before = jnp.int32(0)
            for other in range(members):
                before = before + lengths_ref[other]
                start = jnp.where(number >= before, before, start)
            angle = (number - start).astype(F32) * frequency_ref[...]
            sine = jnp.sin(angle)
            lower = iota((rows, HEAD_SIZE), 1) < HEAD_SIZE // 2
            out_refs[2 * group][first : first + rows, :] = jnp.cos(angle)
            out_refs[2 * group + 1][first : first + rows, :] = jnp.where(lower, -sine, sine)
            first += rows


def angles(groups, lengths, frequency, anchor):
    shapes = [
        jax.ShapeDtypeStruct((sum(sizes), HEAD_SIZE), F32) for _, sizes in groups for _ in range(2)
    ]
    vmem = pl.BlockSpec(memory_space=pltpu.VMEM)
    tables = pl.pallas_call(
        functools.partial(angles_kernel, groups, lengths.shape[0]),
        in_specs=[
            pl.BlockSpec(memory_space=pltpu.SMEM),
            vmem,
            pl.BlockSpec(memory_space=pl.ANY),
        ],
        out_specs=[vmem] * len(shapes),
        out_shape=shapes,
        compiler_params=pltpu.CompilerParams(vmem_limit_bytes=4 * MEBI),
        name="angles",
    )(lengths, frequency, anchor)
    return [tables[at : at + 2] for at in range(0, len(tables), 2)]


def load(weight, anchor):
    parts = 8
    depth = weight.shape[0] // parts

    def kernel(weight_ref, anchor_ref, out_ref, token_ref, sems):
        copies = [
            pltpu.make_async_copy(
                weight_ref.at[pl.ds(part * depth, depth), :],
                out_ref.at[pl.ds(part * depth, depth), :],
                sems.at[part],
            )
            for part in range(parts)
        ]
        for copy in copies:
            copy.start()
        token_ref[...] = jnp.zeros_like(token_ref)
        for copy in copies:
            copy.wait()

    vmem, anywhere = pl.BlockSpec(memory_space=pltpu.VMEM), pl.BlockSpec(memory_space=pl.ANY)
    return pl.pallas_call(
        kernel,
        in_specs=[anywhere, anywhere],
        out_specs=[vmem, vmem],
        out_shape=[
            jax.ShapeDtypeStruct(weight.shape, weight.dtype),
            jax.ShapeDtypeStruct((8, 128), F32),
        ],
        scratch_shapes=[pltpu.SemaphoreType.DMA((parts,))],
        compiler_params=pltpu.CompilerParams(vmem_limit_bytes=2 * MEBI),
        name="load",
    )(pltpu.with_memory_space_constraint(weight, pltpu.HBM), anchor)


def project_kernel(count, carries, final, shards, visits, sizes, place_ref, *refs):
    chunks = len(sizes)
    pieces, refs = refs[: count * chunks], refs[count * chunks :]
    (gain_ref, *weights), refs = refs[:4], refs[4:]
    if carries:
        carried, refs = refs[: 2 * chunks], refs[2 * chunks :]
    if final:
        cosine_ref, sine_ref, out_ref, *refs = refs
    sums, squares, chosen = refs[: 2 * chunks : 2], refs[1 : 2 * chunks : 2], refs[-1]
    width = chosen.shape[1]
    depth = min(DEPTH, width)
    spans, first = [], 0
    for size in sizes:
        spans.append(slice(first, first + size))
        first += size
    for at in range(chunks):
        sums[at][...] = carried[2 * at][...] if carries else jnp.zeros_like(sums[at])
        squares[at][...] = carried[2 * at + 1][...] if carries else jnp.zeros_like(squares[at])

    def add_shard(visit, carry):
        piece, shard = place_ref[visit], place_ref[visits + visit]
        for index in range(count):

            @pl.when(piece == index)
            def _():
                for chunk, span in enumerate(spans):
                    chosen[span, :] = pieces[chunk * count + index][...]

        def add_part(part, carry):
            at = pl.multiple_of(part * depth, depth)
            deep = pl.ds(pl.multiple_of(shard * width + at, depth), depth)
            wide = chosen[:, pl.ds(at, depth)].astype(F32)
            square = wide * wide
            lanes = square[:, :128]
            for left in range(128, depth, 128):
                lanes = lanes + square[:, left : left + 128]
            for at, span in enumerate(spans):
                squares[at][...] += lanes[span]
            scaled = (wide * gain_ref[:, deep]).astype(BF16)
            left = 0
            for weight in weights:
                columns = slice(left, left + weight.shape[1])
                product = jnp.dot(scaled, weight[deep, :], preferred_element_type=F32)
                for at, span in enumerate(spans):
                    sums[at][:, columns] += product[span]
                left += weight.shape[1]
            return carry

        @pl.when(piece >= 0)
        def _():
            lax.fori_loop(0, width // depth, add_part, 0)

        return carry

    lax.fori_loop(0, visits, add_shard, 0)
    if final:
        mean = jnp.sum(squares[0][...], axis=1, keepdims=True) / (shards * width)
        scale = lax.rsqrt(mean + 1e-05)
        turned = sums[0].shape[1] - weights[-1].shape[1]
        for left in range(0, sums[0].shape[1], HEAD_SIZE):
            columns = slice(left, left + HEAD_SIZE)
            head = sums[0][:, columns] * scale
            if left < turned:
                head = head * cosine_ref[...] + pltpu.roll(
                    head, HEAD_SIZE // 2, 1
                ) * sine_ref[...]
            out_ref[:, columns] = head.astype(BF16)


def project(final, shards, sizes, place, lines, gain, weights, carried, tables):
    place, visits = place
    pieces = [piece for line in lines for piece in line]
    rows, width = sum(sizes), pieces[0].shape[1]
    columns = sum(weight.shape[1] for weight in weights)
    operands = [*pieces, gain, *weights, *carried, *tables]
    scratch = [pltpu.VMEM((rows, width), BF16)]
    if final:
        out_shape = [jax.ShapeDtypeStruct((rows, columns), BF16)]
        scratch = [pltpu.VMEM((rows, columns), F32), pltpu.VMEM((rows, 128), F32), *scratch]
    else:
        out_shape = [
            jax.ShapeDtypeStruct((size, wide), F32) for size in sizes for wide in (columns, 128)
        ]
    vmem = pl.BlockSpec(memory_space=pltpu.VMEM)
    return pl.pallas_call(
        functools.partial(
            project_kernel, len(lines[0]), bool(carried), final, shards, visits, sizes
        ),
        in_specs=[pl.BlockSpec(memory_space=pltpu.SMEM)] + [vmem] * len(operands),
        out_specs=[vmem] * len(out_shape),
        out_shape=out_shape,
        scratch_shapes=scratch,
        compiler_params=pltpu.CompilerParams(vmem_limit_bytes=6 * MEBI),
        name="project",
    )(place, *operands)


def attend_kernel(
    chips, groups, known, prior, query_width, key_width, lengths_ref, plan_ref, *refs
):
    blocks, refs = refs[: -13 if prior else -11], refs[-11:]
    attended_out, cache_out, token_ref, attended_ref, cache_ref, rows_ref, queries_ref = refs[:7]
    scores_ref, top_ref, sems, out_sems = refs[7:]
    token_ref[...] = jnp.zeros_like(token_ref)
    workers = 2 * chips
    me = lax.axis_index("req")
    chip, core = lax.div(me, 2), lax.rem(me, 2)
    slots = cache_ref.shape[1]
    spans = slots // SPAN
    total = workers * sum(sum(sizes) for _, sizes in groups)
    end = needed = jnp.int32(0)
    for other in range(workers):
        end = end + lengths_ref[other]
        needed = jnp.where(end <= prior, end, needed)
    copies = []
    for group, (bases, sizes) in enumerate(groups):
        for hop in range(chips):
            source = lax.rem(chip - hop + chips, chips) * 2
            for twin in range(2):
                owner = source + (core if twin == 0 else 1 - core)
                block = blocks[(group * chips + hop) * 2 + twin]
                first = 0
                for base, rows in zip(bases, sizes):
                    at = pl.multiple_of(base + owner * rows, ALIGN)
                    copy = pltpu.make_async_copy(
                        block.at[pl.ds(first, rows), :],
                        rows_ref.at[pl.ds(at, rows), :],
                        sems.at[len(copies)],
                    )
                    copies.append((at + rows > needed, copy))
                    first += rows
    for wanted, copy in copies:

        @pl.when(wanted)
        def _():
            copy.start()

    rows_ref[total:, :] = jnp.zeros((rows_ref.shape[0] - total, rows_ref.shape[1]), BF16)
    for wanted, copy in copies:

        @pl.when(wanted)
        def _():
            copy.wait()

    def window(row, columns):
        first = pl.multiple_of(lax.div(row, ALIGN) * ALIGN, ALIGN)
        shape = (SPAN, 2 * SPAN)
        hot = (iota(shape, 1) == iota(shape, 0) + (row - first)).astype(BF16)
        return jnp.dot(
            hot, rows_ref[pl.ds(first, 2 * SPAN), columns], preferred_element_type=F32
        )

    own_start, own_length = run_of(lengths_ref, me, workers)
    mine = (own_start + own_length <= known) & (own_start + own_length > prior)
    cache_copy = pltpu.make_async_copy(cache_ref, cache_out, out_sems.at[spans])

    @pl.when(mine)
    def _():
        def step(part, carry):
            at = pl.multiple_of(part * SPAN, SPAN)

            @pl.when(at < own_length)
            def _():
                picked = window(own_start + at, slice(query_width, query_width + 2 * key_width))
                live = at + iota(picked.shape, 0) < own_length
                picked = jnp.where(live, picked, 0.0).astype(BF16)
                cache_ref[0, pl.ds(at, SPAN), :] = picked[:, :key_width]
                cache_ref[1, pl.ds(at, SPAN), :] = picked[:, key_width:]

            @pl.when(at >= own_length)
            def _():
                empty = jnp.zeros((SPAN, key_width), BF16)
                cache_ref[0, pl.ds(at, SPAN), :] = empty
                cache_ref[1, pl.ds(at, SPAN), :] = empty

            return carry

        lax.fori_loop(0, spans, step, 0)
        cache_copy.start()

    heads, key_heads = query_width // HEAD_SIZE, key_width // HEAD_SIZE
    group = heads // key_heads
    factor = math.log2(math.e) / math.sqrt(HEAD_SIZE)
    tall = group * SPAN

    def span_of(slot):
        span = plan_ref[me * spans + slot]
        start, length = run_of(lengths_ref, lax.div(span, spans), workers)
        offset = lax.rem(span, spans) * SPAN
        dead = offset >= length
        needed = start + jnp.minimum(offset + SPAN, length)
        due = jnp.logical_not(dead) & (needed <= known) & (needed > prior)
        return start, length, offset, dead, due

    def result(slot):
        rows = pl.ds(pl.multiple_of(slot * SPAN, SPAN), SPAN)
        return pltpu.make_async_copy(
            attended_ref.at[rows, :], attended_out.at[rows, :], out_sems.at[slot]
        )

    def attend_slot(slot, carry):
        start, length, offset, dead, due = span_of(slot)
        out_rows = pl.ds(pl.multiple_of(slot * SPAN, SPAN), SPAN)

        if not prior:

            @pl.when(dead)
            def _():
                attended_ref[out_rows, :] = jnp.zeros((SPAN, query_width), BF16)
                result(slot).start()

        @pl.when(due)
        def _():
            queries = window(start + offset, slice(0, query_width)).astype(BF16)
            for head in range(heads):
                at = head % group * SPAN
                queries_ref[head // group, at : at + SPAN, :] = queries[
                    :, head * HEAD_SIZE : (head + 1) * HEAD_SIZE
                ]
            first = pl.multiple_of(lax.div(start, ALIGN) * ALIGN, ALIGN)
            shift = start - first
            reach = shift + jnp.minimum(offset + SPAN, length)
            tiles = lax.div(reach + TILE - 1, TILE)

            def columns(at, head):
                return slice(at + head * HEAD_SIZE, at + (head + 1) * HEAD_SIZE)

            def tile_rows(tile):
                return pl.ds(pl.multiple_of(first + tile * TILE, ALIGN), TILE)

            top_ref[...] = jnp.full(top_ref.shape, -1e30, F32)

            def score(tile, carry):
                key_pos = tile * TILE + iota((SPAN, TILE), 1) - shift
                query_pos = offset + iota((SPAN, TILE), 0)
                allowed = (key_pos >= 0) & (key_pos <= query_pos) & (key_pos < length)
                bias = jnp.where(allowed, 0.0, -1e30)
                bias = jnp.concatenate([bias] * group, axis=0)
                for head in range(key_heads):
                    scores = lax.dot_general(
                        queries_ref[head],
                        rows_ref[tile_rows(tile), columns(query_width, head)],
                        (((1,), (1,)), ((), ())),
                        preferred_element_type=F32,
                    )
                    scores = scores + bias
                    scores_ref[head, tile] = scores
                    top_ref[head] = jnp.maximum(top_ref[head], scores)
                return carry

            lax.fori_loop(0, tiles, score, 0)
            tops = [jnp.max(top_ref[head], axis=1, keepdims=True) for head in range(key_heads)]

            def mix(tile, carry):
                ones = jnp.ones((TILE, HEAD_SIZE), BF16)
                totals = []
                for head in range(key_heads):
                    weights = jnp.exp2((scores_ref[head, tile] - tops[head]) * factor)
                    values = rows_ref[tile_rows(tile), columns(query_width + key_width, head)]
                    values = jnp.concatenate([values, ones], axis=1)
                    totals.append(
                        carry[head]
                        + jnp.dot(weights.astype(BF16), values, preferred_element_type=F32)
                    )
                return tuple(totals)

            empty = jnp.zeros((tall, 2 * HEAD_SIZE), F32)
            mixed = lax.fori_loop(0, tiles, mix, (empty,) * key_heads)
            live = offset + iota((SPAN, HEAD_SIZE), 0) < length
            for head in range(heads):
                at = head % group * SPAN
                part = mixed[head // group][at : at + SPAN]
                part = part[:, :HEAD_SIZE] / part[:, HEAD_SIZE:]
                attended_ref[out_rows, columns(0, head)] = jnp.where(live, part, 0.0).astype(BF16)

            result(slot).start()

        return carry

    lax.fori_loop(0, spans, attend_slot, 0)

    def finish(slot, carry):
        _, _, _, dead, due = span_of(slot)

        @pl.when(due if prior else due | dead)
        def _():
            result(slot).wait()

        return carry

    lax.fori_loop(0, spans, finish, 0)

    @pl.when(mine)
    def _():
        cache_copy.wait()


def attend(chips, groups, known, prior, widths, slots, lengths, plan, blocks, outputs):
    query_width, key_width = widths
    width = query_width + 2 * key_width
    total = 2 * chips * sum(sum(sizes) for _, sizes in groups)
    copies = 2 * chips * sum(len(sizes) for _, sizes in groups)
    key_heads, tall = key_width // HEAD_SIZE, query_width // key_width * SPAN
    at = 2 + len(blocks)
    return pl.pallas_call(
        functools.partial(attend_kernel, chips, groups, known, prior, query_width, key_width),
        in_specs=[pl.BlockSpec(memory_space=pltpu.SMEM)] * 2
        + [pl.BlockSpec(memory_space=pl.ANY)] * (len(blocks) + len(outputs)),
        out_specs=[pl.BlockSpec(memory_space=pl.ANY)] * 2
        + [pl.BlockSpec(memory_space=pltpu.VMEM)],
        out_shape=[
            jax.ShapeDtypeStruct((slots, query_width), BF16),
            jax.ShapeDtypeStruct((2, slots, key_width), BF16),
            jax.ShapeDtypeStruct((8, 128), F32),
        ],
        input_output_aliases={at + index: index for index in range(len(outputs))},
        scratch_shapes=[
            pltpu.VMEM((slots, query_width), BF16),
            pltpu.VMEM((2, slots, key_width), BF16),
            pltpu.VMEM((total + TILE + ALIGN, width), BF16),
            pltpu.VMEM((key_heads, tall, HEAD_SIZE), BF16),
            pltpu.VMEM((key_heads, slots // TILE + 1, tall, TILE), F32),
            pltpu.VMEM((key_heads, tall, TILE), F32),
            pltpu.SemaphoreType.DMA((copies,)),
            pltpu.SemaphoreType.DMA((slots // SPAN + 1,)),
        ],
        compiler_params=pltpu.CompilerParams(vmem_limit_bytes=16 * MEBI),
        name="attend",
    )(lengths, plan, *blocks, *outputs)


def shift_chips(value, hop, chips):
    pairs = [(2 * x + c, 2 * ((x + hop) % chips) + c) for x in range(chips) for c in range(2)]
    return lax.ppermute(value, "req", pairs)


def swap_cores(value, chips):
    return lax.ppermute(value, "req", [(d, d ^ 1) for d in range(2 * chips)])


def local(
    chips, shards, tokens, norm_gain, w_query, key_weight, value_weight, lengths, plan
):
    workers = 2 * chips
    slots = tokens.shape[0]
    live = slots // 2
    sizes = [live * share // sum(SHARES) // ALIGN * ALIGN for share in SHARES]
    sizes[-1] = live - sum(sizes[:-1])
    bases = [workers * sum(sizes[:chunk]) for chunk in range(len(sizes))]
    weights = [w_query, key_weight, value_weight]
    gain = norm_gain.astype(F32).reshape(1, -1)
    halfway = HEAD_SIZE // 2
    frequency = np.exp(-np.arange(halfway) * 2.0 / HEAD_SIZE * math.log(500000.0))
    frequency = jnp.asarray(np.tile(frequency, 2)[None, :], F32)

    twin = swap_cores(tokens, chips)
    first = deal(chips, bases[:1], sizes[:1], lengths, [tokens], [False])
    dealt = [
        *deal(chips, bases[:1], sizes[:1], lengths, [twin], [True], first),
        *deal(chips, bases[1:], sizes[1:], lengths, [tokens, twin], [False, True]),
    ]
    homes, aways = dealt[::2], dealt[1::2]
    routes, owned, depth = routes_of(shards)
    direct = [piece for piece in range(len(owned)) if depth[piece] == 1]

    sources = {source + 1 for source, _ in routes} - {0}
    awaited = [piece for piece in direct if piece in sources or owned[piece][0] >= 0]
    early = [0, *awaited]
    late = [piece for piece in range(len(owned)) if piece not in early]

    kinds = {"own": [0], "first": early, "direct": awaited, "late": late}
    tables, counts = zip(
        *(visits_of([owned[piece] for piece in kind], shards) for kind in kinds.values())
    )
    table = jnp.asarray(np.concatenate(tables, axis=1))
    table = lax.dynamic_index_in_dim(table, lax.axis_index("tp"), 0, keepdims=False)
    ends = [2 * sum(counts[: at + 1]) for at in range(len(counts))]
    places = {
        kind: (table[end - 2 * count : end], count)
        for kind, count, end in zip(kinds, counts, ends)
    }

    groups = [([base], [rows]) for base, rows in zip(bases, sizes)]
    widths = w_query.shape[1], key_weight.shape[1]

    def add(kind, chunks, carried=()):
        held = [[lines[chunk][piece] for piece in kinds[kind]] for chunk in chunks]
        rows = [sizes[chunk] for chunk in chunks]
        turned = turns[chunks[0]] if kind == "late" else ()
        return project(
            kind == "late", shards, rows, places[kind], held, gain, weights, carried, turned
        )

    def from_chips(block):
        return [shift_chips(block, hop, chips) for hop in range(1, chips)]

    def all_blocks(block, arrived):
        return [leaf for piece in (block, *arrived) for leaf in (piece, swap_cores(piece, chips))]

    def start(line, group):
        for index, (source, pairs) in enumerate(routes):
            if index + 1 in group:
                line[index + 1] = lax.ppermute(line[source + 1], "tp", pairs)

    passed = [0, *(piece for piece in awaited if piece in sources)]
    lines, own, sent = [], [], []
    last = len(sizes) - 1
    sums, open_sums = {}, []
    for chunk in range(last + 2):
        fenced, anchors = [], []
        if chunk:
            fenced = [lines[-1][piece] for piece in passed]
            anchors = [lines[-1][piece] for piece in awaited if piece not in passed]
        if chunk <= last:
            arrived = [shift_chips(aways[chunk][hop - 1], hop, chips) for hop in range(1, chips)]
            later = aways[chunk + 1 : chunk + 2]
            block, aways[chunk + 1 : chunk + 2] = merge(homes[chunk], arrived, later)
            lines.append({0: block})
            fenced.append(block)
        if chunk == 2:
            sums[0] = add("first", [0])
            rest = list(range(1, last + 1))
            shared = add("own", rest)
            sums.update({at: shared[2 * index : 2 * index + 2] for index, at in enumerate(rest)})
            anchors += [sums[0][1], shared[1], *(lines[0][piece] for piece in late)]
        if chunk > 2:
            sums[chunk - 2] = add("direct", [chunk - 2], sums[chunk - 2])
            own.append(add("late", [chunk - 2], sums[chunk - 2])[0])
            sent.append(from_chips(own[-1]))
            anchors += [own[-1], *sent[-2]]
        if chunk == 1:
            weights[0], token = load(w_query, lines[0][0])
            anchors.append(token)
        if chunk:
            fenced = after(fenced, anchors)
            before = lines[chunk - 1]
            before.update(zip(passed, fenced))
            if chunk <= last:
                lines[chunk][0] = fenced[-1]
            start(before, late)
        if chunk <= last:
            start(lines[chunk], awaited)
        if chunk == 1:
            turns = angles(groups, lengths, frequency, lines[1][0])
        if chunk == 2:
            own.append(add("late", [0], sums[0])[0])
            sent.append(from_chips(own[0]))
    sums[last] = add("direct", [last], sums[last])
    own.append(add("late", [last], sums[last])[0])
    blocks = []
    for at in range(last):
        blocks += all_blocks(own[at], after(sent[at], own[at + 1 : at + 2]))
    sent.append(from_chips(own[last]))
    known = workers * sum(sizes[:-1])
    common = widths, slots, lengths, plan
    *outputs, token = attend(chips, groups[:-1], known, 0, *common, blocks, ())
    blocks += all_blocks(own[last], after(sent[last], [token]))
    return tuple(attend(chips, groups, workers * live, known, *common, blocks, outputs)[:2])


def solution(mesh):
    placed = (
        P(("groups", "req"), "tp"),
        P(),
        P(None, "tp"),
        P(None, "tp"),
        P(None, "tp"),
        P("groups"),
        P("groups"),
    )
    return jax.shard_map(
        functools.partial(local, mesh.shape["req"] // 2, mesh.shape["tp"]),
        mesh=mesh,
        in_specs=placed,
        out_specs=(P(("groups", "req"), "tp"), P(None, ("groups", "req"), "tp")),
        check_vma=False,
    )
```

```python
import functools
import math

import jax
import jax.numpy as jnp
import numpy as np
from jax import lax
from jax.experimental import pallas as pl
from jax.experimental.pallas import tpu as pltpu
from jax.sharding import PartitionSpec as P

HEAD_SIZE = 128
SPAN = 128
ALIGN = 16
TILE = 2 * SPAN
SHARES = (3, 5, 5, 3)
DEPTH = 1024
MEBI = 1024 * 1024
F32, BF16 = jnp.float32, jnp.bfloat16


def run_of(lengths_ref, request, count):
    start = jnp.int32(0)
    length = jnp.int32(0)
    for other in range(count):
        amount = lengths_ref[other]
        start = start + jnp.where(other < request, amount, 0)
        length = jnp.where(other == request, amount, length)
    return start, length


def iota(shape, dimension):
    return lax.broadcasted_iota(jnp.int32, shape, dimension)


def deal_kernel(chips, bases, sizes, twins, lengths_ref, *refs):
    me = lax.axis_index("req")
    chip, core = lax.div(me, 2), lax.rem(me, 2)
    sources, refs = refs[: len(twins)], refs[len(twins) :]
    count = 2 * len(sizes)
    priors, out_refs = refs[:-count], refs[-count:]
    requests = [me + 1 - 2 * core if twin else me for twin in twins]
    runs = [run_of(lengths_ref, request, 2 * chips) for request in requests]
    slots = sources[0].shape[0]
    for chunk, (base, rows) in enumerate(zip(bases, sizes)):
        home_ref, away_ref = out_refs[2 * chunk : 2 * chunk + 2]
        for hop in range(chips):
            target = lax.rem(chip + hop, chips) * 2 + core
            number = base + target * rows + iota((rows, slots), 0)
            slot = iota((rows, slots), 1)
            total = None
            for (start, length), source in zip(runs, sources):
                hot = ((number - start == slot) & (slot < length)).astype(BF16)
                part = jnp.dot(hot, source[...], preferred_element_type=F32)
                total = part if total is None else total + part
            total = total.astype(BF16)
            if hop == 0:
                home_ref[...] = total + priors[2 * chunk][...] if priors else total
            elif priors:
                away_ref[hop - 1] = total + priors[2 * chunk + 1][hop - 1]
            else:
                away_ref[hop - 1] = total


def deal(chips, bases, sizes, lengths, sources, twins, priors=()):
    slots, width = sources[0].shape
    block = min(1024, width)
    out_specs, out_shape = [], []
    for rows in sizes:
        out_specs += [
            pl.BlockSpec((rows, block), lambda i: (0, i)),
            pl.BlockSpec((chips - 1, rows, block), lambda i: (0, 0, i)),
        ]
        out_shape += [
            jax.ShapeDtypeStruct((rows, width), BF16),
            jax.ShapeDtypeStruct((chips - 1, rows, width), BF16),
        ]
    return pl.pallas_call(
        functools.partial(deal_kernel, chips, bases, sizes, twins),
        grid=(width // block,),
        in_specs=[pl.BlockSpec(memory_space=pltpu.SMEM)]
        + [pl.BlockSpec((slots, block), lambda i: (0, i)) for _ in sources]
        + (out_specs if priors else []),
        out_specs=out_specs,
        out_shape=out_shape,
        compiler_params=pltpu.CompilerParams(vmem_limit_bytes=10 * MEBI),
        name="deal",
    )(lengths, *sources, *priors)


def merge_kernel(count, passed, home_ref, *refs):
    total = home_ref[...]
    for ref in refs[:count]:
        total = total + ref[...]
    refs[len(refs) - 1 - passed][...] = total


def merge(home, arrived, later):
    count = len(arrived)
    vmem, anywhere = pl.BlockSpec(memory_space=pltpu.VMEM), pl.BlockSpec(memory_space=pl.ANY)
    block, *later = pl.pallas_call(
        functools.partial(merge_kernel, count, len(later)),
        in_specs=[vmem] * (count + 1) + [anywhere] * len(later),
        out_specs=[vmem] + [anywhere] * len(later),
        out_shape=[jax.ShapeDtypeStruct(leaf.shape, leaf.dtype) for leaf in (home, *later)],
        input_output_aliases={count + 1 + at: 1 + at for at in range(len(later))},
        compiler_params=pltpu.CompilerParams(vmem_limit_bytes=4 * MEBI),
        name="merge",
    )(home, *arrived, *later)
    return block, later


def after(arrays, anchors):
    def kernel(*refs):
        pass

    anywhere = pl.BlockSpec(memory_space=pl.ANY)
    return pl.pallas_call(
        kernel,
        in_specs=[anywhere] * (len(arrays) + len(anchors)),
        out_specs=[anywhere] * len(arrays),
        out_shape=[jax.ShapeDtypeStruct(leaf.shape, leaf.dtype) for leaf in arrays],
        input_output_aliases={at: at for at in range(len(arrays))},
        compiler_params=pltpu.CompilerParams(vmem_limit_bytes=MEBI),
        name="after",
    )(*arrays, *anchors)


def routes_of(shards):
    routes, masks, distance = [], [0], shards // 2
    while distance:
        for source in range(len(masks)):
            routes.append((source, distance))
            masks.append(masks[source] ^ distance)
        distance //= 2
    return routes, masks


def angles_kernel(groups, members, lengths_ref, frequency_ref, anchor_ref, *out_refs):
    me = lax.axis_index("req")
    for group, (bases, sizes) in enumerate(groups):
        first = 0
        for base, rows in zip(bases, sizes):
            number = base + me * rows + iota((rows, HEAD_SIZE), 0)
            start = jnp.zeros((rows, HEAD_SIZE), jnp.int32)
            before = jnp.int32(0)
            for other in range(members):
                before = before + lengths_ref[other]
                start = jnp.where(number >= before, before, start)
            angle = (number - start).astype(F32) * frequency_ref[...]
            sine = jnp.sin(angle)
            lower = iota((rows, HEAD_SIZE), 1) < HEAD_SIZE // 2
            out_refs[2 * group][first : first + rows, :] = jnp.cos(angle)
            out_refs[2 * group + 1][first : first + rows, :] = jnp.where(lower, -sine, sine)
            first += rows


def angles(groups, lengths, frequency, anchor):
    shapes = [
        jax.ShapeDtypeStruct((sum(sizes), HEAD_SIZE), F32) for _, sizes in groups for _ in range(2)
    ]
    vmem = pl.BlockSpec(memory_space=pltpu.VMEM)
    tables = pl.pallas_call(
        functools.partial(angles_kernel, groups, lengths.shape[0]),
        in_specs=[
            pl.BlockSpec(memory_space=pltpu.SMEM),
            vmem,
            pl.BlockSpec(memory_space=pl.ANY),
        ],
        out_specs=[vmem] * len(shapes),
        out_shape=shapes,
        compiler_params=pltpu.CompilerParams(vmem_limit_bytes=4 * MEBI),
        name="angles",
    )(lengths, frequency, anchor)
    return [tables[at : at + 2] for at in range(0, len(tables), 2)]


def load(weight, anchor):
    parts = 8
    depth = weight.shape[0] // parts

    def kernel(weight_ref, anchor_ref, out_ref, token_ref, sems):
        copies = [
            pltpu.make_async_copy(
                weight_ref.at[pl.ds(part * depth, depth), :],
                out_ref.at[pl.ds(part * depth, depth), :],
                sems.at[part],
            )
            for part in range(parts)
        ]
        for copy in copies:
            copy.start()
        token_ref[...] = jnp.zeros_like(token_ref)
        for copy in copies:
            copy.wait()

    vmem, anywhere = pl.BlockSpec(memory_space=pltpu.VMEM), pl.BlockSpec(memory_space=pl.ANY)
    return pl.pallas_call(
        kernel,
        in_specs=[anywhere, anywhere],
        out_specs=[vmem, vmem],
        out_shape=[
            jax.ShapeDtypeStruct(weight.shape, weight.dtype),
            jax.ShapeDtypeStruct((8, 128), F32),
        ],
        scratch_shapes=[pltpu.SemaphoreType.DMA((parts,))],
        compiler_params=pltpu.CompilerParams(vmem_limit_bytes=2 * MEBI),
        name="load",
    )(pltpu.with_memory_space_constraint(weight, pltpu.HBM), anchor)


def project_kernel(masks, carries, final, shards, *refs):
    pieces, refs = refs[: len(masks)], refs[len(masks) :]
    (gain_ref, *weights), refs = refs[:4], refs[4:]
    if carries:
        sums_in, squares_in, *refs = refs
    if final:
        cosine_ref, sine_ref, out_ref, *refs = refs
    sums, squares = refs
    width = pieces[0].shape[1]
    depth = min(DEPTH, width)
    sums[...] = sums_in[...] if carries else jnp.zeros_like(sums)
    squares[...] = squares_in[...] if carries else jnp.zeros_like(squares)
    for piece, mask in zip(pieces, masks):
        shard = lax.bitwise_xor(lax.axis_index("tp"), jnp.int32(mask))

        def add_part(part, carry):
            at = pl.multiple_of(part * depth, depth)
            deep = pl.ds(pl.multiple_of(shard * width + at, depth), depth)
            wide = piece[:, pl.ds(at, depth)].astype(F32)
            square = wide * wide
            lanes = square[:, :128]
            for left in range(128, depth, 128):
                lanes = lanes + square[:, left : left + 128]
            squares[...] += lanes
            scaled = (wide * gain_ref[:, deep]).astype(BF16)
            left = 0
            for weight in weights:
                columns = slice(left, left + weight.shape[1])
                sums[:, columns] += jnp.dot(
                    scaled, weight[deep, :], preferred_element_type=F32
                )
                left += weight.shape[1]
            return carry

        lax.fori_loop(0, width // depth, add_part, 0)
    if final:
        mean = jnp.sum(squares[...], axis=1, keepdims=True) / (shards * width)
        scale = lax.rsqrt(mean + 1e-05)
        turned = sums.shape[1] - weights[-1].shape[1]
        for left in range(0, sums.shape[1], HEAD_SIZE):
            columns = slice(left, left + HEAD_SIZE)
            head = sums[:, columns] * scale
            if left < turned:
                head = head * cosine_ref[...] + pltpu.roll(
                    head, HEAD_SIZE // 2, 1
                ) * sine_ref[...]
            out_ref[:, columns] = head.astype(BF16)


def project(final, shards, masks, pieces, gain, weights, carried, tables):
    rows = pieces[0].shape[0]
    columns = sum(weight.shape[1] for weight in weights)
    operands = [*pieces, gain, *weights, *carried, *tables]
    sums = (rows, columns), (rows, 128)
    if final:
        out_shape = [jax.ShapeDtypeStruct((rows, columns), BF16)]
        scratch = [pltpu.VMEM(shape, F32) for shape in sums]
    else:
        out_shape = [jax.ShapeDtypeStruct(shape, F32) for shape in sums]
        scratch = []
    vmem = pl.BlockSpec(memory_space=pltpu.VMEM)
    return pl.pallas_call(
        functools.partial(project_kernel, masks, bool(carried), final, shards),
        in_specs=[vmem] * len(operands),
        out_specs=[vmem] * len(out_shape),
        out_shape=out_shape,
        scratch_shapes=scratch,
        compiler_params=pltpu.CompilerParams(vmem_limit_bytes=6 * MEBI),
        name="project",
    )(*operands)


def attend_kernel(
    chips, groups, known, prior, query_width, key_width, lengths_ref, plan_ref, *refs
):
    blocks, refs = refs[: -13 if prior else -11], refs[-11:]
    attended_out, cache_out, token_ref, attended_ref, cache_ref, rows_ref, queries_ref = refs[:7]
    scores_ref, top_ref, sems, out_sems = refs[7:]
    token_ref[...] = jnp.zeros_like(token_ref)
    workers = 2 * chips
    me = lax.axis_index("req")
    chip, core = lax.div(me, 2), lax.rem(me, 2)
    slots = cache_ref.shape[1]
    spans = slots // SPAN
    total = workers * sum(sum(sizes) for _, sizes in groups)
    end = needed = jnp.int32(0)
    for other in range(workers):
        end = end + lengths_ref[other]
        needed = jnp.where(end <= prior, end, needed)
    copies = []
    for group, (bases, sizes) in enumerate(groups):
        for hop in range(chips):
            source = lax.rem(chip - hop + chips, chips) * 2
            for twin in range(2):
                owner = source + (core if twin == 0 else 1 - core)
                block = blocks[(group * chips + hop) * 2 + twin]
                first = 0
                for base, rows in zip(bases, sizes):
                    at = pl.multiple_of(base + owner * rows, ALIGN)
                    copy = pltpu.make_async_copy(
                        block.at[pl.ds(first, rows), :],
                        rows_ref.at[pl.ds(at, rows), :],
                        sems.at[len(copies)],
                    )
                    copies.append((at + rows > needed, copy))
                    first += rows
    for wanted, copy in copies:

        @pl.when(wanted)
        def _():
            copy.start()

    rows_ref[total:, :] = jnp.zeros((rows_ref.shape[0] - total, rows_ref.shape[1]), BF16)
    for wanted, copy in copies:

        @pl.when(wanted)
        def _():
            copy.wait()

    def window(row, columns):
        first = pl.multiple_of(lax.div(row, ALIGN) * ALIGN, ALIGN)
        shape = (SPAN, 2 * SPAN)
        hot = (iota(shape, 1) == iota(shape, 0) + (row - first)).astype(BF16)
        return jnp.dot(
            hot, rows_ref[pl.ds(first, 2 * SPAN), columns], preferred_element_type=F32
        )

    own_start, own_length = run_of(lengths_ref, me, workers)
    mine = (own_start + own_length <= known) & (own_start + own_length > prior)
    cache_copy = pltpu.make_async_copy(cache_ref, cache_out, out_sems.at[spans])

    @pl.when(mine)
    def _():
        def step(part, carry):
            at = pl.multiple_of(part * SPAN, SPAN)

            @pl.when(at < own_length)
            def _():
                picked = window(own_start + at, slice(query_width, query_width + 2 * key_width))
                live = at + iota(picked.shape, 0) < own_length
                picked = jnp.where(live, picked, 0.0).astype(BF16)
                cache_ref[0, pl.ds(at, SPAN), :] = picked[:, :key_width]
                cache_ref[1, pl.ds(at, SPAN), :] = picked[:, key_width:]

            @pl.when(at >= own_length)
            def _():
                empty = jnp.zeros((SPAN, key_width), BF16)
                cache_ref[0, pl.ds(at, SPAN), :] = empty
                cache_ref[1, pl.ds(at, SPAN), :] = empty

            return carry

        lax.fori_loop(0, spans, step, 0)
        cache_copy.start()

    heads, key_heads = query_width // HEAD_SIZE, key_width // HEAD_SIZE
    group = heads // key_heads
    factor = math.log2(math.e) / math.sqrt(HEAD_SIZE)
    tall = group * SPAN

    def span_of(slot):
        span = plan_ref[me * spans + slot]
        start, length = run_of(lengths_ref, lax.div(span, spans), workers)
        offset = lax.rem(span, spans) * SPAN
        dead = offset >= length
        needed = start + jnp.minimum(offset + SPAN, length)
        due = jnp.logical_not(dead) & (needed <= known) & (needed > prior)
        return start, length, offset, dead, due

    def result(slot):
        rows = pl.ds(pl.multiple_of(slot * SPAN, SPAN), SPAN)
        return pltpu.make_async_copy(
            attended_ref.at[rows, :], attended_out.at[rows, :], out_sems.at[slot]
        )

    def attend_slot(slot, carry):
        start, length, offset, dead, due = span_of(slot)
        out_rows = pl.ds(pl.multiple_of(slot * SPAN, SPAN), SPAN)

        if not prior:

            @pl.when(dead)
            def _():
                attended_ref[out_rows, :] = jnp.zeros((SPAN, query_width), BF16)
                result(slot).start()

        @pl.when(due)
        def _():
            queries = window(start + offset, slice(0, query_width)).astype(BF16)
            for head in range(heads):
                at = head % group * SPAN
                queries_ref[head // group, at : at + SPAN, :] = queries[
                    :, head * HEAD_SIZE : (head + 1) * HEAD_SIZE
                ]
            first = pl.multiple_of(lax.div(start, ALIGN) * ALIGN, ALIGN)
            shift = start - first
            reach = shift + jnp.minimum(offset + SPAN, length)
            tiles = lax.div(reach + TILE - 1, TILE)

            def columns(at, head):
                return slice(at + head * HEAD_SIZE, at + (head + 1) * HEAD_SIZE)

            def tile_rows(tile):
                return pl.ds(pl.multiple_of(first + tile * TILE, ALIGN), TILE)

            top_ref[...] = jnp.full(top_ref.shape, -1e30, F32)

            def score(tile, carry):
                key_pos = tile * TILE + iota((SPAN, TILE), 1) - shift
                query_pos = offset + iota((SPAN, TILE), 0)
                allowed = (key_pos >= 0) & (key_pos <= query_pos) & (key_pos < length)
                bias = jnp.where(allowed, 0.0, -1e30)
                bias = jnp.concatenate([bias] * group, axis=0)
                for head in range(key_heads):
                    scores = lax.dot_general(
                        queries_ref[head],
                        rows_ref[tile_rows(tile), columns(query_width, head)],
                        (((1,), (1,)), ((), ())),
                        preferred_element_type=F32,
                    )
                    scores = scores + bias
                    scores_ref[head, tile] = scores
                    top_ref[head] = jnp.maximum(top_ref[head], scores)
                return carry

            lax.fori_loop(0, tiles, score, 0)
            tops = [jnp.max(top_ref[head], axis=1, keepdims=True) for head in range(key_heads)]

            def mix(tile, carry):
                ones = jnp.ones((TILE, HEAD_SIZE), BF16)
                totals = []
                for head in range(key_heads):
                    weights = jnp.exp2((scores_ref[head, tile] - tops[head]) * factor)
                    values = rows_ref[tile_rows(tile), columns(query_width + key_width, head)]
                    values = jnp.concatenate([values, ones], axis=1)
                    totals.append(
                        carry[head]
                        + jnp.dot(weights.astype(BF16), values, preferred_element_type=F32)
                    )
                return tuple(totals)

            empty = jnp.zeros((tall, 2 * HEAD_SIZE), F32)
            mixed = lax.fori_loop(0, tiles, mix, (empty,) * key_heads)
            live = offset + iota((SPAN, HEAD_SIZE), 0) < length
            for head in range(heads):
                at = head % group * SPAN
                part = mixed[head // group][at : at + SPAN]
                part = part[:, :HEAD_SIZE] / part[:, HEAD_SIZE:]
                attended_ref[out_rows, columns(0, head)] = jnp.where(live, part, 0.0).astype(BF16)

            result(slot).start()

        return carry

    lax.fori_loop(0, spans, attend_slot, 0)

    def finish(slot, carry):
        _, _, _, dead, due = span_of(slot)

        @pl.when(due if prior else due | dead)
        def _():
            result(slot).wait()

        return carry

    lax.fori_loop(0, spans, finish, 0)

    @pl.when(mine)
    def _():
        cache_copy.wait()


def attend(chips, groups, known, prior, widths, slots, lengths, plan, blocks, outputs):
    query_width, key_width = widths
    width = query_width + 2 * key_width
    total = 2 * chips * sum(sum(sizes) for _, sizes in groups)
    copies = 2 * chips * sum(len(sizes) for _, sizes in groups)
    key_heads, tall = key_width // HEAD_SIZE, query_width // key_width * SPAN
    at = 2 + len(blocks)
    return pl.pallas_call(
        functools.partial(attend_kernel, chips, groups, known, prior, query_width, key_width),
        in_specs=[pl.BlockSpec(memory_space=pltpu.SMEM)] * 2
        + [pl.BlockSpec(memory_space=pl.ANY)] * (len(blocks) + len(outputs)),
        out_specs=[pl.BlockSpec(memory_space=pl.ANY)] * 2
        + [pl.BlockSpec(memory_space=pltpu.VMEM)],
        out_shape=[
            jax.ShapeDtypeStruct((slots, query_width), BF16),
            jax.ShapeDtypeStruct((2, slots, key_width), BF16),
            jax.ShapeDtypeStruct((8, 128), F32),
        ],
        input_output_aliases={at + index: index for index in range(len(outputs))},
        scratch_shapes=[
            pltpu.VMEM((slots, query_width), BF16),
            pltpu.VMEM((2, slots, key_width), BF16),
            pltpu.VMEM((total + TILE + ALIGN, width), BF16),
            pltpu.VMEM((key_heads, tall, HEAD_SIZE), BF16),
            pltpu.VMEM((key_heads, slots // TILE + 1, tall, TILE), F32),
            pltpu.VMEM((key_heads, tall, TILE), F32),
            pltpu.SemaphoreType.DMA((copies,)),
            pltpu.SemaphoreType.DMA((slots // SPAN + 1,)),
        ],
        compiler_params=pltpu.CompilerParams(vmem_limit_bytes=16 * MEBI),
        name="attend",
    )(lengths, plan, *blocks, *outputs)


def shift_chips(value, hop, chips):
    pairs = [(2 * x + c, 2 * ((x + hop) % chips) + c) for x in range(chips) for c in range(2)]
    return lax.ppermute(value, "req", pairs)


def swap_cores(value, chips):
    return lax.ppermute(value, "req", [(d, d ^ 1) for d in range(2 * chips)])


def local(
    chips, shards, tokens, norm_gain, w_query, key_weight, value_weight, lengths, plan
):
    workers = 2 * chips
    slots = tokens.shape[0]
    live = slots // 2
    sizes = [live * share // sum(SHARES) // ALIGN * ALIGN for share in SHARES]
    sizes[-1] = live - sum(sizes[:-1])
    bases = [workers * sum(sizes[:chunk]) for chunk in range(len(sizes))]
    weights = [w_query, key_weight, value_weight]
    gain = norm_gain.astype(F32).reshape(1, -1)
    halfway = HEAD_SIZE // 2
    frequency = np.exp(-np.arange(halfway) * 2.0 / HEAD_SIZE * math.log(500000.0))
    frequency = jnp.asarray(np.tile(frequency, 2)[None, :], F32)

    twin = swap_cores(tokens, chips)
    first = deal(chips, bases[:1], sizes[:1], lengths, [tokens], [False])
    dealt = [
        *deal(chips, bases[:1], sizes[:1], lengths, [twin], [True], first),
        *deal(chips, bases[1:], sizes[1:], lengths, [tokens, twin], [False, True]),
    ]
    homes, aways = dealt[::2], dealt[1::2]
    routes, masks = routes_of(shards)
    direct = [at + 1 for at, (source, _) in enumerate(routes) if source == 0]
    kinds = {"first": [0, *direct]}
    kinds["late"] = [piece for piece in range(len(masks)) if piece not in kinds["first"]]
    relayed = [piece for piece in direct if piece in {source for source, _ in routes}]

    groups = [([base], [rows]) for base, rows in zip(bases, sizes)]
    widths = w_query.shape[1], key_weight.shape[1]

    def add(kind, chunk, carried=()):
        pieces = [lines[chunk][piece] for piece in kinds[kind]]
        final = kind == "late"
        turned = turns[chunk] if final else ()
        offsets = [masks[piece] for piece in kinds[kind]]
        return project(final, shards, offsets, pieces, gain, weights, carried, turned)

    def from_chips(block):
        return [shift_chips(block, hop, chips) for hop in range(1, chips)]

    def all_blocks(block, arrived):
        return [leaf for piece in (block, *arrived) for leaf in (piece, swap_cores(piece, chips))]

    def start(line, group):
        for index, (source, distance) in enumerate(routes):
            if index + 1 in group:
                pairs = [(at, at ^ distance) for at in range(shards)]
                line[index + 1] = lax.ppermute(line[source], "tp", pairs)

    lines, own, sent = [], [], []
    last = len(sizes) - 1

    def finish(chunk):
        own.append(add("late", chunk, add("first", chunk))[0])
        sent.append(from_chips(own[-1]))

    def fence(chunk, block):
        passed, anchors = [], []
        if chunk:
            before = lines[chunk - 1]
            passed = [before[piece] for piece in relayed]
            anchors += [before[piece] for piece in direct if piece not in relayed]
        if chunk == 1:
            weights[0], token = load(w_query, lines[0][0])
            anchors.append(token)
        if 1 < chunk <= last:
            finish(chunk - 2)
            anchors.append(own[-1])
        if chunk > 2:
            anchors += sent[chunk - 3]
        if passed:
            passed = after([*passed, *block], anchors)
            before.update(zip(relayed, passed))
            block = passed[len(relayed) :]
        return block

    for chunk in range(last + 1):
        arrived = [shift_chips(aways[chunk][hop - 1], hop, chips) for hop in range(1, chips)]
        later = aways[chunk + 1 : chunk + 2]
        block, aways[chunk + 1 : chunk + 2] = merge(homes[chunk], arrived, later)
        lines.append({0: fence(chunk, [block])[0]})
        if chunk:
            start(lines[-2], kinds["late"])
        start(lines[-1], direct)
        if chunk == 1:
            turns = angles(groups, lengths, frequency, lines[1][0])
    fence(last + 1, [])
    start(lines[-1], kinds["late"])
    for chunk in (last - 1, last):
        finish(chunk)
    blocks = []
    for at in range(last):
        blocks += all_blocks(own[at], after(sent[at], own[at + 1 : at + 2]))
    sent.append(from_chips(own[last]))
    known = workers * sum(sizes[:-1])
    common = widths, slots, lengths, plan
    *outputs, token = attend(chips, groups[:-1], known, 0, *common, blocks, ())
    blocks += all_blocks(own[last], after(sent[last], [token]))
    return tuple(attend(chips, groups, workers * live, known, *common, blocks, outputs)[:2])


def solution(mesh):
    placed = (
        P(("groups", "req"), "tp"),
        P(),
        P(None, "tp"),
        P(None, "tp"),
        P(None, "tp"),
        P("groups"),
        P("groups"),
    )
    return jax.shard_map(
        functools.partial(local, mesh.shape["req"] // 2, mesh.shape["tp"]),
        mesh=mesh,
        in_specs=placed,
        out_specs=(P(("groups", "req"), "tp"), P(None, ("groups", "req"), "tp")),
        check_vma=False,
    )
```

```python
import functools
import math

import jax
import jax.numpy as jnp
import numpy as np
from jax import lax
from jax.experimental import pallas as pl
from jax.experimental.pallas import tpu as pltpu
from jax.sharding import PartitionSpec as P

HEAD_SIZE = 128
SPAN = 128
ALIGN = 16
TILE = 2 * SPAN
SHARES = (3, 5, 5, 3)
DEPTH = 1024
MEBI = 1024 * 1024
F32, BF16 = jnp.float32, jnp.bfloat16


def run_of(lengths_ref, request, count):
    start = jnp.int32(0)
    length = jnp.int32(0)
    for other in range(count):
        amount = lengths_ref[other]
        start = start + jnp.where(other < request, amount, 0)
        length = jnp.where(other == request, amount, length)
    return start, length


def iota(shape, dimension):
    return lax.broadcasted_iota(jnp.int32, shape, dimension)


def deal_kernel(chips, bases, sizes, twins, lengths_ref, *refs):
    me = lax.axis_index("req")
    chip, core = lax.div(me, 2), lax.rem(me, 2)
    sources, refs = refs[: len(twins)], refs[len(twins) :]
    count = 2 * len(sizes)
    priors, out_refs = refs[:-count], refs[-count:]
    requests = [me + 1 - 2 * core if twin else me for twin in twins]
    runs = [run_of(lengths_ref, request, 2 * chips) for request in requests]
    slots = sources[0].shape[0]
    total = None
    for (start, length), source in zip(runs, sources):
        hots = []
        for base, rows in zip(bases, sizes):
            for hop in range(chips):
                target = lax.rem(chip + hop, chips) * 2 + core
                number = base + target * rows + iota((rows, slots), 0)
                slot = iota((rows, slots), 1)
                hot = (number - start == slot) & (slot < length)
                hots.append(hot.astype(F32).astype(BF16))
        hot = jnp.concatenate(hots, axis=0) if len(hots) > 1 else hots[0]
        part = jnp.dot(hot, source[...], preferred_element_type=F32)
        total = part if total is None else total + part
    total = total.astype(BF16)
    at = 0
    for chunk, rows in enumerate(sizes):
        for hop in range(chips):
            picked = total[at : at + rows]
            at += rows
            if priors:
                prior = priors[2 * chunk + 1][hop - 1] if hop else priors[2 * chunk][...]
                picked = picked + prior
            if hop:
                out_refs[2 * chunk + 1][hop - 1] = picked
            else:
                out_refs[2 * chunk][...] = picked


def deal(chips, bases, sizes, lengths, sources, twins, priors=()):
    slots, width = sources[0].shape
    block = min(1024, width)
    out_specs, out_shape = [], []
    for rows in sizes:
        out_specs += [
            pl.BlockSpec((rows, block), lambda i: (0, i)),
            pl.BlockSpec((chips - 1, rows, block), lambda i: (0, 0, i)),
        ]
        out_shape += [
            jax.ShapeDtypeStruct((rows, width), BF16),
            jax.ShapeDtypeStruct((chips - 1, rows, width), BF16),
        ]
    return pl.pallas_call(
        functools.partial(deal_kernel, chips, bases, sizes, twins),
        grid=(width // block,),
        in_specs=[pl.BlockSpec(memory_space=pltpu.SMEM)]
        + [pl.BlockSpec((slots, block), lambda i: (0, i)) for _ in sources]
        + (out_specs if priors else []),
        out_specs=out_specs,
        out_shape=out_shape,
        compiler_params=pltpu.CompilerParams(vmem_limit_bytes=10 * MEBI),
        name="deal",
    )(lengths, *sources, *priors)


def merge_kernel(count, passed, home_ref, *refs):
    total = home_ref[...]
    for ref in refs[:count]:
        total = total + ref[...]
    refs[len(refs) - 1 - passed][...] = total


def merge(home, arrived, later):
    count = len(arrived)
    vmem, anywhere = pl.BlockSpec(memory_space=pltpu.VMEM), pl.BlockSpec(memory_space=pl.ANY)
    block, *later = pl.pallas_call(
        functools.partial(merge_kernel, count, len(later)),
        in_specs=[vmem] * (count + 1) + [anywhere] * len(later),
        out_specs=[vmem] + [anywhere] * len(later),
        out_shape=[jax.ShapeDtypeStruct(leaf.shape, leaf.dtype) for leaf in (home, *later)],
        input_output_aliases={count + 1 + at: 1 + at for at in range(len(later))},
        compiler_params=pltpu.CompilerParams(vmem_limit_bytes=4 * MEBI),
        name="merge",
    )(home, *arrived, *later)
    return block, later


def after(arrays, anchors):
    def kernel(*refs):
        pass

    anywhere = pl.BlockSpec(memory_space=pl.ANY)
    return pl.pallas_call(
        kernel,
        in_specs=[anywhere] * (len(arrays) + len(anchors)),
        out_specs=[anywhere] * len(arrays),
        out_shape=[jax.ShapeDtypeStruct(leaf.shape, leaf.dtype) for leaf in arrays],
        input_output_aliases={at: at for at in range(len(arrays))},
        compiler_params=pltpu.CompilerParams(vmem_limit_bytes=MEBI),
        name="after",
    )(*arrays, *anchors)


def routes_of(shards):
    routes, masks, distance = [], [0], shards // 2
    while distance:
        for source in range(len(masks)):
            routes.append((source, distance))
            masks.append(masks[source] ^ distance)
        distance //= 2
    return routes, masks


def angles_kernel(groups, members, lengths_ref, frequency_ref, anchor_ref, *out_refs):
    me = lax.axis_index("req")
    for group, (bases, sizes) in enumerate(groups):
        first = 0
        for base, rows in zip(bases, sizes):
            number = base + me * rows + iota((rows, HEAD_SIZE), 0)
            start = jnp.zeros((rows, HEAD_SIZE), jnp.int32)
            before = jnp.int32(0)
            for other in range(members):
                before = before + lengths_ref[other]
                start = jnp.where(number >= before, before, start)
            angle = (number - start).astype(F32) * frequency_ref[...]
            sine = jnp.sin(angle)
            lower = iota((rows, HEAD_SIZE), 1) < HEAD_SIZE // 2
            out_refs[2 * group][first : first + rows, :] = jnp.cos(angle)
            out_refs[2 * group + 1][first : first + rows, :] = jnp.where(lower, -sine, sine)
            first += rows


def angles(groups, lengths, frequency, anchor):
    shapes = [
        jax.ShapeDtypeStruct((sum(sizes), HEAD_SIZE), F32) for _, sizes in groups for _ in range(2)
    ]
    vmem = pl.BlockSpec(memory_space=pltpu.VMEM)
    tables = pl.pallas_call(
        functools.partial(angles_kernel, groups, lengths.shape[0]),
        in_specs=[
            pl.BlockSpec(memory_space=pltpu.SMEM),
            vmem,
            pl.BlockSpec(memory_space=pl.ANY),
        ],
        out_specs=[vmem] * len(shapes),
        out_shape=shapes,
        compiler_params=pltpu.CompilerParams(vmem_limit_bytes=4 * MEBI),
        name="angles",
    )(lengths, frequency, anchor)
    return [tables[at : at + 2] for at in range(0, len(tables), 2)]


def load(weight, anchor):
    parts = 8
    depth = weight.shape[0] // parts

    def kernel(weight_ref, anchor_ref, out_ref, token_ref, sems):
        copies = [
            pltpu.make_async_copy(
                weight_ref.at[pl.ds(part * depth, depth), :],
                out_ref.at[pl.ds(part * depth, depth), :],
                sems.at[part],
            )
            for part in range(parts)
        ]
        for copy in copies:
            copy.start()
        token_ref[...] = jnp.zeros_like(token_ref)
        for copy in copies:
            copy.wait()

    vmem, anywhere = pl.BlockSpec(memory_space=pltpu.VMEM), pl.BlockSpec(memory_space=pl.ANY)
    return pl.pallas_call(
        kernel,
        in_specs=[anywhere, anywhere],
        out_specs=[vmem, vmem],
        out_shape=[
            jax.ShapeDtypeStruct(weight.shape, weight.dtype),
            jax.ShapeDtypeStruct((8, 128), F32),
        ],
        scratch_shapes=[pltpu.SemaphoreType.DMA((parts,))],
        compiler_params=pltpu.CompilerParams(vmem_limit_bytes=2 * MEBI),
        name="load",
    )(pltpu.with_memory_space_constraint(weight, pltpu.HBM), anchor)


def project_kernel(masks, carries, final, shards, *refs):
    pieces, refs = refs[: len(masks)], refs[len(masks) :]
    (gain_ref, *weights), refs = refs[:4], refs[4:]
    if carries:
        sums_in, squares_in, *refs = refs
    if final:
        cosine_ref, sine_ref, out_ref, *refs = refs
    sums, squares = refs
    width = pieces[0].shape[1]
    depth = min(DEPTH, width)
    sums[...] = sums_in[...] if carries else jnp.zeros_like(sums)
    squares[...] = squares_in[...] if carries else jnp.zeros_like(squares)
    for piece, mask in zip(pieces, masks):
        shard = lax.bitwise_xor(lax.axis_index("tp"), jnp.int32(mask))

        def add_part(part, carry):
            at = pl.multiple_of(part * depth, depth)
            deep = pl.ds(pl.multiple_of(shard * width + at, depth), depth)
            wide = piece[:, pl.ds(at, depth)].astype(F32)
            square = wide * wide
            lanes = square[:, :128]
            for left in range(128, depth, 128):
                lanes = lanes + square[:, left : left + 128]
            squares[...] += lanes
            scaled = (wide * gain_ref[:, deep]).astype(BF16)
            left = 0
            for weight in weights:
                columns = slice(left, left + weight.shape[1])
                sums[:, columns] += jnp.dot(
                    scaled, weight[deep, :], preferred_element_type=F32
                )
                left += weight.shape[1]
            return carry

        lax.fori_loop(0, width // depth, add_part, 0)
    if final:
        mean = jnp.sum(squares[...], axis=1, keepdims=True) / (shards * width)
        scale = lax.rsqrt(mean + 1e-05)
        turned = sums.shape[1] - weights[-1].shape[1]
        for left in range(0, sums.shape[1], HEAD_SIZE):
            columns = slice(left, left + HEAD_SIZE)
            head = sums[:, columns] * scale
            if left < turned:
                head = head * cosine_ref[...] + pltpu.roll(
                    head, HEAD_SIZE // 2, 1
                ) * sine_ref[...]
            out_ref[:, columns] = head.astype(BF16)


def project(final, shards, masks, pieces, gain, weights, carried, tables):
    rows = pieces[0].shape[0]
    columns = sum(weight.shape[1] for weight in weights)
    operands = [*pieces, gain, *weights, *carried, *tables]
    sums = (rows, columns), (rows, 128)
    if final:
        out_shape = [jax.ShapeDtypeStruct((rows, columns), BF16)]
        scratch = [pltpu.VMEM(shape, F32) for shape in sums]
    else:
        out_shape = [jax.ShapeDtypeStruct(shape, F32) for shape in sums]
        scratch = []
    vmem = pl.BlockSpec(memory_space=pltpu.VMEM)
    return pl.pallas_call(
        functools.partial(project_kernel, masks, bool(carried), final, shards),
        in_specs=[vmem] * len(operands),
        out_specs=[vmem] * len(out_shape),
        out_shape=out_shape,
        scratch_shapes=scratch,
        compiler_params=pltpu.CompilerParams(vmem_limit_bytes=6 * MEBI),
        name="project",
    )(*operands)


def attend_kernel(
    chips, groups, known, prior, query_width, key_width, lengths_ref, plan_ref, *refs
):
    blocks, refs = refs[: -13 if prior else -11], refs[-11:]
    attended_out, cache_out, token_ref, attended_ref, cache_ref, rows_ref, queries_ref = refs[:7]
    scores_ref, top_ref, sems, out_sems = refs[7:]
    token_ref[...] = jnp.zeros_like(token_ref)
    workers = 2 * chips
    me = lax.axis_index("req")
    chip, core = lax.div(me, 2), lax.rem(me, 2)
    slots = cache_ref.shape[1]
    spans = slots // SPAN
    total = workers * sum(sum(sizes) for _, sizes in groups)
    end = needed = jnp.int32(0)
    for other in range(workers):
        end = end + lengths_ref[other]
        needed = jnp.where(end <= prior, end, needed)
    copies = []
    for group, (bases, sizes) in enumerate(groups):
        for hop in range(chips):
            source = lax.rem(chip - hop + chips, chips) * 2
            for twin in range(2):
                owner = source + (core if twin == 0 else 1 - core)
                block = blocks[(group * chips + hop) * 2 + twin]
                first = 0
                for base, rows in zip(bases, sizes):
                    at = pl.multiple_of(base + owner * rows, ALIGN)
                    copy = pltpu.make_async_copy(
                        block.at[pl.ds(first, rows), :],
                        rows_ref.at[pl.ds(at, rows), :],
                        sems.at[len(copies)],
                    )
                    copies.append((at + rows > needed, copy))
                    first += rows
    for wanted, copy in copies:

        @pl.when(wanted)
        def _():
            copy.start()

    rows_ref[total:, :] = jnp.zeros((rows_ref.shape[0] - total, rows_ref.shape[1]), BF16)
    for wanted, copy in copies:

        @pl.when(wanted)
        def _():
            copy.wait()

    def window(row, columns):
        first = pl.multiple_of(lax.div(row, ALIGN) * ALIGN, ALIGN)
        shape = (SPAN, 2 * SPAN)
        hot = (iota(shape, 1) == iota(shape, 0) + (row - first)).astype(BF16)
        return jnp.dot(
            hot, rows_ref[pl.ds(first, 2 * SPAN), columns], preferred_element_type=F32
        )

    own_start, own_length = run_of(lengths_ref, me, workers)
    mine = (own_start + own_length <= known) & (own_start + own_length > prior)
    cache_copy = pltpu.make_async_copy(cache_ref, cache_out, out_sems.at[spans])

    @pl.when(mine)
    def _():
        def step(part, carry):
            at = pl.multiple_of(part * SPAN, SPAN)

            @pl.when(at < own_length)
            def _():
                picked = window(own_start + at, slice(query_width, query_width + 2 * key_width))
                live = at + iota(picked.shape, 0) < own_length
                picked = jnp.where(live, picked, 0.0).astype(BF16)
                cache_ref[0, pl.ds(at, SPAN), :] = picked[:, :key_width]
                cache_ref[1, pl.ds(at, SPAN), :] = picked[:, key_width:]

            @pl.when(at >= own_length)
            def _():
                empty = jnp.zeros((SPAN, key_width), BF16)
                cache_ref[0, pl.ds(at, SPAN), :] = empty
                cache_ref[1, pl.ds(at, SPAN), :] = empty

            return carry

        lax.fori_loop(0, spans, step, 0)
        cache_copy.start()

    heads, key_heads = query_width // HEAD_SIZE, key_width // HEAD_SIZE
    group = heads // key_heads
    factor = math.log2(math.e) / math.sqrt(HEAD_SIZE)
    tall = group * SPAN

    def span_of(slot):
        span = plan_ref[me * spans + slot]
        start, length = run_of(lengths_ref, lax.div(span, spans), workers)
        offset = lax.rem(span, spans) * SPAN
        dead = offset >= length
        needed = start + jnp.minimum(offset + SPAN, length)
        due = jnp.logical_not(dead) & (needed <= known) & (needed > prior)
        return start, length, offset, dead, due

    def result(slot):
        rows = pl.ds(pl.multiple_of(slot * SPAN, SPAN), SPAN)
        return pltpu.make_async_copy(
            attended_ref.at[rows, :], attended_out.at[rows, :], out_sems.at[slot]
        )

    def attend_slot(slot, carry):
        start, length, offset, dead, due = span_of(slot)
        out_rows = pl.ds(pl.multiple_of(slot * SPAN, SPAN), SPAN)

        if not prior:

            @pl.when(dead)
            def _():
                attended_ref[out_rows, :] = jnp.zeros((SPAN, query_width), BF16)
                result(slot).start()

        @pl.when(due)
        def _():
            queries = window(start + offset, slice(0, query_width)).astype(BF16)
            for head in range(heads):
                at = head % group * SPAN
                queries_ref[head // group, at : at + SPAN, :] = queries[
                    :, head * HEAD_SIZE : (head + 1) * HEAD_SIZE
                ]
            first = pl.multiple_of(lax.div(start, ALIGN) * ALIGN, ALIGN)
            shift = start - first
            reach = shift + jnp.minimum(offset + SPAN, length)
            tiles = lax.div(reach + TILE - 1, TILE)

            def columns(at, head):
                return slice(at + head * HEAD_SIZE, at + (head + 1) * HEAD_SIZE)

            def tile_rows(tile):
                return pl.ds(pl.multiple_of(first + tile * TILE, ALIGN), TILE)

            top_ref[...] = jnp.full(top_ref.shape, -1e30, F32)

            def score(tile, carry):
                key_pos = tile * TILE + iota((SPAN, TILE), 1) - shift
                query_pos = offset + iota((SPAN, TILE), 0)
                allowed = (key_pos >= 0) & (key_pos <= query_pos) & (key_pos < length)
                bias = jnp.where(allowed, 0.0, -1e30)
                bias = jnp.concatenate([bias] * group, axis=0)
                for head in range(key_heads):
                    scores = lax.dot_general(
                        queries_ref[head],
                        rows_ref[tile_rows(tile), columns(query_width, head)],
                        (((1,), (1,)), ((), ())),
                        preferred_element_type=F32,
                    )
                    scores = scores + bias
                    scores_ref[head, tile] = scores
                    top_ref[head] = jnp.maximum(top_ref[head], scores)
                return carry

            lax.fori_loop(0, tiles, score, 0)
            tops = [jnp.max(top_ref[head], axis=1, keepdims=True) for head in range(key_heads)]

            def mix(tile, carry):
                ones = jnp.ones((TILE, HEAD_SIZE), BF16)
                totals = []
                for head in range(key_heads):
                    weights = jnp.exp2((scores_ref[head, tile] - tops[head]) * factor)
                    values = rows_ref[tile_rows(tile), columns(query_width + key_width, head)]
                    values = jnp.concatenate([values, ones], axis=1)
                    totals.append(
                        carry[head]
                        + jnp.dot(weights.astype(BF16), values, preferred_element_type=F32)
                    )
                return tuple(totals)

            empty = jnp.zeros((tall, 2 * HEAD_SIZE), F32)
            mixed = lax.fori_loop(0, tiles, mix, (empty,) * key_heads)
            live = offset + iota((SPAN, HEAD_SIZE), 0) < length
            for head in range(heads):
                at = head % group * SPAN
                part = mixed[head // group][at : at + SPAN]
                part = part[:, :HEAD_SIZE] / part[:, HEAD_SIZE:]
                attended_ref[out_rows, columns(0, head)] = jnp.where(live, part, 0.0).astype(BF16)

            result(slot).start()

        return carry

    lax.fori_loop(0, spans, attend_slot, 0)

    def finish(slot, carry):
        _, _, _, dead, due = span_of(slot)

        @pl.when(due if prior else due | dead)
        def _():
            result(slot).wait()

        return carry

    lax.fori_loop(0, spans, finish, 0)

    @pl.when(mine)
    def _():
        cache_copy.wait()


def attend(chips, groups, known, prior, widths, slots, lengths, plan, blocks, outputs):
    query_width, key_width = widths
    width = query_width + 2 * key_width
    total = 2 * chips * sum(sum(sizes) for _, sizes in groups)
    copies = 2 * chips * sum(len(sizes) for _, sizes in groups)
    key_heads, tall = key_width // HEAD_SIZE, query_width // key_width * SPAN
    at = 2 + len(blocks)
    return pl.pallas_call(
        functools.partial(attend_kernel, chips, groups, known, prior, query_width, key_width),
        in_specs=[pl.BlockSpec(memory_space=pltpu.SMEM)] * 2
        + [pl.BlockSpec(memory_space=pl.ANY)] * (len(blocks) + len(outputs)),
        out_specs=[pl.BlockSpec(memory_space=pl.ANY)] * 2
        + [pl.BlockSpec(memory_space=pltpu.VMEM)],
        out_shape=[
            jax.ShapeDtypeStruct((slots, query_width), BF16),
            jax.ShapeDtypeStruct((2, slots, key_width), BF16),
            jax.ShapeDtypeStruct((8, 128), F32),
        ],
        input_output_aliases={at + index: index for index in range(len(outputs))},
        scratch_shapes=[
            pltpu.VMEM((slots, query_width), BF16),
            pltpu.VMEM((2, slots, key_width), BF16),
            pltpu.VMEM((total + TILE + ALIGN, width), BF16),
            pltpu.VMEM((key_heads, tall, HEAD_SIZE), BF16),
            pltpu.VMEM((key_heads, slots // TILE + 1, tall, TILE), F32),
            pltpu.VMEM((key_heads, tall, TILE), F32),
            pltpu.SemaphoreType.DMA((copies,)),
            pltpu.SemaphoreType.DMA((slots // SPAN + 1,)),
        ],
        compiler_params=pltpu.CompilerParams(vmem_limit_bytes=16 * MEBI),
        name="attend",
    )(lengths, plan, *blocks, *outputs)


def shift_chips(value, hop, chips):
    pairs = [(2 * x + c, 2 * ((x + hop) % chips) + c) for x in range(chips) for c in range(2)]
    return lax.ppermute(value, "req", pairs)


def swap_cores(value, chips):
    return lax.ppermute(value, "req", [(d, d ^ 1) for d in range(2 * chips)])


def local(
    chips, shards, tokens, norm_gain, w_query, key_weight, value_weight, lengths, plan
):
    workers = 2 * chips
    slots = tokens.shape[0]
    live = slots // 2
    sizes = [live * share // sum(SHARES) // ALIGN * ALIGN for share in SHARES]
    sizes[-1] = live - sum(sizes[:-1])
    bases = [workers * sum(sizes[:chunk]) for chunk in range(len(sizes))]
    weights = [w_query, key_weight, value_weight]
    gain = norm_gain.astype(F32).reshape(1, -1)
    halfway = HEAD_SIZE // 2
    frequency = np.exp(-np.arange(halfway) * 2.0 / HEAD_SIZE * math.log(500000.0))
    frequency = jnp.asarray(np.tile(frequency, 2)[None, :], F32)

    twin = swap_cores(tokens, chips)
    first = deal(chips, bases[:1], sizes[:1], lengths, [tokens], [False])
    dealt = [
        *deal(chips, bases[:1], sizes[:1], lengths, [twin], [True], first),
        *deal(chips, bases[1:], sizes[1:], lengths, [tokens, twin], [False, True]),
    ]
    homes, aways = dealt[::2], dealt[1::2]
    routes, masks = routes_of(shards)
    direct = [at + 1 for at, (source, _) in enumerate(routes) if source == 0]
    kinds = {"first": [0, *direct]}
    kinds["late"] = [piece for piece in range(len(masks)) if piece not in kinds["first"]]
    relayed = [piece for piece in direct if piece in {source for source, _ in routes}]

    groups = [([base], [rows]) for base, rows in zip(bases, sizes)]
    widths = w_query.shape[1], key_weight.shape[1]

    def add(kind, chunk, carried=()):
        pieces = [lines[chunk][piece] for piece in kinds[kind]]
        final = kind == "late"
        turned = turns[chunk] if final else ()
        offsets = [masks[piece] for piece in kinds[kind]]
        return project(final, shards, offsets, pieces, gain, weights, carried, turned)

    def from_chips(block):
        return [shift_chips(block, hop, chips) for hop in range(1, chips)]

    def all_blocks(block, arrived):
        return [leaf for piece in (block, *arrived) for leaf in (piece, swap_cores(piece, chips))]

    def start(line, group):
        for index, (source, distance) in enumerate(routes):
            if index + 1 in group:
                pairs = [(at, at ^ distance) for at in range(shards)]
                line[index + 1] = lax.ppermute(line[source], "tp", pairs)

    lines, own, sent = [], [], []
    last = len(sizes) - 1

    def finish(chunk):
        own.append(add("late", chunk, add("first", chunk))[0])
        sent.append(from_chips(own[-1]))

    def fence(chunk, block):
        passed, anchors = [], []
        if chunk:
            before = lines[chunk - 1]
            passed = [before[piece] for piece in relayed]
            anchors += [before[piece] for piece in direct if piece not in relayed]
        if chunk == 1:
            weights[0], token = load(w_query, lines[0][0])
            anchors.append(token)
        if 1 < chunk <= last:
            finish(chunk - 2)
            anchors.append(own[-1])
        if chunk > 2:
            anchors += sent[chunk - 3]
        if passed:
            passed = after([*passed, *block], anchors)
            before.update(zip(relayed, passed))
            block = passed[len(relayed) :]
        return block

    for chunk in range(last + 1):
        arrived = [shift_chips(aways[chunk][hop - 1], hop, chips) for hop in range(1, chips)]
        later = aways[chunk + 1 : chunk + 2]
        block, aways[chunk + 1 : chunk + 2] = merge(homes[chunk], arrived, later)
        lines.append({0: fence(chunk, [block])[0]})
        if chunk:
            start(lines[-2], kinds["late"])
        start(lines[-1], direct)
        if chunk == 1:
            turns = angles(groups, lengths, frequency, lines[1][0])
    fence(last + 1, [])
    start(lines[-1], kinds["late"])
    for chunk in (last - 1, last):
        finish(chunk)
    blocks = []
    for at in range(last):
        blocks += all_blocks(own[at], after(sent[at], own[at + 1 : at + 2]))
    sent.append(from_chips(own[last]))
    known = workers * sum(sizes[:-1])
    common = widths, slots, lengths, plan
    *outputs, token = attend(chips, groups[:-1], known, 0, *common, blocks, ())
    blocks += all_blocks(own[last], after(sent[last], [token]))
    return tuple(attend(chips, groups, workers * live, known, *common, blocks, outputs)[:2])


def solution(mesh):
    placed = (
        P(("groups", "req"), "tp"),
        P(),
        P(None, "tp"),
        P(None, "tp"),
        P(None, "tp"),
        P("groups"),
        P("groups"),
    )
    return jax.shard_map(
        functools.partial(local, mesh.shape["req"] // 2, mesh.shape["tp"]),
        mesh=mesh,
        in_specs=placed,
        out_specs=(P(("groups", "req"), "tp"), P(None, ("groups", "req"), "tp")),
        check_vma=False,
    )
```

```python
import functools
import math

import jax
import jax.numpy as jnp
import numpy as np
from jax import lax
from jax.experimental import pallas as pl
from jax.experimental.pallas import tpu as pltpu
from jax.sharding import PartitionSpec as P

HEAD_SIZE = 128
SPAN = 128
ALIGN = 16
TILE = 2 * SPAN
SHARES = (3, 5, 5, 3)
DEPTH = 1024
MEBI = 1024 * 1024
F32, BF16 = jnp.float32, jnp.bfloat16


def run_of(lengths_ref, request, count):
    start = jnp.int32(0)
    length = jnp.int32(0)
    for other in range(count):
        amount = lengths_ref[other]
        start = start + jnp.where(other < request, amount, 0)
        length = jnp.where(other == request, amount, length)
    return start, length


def iota(shape, dimension):
    return lax.broadcasted_iota(jnp.int32, shape, dimension)


def deal_kernel(chips, bases, sizes, twins, lengths_ref, *refs):
    me = lax.axis_index("req")
    chip, core = lax.div(me, 2), lax.rem(me, 2)
    sources, refs = refs[: len(twins)], refs[len(twins) :]
    count = 2 * len(sizes)
    priors, out_refs = refs[:-count], refs[-count:]
    requests = [me + 1 - 2 * core if twin else me for twin in twins]
    runs = [run_of(lengths_ref, request, 2 * chips) for request in requests]
    slots = sources[0].shape[0]
    total = None
    for (start, length), source in zip(runs, sources):
        hots = []
        for base, rows in zip(bases, sizes):
            for hop in range(chips):
                target = lax.rem(chip + hop, chips) * 2 + core
                number = base + target * rows + iota((rows, slots), 0)
                slot = iota((rows, slots), 1)
                hot = (number - start == slot) & (slot < length)
                hots.append(hot.astype(F32).astype(BF16))
        hot = jnp.concatenate(hots, axis=0) if len(hots) > 1 else hots[0]
        part = jnp.dot(hot, source[...], preferred_element_type=F32)
        total = part if total is None else total + part
    total = total.astype(BF16)
    at = 0
    for chunk, rows in enumerate(sizes):
        for hop in range(chips):
            picked = total[at : at + rows]
            at += rows
            if priors:
                prior = priors[2 * chunk + 1][hop - 1] if hop else priors[2 * chunk][...]
                picked = picked + prior
            if hop:
                out_refs[2 * chunk + 1][hop - 1] = picked
            else:
                out_refs[2 * chunk][...] = picked


def deal(chips, bases, sizes, lengths, sources, twins, priors=()):
    slots, width = sources[0].shape
    block = min(1024, width)
    out_specs, out_shape = [], []
    for rows in sizes:
        out_specs += [
            pl.BlockSpec((rows, block), lambda i: (0, i)),
            pl.BlockSpec((chips - 1, rows, block), lambda i: (0, 0, i)),
        ]
        out_shape += [
            jax.ShapeDtypeStruct((rows, width), BF16),
            jax.ShapeDtypeStruct((chips - 1, rows, width), BF16),
        ]
    return pl.pallas_call(
        functools.partial(deal_kernel, chips, bases, sizes, twins),
        grid=(width // block,),
        in_specs=[pl.BlockSpec(memory_space=pltpu.SMEM)]
        + [pl.BlockSpec((slots, block), lambda i: (0, i)) for _ in sources]
        + (out_specs if priors else []),
        out_specs=out_specs,
        out_shape=out_shape,
        compiler_params=pltpu.CompilerParams(vmem_limit_bytes=10 * MEBI),
        name="deal",
    )(lengths, *sources, *priors)


def merge_kernel(count, passed, home_ref, *refs):
    total = home_ref[...]
    for ref in refs[:count]:
        total = total + ref[...]
    refs[len(refs) - 1 - passed][...] = total


def merge(home, arrived, later):
    count = len(arrived)
    vmem, anywhere = pl.BlockSpec(memory_space=pltpu.VMEM), pl.BlockSpec(memory_space=pl.ANY)
    block, *later = pl.pallas_call(
        functools.partial(merge_kernel, count, len(later)),
        in_specs=[vmem] * (count + 1) + [anywhere] * len(later),
        out_specs=[vmem] + [anywhere] * len(later),
        out_shape=[jax.ShapeDtypeStruct(leaf.shape, leaf.dtype) for leaf in (home, *later)],
        input_output_aliases={count + 1 + at: 1 + at for at in range(len(later))},
        compiler_params=pltpu.CompilerParams(vmem_limit_bytes=4 * MEBI),
        name="merge",
    )(home, *arrived, *later)
    return block, later


def after(arrays, anchors):
    def kernel(*refs):
        pass

    anywhere = pl.BlockSpec(memory_space=pl.ANY)
    return pl.pallas_call(
        kernel,
        in_specs=[anywhere] * (len(arrays) + len(anchors)),
        out_specs=[anywhere] * len(arrays),
        out_shape=[jax.ShapeDtypeStruct(leaf.shape, leaf.dtype) for leaf in arrays],
        input_output_aliases={at: at for at in range(len(arrays))},
        compiler_params=pltpu.CompilerParams(vmem_limit_bytes=MEBI),
        name="after",
    )(*arrays, *anchors)


def routes_of(shards):
    routes, masks, distance = [], [0], shards // 2
    while distance:
        for source in range(len(masks)):
            routes.append((source, distance))
            masks.append(masks[source] ^ distance)
        distance //= 2
    return routes, masks


def angles_kernel(groups, members, lengths_ref, frequency_ref, anchor_ref, *out_refs):
    me = lax.axis_index("req")
    for group, (bases, sizes) in enumerate(groups):
        first = 0
        for base, rows in zip(bases, sizes):
            number = base + me * rows + iota((rows, HEAD_SIZE), 0)
            start = jnp.zeros((rows, HEAD_SIZE), jnp.int32)
            before = jnp.int32(0)
            for other in range(members):
                before = before + lengths_ref[other]
                start = jnp.where(number >= before, before, start)
            angle = (number - start).astype(F32) * frequency_ref[...]
            sine = jnp.sin(angle)
            lower = iota((rows, HEAD_SIZE), 1) < HEAD_SIZE // 2
            out_refs[2 * group][first : first + rows, :] = jnp.cos(angle)
            out_refs[2 * group + 1][first : first + rows, :] = jnp.where(lower, -sine, sine)
            first += rows


def angles(groups, lengths, frequency, anchor):
    shapes = [
        jax.ShapeDtypeStruct((sum(sizes), HEAD_SIZE), F32) for _, sizes in groups for _ in range(2)
    ]
    vmem = pl.BlockSpec(memory_space=pltpu.VMEM)
    tables = pl.pallas_call(
        functools.partial(angles_kernel, groups, lengths.shape[0]),
        in_specs=[
            pl.BlockSpec(memory_space=pltpu.SMEM),
            vmem,
            pl.BlockSpec(memory_space=pl.ANY),
        ],
        out_specs=[vmem] * len(shapes),
        out_shape=shapes,
        compiler_params=pltpu.CompilerParams(vmem_limit_bytes=4 * MEBI),
        name="angles",
    )(lengths, frequency, anchor)
    return [tables[at : at + 2] for at in range(0, len(tables), 2)]


def load(weight, anchor):
    parts = 8
    depth = weight.shape[0] // parts

    def kernel(weight_ref, anchor_ref, out_ref, token_ref, sems):
        copies = [
            pltpu.make_async_copy(
                weight_ref.at[pl.ds(part * depth, depth), :],
                out_ref.at[pl.ds(part * depth, depth), :],
                sems.at[part],
            )
            for part in range(parts)
        ]
        for copy in copies:
            copy.start()
        token_ref[...] = jnp.zeros_like(token_ref)
        for copy in copies:
            copy.wait()

    vmem, anywhere = pl.BlockSpec(memory_space=pltpu.VMEM), pl.BlockSpec(memory_space=pl.ANY)
    return pl.pallas_call(
        kernel,
        in_specs=[anywhere, anywhere],
        out_specs=[vmem, vmem],
        out_shape=[
            jax.ShapeDtypeStruct(weight.shape, weight.dtype),
            jax.ShapeDtypeStruct((8, 128), F32),
        ],
        scratch_shapes=[pltpu.SemaphoreType.DMA((parts,))],
        compiler_params=pltpu.CompilerParams(vmem_limit_bytes=2 * MEBI),
        name="load",
    )(pltpu.with_memory_space_constraint(weight, pltpu.HBM), anchor)


def project_kernel(masks, carries, final, shards, *refs):
    pieces, refs = refs[: len(masks)], refs[len(masks) :]
    (gain_ref, *weights), refs = refs[:4], refs[4:]
    if carries:
        sums_in, squares_in, *refs = refs
    if final:
        cosine_ref, sine_ref, out_ref, *refs = refs
    sums, squares = refs
    width = pieces[0].shape[1]
    depth = min(DEPTH, width)
    sums[...] = sums_in[...] if carries else jnp.zeros_like(sums)
    squares[...] = squares_in[...] if carries else jnp.zeros_like(squares)
    for piece, mask in zip(pieces, masks):
        shard = lax.bitwise_xor(lax.axis_index("tp"), jnp.int32(mask))

        def add_part(part, carry):
            at = pl.multiple_of(part * depth, depth)
            deep = pl.ds(pl.multiple_of(shard * width + at, depth), depth)
            wide = piece[:, pl.ds(at, depth)].astype(F32)
            square = wide * wide
            lanes = square[:, :128]
            for left in range(128, depth, 128):
                lanes = lanes + square[:, left : left + 128]
            squares[...] += lanes
            scaled = (wide * gain_ref[:, deep]).astype(BF16)
            left = 0
            for weight in weights:
                columns = slice(left, left + weight.shape[1])
                sums[:, columns] += jnp.dot(
                    scaled, weight[deep, :], preferred_element_type=F32
                )
                left += weight.shape[1]
            return carry

        lax.fori_loop(0, width // depth, add_part, 0)
    if final:
        mean = jnp.sum(squares[...], axis=1, keepdims=True) / (shards * width)
        scale = lax.rsqrt(mean + 1e-05)
        turned = sums.shape[1] - weights[-1].shape[1]
        for left in range(0, sums.shape[1], HEAD_SIZE):
            columns = slice(left, left + HEAD_SIZE)
            head = sums[:, columns] * scale
            if left < turned:
                head = head * cosine_ref[...] + pltpu.roll(
                    head, HEAD_SIZE // 2, 1
                ) * sine_ref[...]
            out_ref[:, columns] = head.astype(BF16)


def project(final, shards, masks, pieces, gain, weights, carried, tables):
    rows = pieces[0].shape[0]
    columns = sum(weight.shape[1] for weight in weights)
    operands = [*pieces, gain, *weights, *carried, *tables]
    sums = (rows, columns), (rows, 128)
    if final:
        out_shape = [jax.ShapeDtypeStruct((rows, columns), BF16)]
        scratch = [pltpu.VMEM(shape, F32) for shape in sums]
    else:
        out_shape = [jax.ShapeDtypeStruct(shape, F32) for shape in sums]
        scratch = []
    vmem = pl.BlockSpec(memory_space=pltpu.VMEM)
    return pl.pallas_call(
        functools.partial(project_kernel, masks, bool(carried), final, shards),
        in_specs=[vmem] * len(operands),
        out_specs=[vmem] * len(out_shape),
        out_shape=out_shape,
        scratch_shapes=scratch,
        compiler_params=pltpu.CompilerParams(vmem_limit_bytes=6 * MEBI),
        name="project",
    )(*operands)


def attend_kernel(
    chips, groups, known, prior, query_width, key_width, lengths_ref, plan_ref, *refs
):
    blocks, refs = refs[: -13 if prior else -11], refs[-11:]
    attended_out, cache_out, token_ref, attended_ref, cache_ref, rows_ref, queries_ref = refs[:7]
    scores_ref, top_ref, sems, out_sems = refs[7:]
    token_ref[...] = jnp.zeros_like(token_ref)
    workers = 2 * chips
    me = lax.axis_index("req")
    chip, core = lax.div(me, 2), lax.rem(me, 2)
    slots = cache_ref.shape[1]
    spans = slots // SPAN
    total = workers * sum(sum(sizes) for _, sizes in groups)
    end = needed = jnp.int32(0)
    for other in range(workers):
        end = end + lengths_ref[other]
        needed = jnp.where(end <= prior, end, needed)
    copies = []
    for group, (bases, sizes) in enumerate(groups):
        for hop in range(chips):
            source = lax.rem(chip - hop + chips, chips) * 2
            for twin in range(2):
                owner = source + (core if twin == 0 else 1 - core)
                block = blocks[(group * chips + hop) * 2 + twin]
                first = 0
                for base, rows in zip(bases, sizes):
                    at = pl.multiple_of(base + owner * rows, ALIGN)
                    copy = pltpu.make_async_copy(
                        block.at[pl.ds(first, rows), :],
                        rows_ref.at[pl.ds(at, rows), :],
                        sems.at[len(copies)],
                    )
                    copies.append((at + rows > needed, copy))
                    first += rows
    for wanted, copy in copies:

        @pl.when(wanted)
        def _():
            copy.start()

    rows_ref[total:, :] = jnp.zeros((rows_ref.shape[0] - total, rows_ref.shape[1]), BF16)
    for wanted, copy in copies:

        @pl.when(wanted)
        def _():
            copy.wait()

    def window(row, columns):
        first = pl.multiple_of(lax.div(row, ALIGN) * ALIGN, ALIGN)
        shape = (SPAN, 2 * SPAN)
        hot = (iota(shape, 1) == iota(shape, 0) + (row - first)).astype(BF16)
        return jnp.dot(
            hot, rows_ref[pl.ds(first, 2 * SPAN), columns], preferred_element_type=F32
        )

    own_start, own_length = run_of(lengths_ref, me, workers)
    mine = (own_start + own_length <= known) & (own_start + own_length > prior)
    cache_copy = pltpu.make_async_copy(cache_ref, cache_out, out_sems.at[spans])

    @pl.when(mine)
    def _():
        def step(part, carry):
            at = pl.multiple_of(part * SPAN, SPAN)

            @pl.when(at < own_length)
            def _():
                picked = window(own_start + at, slice(query_width, query_width + 2 * key_width))
                live = at + iota(picked.shape, 0) < own_length
                picked = jnp.where(live, picked, 0.0).astype(BF16)
                cache_ref[0, pl.ds(at, SPAN), :] = picked[:, :key_width]
                cache_ref[1, pl.ds(at, SPAN), :] = picked[:, key_width:]

            @pl.when(at >= own_length)
            def _():
                empty = jnp.zeros((SPAN, key_width), BF16)
                cache_ref[0, pl.ds(at, SPAN), :] = empty
                cache_ref[1, pl.ds(at, SPAN), :] = empty

            return carry

        lax.fori_loop(0, spans, step, 0)
        cache_copy.start()

    heads, key_heads = query_width // HEAD_SIZE, key_width // HEAD_SIZE
    group = heads // key_heads
    factor = math.log2(math.e) / math.sqrt(HEAD_SIZE)
    tall = group * SPAN

    def span_of(slot):
        span = plan_ref[me * spans + slot]
        start, length = run_of(lengths_ref, lax.div(span, spans), workers)
        offset = lax.rem(span, spans) * SPAN
        dead = offset >= length
        needed = start + jnp.minimum(offset + SPAN, length)
        due = jnp.logical_not(dead) & (needed <= known) & (needed > prior)
        return start, length, offset, dead, due

    def result(slot):
        rows = pl.ds(pl.multiple_of(slot * SPAN, SPAN), SPAN)
        return pltpu.make_async_copy(
            attended_ref.at[rows, :], attended_out.at[rows, :], out_sems.at[slot]
        )

    def attend_slot(slot, carry):
        start, length, offset, dead, due = span_of(slot)
        out_rows = pl.ds(pl.multiple_of(slot * SPAN, SPAN), SPAN)

        if not prior:

            @pl.when(dead)
            def _():
                attended_ref[out_rows, :] = jnp.zeros((SPAN, query_width), BF16)
                result(slot).start()

        @pl.when(due)
        def _():
            queries = window(start + offset, slice(0, query_width)).astype(BF16)
            for head in range(heads):
                at = head % group * SPAN
                queries_ref[head // group, at : at + SPAN, :] = queries[
                    :, head * HEAD_SIZE : (head + 1) * HEAD_SIZE
                ]
            first = pl.multiple_of(lax.div(start, ALIGN) * ALIGN, ALIGN)
            shift = start - first
            reach = shift + jnp.minimum(offset + SPAN, length)
            tiles = lax.div(reach + TILE - 1, TILE)

            def columns(at, head):
                return slice(at + head * HEAD_SIZE, at + (head + 1) * HEAD_SIZE)

            def tile_rows(tile):
                return pl.ds(pl.multiple_of(first + tile * TILE, ALIGN), TILE)

            top_ref[...] = jnp.full(top_ref.shape, -1e30, F32)

            def score(tile, carry):
                key_pos = tile * TILE + iota((SPAN, TILE), 1) - shift
                query_pos = offset + iota((SPAN, TILE), 0)
                allowed = (key_pos >= 0) & (key_pos <= query_pos) & (key_pos < length)
                bias = jnp.where(allowed, 0.0, -1e30)
                bias = jnp.concatenate([bias] * group, axis=0)
                for head in range(key_heads):
                    scores = lax.dot_general(
                        queries_ref[head],
                        rows_ref[tile_rows(tile), columns(query_width, head)],
                        (((1,), (1,)), ((), ())),
                        preferred_element_type=F32,
                    )
                    scores = scores + bias
                    scores_ref[head, tile] = scores
                    top_ref[head] = jnp.maximum(top_ref[head], scores)
                return carry

            lax.fori_loop(0, tiles, score, 0)
            tops = [jnp.max(top_ref[head], axis=1, keepdims=True) for head in range(key_heads)]

            def mix(tile, carry):
                ones = jnp.ones((TILE, HEAD_SIZE), BF16)
                totals = []
                for head in range(key_heads):
                    weights = jnp.exp2((scores_ref[head, tile] - tops[head]) * factor)
                    values = rows_ref[tile_rows(tile), columns(query_width + key_width, head)]
                    values = jnp.concatenate([values, ones], axis=1)
                    totals.append(
                        carry[head]
                        + jnp.dot(weights.astype(BF16), values, preferred_element_type=F32)
                    )
                return tuple(totals)

            empty = jnp.zeros((tall, 2 * HEAD_SIZE), F32)
            mixed = lax.fori_loop(0, tiles, mix, (empty,) * key_heads)
            live = offset + iota((SPAN, HEAD_SIZE), 0) < length
            for head in range(heads):
                at = head % group * SPAN
                part = mixed[head // group][at : at + SPAN]
                part = part[:, :HEAD_SIZE] / part[:, HEAD_SIZE:]
                attended_ref[out_rows, columns(0, head)] = jnp.where(live, part, 0.0).astype(BF16)

            result(slot).start()

        return carry

    lax.fori_loop(0, spans, attend_slot, 0)

    def finish(slot, carry):
        _, _, _, dead, due = span_of(slot)

        @pl.when(due if prior else due | dead)
        def _():
            result(slot).wait()

        return carry

    lax.fori_loop(0, spans, finish, 0)

    @pl.when(mine)
    def _():
        cache_copy.wait()


def attend(chips, groups, known, prior, widths, slots, lengths, plan, blocks, outputs):
    query_width, key_width = widths
    width = query_width + 2 * key_width
    total = 2 * chips * sum(sum(sizes) for _, sizes in groups)
    copies = 2 * chips * sum(len(sizes) for _, sizes in groups)
    key_heads, tall = key_width // HEAD_SIZE, query_width // key_width * SPAN
    at = 2 + len(blocks)
    return pl.pallas_call(
        functools.partial(attend_kernel, chips, groups, known, prior, query_width, key_width),
        in_specs=[pl.BlockSpec(memory_space=pltpu.SMEM)] * 2
        + [pl.BlockSpec(memory_space=pl.ANY)] * (len(blocks) + len(outputs)),
        out_specs=[pl.BlockSpec(memory_space=pl.ANY)] * 2
        + [pl.BlockSpec(memory_space=pltpu.VMEM)],
        out_shape=[
            jax.ShapeDtypeStruct((slots, query_width), BF16),
            jax.ShapeDtypeStruct((2, slots, key_width), BF16),
            jax.ShapeDtypeStruct((8, 128), F32),
        ],
        input_output_aliases={at + index: index for index in range(len(outputs))},
        scratch_shapes=[
            pltpu.VMEM((slots, query_width), BF16),
            pltpu.VMEM((2, slots, key_width), BF16),
            pltpu.VMEM((total + TILE + ALIGN, width), BF16),
            pltpu.VMEM((key_heads, tall, HEAD_SIZE), BF16),
            pltpu.VMEM((key_heads, slots // TILE + 1, tall, TILE), F32),
            pltpu.VMEM((key_heads, tall, TILE), F32),
            pltpu.SemaphoreType.DMA((copies,)),
            pltpu.SemaphoreType.DMA((slots // SPAN + 1,)),
        ],
        compiler_params=pltpu.CompilerParams(vmem_limit_bytes=16 * MEBI),
        name="attend",
    )(lengths, plan, *blocks, *outputs)


def shift_chips(value, hop, chips):
    pairs = [(2 * x + c, 2 * ((x + hop) % chips) + c) for x in range(chips) for c in range(2)]
    return lax.ppermute(value, "req", pairs)


def swap_cores(value, chips):
    return lax.ppermute(value, "req", [(d, d ^ 1) for d in range(2 * chips)])


def local(
    chips, shards, tokens, norm_gain, w_query, key_weight, value_weight, lengths, plan
):
    workers = 2 * chips
    slots = tokens.shape[0]
    live = slots // 2
    sizes = [live * share // sum(SHARES) // ALIGN * ALIGN for share in SHARES]
    sizes[-1] = live - sum(sizes[:-1])
    bases = [workers * sum(sizes[:chunk]) for chunk in range(len(sizes))]
    weights = [w_query, key_weight, value_weight]
    gain = norm_gain.astype(F32).reshape(1, -1)
    halfway = HEAD_SIZE // 2
    frequency = np.exp(-np.arange(halfway) * 2.0 / HEAD_SIZE * math.log(500000.0))
    frequency = jnp.asarray(np.tile(frequency, 2)[None, :], F32)

    twin = swap_cores(tokens, chips)
    first = deal(chips, bases[:1], sizes[:1], lengths, [tokens], [False])
    dealt = [
        *deal(chips, bases[:1], sizes[:1], lengths, [twin], [True], first),
        *deal(chips, bases[1:], sizes[1:], lengths, [tokens, twin], [False, True]),
    ]
    homes, aways = dealt[::2], dealt[1::2]
    routes, masks = routes_of(shards)
    direct = [at + 1 for at, (source, _) in enumerate(routes) if source == 0]
    kinds = {"first": [0, *direct]}
    kinds["late"] = [piece for piece in range(len(masks)) if piece not in kinds["first"]]
    relayed = [piece for piece in direct if piece in {source for source, _ in routes}]

    groups = [([base], [rows]) for base, rows in zip(bases, sizes)]
    widths = w_query.shape[1], key_weight.shape[1]

    def add(kind, chunk, carried=()):
        pieces = [lines[chunk][piece] for piece in kinds[kind]]
        final = kind == "late"
        turned = turns[chunk] if final else ()
        offsets = [masks[piece] for piece in kinds[kind]]
        return project(final, shards, offsets, pieces, gain, weights, carried, turned)

    def from_chips(block):
        return [shift_chips(block, hop, chips) for hop in range(1, chips)]

    def all_blocks(block, arrived):
        return [leaf for piece in (block, *arrived) for leaf in (piece, swap_cores(piece, chips))]

    def start(line, group):
        for index, (source, distance) in enumerate(routes):
            if index + 1 in group:
                pairs = [(at, at ^ distance) for at in range(shards)]
                line[index + 1] = lax.ppermute(line[source], "tp", pairs)

    lines, own, sent, blocks = [], [], [], []
    last = len(sizes) - 1

    def finish(chunk):
        own.append(add("late", chunk, add("first", chunk))[0])
        sent.append(from_chips(own[-1]))

    def fence(chunk, block, *anchors):
        passed, anchors = [], list(anchors)
        if chunk:
            before = lines[chunk - 1]
            passed = [before[piece] for piece in relayed]
            anchors += [before[piece] for piece in direct if piece not in relayed]
        if chunk == 1:
            weights[0], token = load(w_query, lines[0][0])
            anchors.append(token)
        if 1 < chunk <= last:
            finish(chunk - 2)
            anchors.append(own[-1])
        if 2 < chunk <= last:
            arrived = after(sent[chunk - 3], own[-1:])
            blocks.extend(all_blocks(own[chunk - 3], arrived))
            anchors += blocks[-2 * chips :]
        if passed:
            passed = after([*passed, *block], anchors)
            before.update(zip(relayed, passed))
            block = passed[len(relayed) :]
        return block

    for chunk in range(last + 1):
        arrived = [shift_chips(aways[chunk][hop - 1], hop, chips) for hop in range(1, chips)]
        later = aways[chunk + 1 : chunk + 2]
        block, aways[chunk + 1 : chunk + 2] = merge(homes[chunk], arrived, later)
        lines.append({0: fence(chunk, [block])[0]})
        if chunk:
            start(lines[-2], kinds["late"])
        start(lines[-1], direct)
        if chunk == 1:
            turns = angles(groups, lengths, frequency, lines[1][0])
    common = widths, slots, lengths, plan

    def attended(at, prior, blocks, outputs):
        known = workers * sum(sizes[: at + 1])
        return attend(chips, groups[: at + 1], known, prior, *common, blocks, outputs)

    sums = list(add("first", last - 1))
    for at in range(last - 2, last - 1):
        blocks += all_blocks(own[at], after(sent[at], own[at + 1 : at + 2] or [sums[1]]))
    *outputs, token = attended(last - 2, 0, blocks, ())
    sums[1:] = after(sums[1:], [token])
    fence(last + 1, [])
    start(lines[-1], kinds["late"])
    own.append(add("late", last - 1, sums)[0])
    sent.append(from_chips(own[-1]))
    finish(last)
    blocks += all_blocks(own[last - 1], after(sent[last - 1], own[last:]))
    prior = workers * sum(sizes[:-2])
    *outputs, token = attended(last - 1, prior, blocks, outputs)
    blocks += all_blocks(own[last], after(sent[last], [token]))
    prior = workers * sum(sizes[:-1])
    return tuple(attended(last, prior, blocks, outputs)[:2])


def solution(mesh):
    placed = (
        P(("groups", "req"), "tp"),
        P(),
        P(None, "tp"),
        P(None, "tp"),
        P(None, "tp"),
        P("groups"),
        P("groups"),
    )
    return jax.shard_map(
        functools.partial(local, mesh.shape["req"] // 2, mesh.shape["tp"]),
        mesh=mesh,
        in_specs=placed,
        out_specs=(P(("groups", "req"), "tp"), P(None, ("groups", "req"), "tp")),
        check_vma=False,
    )
```

```python
import functools
import math

import jax
import jax.numpy as jnp
import numpy as np
from jax import lax
from jax.experimental import pallas as pl
from jax.experimental.pallas import tpu as pltpu
from jax.sharding import PartitionSpec as P

HEAD_SIZE = 128
SPAN = 128
ALIGN = 16
TILE = 2 * SPAN
SHARES = (3, 5, 5, 3)
DEPTH = 1024
MEBI = 1024 * 1024
F32, BF16 = jnp.float32, jnp.bfloat16


def run_of(lengths_ref, request, count):
    start = jnp.int32(0)
    length = jnp.int32(0)
    for other in range(count):
        amount = lengths_ref[other]
        start = start + jnp.where(other < request, amount, 0)
        length = jnp.where(other == request, amount, length)
    return start, length


def iota(shape, dimension):
    return lax.broadcasted_iota(jnp.int32, shape, dimension)


def deal_kernel(chips, bases, sizes, twins, lengths_ref, *refs):
    me = lax.axis_index("req")
    chip, core = lax.div(me, 2), lax.rem(me, 2)
    sources, refs = refs[: len(twins)], refs[len(twins) :]
    count = 2 * len(sizes)
    priors, out_refs = refs[:-count], refs[-count:]
    requests = [me + 1 - 2 * core if twin else me for twin in twins]
    runs = [run_of(lengths_ref, request, 2 * chips) for request in requests]
    slots = sources[0].shape[0]
    total = None
    for (start, length), source in zip(runs, sources):
        hots = []
        for base, rows in zip(bases, sizes):
            for hop in range(chips):
                target = lax.rem(chip + hop, chips) * 2 + core
                number = base + target * rows + iota((rows, slots), 0)
                slot = iota((rows, slots), 1)
                hot = (number - start == slot) & (slot < length)
                hots.append(hot.astype(F32).astype(BF16))
        hot = jnp.concatenate(hots, axis=0) if len(hots) > 1 else hots[0]
        part = jnp.dot(hot, source[...], preferred_element_type=F32)
        total = part if total is None else total + part
    total = total.astype(BF16)
    at = 0
    for chunk, rows in enumerate(sizes):
        for hop in range(chips):
            picked = total[at : at + rows]
            at += rows
            if priors:
                prior = priors[2 * chunk + 1][hop - 1] if hop else priors[2 * chunk][...]
                picked = picked + prior
            if hop:
                out_refs[2 * chunk + 1][hop - 1] = picked
            else:
                out_refs[2 * chunk][...] = picked


def deal(chips, bases, sizes, lengths, sources, twins, priors=()):
    slots, width = sources[0].shape
    block = min(1024, width)
    out_specs, out_shape = [], []
    for rows in sizes:
        out_specs += [
            pl.BlockSpec((rows, block), lambda i: (0, i)),
            pl.BlockSpec((chips - 1, rows, block), lambda i: (0, 0, i)),
        ]
        out_shape += [
            jax.ShapeDtypeStruct((rows, width), BF16),
            jax.ShapeDtypeStruct((chips - 1, rows, width), BF16),
        ]
    return pl.pallas_call(
        functools.partial(deal_kernel, chips, bases, sizes, twins),
        grid=(width // block,),
        in_specs=[pl.BlockSpec(memory_space=pltpu.SMEM)]
        + [pl.BlockSpec((slots, block), lambda i: (0, i)) for _ in sources]
        + (out_specs if priors else []),
        out_specs=out_specs,
        out_shape=out_shape,
        compiler_params=pltpu.CompilerParams(vmem_limit_bytes=10 * MEBI),
        name="deal",
    )(lengths, *sources, *priors)


def merge_kernel(count, passed, home_ref, *refs):
    total = home_ref[...]
    for ref in refs[:count]:
        total = total + ref[...]
    refs[len(refs) - 1 - passed][...] = total


def merge(home, arrived, later):
    count = len(arrived)
    vmem, anywhere = pl.BlockSpec(memory_space=pltpu.VMEM), pl.BlockSpec(memory_space=pl.ANY)
    block, *later = pl.pallas_call(
        functools.partial(merge_kernel, count, len(later)),
        in_specs=[vmem] * (count + 1) + [anywhere] * len(later),
        out_specs=[vmem] + [anywhere] * len(later),
        out_shape=[jax.ShapeDtypeStruct(leaf.shape, leaf.dtype) for leaf in (home, *later)],
        input_output_aliases={count + 1 + at: 1 + at for at in range(len(later))},
        compiler_params=pltpu.CompilerParams(vmem_limit_bytes=4 * MEBI),
        name="merge",
    )(home, *arrived, *later)
    return block, later


def after(arrays, anchors):
    def kernel(*refs):
        pass

    anywhere = pl.BlockSpec(memory_space=pl.ANY)
    return pl.pallas_call(
        kernel,
        in_specs=[anywhere] * (len(arrays) + len(anchors)),
        out_specs=[anywhere] * len(arrays),
        out_shape=[jax.ShapeDtypeStruct(leaf.shape, leaf.dtype) for leaf in arrays],
        input_output_aliases={at: at for at in range(len(arrays))},
        compiler_params=pltpu.CompilerParams(vmem_limit_bytes=MEBI),
        name="after",
    )(*arrays, *anchors)


def routes_of(shards):
    routes, masks, distance = [], [0], shards // 2
    while distance:
        for source in range(len(masks)):
            routes.append((source, distance))
            masks.append(masks[source] ^ distance)
        distance //= 2
    return routes, masks


def angles_kernel(groups, members, lengths_ref, frequency_ref, anchor_ref, *out_refs):
    me = lax.axis_index("req")
    for group, (bases, sizes) in enumerate(groups):
        first = 0
        for base, rows in zip(bases, sizes):
            number = base + me * rows + iota((rows, HEAD_SIZE), 0)
            start = jnp.zeros((rows, HEAD_SIZE), jnp.int32)
            before = jnp.int32(0)
            for other in range(members):
                before = before + lengths_ref[other]
                start = jnp.where(number >= before, before, start)
            angle = (number - start).astype(F32) * frequency_ref[...]
            sine = jnp.sin(angle)
            lower = iota((rows, HEAD_SIZE), 1) < HEAD_SIZE // 2
            out_refs[2 * group][first : first + rows, :] = jnp.cos(angle)
            out_refs[2 * group + 1][first : first + rows, :] = jnp.where(lower, -sine, sine)
            first += rows


def angles(groups, lengths, frequency, anchor):
    shapes = [
        jax.ShapeDtypeStruct((sum(sizes), HEAD_SIZE), F32) for _, sizes in groups for _ in range(2)
    ]
    vmem = pl.BlockSpec(memory_space=pltpu.VMEM)
    tables = pl.pallas_call(
        functools.partial(angles_kernel, groups, lengths.shape[0]),
        in_specs=[
            pl.BlockSpec(memory_space=pltpu.SMEM),
            vmem,
            pl.BlockSpec(memory_space=pl.ANY),
        ],
        out_specs=[vmem] * len(shapes),
        out_shape=shapes,
        compiler_params=pltpu.CompilerParams(vmem_limit_bytes=4 * MEBI),
        name="angles",
    )(lengths, frequency, anchor)
    return [tables[at : at + 2] for at in range(0, len(tables), 2)]


def load(weight, anchor):
    parts = 8
    depth = weight.shape[0] // parts

    def kernel(weight_ref, anchor_ref, out_ref, token_ref, sems):
        copies = [
            pltpu.make_async_copy(
                weight_ref.at[pl.ds(part * depth, depth), :],
                out_ref.at[pl.ds(part * depth, depth), :],
                sems.at[part],
            )
            for part in range(parts)
        ]
        for copy in copies:
            copy.start()
        token_ref[...] = jnp.zeros_like(token_ref)
        for copy in copies:
            copy.wait()

    vmem, anywhere = pl.BlockSpec(memory_space=pltpu.VMEM), pl.BlockSpec(memory_space=pl.ANY)
    return pl.pallas_call(
        kernel,
        in_specs=[anywhere, anywhere],
        out_specs=[vmem, vmem],
        out_shape=[
            jax.ShapeDtypeStruct(weight.shape, weight.dtype),
            jax.ShapeDtypeStruct((8, 128), F32),
        ],
        scratch_shapes=[pltpu.SemaphoreType.DMA((parts,))],
        compiler_params=pltpu.CompilerParams(vmem_limit_bytes=2 * MEBI),
        name="load",
    )(pltpu.with_memory_space_constraint(weight, pltpu.HBM), anchor)


def project_kernel(masks, carries, final, shards, *refs):
    pieces, refs = refs[: len(masks)], refs[len(masks) :]
    (gain_ref, *weights), refs = refs[:4], refs[4:]
    if carries:
        sums_in, squares_in, *refs = refs
    if final:
        cosine_ref, sine_ref, out_ref, *refs = refs
    sums, squares = refs
    width = pieces[0].shape[1]
    depth = min(DEPTH, width)
    sums[...] = sums_in[...] if carries else jnp.zeros_like(sums)
    squares[...] = squares_in[...] if carries else jnp.zeros_like(squares)
    for piece, mask in zip(pieces, masks):
        shard = lax.bitwise_xor(lax.axis_index("tp"), jnp.int32(mask))

        def add_part(part, carry):
            at = pl.multiple_of(part * depth, depth)
            deep = pl.ds(pl.multiple_of(shard * width + at, depth), depth)
            wide = piece[:, pl.ds(at, depth)].astype(F32)
            square = wide * wide
            lanes = square[:, :128]
            for left in range(128, depth, 128):
                lanes = lanes + square[:, left : left + 128]
            squares[...] += lanes
            scaled = (wide * gain_ref[:, deep]).astype(BF16)
            left = 0
            for weight in weights:
                columns = slice(left, left + weight.shape[1])
                sums[:, columns] += jnp.dot(
                    scaled, weight[deep, :], preferred_element_type=F32
                )
                left += weight.shape[1]
            return carry

        lax.fori_loop(0, width // depth, add_part, 0)
    if final:
        mean = jnp.sum(squares[...], axis=1, keepdims=True) / (shards * width)
        scale = lax.rsqrt(mean + 1e-05)
        turned = sums.shape[1] - weights[-1].shape[1]
        for left in range(0, sums.shape[1], HEAD_SIZE):
            columns = slice(left, left + HEAD_SIZE)
            head = sums[:, columns] * scale
            if left < turned:
                head = head * cosine_ref[...] + pltpu.roll(
                    head, HEAD_SIZE // 2, 1
                ) * sine_ref[...]
            out_ref[:, columns] = head.astype(BF16)


def project(final, shards, masks, pieces, gain, weights, carried, tables):
    rows = pieces[0].shape[0]
    columns = sum(weight.shape[1] for weight in weights)
    operands = [*pieces, gain, *weights, *carried, *tables]
    sums = (rows, columns), (rows, 128)
    if final:
        out_shape = [jax.ShapeDtypeStruct((rows, columns), BF16)]
        scratch = [pltpu.VMEM(shape, F32) for shape in sums]
    else:
        out_shape = [jax.ShapeDtypeStruct(shape, F32) for shape in sums]
        scratch = []
    vmem = pl.BlockSpec(memory_space=pltpu.VMEM)
    return pl.pallas_call(
        functools.partial(project_kernel, masks, bool(carried), final, shards),
        in_specs=[vmem] * len(operands),
        out_specs=[vmem] * len(out_shape),
        out_shape=out_shape,
        scratch_shapes=scratch,
        compiler_params=pltpu.CompilerParams(vmem_limit_bytes=6 * MEBI),
        name="project",
    )(*operands)


def attend_kernel(
    chips, groups, known, prior, query_width, key_width, lengths_ref, plan_ref, *refs
):
    blocks, refs = refs[: -13 if prior else -11], refs[-11:]
    attended_out, cache_out, token_ref, attended_ref, cache_ref, rows_ref, queries_ref = refs[:7]
    scores_ref, top_ref, sems, out_sems = refs[7:]
    token_ref[...] = jnp.zeros_like(token_ref)
    workers = 2 * chips
    me = lax.axis_index("req")
    chip, core = lax.div(me, 2), lax.rem(me, 2)
    slots = cache_ref.shape[1]
    spans = slots // SPAN
    total = workers * sum(sum(sizes) for _, sizes in groups)
    end = needed = jnp.int32(0)
    for other in range(workers):
        end = end + lengths_ref[other]
        needed = jnp.where(end <= prior, end, needed)
    copies = []
    for group, (bases, sizes) in enumerate(groups):
        for hop in range(chips):
            source = lax.rem(chip - hop + chips, chips) * 2
            for twin in range(2):
                owner = source + (core if twin == 0 else 1 - core)
                block = blocks[(group * chips + hop) * 2 + twin]
                first = 0
                for base, rows in zip(bases, sizes):
                    at = pl.multiple_of(base + owner * rows, ALIGN)
                    for columns, least in (
                        (slice(query_width, None), needed),
                        (slice(0, query_width), prior - SPAN - ALIGN),
                    ):
                        copy = pltpu.make_async_copy(
                            block.at[pl.ds(first, rows), columns],
                            rows_ref.at[pl.ds(at, rows), columns],
                            sems.at[len(copies)],
                        )
                        copies.append((at + rows > least, copy))
                    first += rows
    for wanted, copy in copies:

        @pl.when(wanted)
        def _():
            copy.start()

    rows_ref[total:, :] = jnp.zeros((rows_ref.shape[0] - total, rows_ref.shape[1]), BF16)
    for wanted, copy in copies:

        @pl.when(wanted)
        def _():
            copy.wait()

    def window(row, columns):
        first = pl.multiple_of(lax.div(row, ALIGN) * ALIGN, ALIGN)
        shape = (SPAN, 2 * SPAN)
        hot = (iota(shape, 1) == iota(shape, 0) + (row - first)).astype(BF16)
        return jnp.dot(
            hot, rows_ref[pl.ds(first, 2 * SPAN), columns], preferred_element_type=F32
        )

    own_start, own_length = run_of(lengths_ref, me, workers)
    mine = (own_start + own_length <= known) & (own_start + own_length > prior)
    cache_copy = pltpu.make_async_copy(cache_ref, cache_out, out_sems.at[spans])

    @pl.when(mine)
    def _():
        def step(part, carry):
            at = pl.multiple_of(part * SPAN, SPAN)

            @pl.when(at < own_length)
            def _():
                picked = window(own_start + at, slice(query_width, query_width + 2 * key_width))
                live = at + iota(picked.shape, 0) < own_length
                picked = jnp.where(live, picked, 0.0).astype(BF16)
                cache_ref[0, pl.ds(at, SPAN), :] = picked[:, :key_width]
                cache_ref[1, pl.ds(at, SPAN), :] = picked[:, key_width:]

            @pl.when(at >= own_length)
            def _():
                empty = jnp.zeros((SPAN, key_width), BF16)
                cache_ref[0, pl.ds(at, SPAN), :] = empty
                cache_ref[1, pl.ds(at, SPAN), :] = empty

            return carry

        lax.fori_loop(0, spans, step, 0)
        cache_copy.start()

    heads, key_heads = query_width // HEAD_SIZE, key_width // HEAD_SIZE
    group = heads // key_heads
    factor = math.log2(math.e) / math.sqrt(HEAD_SIZE)
    tall = group * SPAN

    def span_of(slot):
        span = plan_ref[me * spans + slot]
        start, length = run_of(lengths_ref, lax.div(span, spans), workers)
        offset = lax.rem(span, spans) * SPAN
        dead = offset >= length
        needed = start + jnp.minimum(offset + SPAN, length)
        due = jnp.logical_not(dead) & (needed <= known) & (needed > prior)
        return start, length, offset, dead, due

    def result(slot):
        rows = pl.ds(pl.multiple_of(slot * SPAN, SPAN), SPAN)
        return pltpu.make_async_copy(
            attended_ref.at[rows, :], attended_out.at[rows, :], out_sems.at[slot]
        )

    def attend_slot(slot, carry):
        start, length, offset, dead, due = span_of(slot)
        out_rows = pl.ds(pl.multiple_of(slot * SPAN, SPAN), SPAN)

        if not prior:

            @pl.when(dead)
            def _():
                attended_ref[out_rows, :] = jnp.zeros((SPAN, query_width), BF16)
                result(slot).start()

        @pl.when(due)
        def _():
            queries = window(start + offset, slice(0, query_width)).astype(BF16)
            for head in range(heads):
                at = head % group * SPAN
                queries_ref[head // group, at : at + SPAN, :] = queries[
                    :, head * HEAD_SIZE : (head + 1) * HEAD_SIZE
                ]
            first = pl.multiple_of(lax.div(start, ALIGN) * ALIGN, ALIGN)
            shift = start - first
            reach = shift + jnp.minimum(offset + SPAN, length)
            tiles = lax.div(reach + TILE - 1, TILE)

            def columns(at, head):
                return slice(at + head * HEAD_SIZE, at + (head + 1) * HEAD_SIZE)

            def tile_rows(tile):
                return pl.ds(pl.multiple_of(first + tile * TILE, ALIGN), TILE)

            top_ref[...] = jnp.full(top_ref.shape, -1e30, F32)

            def score(tile, carry):
                key_pos = tile * TILE + iota((SPAN, TILE), 1) - shift
                query_pos = offset + iota((SPAN, TILE), 0)
                allowed = (key_pos >= 0) & (key_pos <= query_pos) & (key_pos < length)
                bias = jnp.where(allowed, 0.0, -1e30)
                bias = jnp.concatenate([bias] * group, axis=0)
                for head in range(key_heads):
                    scores = lax.dot_general(
                        queries_ref[head],
                        rows_ref[tile_rows(tile), columns(query_width, head)],
                        (((1,), (1,)), ((), ())),
                        preferred_element_type=F32,
                    )
                    scores = scores + bias
                    scores_ref[head, tile] = scores
                    top_ref[head] = jnp.maximum(top_ref[head], scores)
                return carry

            lax.fori_loop(0, tiles, score, 0)
            tops = [jnp.max(top_ref[head], axis=1, keepdims=True) for head in range(key_heads)]

            def mix(tile, carry):
                ones = jnp.ones((TILE, HEAD_SIZE), BF16)
                totals = []
                for head in range(key_heads):
                    weights = jnp.exp2((scores_ref[head, tile] - tops[head]) * factor)
                    values = rows_ref[tile_rows(tile), columns(query_width + key_width, head)]
                    values = jnp.concatenate([values, ones], axis=1)
                    totals.append(
                        carry[head]
                        + jnp.dot(weights.astype(BF16), values, preferred_element_type=F32)
                    )
                return tuple(totals)

            empty = jnp.zeros((tall, 2 * HEAD_SIZE), F32)
            mixed = lax.fori_loop(0, tiles, mix, (empty,) * key_heads)
            live = offset + iota((SPAN, HEAD_SIZE), 0) < length
            for head in range(heads):
                at = head % group * SPAN
                part = mixed[head // group][at : at + SPAN]
                part = part[:, :HEAD_SIZE] / part[:, HEAD_SIZE:]
                attended_ref[out_rows, columns(0, head)] = jnp.where(live, part, 0.0).astype(BF16)

            result(slot).start()

        return carry

    lax.fori_loop(0, spans, attend_slot, 0)

    def finish(slot, carry):
        _, _, _, dead, due = span_of(slot)

        @pl.when(due if prior else due | dead)
        def _():
            result(slot).wait()

        return carry

    lax.fori_loop(0, spans, finish, 0)

    @pl.when(mine)
    def _():
        cache_copy.wait()


def attend(chips, groups, known, prior, widths, slots, lengths, plan, blocks, outputs):
    query_width, key_width = widths
    width = query_width + 2 * key_width
    total = 2 * chips * sum(sum(sizes) for _, sizes in groups)
    copies = 4 * chips * sum(len(sizes) for _, sizes in groups)
    key_heads, tall = key_width // HEAD_SIZE, query_width // key_width * SPAN
    at = 2 + len(blocks)
    return pl.pallas_call(
        functools.partial(attend_kernel, chips, groups, known, prior, query_width, key_width),
        in_specs=[pl.BlockSpec(memory_space=pltpu.SMEM)] * 2
        + [pl.BlockSpec(memory_space=pl.ANY)] * (len(blocks) + len(outputs)),
        out_specs=[pl.BlockSpec(memory_space=pl.ANY)] * 2
        + [pl.BlockSpec(memory_space=pltpu.VMEM)],
        out_shape=[
            jax.ShapeDtypeStruct((slots, query_width), BF16),
            jax.ShapeDtypeStruct((2, slots, key_width), BF16),
            jax.ShapeDtypeStruct((8, 128), F32),
        ],
        input_output_aliases={at + index: index for index in range(len(outputs))},
        scratch_shapes=[
            pltpu.VMEM((slots, query_width), BF16),
            pltpu.VMEM((2, slots, key_width), BF16),
            pltpu.VMEM((total + TILE + ALIGN, width), BF16),
            pltpu.VMEM((key_heads, tall, HEAD_SIZE), BF16),
            pltpu.VMEM((key_heads, slots // TILE + 1, tall, TILE), F32),
            pltpu.VMEM((key_heads, tall, TILE), F32),
            pltpu.SemaphoreType.DMA((copies,)),
            pltpu.SemaphoreType.DMA((slots // SPAN + 1,)),
        ],
        compiler_params=pltpu.CompilerParams(vmem_limit_bytes=16 * MEBI),
        name="attend",
    )(lengths, plan, *blocks, *outputs)


def shift_chips(value, hop, chips):
    pairs = [(2 * x + c, 2 * ((x + hop) % chips) + c) for x in range(chips) for c in range(2)]
    return lax.ppermute(value, "req", pairs)


def swap_cores(value, chips):
    return lax.ppermute(value, "req", [(d, d ^ 1) for d in range(2 * chips)])


def local(
    chips, shards, tokens, norm_gain, w_query, key_weight, value_weight, lengths, plan
):
    workers = 2 * chips
    slots = tokens.shape[0]
    live = slots // 2
    sizes = [live * share // sum(SHARES) // ALIGN * ALIGN for share in SHARES]
    sizes[-1] = live - sum(sizes[:-1])
    bases = [workers * sum(sizes[:chunk]) for chunk in range(len(sizes))]
    weights = [w_query, key_weight, value_weight]
    gain = norm_gain.astype(F32).reshape(1, -1)
    halfway = HEAD_SIZE // 2
    frequency = np.exp(-np.arange(halfway) * 2.0 / HEAD_SIZE * math.log(500000.0))
    frequency = jnp.asarray(np.tile(frequency, 2)[None, :], F32)

    twin = swap_cores(tokens, chips)
    first = deal(chips, bases[:1], sizes[:1], lengths, [tokens], [False])
    dealt = [
        *deal(chips, bases[:1], sizes[:1], lengths, [twin], [True], first),
        *deal(chips, bases[1:], sizes[1:], lengths, [tokens, twin], [False, True]),
    ]
    homes, aways = dealt[::2], dealt[1::2]
    routes, masks = routes_of(shards)
    direct = [at + 1 for at, (source, _) in enumerate(routes) if source == 0]
    kinds = {"first": [0, *direct]}
    kinds["late"] = [piece for piece in range(len(masks)) if piece not in kinds["first"]]
    relayed = [piece for piece in direct if piece in {source for source, _ in routes}]

    groups = [([base], [rows]) for base, rows in zip(bases, sizes)]
    widths = w_query.shape[1], key_weight.shape[1]

    def add(kind, chunk, carried=()):
        pieces = [lines[chunk][piece] for piece in kinds[kind]]
        final = kind == "late"
        turned = turns[chunk] if final else ()
        offsets = [masks[piece] for piece in kinds[kind]]
        return project(final, shards, offsets, pieces, gain, weights, carried, turned)

    def from_chips(block):
        return [shift_chips(block, hop, chips) for hop in range(1, chips)]

    def all_blocks(block, arrived):
        return [leaf for piece in (block, *arrived) for leaf in (piece, swap_cores(piece, chips))]

    def start(line, group):
        for index, (source, distance) in enumerate(routes):
            if index + 1 in group:
                pairs = [(at, at ^ distance) for at in range(shards)]
                line[index + 1] = lax.ppermute(line[source], "tp", pairs)

    lines, own, sent, blocks = [], [], [], []
    last = len(sizes) - 1

    def finish(chunk):
        own.append(add("late", chunk, add("first", chunk))[0])
        sent.append(from_chips(own[-1]))

    def fence(chunk, block, *anchors):
        passed, anchors = [], list(anchors)
        if chunk:
            before = lines[chunk - 1]
            passed = [before[piece] for piece in relayed]
            anchors += [before[piece] for piece in direct if piece not in relayed]
        if chunk == 1:
            weights[0], token = load(w_query, lines[0][0])
            anchors.append(token)
        if 1 < chunk <= last:
            finish(chunk - 2)
            anchors.append(own[-1])
        if 2 < chunk <= last:
            arrived = after(sent[chunk - 3], own[-1:])
            blocks.extend(all_blocks(own[chunk - 3], arrived))
            anchors += blocks[-2 * chips :]
        if passed:
            passed = after([*passed, *block], anchors)
            before.update(zip(relayed, passed))
            block = passed[len(relayed) :]
        return block

    for chunk in range(last + 1):
        arrived = [shift_chips(aways[chunk][hop - 1], hop, chips) for hop in range(1, chips)]
        later = aways[chunk + 1 : chunk + 2]
        block, aways[chunk + 1 : chunk + 2] = merge(homes[chunk], arrived, later)
        lines.append({0: fence(chunk, [block])[0]})
        if chunk:
            start(lines[-2], kinds["late"])
        start(lines[-1], direct)
        if chunk == 1:
            turns = angles(groups, lengths, frequency, lines[1][0])
    common = widths, slots, lengths, plan

    def attended(at, prior, blocks, outputs):
        known = workers * sum(sizes[: at + 1])
        return attend(chips, groups[: at + 1], known, prior, *common, blocks, outputs)

    sums = list(add("first", last - 1))
    for at in range(last - 2, last - 1):
        blocks += all_blocks(own[at], after(sent[at], own[at + 1 : at + 2] or [sums[1]]))
    *outputs, token = attended(last - 2, 0, blocks, ())
    sums[1:] = after(sums[1:], [token])
    fence(last + 1, [])
    start(lines[-1], kinds["late"])
    own.append(add("late", last - 1, sums)[0])
    sent.append(from_chips(own[-1]))
    finish(last)
    blocks += all_blocks(own[last - 1], after(sent[last - 1], own[last:]))
    prior = workers * sum(sizes[:-2])
    *outputs, token = attended(last - 1, prior, blocks, outputs)
    blocks += all_blocks(own[last], after(sent[last], [token]))
    prior = workers * sum(sizes[:-1])
    return tuple(attended(last, prior, blocks, outputs)[:2])


def solution(mesh):
    placed = (
        P(("groups", "req"), "tp"),
        P(),
        P(None, "tp"),
        P(None, "tp"),
        P(None, "tp"),
        P("groups"),
        P("groups"),
    )
    return jax.shard_map(
        functools.partial(local, mesh.shape["req"] // 2, mesh.shape["tp"]),
        mesh=mesh,
        in_specs=placed,
        out_specs=(P(("groups", "req"), "tp"), P(None, ("groups", "req"), "tp")),
        check_vma=False,
    )
```

```python
import functools
import math

import jax
import jax.numpy as jnp
import numpy as np
from jax import lax
from jax.experimental import pallas as pl
from jax.experimental.pallas import tpu as pltpu
from jax.sharding import PartitionSpec as P

HEAD_SIZE = 128
SPAN = 128
ALIGN = 16
TILE = 2 * SPAN
SHARES = (3, 5, 5, 3)
DEPTH = 1024
MEBI = 1024 * 1024
F32, BF16 = jnp.float32, jnp.bfloat16


def run_of(lengths_ref, request, count):
    start = jnp.int32(0)
    length = jnp.int32(0)
    for other in range(count):
        amount = lengths_ref[other]
        start = start + jnp.where(other < request, amount, 0)
        length = jnp.where(other == request, amount, length)
    return start, length


def iota(shape, dimension):
    return lax.broadcasted_iota(jnp.int32, shape, dimension)


def deal_kernel(chips, bases, sizes, twins, lengths_ref, *refs):
    me = lax.axis_index("req")
    chip, core = lax.div(me, 2), lax.rem(me, 2)
    sources, refs = refs[: len(twins)], refs[len(twins) :]
    count = 2 * len(sizes)
    priors, out_refs = refs[:-count], refs[-count:]
    requests = [me + 1 - 2 * core if twin else me for twin in twins]
    runs = [run_of(lengths_ref, request, 2 * chips) for request in requests]
    slots = sources[0].shape[0]
    total = None
    for (start, length), source in zip(runs, sources):
        hots = []
        for base, rows in zip(bases, sizes):
            for hop in range(chips):
                target = lax.rem(chip + hop, chips) * 2 + core
                number = base + target * rows + iota((rows, slots), 0)
                slot = iota((rows, slots), 1)
                hot = (number - start == slot) & (slot < length)
                hots.append(hot.astype(F32).astype(BF16))
        hot = jnp.concatenate(hots, axis=0) if len(hots) > 1 else hots[0]
        part = jnp.dot(hot, source[...], preferred_element_type=F32)
        total = part if total is None else total + part
    total = total.astype(BF16)
    at = 0
    for chunk, rows in enumerate(sizes):
        for hop in range(chips):
            picked = total[at : at + rows]
            at += rows
            if priors:
                prior = priors[2 * chunk + 1][hop - 1] if hop else priors[2 * chunk][...]
                picked = picked + prior
            if hop:
                out_refs[2 * chunk + 1][hop - 1] = picked
            else:
                out_refs[2 * chunk][...] = picked


def deal(chips, bases, sizes, lengths, sources, twins, priors=()):
    slots, width = sources[0].shape
    block = min(1024, width)
    out_specs, out_shape = [], []
    for rows in sizes:
        out_specs += [
            pl.BlockSpec((rows, block), lambda i: (0, i)),
            pl.BlockSpec((chips - 1, rows, block), lambda i: (0, 0, i)),
        ]
        out_shape += [
            jax.ShapeDtypeStruct((rows, width), BF16),
            jax.ShapeDtypeStruct((chips - 1, rows, width), BF16),
        ]
    return pl.pallas_call(
        functools.partial(deal_kernel, chips, bases, sizes, twins),
        grid=(width // block,),
        in_specs=[pl.BlockSpec(memory_space=pltpu.SMEM)]
        + [pl.BlockSpec((slots, block), lambda i: (0, i)) for _ in sources]
        + (out_specs if priors else []),
        out_specs=out_specs,
        out_shape=out_shape,
        compiler_params=pltpu.CompilerParams(vmem_limit_bytes=10 * MEBI),
        name="deal",
    )(lengths, *sources, *priors)


def merge_kernel(count, passed, home_ref, *refs):
    total = home_ref[...]
    for ref in refs[:count]:
        total = total + ref[...]
    refs[len(refs) - 1 - passed][...] = total


def merge(home, arrived, later):
    count = len(arrived)
    vmem, anywhere = pl.BlockSpec(memory_space=pltpu.VMEM), pl.BlockSpec(memory_space=pl.ANY)
    block, *later = pl.pallas_call(
        functools.partial(merge_kernel, count, len(later)),
        in_specs=[vmem] * (count + 1) + [anywhere] * len(later),
        out_specs=[vmem] + [anywhere] * len(later),
        out_shape=[jax.ShapeDtypeStruct(leaf.shape, leaf.dtype) for leaf in (home, *later)],
        input_output_aliases={count + 1 + at: 1 + at for at in range(len(later))},
        compiler_params=pltpu.CompilerParams(vmem_limit_bytes=4 * MEBI),
        name="merge",
    )(home, *arrived, *later)
    return block, later


def after(arrays, anchors):
    def kernel(*refs):
        pass

    anywhere = pl.BlockSpec(memory_space=pl.ANY)
    return pl.pallas_call(
        kernel,
        in_specs=[anywhere] * (len(arrays) + len(anchors)),
        out_specs=[anywhere] * len(arrays),
        out_shape=[jax.ShapeDtypeStruct(leaf.shape, leaf.dtype) for leaf in arrays],
        input_output_aliases={at: at for at in range(len(arrays))},
        compiler_params=pltpu.CompilerParams(vmem_limit_bytes=MEBI),
        name="after",
    )(*arrays, *anchors)


def routes_of(shards):
    routes, masks, distance = [], [0], shards // 2
    while distance:
        for source in range(len(masks)):
            routes.append((source, distance))
            masks.append(masks[source] ^ distance)
        distance //= 2
    return routes, masks


def angles_kernel(groups, members, lengths_ref, frequency_ref, anchor_ref, *out_refs):
    me = lax.axis_index("req")
    for group, (bases, sizes) in enumerate(groups):
        first = 0
        for base, rows in zip(bases, sizes):
            number = base + me * rows + iota((rows, HEAD_SIZE), 0)
            start = jnp.zeros((rows, HEAD_SIZE), jnp.int32)
            before = jnp.int32(0)
            for other in range(members):
                before = before + lengths_ref[other]
                start = jnp.where(number >= before, before, start)
            angle = (number - start).astype(F32) * frequency_ref[...]
            sine = jnp.sin(angle)
            lower = iota((rows, HEAD_SIZE), 1) < HEAD_SIZE // 2
            out_refs[2 * group][first : first + rows, :] = jnp.cos(angle)
            out_refs[2 * group + 1][first : first + rows, :] = jnp.where(lower, -sine, sine)
            first += rows


def angles(groups, lengths, frequency, anchor):
    shapes = [
        jax.ShapeDtypeStruct((sum(sizes), HEAD_SIZE), F32) for _, sizes in groups for _ in range(2)
    ]
    vmem = pl.BlockSpec(memory_space=pltpu.VMEM)
    tables = pl.pallas_call(
        functools.partial(angles_kernel, groups, lengths.shape[0]),
        in_specs=[
            pl.BlockSpec(memory_space=pltpu.SMEM),
            vmem,
            pl.BlockSpec(memory_space=pl.ANY),
        ],
        out_specs=[vmem] * len(shapes),
        out_shape=shapes,
        compiler_params=pltpu.CompilerParams(vmem_limit_bytes=4 * MEBI),
        name="angles",
    )(lengths, frequency, anchor)
    return [tables[at : at + 2] for at in range(0, len(tables), 2)]


def load(weight, anchor):
    parts = 8
    depth = weight.shape[0] // parts

    def kernel(weight_ref, anchor_ref, out_ref, token_ref, sems):
        copies = [
            pltpu.make_async_copy(
                weight_ref.at[pl.ds(part * depth, depth), :],
                out_ref.at[pl.ds(part * depth, depth), :],
                sems.at[part],
            )
            for part in range(parts)
        ]
        for copy in copies:
            copy.start()
        token_ref[...] = jnp.zeros_like(token_ref)
        for copy in copies:
            copy.wait()

    vmem, anywhere = pl.BlockSpec(memory_space=pltpu.VMEM), pl.BlockSpec(memory_space=pl.ANY)
    return pl.pallas_call(
        kernel,
        in_specs=[anywhere, anywhere],
        out_specs=[vmem, vmem],
        out_shape=[
            jax.ShapeDtypeStruct(weight.shape, weight.dtype),
            jax.ShapeDtypeStruct((8, 128), F32),
        ],
        scratch_shapes=[pltpu.SemaphoreType.DMA((parts,))],
        compiler_params=pltpu.CompilerParams(vmem_limit_bytes=2 * MEBI),
        name="load",
    )(pltpu.with_memory_space_constraint(weight, pltpu.HBM), anchor)


def project_kernel(masks, carries, final, shards, *refs):
    pieces, refs = refs[: len(masks)], refs[len(masks) :]
    (gain_ref, *weights), refs = refs[:4], refs[4:]
    if carries:
        sums_in, squares_in, *refs = refs
    if final:
        cosine_ref, sine_ref, out_ref, *refs = refs
    sums, squares = refs
    width = pieces[0].shape[1]
    depth = min(DEPTH, width)
    sums[...] = sums_in[...] if carries else jnp.zeros_like(sums)
    squares[...] = squares_in[...] if carries else jnp.zeros_like(squares)
    for piece, mask in zip(pieces, masks):
        shard = lax.bitwise_xor(lax.axis_index("tp"), jnp.int32(mask))

        def add_part(part, carry):
            at = pl.multiple_of(part * depth, depth)
            deep = pl.ds(pl.multiple_of(shard * width + at, depth), depth)
            wide = piece[:, pl.ds(at, depth)].astype(F32)
            square = wide * wide
            lanes = square[:, :128]
            for left in range(128, depth, 128):
                lanes = lanes + square[:, left : left + 128]
            squares[...] += lanes
            scaled = (wide * gain_ref[:, deep]).astype(BF16)
            left = 0
            for weight in weights:
                columns = slice(left, left + weight.shape[1])
                sums[:, columns] += jnp.dot(
                    scaled, weight[deep, :], preferred_element_type=F32
                )
                left += weight.shape[1]
            return carry

        lax.fori_loop(0, width // depth, add_part, 0)
    if final:
        mean = jnp.sum(squares[...], axis=1, keepdims=True) / (shards * width)
        scale = lax.rsqrt(mean + 1e-05)
        turned = sums.shape[1] - weights[-1].shape[1]
        for left in range(0, sums.shape[1], HEAD_SIZE):
            columns = slice(left, left + HEAD_SIZE)
            head = sums[:, columns] * scale
            if left < turned:
                head = head * cosine_ref[...] + pltpu.roll(
                    head, HEAD_SIZE // 2, 1
                ) * sine_ref[...]
            out_ref[:, columns] = head.astype(BF16)


def project(final, shards, masks, pieces, gain, weights, carried, tables):
    rows = pieces[0].shape[0]
    columns = sum(weight.shape[1] for weight in weights)
    operands = [*pieces, gain, *weights, *carried, *tables]
    sums = (rows, columns), (rows, 128)
    if final:
        out_shape = [jax.ShapeDtypeStruct((rows, columns), BF16)]
        scratch = [pltpu.VMEM(shape, F32) for shape in sums]
    else:
        out_shape = [jax.ShapeDtypeStruct(shape, F32) for shape in sums]
        scratch = []
    vmem = pl.BlockSpec(memory_space=pltpu.VMEM)
    return pl.pallas_call(
        functools.partial(project_kernel, masks, bool(carried), final, shards),
        in_specs=[vmem] * len(operands),
        out_specs=[vmem] * len(out_shape),
        out_shape=out_shape,
        scratch_shapes=scratch,
        compiler_params=pltpu.CompilerParams(vmem_limit_bytes=6 * MEBI),
        name="project",
    )(*operands)


def attend_kernel(
    chips, groups, known, prior, query_width, key_width, lengths_ref, plan_ref, *refs
):
    blocks, refs = refs[: -13 if prior else -11], refs[-11:]
    attended_out, cache_out, token_ref, attended_ref, cache_ref, rows_ref, queries_ref = refs[:7]
    scores_ref, top_ref, sems, out_sems = refs[7:]
    token_ref[...] = jnp.zeros_like(token_ref)
    workers = 2 * chips
    me = lax.axis_index("req")
    chip, core = lax.div(me, 2), lax.rem(me, 2)
    slots = cache_ref.shape[1]
    spans = slots // SPAN
    total = workers * sum(sum(sizes) for _, sizes in groups)
    end = needed = jnp.int32(0)
    for other in range(workers):
        end = end + lengths_ref[other]
        needed = jnp.where(end <= prior, end, needed)
    copies = []
    for group, (bases, sizes) in enumerate(groups):
        for hop in range(chips):
            source = lax.rem(chip - hop + chips, chips) * 2
            for twin in range(2):
                owner = source + (core if twin == 0 else 1 - core)
                block = blocks[(group * chips + hop) * 2 + twin]
                first = 0
                for base, rows in zip(bases, sizes):
                    at = pl.multiple_of(base + owner * rows, ALIGN)
                    for columns, least in (
                        (slice(query_width, None), needed),
                        (slice(0, query_width), prior - SPAN - ALIGN),
                    ):
                        copy = pltpu.make_async_copy(
                            block.at[pl.ds(first, rows), columns],
                            rows_ref.at[pl.ds(at, rows), columns],
                            sems.at[len(copies)],
                        )
                        copies.append((at + rows > least, copy))
                    first += rows
    for wanted, copy in copies:

        @pl.when(wanted)
        def _():
            copy.start()

    rows_ref[total:, :] = jnp.zeros((rows_ref.shape[0] - total, rows_ref.shape[1]), BF16)
    for wanted, copy in copies:

        @pl.when(wanted)
        def _():
            copy.wait()

    def window(row, columns):
        first = pl.multiple_of(lax.div(row, ALIGN) * ALIGN, ALIGN)
        shape = (SPAN, 2 * SPAN)
        hot = (iota(shape, 1) == iota(shape, 0) + (row - first)).astype(BF16)
        return jnp.dot(
            hot, rows_ref[pl.ds(first, 2 * SPAN), columns], preferred_element_type=F32
        )

    own_start, own_length = run_of(lengths_ref, me, workers)
    mine = (own_start + own_length <= known) & (own_start + own_length > prior)
    cache_copy = pltpu.make_async_copy(cache_ref, cache_out, out_sems.at[spans])

    @pl.when(mine)
    def _():
        def step(part, carry):
            at = pl.multiple_of(part * SPAN, SPAN)

            @pl.when(at < own_length)
            def _():
                picked = window(own_start + at, slice(query_width, query_width + 2 * key_width))
                live = at + iota(picked.shape, 0) < own_length
                picked = jnp.where(live, picked, 0.0).astype(BF16)
                cache_ref[0, pl.ds(at, SPAN), :] = picked[:, :key_width]
                cache_ref[1, pl.ds(at, SPAN), :] = picked[:, key_width:]

            @pl.when(at >= own_length)
            def _():
                empty = jnp.zeros((SPAN, key_width), BF16)
                cache_ref[0, pl.ds(at, SPAN), :] = empty
                cache_ref[1, pl.ds(at, SPAN), :] = empty

            return carry

        lax.fori_loop(0, spans, step, 0)
        cache_copy.start()

    heads, key_heads = query_width // HEAD_SIZE, key_width // HEAD_SIZE
    group = heads // key_heads
    factor = math.log2(math.e) / math.sqrt(HEAD_SIZE)
    tall = group * SPAN

    def span_of(slot):
        span = plan_ref[me * spans + slot]
        start, length = run_of(lengths_ref, lax.div(span, spans), workers)
        offset = lax.rem(span, spans) * SPAN
        dead = offset >= length
        needed = start + jnp.minimum(offset + SPAN, length)
        due = jnp.logical_not(dead) & (needed <= known) & (needed > prior)
        return start, length, offset, dead, due

    def result(slot):
        rows = pl.ds(pl.multiple_of(slot * SPAN, SPAN), SPAN)
        return pltpu.make_async_copy(
            attended_ref.at[rows, :], attended_out.at[rows, :], out_sems.at[slot]
        )

    def attend_slot(slot, carry):
        start, length, offset, dead, due = span_of(slot)
        out_rows = pl.ds(pl.multiple_of(slot * SPAN, SPAN), SPAN)

        if not prior:

            @pl.when(dead)
            def _():
                attended_ref[out_rows, :] = jnp.zeros((SPAN, query_width), BF16)
                result(slot).start()

        @pl.when(due)
        def _():
            queries = window(start + offset, slice(0, query_width)).astype(BF16)
            for head in range(heads):
                at = head % group * SPAN
                queries_ref[head // group, at : at + SPAN, :] = queries[
                    :, head * HEAD_SIZE : (head + 1) * HEAD_SIZE
                ]
            first = pl.multiple_of(lax.div(start, ALIGN) * ALIGN, ALIGN)
            shift = start - first
            reach = shift + jnp.minimum(offset + SPAN, length)
            tiles = lax.div(reach + TILE - 1, TILE)

            def columns(at, head):
                return slice(at + head * HEAD_SIZE, at + (head + 1) * HEAD_SIZE)

            def tile_rows(tile):
                return pl.ds(pl.multiple_of(first + tile * TILE, ALIGN), TILE)

            top_ref[...] = jnp.full(top_ref.shape, -1e30, F32)

            def score(tile, carry):
                key_pos = tile * TILE + iota((SPAN, TILE), 1) - shift
                query_pos = offset + iota((SPAN, TILE), 0)
                allowed = (key_pos >= 0) & (key_pos <= query_pos) & (key_pos < length)
                bias = jnp.where(allowed, 0.0, -1e30)
                bias = jnp.concatenate([bias] * group, axis=0)
                for head in range(key_heads):
                    scores = lax.dot_general(
                        queries_ref[head],
                        rows_ref[tile_rows(tile), columns(query_width, head)],
                        (((1,), (1,)), ((), ())),
                        preferred_element_type=F32,
                    )
                    scores = scores + bias
                    scores_ref[head, tile] = scores
                    top_ref[head] = jnp.maximum(top_ref[head], scores)
                return carry

            lax.fori_loop(0, tiles, score, 0)
            tops = [jnp.max(top_ref[head], axis=1, keepdims=True) for head in range(key_heads)]

            def mix(tile, carry):
                ones = jnp.ones((TILE, HEAD_SIZE), BF16)
                totals = []
                for head in range(key_heads):
                    weights = jnp.exp2((scores_ref[head, tile] - tops[head]) * factor)
                    values = rows_ref[tile_rows(tile), columns(query_width + key_width, head)]
                    values = jnp.concatenate([values, ones], axis=1)
                    totals.append(
                        carry[head]
                        + jnp.dot(weights.astype(BF16), values, preferred_element_type=F32)
                    )
                return tuple(totals)

            empty = jnp.zeros((tall, 2 * HEAD_SIZE), F32)
            mixed = lax.fori_loop(0, tiles, mix, (empty,) * key_heads)
            live = offset + iota((SPAN, HEAD_SIZE), 0) < length
            for head in range(heads):
                at = head % group * SPAN
                part = mixed[head // group][at : at + SPAN]
                part = part[:, :HEAD_SIZE] / part[:, HEAD_SIZE:]
                attended_ref[out_rows, columns(0, head)] = jnp.where(live, part, 0.0).astype(BF16)

            result(slot).start()

        return carry

    lax.fori_loop(0, spans, attend_slot, 0)

    def finish(slot, carry):
        _, _, _, dead, due = span_of(slot)

        @pl.when(due if prior else due | dead)
        def _():
            result(slot).wait()

        return carry

    lax.fori_loop(0, spans, finish, 0)

    @pl.when(mine)
    def _():
        cache_copy.wait()


def attend(chips, groups, known, prior, widths, slots, lengths, plan, blocks, outputs):
    query_width, key_width = widths
    width = query_width + 2 * key_width
    total = 2 * chips * sum(sum(sizes) for _, sizes in groups)
    copies = 4 * chips * sum(len(sizes) for _, sizes in groups)
    key_heads, tall = key_width // HEAD_SIZE, query_width // key_width * SPAN
    at = 2 + len(blocks)
    return pl.pallas_call(
        functools.partial(attend_kernel, chips, groups, known, prior, query_width, key_width),
        in_specs=[pl.BlockSpec(memory_space=pltpu.SMEM)] * 2
        + [pl.BlockSpec(memory_space=pl.ANY)] * (len(blocks) + len(outputs)),
        out_specs=[pl.BlockSpec(memory_space=pl.ANY)] * 2
        + [pl.BlockSpec(memory_space=pltpu.VMEM)],
        out_shape=[
            jax.ShapeDtypeStruct((slots, query_width), BF16),
            jax.ShapeDtypeStruct((2, slots, key_width), BF16),
            jax.ShapeDtypeStruct((8, 128), F32),
        ],
        input_output_aliases={at + index: index for index in range(len(outputs))},
        scratch_shapes=[
            pltpu.VMEM((slots, query_width), BF16),
            pltpu.VMEM((2, slots, key_width), BF16),
            pltpu.VMEM((total + TILE + ALIGN, width), BF16),
            pltpu.VMEM((key_heads, tall, HEAD_SIZE), BF16),
            pltpu.VMEM((key_heads, slots // TILE + 1, tall, TILE), F32),
            pltpu.VMEM((key_heads, tall, TILE), F32),
            pltpu.SemaphoreType.DMA((copies,)),
            pltpu.SemaphoreType.DMA((slots // SPAN + 1,)),
        ],
        compiler_params=pltpu.CompilerParams(vmem_limit_bytes=16 * MEBI),
        name="attend",
    )(lengths, plan, *blocks, *outputs)


def shift_chips(value, hop, chips):
    pairs = [(2 * x + c, 2 * ((x + hop) % chips) + c) for x in range(chips) for c in range(2)]
    return lax.ppermute(value, "req", pairs)


def swap_cores(value, chips):
    return lax.ppermute(value, "req", [(d, d ^ 1) for d in range(2 * chips)])


def local(
    chips, shards, tokens, norm_gain, w_query, key_weight, value_weight, lengths, plan
):
    workers = 2 * chips
    slots = tokens.shape[0]
    live = slots // 2
    sizes = [live * share // sum(SHARES) // ALIGN * ALIGN for share in SHARES]
    sizes[-1] = live - sum(sizes[:-1])
    bases = [workers * sum(sizes[:chunk]) for chunk in range(len(sizes))]
    weights = [w_query, key_weight, value_weight]
    gain = norm_gain.astype(F32).reshape(1, -1)
    halfway = HEAD_SIZE // 2
    frequency = np.exp(-np.arange(halfway) * 2.0 / HEAD_SIZE * math.log(500000.0))
    frequency = jnp.asarray(np.tile(frequency, 2)[None, :], F32)

    twin = swap_cores(tokens, chips)
    first = deal(chips, bases[:1], sizes[:1], lengths, [tokens], [False])
    dealt = [
        *deal(chips, bases[:1], sizes[:1], lengths, [twin], [True], first),
        *deal(chips, bases[1:], sizes[1:], lengths, [tokens, twin], [False, True]),
    ]
    homes, aways = dealt[::2], dealt[1::2]
    routes, masks = routes_of(shards)
    direct = [at + 1 for at, (source, _) in enumerate(routes) if source == 0]
    kinds = {"first": [0, *direct]}
    kinds["late"] = [piece for piece in range(len(masks)) if piece not in kinds["first"]]
    relayed = [piece for piece in direct if piece in {source for source, _ in routes}]

    groups = [([base], [rows]) for base, rows in zip(bases, sizes)]
    widths = w_query.shape[1], key_weight.shape[1]

    def add(kind, chunk, carried=()):
        pieces = [lines[chunk][piece] for piece in kinds[kind]]
        final = kind == "late"
        turned = turns[chunk] if final else ()
        offsets = [masks[piece] for piece in kinds[kind]]
        return project(final, shards, offsets, pieces, gain, weights, carried, turned)

    def from_chips(block):
        return [shift_chips(block, hop, chips) for hop in range(1, chips)]

    def all_blocks(block, arrived):
        return [leaf for piece in (block, *arrived) for leaf in (piece, swap_cores(piece, chips))]

    def start(line, group):
        for index, (source, distance) in enumerate(routes):
            if index + 1 in group:
                pairs = [(at, at ^ distance) for at in range(shards)]
                line[index + 1] = lax.ppermute(line[source], "tp", pairs)

    lines, own, sent = [], [], []
    last = len(sizes) - 1

    def finish(chunk):
        own.append(add("late", chunk, add("first", chunk))[0])
        sent.append(from_chips(own[-1]))

    def fence(chunk, block):
        passed, anchors = [], []
        if chunk:
            before = lines[chunk - 1]
            passed = [before[piece] for piece in relayed]
            anchors += [before[piece] for piece in direct if piece not in relayed]
        if chunk == 1:
            weights[0], token = load(w_query, lines[0][0])
            anchors.append(token)
        if 1 < chunk <= last:
            finish(chunk - 2)
            anchors.append(own[-1])
        if chunk > 2:
            anchors += sent[chunk - 3]
        if passed:
            passed = after([*passed, *block], anchors)
            before.update(zip(relayed, passed))
            block = passed[len(relayed) :]
        return block

    for chunk in range(last + 1):
        arrived = [shift_chips(aways[chunk][hop - 1], hop, chips) for hop in range(1, chips)]
        later = aways[chunk + 1 : chunk + 2]
        block, aways[chunk + 1 : chunk + 2] = merge(homes[chunk], arrived, later)
        lines.append({0: fence(chunk, [block])[0]})
        if chunk:
            start(lines[-2], kinds["late"])
        start(lines[-1], direct)
        if chunk == 1:
            turns = angles(groups, lengths, frequency, lines[1][0])
    fence(last + 1, [])
    start(lines[-1], kinds["late"])
    for chunk in (last - 1, last):
        finish(chunk)
    blocks = []
    for at in range(last):
        blocks += all_blocks(own[at], after(sent[at], own[at + 1 : at + 2]))
    sent.append(from_chips(own[last]))
    known = workers * sum(sizes[:-1])
    common = widths, slots, lengths, plan
    *outputs, token = attend(chips, groups[:-1], known, 0, *common, blocks, ())
    blocks += all_blocks(own[last], after(sent[last], [token]))
    return tuple(attend(chips, groups, workers * live, known, *common, blocks, outputs)[:2])


def solution(mesh):
    placed = (
        P(("groups", "req"), "tp"),
        P(),
        P(None, "tp"),
        P(None, "tp"),
        P(None, "tp"),
        P("groups"),
        P("groups"),
    )
    return jax.shard_map(
        functools.partial(local, mesh.shape["req"] // 2, mesh.shape["tp"]),
        mesh=mesh,
        in_specs=placed,
        out_specs=(P(("groups", "req"), "tp"), P(None, ("groups", "req"), "tp")),
        check_vma=False,
    )
```

```python
import functools
import math

import jax
import jax.numpy as jnp
import numpy as np
from jax import lax
from jax.experimental import pallas as pl
from jax.experimental.pallas import tpu as pltpu
from jax.sharding import PartitionSpec as P

HEAD_SIZE = 128
SPAN = 128
ALIGN = 16
TILE = 2 * SPAN
SHARES = (2, 6, 5, 3)
DEPTH = 1024
MEBI = 1024 * 1024
F32, BF16 = jnp.float32, jnp.bfloat16


def run_of(lengths_ref, request, count):
    start = jnp.int32(0)
    length = jnp.int32(0)
    for other in range(count):
        amount = lengths_ref[other]
        start = start + jnp.where(other < request, amount, 0)
        length = jnp.where(other == request, amount, length)
    return start, length


def iota(shape, dimension):
    return lax.broadcasted_iota(jnp.int32, shape, dimension)


def deal_kernel(chips, bases, sizes, twins, lengths_ref, *refs):
    me = lax.axis_index("req")
    chip, core = lax.div(me, 2), lax.rem(me, 2)
    sources, refs = refs[: len(twins)], refs[len(twins) :]
    count = 2 * len(sizes)
    priors, out_refs = refs[:-count], refs[-count:]
    requests = [me + 1 - 2 * core if twin else me for twin in twins]
    runs = [run_of(lengths_ref, request, 2 * chips) for request in requests]
    slots = sources[0].shape[0]
    total = None
    for (start, length), source in zip(runs, sources):
        hots = []
        for base, rows in zip(bases, sizes):
            for hop in range(chips):
                target = lax.rem(chip + hop, chips) * 2 + core
                number = base + target * rows + iota((rows, slots), 0)
                slot = iota((rows, slots), 1)
                hot = (number - start == slot) & (slot < length)
                hots.append(hot.astype(F32).astype(BF16))
        hot = jnp.concatenate(hots, axis=0) if len(hots) > 1 else hots[0]
        part = jnp.dot(hot, source[...], preferred_element_type=F32)
        total = part if total is None else total + part
    total = total.astype(BF16)
    at = 0
    for chunk, rows in enumerate(sizes):
        for hop in range(chips):
            picked = total[at : at + rows]
            at += rows
            if priors:
                prior = priors[2 * chunk + 1][hop - 1] if hop else priors[2 * chunk][...]
                picked = picked + prior
            if hop:
                out_refs[2 * chunk + 1][hop - 1] = picked
            else:
                out_refs[2 * chunk][...] = picked


def deal(chips, bases, sizes, lengths, sources, twins, priors=()):
    slots, width = sources[0].shape
    block = min(1024, width)
    out_specs, out_shape = [], []
    for rows in sizes:
        out_specs += [
            pl.BlockSpec((rows, block), lambda i: (0, i)),
            pl.BlockSpec((chips - 1, rows, block), lambda i: (0, 0, i)),
        ]
        out_shape += [
            jax.ShapeDtypeStruct((rows, width), BF16),
            jax.ShapeDtypeStruct((chips - 1, rows, width), BF16),
        ]
    return pl.pallas_call(
        functools.partial(deal_kernel, chips, bases, sizes, twins),
        grid=(width // block,),
        in_specs=[pl.BlockSpec(memory_space=pltpu.SMEM)]
        + [pl.BlockSpec((slots, block), lambda i: (0, i)) for _ in sources]
        + (out_specs if priors else []),
        out_specs=out_specs,
        out_shape=out_shape,
        compiler_params=pltpu.CompilerParams(vmem_limit_bytes=10 * MEBI),
        name="deal",
    )(lengths, *sources, *priors)


def merge_kernel(count, passed, home_ref, *refs):
    total = home_ref[...]
    for ref in refs[:count]:
        total = total + ref[...]
    refs[len(refs) - 1 - passed][...] = total


def merge(home, arrived, later):
    count = len(arrived)
    vmem, anywhere = pl.BlockSpec(memory_space=pltpu.VMEM), pl.BlockSpec(memory_space=pl.ANY)
    block, *later = pl.pallas_call(
        functools.partial(merge_kernel, count, len(later)),
        in_specs=[vmem] * (count + 1) + [anywhere] * len(later),
        out_specs=[vmem] + [anywhere] * len(later),
        out_shape=[jax.ShapeDtypeStruct(leaf.shape, leaf.dtype) for leaf in (home, *later)],
        input_output_aliases={count + 1 + at: 1 + at for at in range(len(later))},
        compiler_params=pltpu.CompilerParams(vmem_limit_bytes=4 * MEBI),
        name="merge",
    )(home, *arrived, *later)
    return block, later


def after(arrays, anchors):
    def kernel(*refs):
        pass

    anywhere = pl.BlockSpec(memory_space=pl.ANY)
    return pl.pallas_call(
        kernel,
        in_specs=[anywhere] * (len(arrays) + len(anchors)),
        out_specs=[anywhere] * len(arrays),
        out_shape=[jax.ShapeDtypeStruct(leaf.shape, leaf.dtype) for leaf in arrays],
        input_output_aliases={at: at for at in range(len(arrays))},
        compiler_params=pltpu.CompilerParams(vmem_limit_bytes=MEBI),
        name="after",
    )(*arrays, *anchors)


def routes_of(shards):
    routes, masks, distance = [], [0], shards // 2
    while distance:
        for source in range(len(masks)):
            routes.append((source, distance))
            masks.append(masks[source] ^ distance)
        distance //= 2
    return routes, masks


def angles_kernel(groups, members, lengths_ref, frequency_ref, anchor_ref, *out_refs):
    me = lax.axis_index("req")
    for group, (bases, sizes) in enumerate(groups):
        first = 0
        for base, rows in zip(bases, sizes):
            number = base + me * rows + iota((rows, HEAD_SIZE), 0)
            start = jnp.zeros((rows, HEAD_SIZE), jnp.int32)
            before = jnp.int32(0)
            for other in range(members):
                before = before + lengths_ref[other]
                start = jnp.where(number >= before, before, start)
            angle = (number - start).astype(F32) * frequency_ref[...]
            sine = jnp.sin(angle)
            lower = iota((rows, HEAD_SIZE), 1) < HEAD_SIZE // 2
            out_refs[2 * group][first : first + rows, :] = jnp.cos(angle)
            out_refs[2 * group + 1][first : first + rows, :] = jnp.where(lower, -sine, sine)
            first += rows


def angles(groups, lengths, frequency, anchor):
    shapes = [
        jax.ShapeDtypeStruct((sum(sizes), HEAD_SIZE), F32) for _, sizes in groups for _ in range(2)
    ]
    vmem = pl.BlockSpec(memory_space=pltpu.VMEM)
    tables = pl.pallas_call(
        functools.partial(angles_kernel, groups, lengths.shape[0]),
        in_specs=[
            pl.BlockSpec(memory_space=pltpu.SMEM),
            vmem,
            pl.BlockSpec(memory_space=pl.ANY),
        ],
        out_specs=[vmem] * len(shapes),
        out_shape=shapes,
        compiler_params=pltpu.CompilerParams(vmem_limit_bytes=4 * MEBI),
        name="angles",
    )(lengths, frequency, anchor)
    return [tables[at : at + 2] for at in range(0, len(tables), 2)]


def load(weight, anchor):
    parts = 8
    depth = weight.shape[0] // parts

    def kernel(weight_ref, anchor_ref, out_ref, token_ref, sems):
        copies = [
            pltpu.make_async_copy(
                weight_ref.at[pl.ds(part * depth, depth), :],
                out_ref.at[pl.ds(part * depth, depth), :],
                sems.at[part],
            )
            for part in range(parts)
        ]
        for copy in copies:
            copy.start()
        token_ref[...] = jnp.zeros_like(token_ref)
        for copy in copies:
            copy.wait()

    vmem, anywhere = pl.BlockSpec(memory_space=pltpu.VMEM), pl.BlockSpec(memory_space=pl.ANY)
    return pl.pallas_call(
        kernel,
        in_specs=[anywhere, anywhere],
        out_specs=[vmem, vmem],
        out_shape=[
            jax.ShapeDtypeStruct(weight.shape, weight.dtype),
            jax.ShapeDtypeStruct((8, 128), F32),
        ],
        scratch_shapes=[pltpu.SemaphoreType.DMA((parts,))],
        compiler_params=pltpu.CompilerParams(vmem_limit_bytes=2 * MEBI),
        name="load",
    )(pltpu.with_memory_space_constraint(weight, pltpu.HBM), anchor)


def project_kernel(masks, carries, final, shards, *refs):
    pieces, refs = refs[: len(masks)], refs[len(masks) :]
    (gain_ref, *weights), refs = refs[:4], refs[4:]
    if carries:
        sums_in, squares_in, *refs = refs
    if final:
        cosine_ref, sine_ref, out_ref, *refs = refs
    sums, squares = refs
    width = pieces[0].shape[1]
    depth = min(DEPTH, width)
    sums[...] = sums_in[...] if carries else jnp.zeros_like(sums)
    squares[...] = squares_in[...] if carries else jnp.zeros_like(squares)
    for piece, mask in zip(pieces, masks):
        shard = lax.bitwise_xor(lax.axis_index("tp"), jnp.int32(mask))

        def add_part(part, carry):
            at = pl.multiple_of(part * depth, depth)
            deep = pl.ds(pl.multiple_of(shard * width + at, depth), depth)
            wide = piece[:, pl.ds(at, depth)].astype(F32)
            square = wide * wide
            lanes = square[:, :128]
            for left in range(128, depth, 128):
                lanes = lanes + square[:, left : left + 128]
            squares[...] += lanes
            scaled = (wide * gain_ref[:, deep]).astype(BF16)
            left = 0
            for weight in weights:
                columns = slice(left, left + weight.shape[1])
                sums[:, columns] += jnp.dot(
                    scaled, weight[deep, :], preferred_element_type=F32
                )
                left += weight.shape[1]
            return carry

        lax.fori_loop(0, width // depth, add_part, 0)
    if final:
        mean = jnp.sum(squares[...], axis=1, keepdims=True) / (shards * width)
        scale = lax.rsqrt(mean + 1e-05)
        turned = sums.shape[1] - weights[-1].shape[1]
        for left in range(0, sums.shape[1], HEAD_SIZE):
            columns = slice(left, left + HEAD_SIZE)
            head = sums[:, columns] * scale
            if left < turned:
                head = head * cosine_ref[...] + pltpu.roll(
                    head, HEAD_SIZE // 2, 1
                ) * sine_ref[...]
            out_ref[:, columns] = head.astype(BF16)


def project(final, shards, masks, pieces, gain, weights, carried, tables):
    rows = pieces[0].shape[0]
    columns = sum(weight.shape[1] for weight in weights)
    operands = [*pieces, gain, *weights, *carried, *tables]
    sums = (rows, columns), (rows, 128)
    if final:
        out_shape = [jax.ShapeDtypeStruct((rows, columns), BF16)]
        scratch = [pltpu.VMEM(shape, F32) for shape in sums]
    else:
        out_shape = [jax.ShapeDtypeStruct(shape, F32) for shape in sums]
        scratch = []
    vmem = pl.BlockSpec(memory_space=pltpu.VMEM)
    return pl.pallas_call(
        functools.partial(project_kernel, masks, bool(carried), final, shards),
        in_specs=[vmem] * len(operands),
        out_specs=[vmem] * len(out_shape),
        out_shape=out_shape,
        scratch_shapes=scratch,
        compiler_params=pltpu.CompilerParams(vmem_limit_bytes=6 * MEBI),
        name="project",
    )(*operands)


def attend_kernel(
    chips, groups, known, prior, query_width, key_width, lengths_ref, plan_ref, *refs
):
    blocks, refs = refs[: -13 if prior else -11], refs[-11:]
    attended_out, cache_out, token_ref, attended_ref, cache_ref, rows_ref, queries_ref = refs[:7]
    scores_ref, top_ref, sems, out_sems = refs[7:]
    token_ref[...] = jnp.zeros_like(token_ref)
    workers = 2 * chips
    me = lax.axis_index("req")
    chip, core = lax.div(me, 2), lax.rem(me, 2)
    slots = cache_ref.shape[1]
    spans = slots // SPAN
    total = workers * sum(sum(sizes) for _, sizes in groups)
    end = needed = jnp.int32(0)
    for other in range(workers):
        end = end + lengths_ref[other]
        needed = jnp.where(end <= prior, end, needed)
    copies = []
    for group, (bases, sizes) in enumerate(groups):
        for hop in range(chips):
            source = lax.rem(chip - hop + chips, chips) * 2
            for twin in range(2):
                owner = source + (core if twin == 0 else 1 - core)
                block = blocks[(group * chips + hop) * 2 + twin]
                first = 0
                for base, rows in zip(bases, sizes):
                    at = pl.multiple_of(base + owner * rows, ALIGN)
                    for columns, least in (
                        (slice(query_width, None), needed),
                        (slice(0, query_width), prior - SPAN - ALIGN),
                    ):
                        copy = pltpu.make_async_copy(
                            block.at[pl.ds(first, rows), columns],
                            rows_ref.at[pl.ds(at, rows), columns],
                            sems.at[len(copies)],
                        )
                        copies.append((at + rows > least, copy))
                    first += rows
    for wanted, copy in copies:

        @pl.when(wanted)
        def _():
            copy.start()

    rows_ref[total:, :] = jnp.zeros((rows_ref.shape[0] - total, rows_ref.shape[1]), BF16)
    for wanted, copy in copies:

        @pl.when(wanted)
        def _():
            copy.wait()

    def window(row, columns):
        first = pl.multiple_of(lax.div(row, ALIGN) * ALIGN, ALIGN)
        shape = (SPAN, 2 * SPAN)
        hot = (iota(shape, 1) == iota(shape, 0) + (row - first)).astype(BF16)
        return jnp.dot(
            hot, rows_ref[pl.ds(first, 2 * SPAN), columns], preferred_element_type=F32
        )

    own_start, own_length = run_of(lengths_ref, me, workers)
    mine = (own_start + own_length <= known) & (own_start + own_length > prior)
    cache_copy = pltpu.make_async_copy(cache_ref, cache_out, out_sems.at[spans])

    @pl.when(mine)
    def _():
        def step(part, carry):
            at = pl.multiple_of(part * SPAN, SPAN)

            @pl.when(at < own_length)
            def _():
                picked = window(own_start + at, slice(query_width, query_width + 2 * key_width))
                live = at + iota(picked.shape, 0) < own_length
                picked = jnp.where(live, picked, 0.0).astype(BF16)
                cache_ref[0, pl.ds(at, SPAN), :] = picked[:, :key_width]
                cache_ref[1, pl.ds(at, SPAN), :] = picked[:, key_width:]

            @pl.when(at >= own_length)
            def _():
                empty = jnp.zeros((SPAN, key_width), BF16)
                cache_ref[0, pl.ds(at, SPAN), :] = empty
                cache_ref[1, pl.ds(at, SPAN), :] = empty

            return carry

        lax.fori_loop(0, spans, step, 0)
        cache_copy.start()

    heads, key_heads = query_width // HEAD_SIZE, key_width // HEAD_SIZE
    group = heads // key_heads
    factor = math.log2(math.e) / math.sqrt(HEAD_SIZE)
    tall = group * SPAN

    def span_of(slot):
        span = plan_ref[me * spans + slot]
        start, length = run_of(lengths_ref, lax.div(span, spans), workers)
        offset = lax.rem(span, spans) * SPAN
        dead = offset >= length
        needed = start + jnp.minimum(offset + SPAN, length)
        due = jnp.logical_not(dead) & (needed <= known) & (needed > prior)
        return start, length, offset, dead, due

    def result(slot):
        rows = pl.ds(pl.multiple_of(slot * SPAN, SPAN), SPAN)
        return pltpu.make_async_copy(
            attended_ref.at[rows, :], attended_out.at[rows, :], out_sems.at[slot]
        )

    def attend_slot(slot, carry):
        start, length, offset, dead, due = span_of(slot)
        out_rows = pl.ds(pl.multiple_of(slot * SPAN, SPAN), SPAN)

        if not prior:

            @pl.when(dead)
            def _():
                attended_ref[out_rows, :] = jnp.zeros((SPAN, query_width), BF16)
                result(slot).start()

        @pl.when(due)
        def _():
            queries = window(start + offset, slice(0, query_width)).astype(BF16)
            for head in range(heads):
                at = head % group * SPAN
                queries_ref[head // group, at : at + SPAN, :] = queries[
                    :, head * HEAD_SIZE : (head + 1) * HEAD_SIZE
                ]
            first = pl.multiple_of(lax.div(start, ALIGN) * ALIGN, ALIGN)
            shift = start - first
            reach = shift + jnp.minimum(offset + SPAN, length)
            tiles = lax.div(reach + TILE - 1, TILE)

            def columns(at, head):
                return slice(at + head * HEAD_SIZE, at + (head + 1) * HEAD_SIZE)

            def tile_rows(tile):
                return pl.ds(pl.multiple_of(first + tile * TILE, ALIGN), TILE)

            top_ref[...] = jnp.full(top_ref.shape, -1e30, F32)

            def score(tile, carry):
                key_pos = tile * TILE + iota((SPAN, TILE), 1) - shift
                query_pos = offset + iota((SPAN, TILE), 0)
                allowed = (key_pos >= 0) & (key_pos <= query_pos) & (key_pos < length)
                bias = jnp.where(allowed, 0.0, -1e30)
                bias = jnp.concatenate([bias] * group, axis=0)
                for head in range(key_heads):
                    scores = lax.dot_general(
                        queries_ref[head],
                        rows_ref[tile_rows(tile), columns(query_width, head)],
                        (((1,), (1,)), ((), ())),
                        preferred_element_type=F32,
                    )
                    scores = scores + bias
                    scores_ref[head, tile] = scores
                    top_ref[head] = jnp.maximum(top_ref[head], scores)
                return carry

            lax.fori_loop(0, tiles, score, 0)
            tops = [jnp.max(top_ref[head], axis=1, keepdims=True) for head in range(key_heads)]

            def mix(tile, carry):
                ones = jnp.ones((TILE, HEAD_SIZE), BF16)
                totals = []
                for head in range(key_heads):
                    weights = jnp.exp2((scores_ref[head, tile] - tops[head]) * factor)
                    values = rows_ref[tile_rows(tile), columns(query_width + key_width, head)]
                    values = jnp.concatenate([values, ones], axis=1)
                    totals.append(
                        carry[head]
                        + jnp.dot(weights.astype(BF16), values, preferred_element_type=F32)
                    )
                return tuple(totals)

            empty = jnp.zeros((tall, 2 * HEAD_SIZE), F32)
            mixed = lax.fori_loop(0, tiles, mix, (empty,) * key_heads)
            live = offset + iota((SPAN, HEAD_SIZE), 0) < length
            for head in range(heads):
                at = head % group * SPAN
                part = mixed[head // group][at : at + SPAN]
                part = part[:, :HEAD_SIZE] / part[:, HEAD_SIZE:]
                attended_ref[out_rows, columns(0, head)] = jnp.where(live, part, 0.0).astype(BF16)

            result(slot).start()

        return carry

    lax.fori_loop(0, spans, attend_slot, 0)

    def finish(slot, carry):
        _, _, _, dead, due = span_of(slot)

        @pl.when(due if prior else due | dead)
        def _():
            result(slot).wait()

        return carry

    lax.fori_loop(0, spans, finish, 0)

    @pl.when(mine)
    def _():
        cache_copy.wait()


def attend(chips, groups, known, prior, widths, slots, lengths, plan, blocks, outputs):
    query_width, key_width = widths
    width = query_width + 2 * key_width
    total = 2 * chips * sum(sum(sizes) for _, sizes in groups)
    copies = 4 * chips * sum(len(sizes) for _, sizes in groups)
    key_heads, tall = key_width // HEAD_SIZE, query_width // key_width * SPAN
    at = 2 + len(blocks)
    return pl.pallas_call(
        functools.partial(attend_kernel, chips, groups, known, prior, query_width, key_width),
        in_specs=[pl.BlockSpec(memory_space=pltpu.SMEM)] * 2
        + [pl.BlockSpec(memory_space=pl.ANY)] * (len(blocks) + len(outputs)),
        out_specs=[pl.BlockSpec(memory_space=pl.ANY)] * 2
        + [pl.BlockSpec(memory_space=pltpu.VMEM)],
        out_shape=[
            jax.ShapeDtypeStruct((slots, query_width), BF16),
            jax.ShapeDtypeStruct((2, slots, key_width), BF16),
            jax.ShapeDtypeStruct((8, 128), F32),
        ],
        input_output_aliases={at + index: index for index in range(len(outputs))},
        scratch_shapes=[
            pltpu.VMEM((slots, query_width), BF16),
            pltpu.VMEM((2, slots, key_width), BF16),
            pltpu.VMEM((total + TILE + ALIGN, width), BF16),
            pltpu.VMEM((key_heads, tall, HEAD_SIZE), BF16),
            pltpu.VMEM((key_heads, slots // TILE + 1, tall, TILE), F32),
            pltpu.VMEM((key_heads, tall, TILE), F32),
            pltpu.SemaphoreType.DMA((copies,)),
            pltpu.SemaphoreType.DMA((slots // SPAN + 1,)),
        ],
        compiler_params=pltpu.CompilerParams(vmem_limit_bytes=16 * MEBI),
        name="attend",
    )(lengths, plan, *blocks, *outputs)


def shift_chips(value, hop, chips):
    pairs = [(2 * x + c, 2 * ((x + hop) % chips) + c) for x in range(chips) for c in range(2)]
    return lax.ppermute(value, "req", pairs)


def swap_cores(value, chips):
    return lax.ppermute(value, "req", [(d, d ^ 1) for d in range(2 * chips)])


def local(
    chips, shards, tokens, norm_gain, w_query, key_weight, value_weight, lengths, plan
):
    workers = 2 * chips
    slots = tokens.shape[0]
    live = slots // 2
    sizes = [live * share // sum(SHARES) // ALIGN * ALIGN for share in SHARES]
    sizes[-1] = live - sum(sizes[:-1])
    bases = [workers * sum(sizes[:chunk]) for chunk in range(len(sizes))]
    weights = [w_query, key_weight, value_weight]
    gain = norm_gain.astype(F32).reshape(1, -1)
    halfway = HEAD_SIZE // 2
    frequency = np.exp(-np.arange(halfway) * 2.0 / HEAD_SIZE * math.log(500000.0))
    frequency = jnp.asarray(np.tile(frequency, 2)[None, :], F32)

    twin = swap_cores(tokens, chips)
    first = deal(chips, bases[:1], sizes[:1], lengths, [tokens], [False])
    dealt = [
        *deal(chips, bases[:1], sizes[:1], lengths, [twin], [True], first),
        *deal(chips, bases[1:], sizes[1:], lengths, [tokens, twin], [False, True]),
    ]
    homes, aways = dealt[::2], dealt[1::2]
    routes, masks = routes_of(shards)
    direct = [at + 1 for at, (source, _) in enumerate(routes) if source == 0]
    kinds = {"first": [0, *direct]}
    kinds["late"] = [piece for piece in range(len(masks)) if piece not in kinds["first"]]
    relayed = [piece for piece in direct if piece in {source for source, _ in routes}]

    groups = [([base], [rows]) for base, rows in zip(bases, sizes)]
    widths = w_query.shape[1], key_weight.shape[1]

    def add(kind, chunk, carried=()):
        pieces = [lines[chunk][piece] for piece in kinds[kind]]
        final = kind == "late"
        turned = turns[chunk] if final else ()
        offsets = [masks[piece] for piece in kinds[kind]]
        return project(final, shards, offsets, pieces, gain, weights, carried, turned)

    def from_chips(block):
        return [shift_chips(block, hop, chips) for hop in range(1, chips)]

    def all_blocks(block, arrived):
        return [leaf for piece in (block, *arrived) for leaf in (piece, swap_cores(piece, chips))]

    def start(line, group):
        for index, (source, distance) in enumerate(routes):
            if index + 1 in group:
                pairs = [(at, at ^ distance) for at in range(shards)]
                line[index + 1] = lax.ppermute(line[source], "tp", pairs)

    lines, own, sent = [], [], []
    last = len(sizes) - 1

    def finish(chunk):
        own.append(add("late", chunk, add("first", chunk))[0])
        sent.append(from_chips(own[-1]))

    def fence(chunk, block):
        passed, anchors = [], []
        if chunk:
            before = lines[chunk - 1]
            passed = [before[piece] for piece in relayed]
            anchors += [before[piece] for piece in direct if piece not in relayed]
        if chunk == 1:
            weights[0], token = load(w_query, lines[0][0])
            anchors.append(token)
        if 1 < chunk <= last:
            finish(chunk - 2)
            anchors.append(own[-1])
        if chunk > 2:
            anchors += sent[chunk - 3]
        if passed:
            passed = after([*passed, *block], anchors)
            before.update(zip(relayed, passed))
            block = passed[len(relayed) :]
        return block

    for chunk in range(last + 1):
        arrived = [shift_chips(aways[chunk][hop - 1], hop, chips) for hop in range(1, chips)]
        later = aways[chunk + 1 : chunk + 2]
        block, aways[chunk + 1 : chunk + 2] = merge(homes[chunk], arrived, later)
        lines.append({0: fence(chunk, [block])[0]})
        if chunk:
            start(lines[-2], kinds["late"])
        start(lines[-1], direct)
        if chunk == 1:
            turns = angles(groups, lengths, frequency, lines[1][0])
    fence(last + 1, [])
    start(lines[-1], kinds["late"])
    finish(last - 1)
    sums = list(add("first", last))
    blocks = []
    for at in range(last - 1):
        blocks += all_blocks(own[at], after(sent[at], own[at + 1 : at + 2]))
    sums[1:] = after(sums[1:], blocks[: 2 * chips])
    own.append(add("late", last, sums)[0])
    blocks += all_blocks(own[last - 1], after(sent[last - 1], own[last:]))
    sent.append(from_chips(own[last]))
    known = workers * sum(sizes[:-1])
    common = widths, slots, lengths, plan
    *outputs, token = attend(chips, groups[:-1], known, 0, *common, blocks, ())
    blocks += all_blocks(own[last], after(sent[last], [token]))
    return tuple(attend(chips, groups, workers * live, known, *common, blocks, outputs)[:2])


def solution(mesh):
    placed = (
        P(("groups", "req"), "tp"),
        P(),
        P(None, "tp"),
        P(None, "tp"),
        P(None, "tp"),
        P("groups"),
        P("groups"),
    )
    return jax.shard_map(
        functools.partial(local, mesh.shape["req"] // 2, mesh.shape["tp"]),
        mesh=mesh,
        in_specs=placed,
        out_specs=(P(("groups", "req"), "tp"), P(None, ("groups", "req"), "tp")),
        check_vma=False,
    )
```

```python
import functools
import math

import jax
import jax.numpy as jnp
import numpy as np
from jax import lax
from jax.experimental import pallas as pl
from jax.experimental.pallas import tpu as pltpu
from jax.sharding import PartitionSpec as P

HEAD_SIZE = 128
SPAN = 128
ALIGN = 16
TILE = 2 * SPAN
SHARES = (3, 5, 5, 3)
DEPTH = 1024
MEBI = 1024 * 1024
F32, BF16 = jnp.float32, jnp.bfloat16


def run_of(lengths_ref, request, count):
    start = jnp.int32(0)
    length = jnp.int32(0)
    for other in range(count):
        amount = lengths_ref[other]
        start = start + jnp.where(other < request, amount, 0)
        length = jnp.where(other == request, amount, length)
    return start, length


def iota(shape, dimension):
    return lax.broadcasted_iota(jnp.int32, shape, dimension)


def deal_kernel(chips, bases, sizes, twins, lengths_ref, *refs):
    me = lax.axis_index("req")
    chip, core = lax.div(me, 2), lax.rem(me, 2)
    sources, refs = refs[: len(twins)], refs[len(twins) :]
    count = 2 * len(sizes)
    priors, out_refs = refs[:-count], refs[-count:]
    requests = [me + 1 - 2 * core if twin else me for twin in twins]
    runs = [run_of(lengths_ref, request, 2 * chips) for request in requests]
    slots = sources[0].shape[0]
    total = None
    for (start, length), source in zip(runs, sources):
        hots = []
        for base, rows in zip(bases, sizes):
            for hop in range(chips):
                target = lax.rem(chip + hop, chips) * 2 + core
                number = base + target * rows + iota((rows, slots), 0)
                slot = iota((rows, slots), 1)
                hot = (number - start == slot) & (slot < length)
                hots.append(hot.astype(F32).astype(BF16))
        hot = jnp.concatenate(hots, axis=0) if len(hots) > 1 else hots[0]
        part = jnp.dot(hot, source[...], preferred_element_type=F32)
        total = part if total is None else total + part
    total = total.astype(BF16)
    at = 0
    for chunk, rows in enumerate(sizes):
        for hop in range(chips):
            picked = total[at : at + rows]
            at += rows
            if priors:
                prior = priors[2 * chunk + 1][hop - 1] if hop else priors[2 * chunk][...]
                picked = picked + prior
            if hop:
                out_refs[2 * chunk + 1][hop - 1] = picked
            else:
                out_refs[2 * chunk][...] = picked


def deal(chips, bases, sizes, lengths, sources, twins, priors=()):
    slots, width = sources[0].shape
    block = min(1024, width)
    out_specs, out_shape = [], []
    for rows in sizes:
        out_specs += [
            pl.BlockSpec((rows, block), lambda i: (0, i)),
            pl.BlockSpec((chips - 1, rows, block), lambda i: (0, 0, i)),
        ]
        out_shape += [
            jax.ShapeDtypeStruct((rows, width), BF16),
            jax.ShapeDtypeStruct((chips - 1, rows, width), BF16),
        ]
    return pl.pallas_call(
        functools.partial(deal_kernel, chips, bases, sizes, twins),
        grid=(width // block,),
        in_specs=[pl.BlockSpec(memory_space=pltpu.SMEM)]
        + [pl.BlockSpec((slots, block), lambda i: (0, i)) for _ in sources]
        + (out_specs if priors else []),
        out_specs=out_specs,
        out_shape=out_shape,
        compiler_params=pltpu.CompilerParams(vmem_limit_bytes=10 * MEBI),
        name="deal",
    )(lengths, *sources, *priors)


def merge_kernel(count, passed, home_ref, *refs):
    total = home_ref[...]
    for ref in refs[:count]:
        total = total + ref[...]
    refs[len(refs) - 1 - passed][...] = total


def merge(home, arrived, later):
    count = len(arrived)
    vmem, anywhere = pl.BlockSpec(memory_space=pltpu.VMEM), pl.BlockSpec(memory_space=pl.ANY)
    block, *later = pl.pallas_call(
        functools.partial(merge_kernel, count, len(later)),
        in_specs=[vmem] * (count + 1) + [anywhere] * len(later),
        out_specs=[vmem] + [anywhere] * len(later),
        out_shape=[jax.ShapeDtypeStruct(leaf.shape, leaf.dtype) for leaf in (home, *later)],
        input_output_aliases={count + 1 + at: 1 + at for at in range(len(later))},
        compiler_params=pltpu.CompilerParams(vmem_limit_bytes=4 * MEBI),
        name="merge",
    )(home, *arrived, *later)
    return block, later


def after(arrays, anchors):
    def kernel(*refs):
        pass

    anywhere = pl.BlockSpec(memory_space=pl.ANY)
    return pl.pallas_call(
        kernel,
        in_specs=[anywhere] * (len(arrays) + len(anchors)),
        out_specs=[anywhere] * len(arrays),
        out_shape=[jax.ShapeDtypeStruct(leaf.shape, leaf.dtype) for leaf in arrays],
        input_output_aliases={at: at for at in range(len(arrays))},
        compiler_params=pltpu.CompilerParams(vmem_limit_bytes=MEBI),
        name="after",
    )(*arrays, *anchors)


def routes_of(shards):
    routes, masks, distance = [], [0], shards // 2
    while distance:
        for source in range(len(masks)):
            routes.append((source, distance))
            masks.append(masks[source] ^ distance)
        distance //= 2
    return routes, masks


def angles_kernel(groups, members, lengths_ref, frequency_ref, anchor_ref, *out_refs):
    me = lax.axis_index("req")
    for group, (bases, sizes) in enumerate(groups):
        first = 0
        for base, rows in zip(bases, sizes):
            number = base + me * rows + iota((rows, HEAD_SIZE), 0)
            start = jnp.zeros((rows, HEAD_SIZE), jnp.int32)
            before = jnp.int32(0)
            for other in range(members):
                before = before + lengths_ref[other]
                start = jnp.where(number >= before, before, start)
            angle = (number - start).astype(F32) * frequency_ref[...]
            sine = jnp.sin(angle)
            lower = iota((rows, HEAD_SIZE), 1) < HEAD_SIZE // 2
            out_refs[2 * group][first : first + rows, :] = jnp.cos(angle)
            out_refs[2 * group + 1][first : first + rows, :] = jnp.where(lower, -sine, sine)
            first += rows


def angles(groups, lengths, frequency, anchor):
    shapes = [
        jax.ShapeDtypeStruct((sum(sizes), HEAD_SIZE), F32) for _, sizes in groups for _ in range(2)
    ]
    vmem = pl.BlockSpec(memory_space=pltpu.VMEM)
    tables = pl.pallas_call(
        functools.partial(angles_kernel, groups, lengths.shape[0]),
        in_specs=[
            pl.BlockSpec(memory_space=pltpu.SMEM),
            vmem,
            pl.BlockSpec(memory_space=pl.ANY),
        ],
        out_specs=[vmem] * len(shapes),
        out_shape=shapes,
        compiler_params=pltpu.CompilerParams(vmem_limit_bytes=4 * MEBI),
        name="angles",
    )(lengths, frequency, anchor)
    return [tables[at : at + 2] for at in range(0, len(tables), 2)]


def load(weight, anchor):
    parts = 8
    depth = weight.shape[0] // parts

    def kernel(weight_ref, anchor_ref, out_ref, token_ref, sems):
        copies = [
            pltpu.make_async_copy(
                weight_ref.at[pl.ds(part * depth, depth), :],
                out_ref.at[pl.ds(part * depth, depth), :],
                sems.at[part],
            )
            for part in range(parts)
        ]
        for copy in copies:
            copy.start()
        token_ref[...] = jnp.zeros_like(token_ref)
        for copy in copies:
            copy.wait()

    vmem, anywhere = pl.BlockSpec(memory_space=pltpu.VMEM), pl.BlockSpec(memory_space=pl.ANY)
    return pl.pallas_call(
        kernel,
        in_specs=[anywhere, anywhere],
        out_specs=[vmem, vmem],
        out_shape=[
            jax.ShapeDtypeStruct(weight.shape, weight.dtype),
            jax.ShapeDtypeStruct((8, 128), F32),
        ],
        scratch_shapes=[pltpu.SemaphoreType.DMA((parts,))],
        compiler_params=pltpu.CompilerParams(vmem_limit_bytes=2 * MEBI),
        name="load",
    )(pltpu.with_memory_space_constraint(weight, pltpu.HBM), anchor)


def project_kernel(masks, carries, final, shards, *refs):
    pieces, refs = refs[: len(masks)], refs[len(masks) :]
    (gain_ref, *weights), refs = refs[:4], refs[4:]
    if carries:
        sums_in, squares_in, *refs = refs
    if final:
        cosine_ref, sine_ref, out_ref, *refs = refs
    sums, squares = refs
    width = pieces[0].shape[1]
    depth = min(DEPTH, width)
    sums[...] = sums_in[...] if carries else jnp.zeros_like(sums)
    squares[...] = squares_in[...] if carries else jnp.zeros_like(squares)
    for piece, mask in zip(pieces, masks):
        shard = lax.bitwise_xor(lax.axis_index("tp"), jnp.int32(mask))

        def add_part(part, carry):
            at = pl.multiple_of(part * depth, depth)
            deep = pl.ds(pl.multiple_of(shard * width + at, depth), depth)
            wide = piece[:, pl.ds(at, depth)].astype(F32)
            square = wide * wide
            lanes = square[:, :128]
            for left in range(128, depth, 128):
                lanes = lanes + square[:, left : left + 128]
            squares[...] += lanes
            scaled = (wide * gain_ref[:, deep]).astype(BF16)
            left = 0
            for weight in weights:
                columns = slice(left, left + weight.shape[1])
                sums[:, columns] += jnp.dot(
                    scaled, weight[deep, :], preferred_element_type=F32
                )
                left += weight.shape[1]
            return carry

        lax.fori_loop(0, width // depth, add_part, 0)
    if final:
        mean = jnp.sum(squares[...], axis=1, keepdims=True) / (shards * width)
        scale = lax.rsqrt(mean + 1e-05)
        turned = sums.shape[1] - weights[-1].shape[1]
        for left in range(0, sums.shape[1], HEAD_SIZE):
            columns = slice(left, left + HEAD_SIZE)
            head = sums[:, columns] * scale
            if left < turned:
                head = head * cosine_ref[...] + pltpu.roll(
                    head, HEAD_SIZE // 2, 1
                ) * sine_ref[...]
            out_ref[:, columns] = head.astype(BF16)


def project(final, shards, masks, pieces, gain, weights, carried, tables):
    rows = pieces[0].shape[0]
    columns = sum(weight.shape[1] for weight in weights)
    operands = [*pieces, gain, *weights, *carried, *tables]
    sums = (rows, columns), (rows, 128)
    if final:
        out_shape = [jax.ShapeDtypeStruct((rows, columns), BF16)]
        scratch = [pltpu.VMEM(shape, F32) for shape in sums]
    else:
        out_shape = [jax.ShapeDtypeStruct(shape, F32) for shape in sums]
        scratch = []
    vmem = pl.BlockSpec(memory_space=pltpu.VMEM)
    return pl.pallas_call(
        functools.partial(project_kernel, masks, bool(carried), final, shards),
        in_specs=[vmem] * len(operands),
        out_specs=[vmem] * len(out_shape),
        out_shape=out_shape,
        scratch_shapes=scratch,
        compiler_params=pltpu.CompilerParams(vmem_limit_bytes=6 * MEBI),
        name="project",
    )(*operands)


def attend_kernel(
    chips, groups, known, prior, query_width, key_width, lengths_ref, plan_ref, *refs
):
    blocks, refs = refs[: -13 if prior else -11], refs[-11:]
    attended_out, cache_out, token_ref, attended_ref, cache_ref, rows_ref, queries_ref = refs[:7]
    scores_ref, top_ref, sems, out_sems = refs[7:]
    token_ref[...] = jnp.zeros_like(token_ref)
    workers = 2 * chips
    me = lax.axis_index("req")
    chip, core = lax.div(me, 2), lax.rem(me, 2)
    slots = cache_ref.shape[1]
    spans = slots // SPAN
    total = workers * sum(sum(sizes) for _, sizes in groups)
    end = needed = jnp.int32(0)
    for other in range(workers):
        end = end + lengths_ref[other]
        needed = jnp.where(end <= prior, end, needed)
    copies = []
    for group, (bases, sizes) in enumerate(groups):
        for hop in range(chips):
            source = lax.rem(chip - hop + chips, chips) * 2
            for twin in range(2):
                owner = source + (core if twin == 0 else 1 - core)
                block = blocks[(group * chips + hop) * 2 + twin]
                first = 0
                for base, rows in zip(bases, sizes):
                    at = pl.multiple_of(base + owner * rows, ALIGN)
                    for columns, least in (
                        (slice(query_width, None), needed),
                        (slice(0, query_width), prior - SPAN - ALIGN),
                    ):
                        copy = pltpu.make_async_copy(
                            block.at[pl.ds(first, rows), columns],
                            rows_ref.at[pl.ds(at, rows), columns],
                            sems.at[len(copies)],
                        )
                        copies.append((at + rows > least, copy))
                    first += rows
    for wanted, copy in copies:

        @pl.when(wanted)
        def _():
            copy.start()

    rows_ref[total:, :] = jnp.zeros((rows_ref.shape[0] - total, rows_ref.shape[1]), BF16)
    for wanted, copy in copies:

        @pl.when(wanted)
        def _():
            copy.wait()

    def window(row, columns):
        first = pl.multiple_of(lax.div(row, ALIGN) * ALIGN, ALIGN)
        shape = (SPAN, 2 * SPAN)
        hot = (iota(shape, 1) == iota(shape, 0) + (row - first)).astype(BF16)
        return jnp.dot(
            hot, rows_ref[pl.ds(first, 2 * SPAN), columns], preferred_element_type=F32
        )

    own_start, own_length = run_of(lengths_ref, me, workers)
    mine = (own_start + own_length <= known) & (own_start + own_length > prior)
    cache_copy = pltpu.make_async_copy(cache_ref, cache_out, out_sems.at[spans])

    @pl.when(mine)
    def _():
        def step(part, carry):
            at = pl.multiple_of(part * SPAN, SPAN)

            @pl.when(at < own_length)
            def _():
                picked = window(own_start + at, slice(query_width, query_width + 2 * key_width))
                live = at + iota(picked.shape, 0) < own_length
                picked = jnp.where(live, picked, 0.0).astype(BF16)
                cache_ref[0, pl.ds(at, SPAN), :] = picked[:, :key_width]
                cache_ref[1, pl.ds(at, SPAN), :] = picked[:, key_width:]

            @pl.when(at >= own_length)
            def _():
                empty = jnp.zeros((SPAN, key_width), BF16)
                cache_ref[0, pl.ds(at, SPAN), :] = empty
                cache_ref[1, pl.ds(at, SPAN), :] = empty

            return carry

        lax.fori_loop(0, spans, step, 0)
        cache_copy.start()

    heads, key_heads = query_width // HEAD_SIZE, key_width // HEAD_SIZE
    group = heads // key_heads
    factor = math.log2(math.e) / math.sqrt(HEAD_SIZE)
    tall = group * SPAN

    def span_of(slot):
        span = plan_ref[me * spans + slot]
        start, length = run_of(lengths_ref, lax.div(span, spans), workers)
        offset = lax.rem(span, spans) * SPAN
        dead = offset >= length
        needed = start + jnp.minimum(offset + SPAN, length)
        due = jnp.logical_not(dead) & (needed <= known) & (needed > prior)
        return start, length, offset, dead, due

    def result(slot):
        rows = pl.ds(pl.multiple_of(slot * SPAN, SPAN), SPAN)
        return pltpu.make_async_copy(
            attended_ref.at[rows, :], attended_out.at[rows, :], out_sems.at[slot]
        )

    def attend_slot(slot, carry):
        start, length, offset, dead, due = span_of(slot)
        out_rows = pl.ds(pl.multiple_of(slot * SPAN, SPAN), SPAN)

        if not prior:

            @pl.when(dead)
            def _():
                attended_ref[out_rows, :] = jnp.zeros((SPAN, query_width), BF16)
                result(slot).start()

        @pl.when(due)
        def _():
            queries = window(start + offset, slice(0, query_width)).astype(BF16)
            for head in range(heads):
                at = head % group * SPAN
                queries_ref[head // group, at : at + SPAN, :] = queries[
                    :, head * HEAD_SIZE : (head + 1) * HEAD_SIZE
                ]
            first = pl.multiple_of(lax.div(start, ALIGN) * ALIGN, ALIGN)
            shift = start - first
            reach = shift + jnp.minimum(offset + SPAN, length)
            tiles = lax.div(reach + TILE - 1, TILE)

            def columns(at, head):
                return slice(at + head * HEAD_SIZE, at + (head + 1) * HEAD_SIZE)

            def tile_rows(tile):
                return pl.ds(pl.multiple_of(first + tile * TILE, ALIGN), TILE)

            top_ref[...] = jnp.full(top_ref.shape, -1e30, F32)

            def score(tile, carry):
                key_pos = tile * TILE + iota((SPAN, TILE), 1) - shift
                query_pos = offset + iota((SPAN, TILE), 0)
                allowed = (key_pos >= 0) & (key_pos <= query_pos) & (key_pos < length)
                bias = jnp.where(allowed, 0.0, -1e30)
                bias = jnp.concatenate([bias] * group, axis=0)
                for head in range(key_heads):
                    scores = lax.dot_general(
                        queries_ref[head],
                        rows_ref[tile_rows(tile), columns(query_width, head)],
                        (((1,), (1,)), ((), ())),
                        preferred_element_type=F32,
                    )
                    scores = scores + bias
                    scores_ref[head, tile] = scores
                    top_ref[head] = jnp.maximum(top_ref[head], scores)
                return carry

            lax.fori_loop(0, tiles, score, 0)
            tops = [jnp.max(top_ref[head], axis=1, keepdims=True) for head in range(key_heads)]

            def mix(tile, carry):
                ones = jnp.ones((TILE, HEAD_SIZE), BF16)
                totals = []
                for head in range(key_heads):
                    weights = jnp.exp2((scores_ref[head, tile] - tops[head]) * factor)
                    values = rows_ref[tile_rows(tile), columns(query_width + key_width, head)]
                    values = jnp.concatenate([values, ones], axis=1)
                    totals.append(
                        carry[head]
                        + jnp.dot(weights.astype(BF16), values, preferred_element_type=F32)
                    )
                return tuple(totals)

            empty = jnp.zeros((tall, 2 * HEAD_SIZE), F32)
            mixed = lax.fori_loop(0, tiles, mix, (empty,) * key_heads)
            live = offset + iota((SPAN, HEAD_SIZE), 0) < length
            for head in range(heads):
                at = head % group * SPAN
                part = mixed[head // group][at : at + SPAN]
                part = part[:, :HEAD_SIZE] / part[:, HEAD_SIZE:]
                attended_ref[out_rows, columns(0, head)] = jnp.where(live, part, 0.0).astype(BF16)

            result(slot).start()

        return carry

    lax.fori_loop(0, spans, attend_slot, 0)

    def finish(slot, carry):
        _, _, _, dead, due = span_of(slot)

        @pl.when(due if prior else due | dead)
        def _():
            result(slot).wait()

        return carry

    lax.fori_loop(0, spans, finish, 0)

    @pl.when(mine)
    def _():
        cache_copy.wait()


def attend(chips, groups, known, prior, widths, slots, lengths, plan, blocks, outputs):
    query_width, key_width = widths
    width = query_width + 2 * key_width
    total = 2 * chips * sum(sum(sizes) for _, sizes in groups)
    copies = 4 * chips * sum(len(sizes) for _, sizes in groups)
    key_heads, tall = key_width // HEAD_SIZE, query_width // key_width * SPAN
    at = 2 + len(blocks)
    return pl.pallas_call(
        functools.partial(attend_kernel, chips, groups, known, prior, query_width, key_width),
        in_specs=[pl.BlockSpec(memory_space=pltpu.SMEM)] * 2
        + [pl.BlockSpec(memory_space=pl.ANY)] * (len(blocks) + len(outputs)),
        out_specs=[pl.BlockSpec(memory_space=pl.ANY)] * 2
        + [pl.BlockSpec(memory_space=pltpu.VMEM)],
        out_shape=[
            jax.ShapeDtypeStruct((slots, query_width), BF16),
            jax.ShapeDtypeStruct((2, slots, key_width), BF16),
            jax.ShapeDtypeStruct((8, 128), F32),
        ],
        input_output_aliases={at + index: index for index in range(len(outputs))},
        scratch_shapes=[
            pltpu.VMEM((slots, query_width), BF16),
            pltpu.VMEM((2, slots, key_width), BF16),
            pltpu.VMEM((total + TILE + ALIGN, width), BF16),
            pltpu.VMEM((key_heads, tall, HEAD_SIZE), BF16),
            pltpu.VMEM((key_heads, slots // TILE + 1, tall, TILE), F32),
            pltpu.VMEM((key_heads, tall, TILE), F32),
            pltpu.SemaphoreType.DMA((copies,)),
            pltpu.SemaphoreType.DMA((slots // SPAN + 1,)),
        ],
        compiler_params=pltpu.CompilerParams(vmem_limit_bytes=16 * MEBI),
        name="attend",
    )(lengths, plan, *blocks, *outputs)


def shift_chips(value, hop, chips):
    pairs = [(2 * x + c, 2 * ((x + hop) % chips) + c) for x in range(chips) for c in range(2)]
    return lax.ppermute(value, "req", pairs)


def swap_cores(value, chips):
    return lax.ppermute(value, "req", [(d, d ^ 1) for d in range(2 * chips)])


def local(
    chips, shards, tokens, norm_gain, w_query, key_weight, value_weight, lengths, plan
):
    workers = 2 * chips
    slots = tokens.shape[0]
    live = slots // 2
    sizes = [live * share // sum(SHARES) // ALIGN * ALIGN for share in SHARES]
    sizes[-1] = live - sum(sizes[:-1])
    bases = [workers * sum(sizes[:chunk]) for chunk in range(len(sizes))]
    weights = [w_query, key_weight, value_weight]
    gain = norm_gain.astype(F32).reshape(1, -1)
    halfway = HEAD_SIZE // 2
    frequency = np.exp(-np.arange(halfway) * 2.0 / HEAD_SIZE * math.log(500000.0))
    frequency = jnp.asarray(np.tile(frequency, 2)[None, :], F32)

    twin = swap_cores(tokens, chips)
    first = deal(chips, bases[:1], sizes[:1], lengths, [tokens], [False])
    dealt = [
        *deal(chips, bases[:1], sizes[:1], lengths, [twin], [True], first),
        *deal(chips, bases[1:], sizes[1:], lengths, [tokens, twin], [False, True]),
    ]
    homes, aways = dealt[::2], dealt[1::2]
    routes, masks = routes_of(shards)
    direct = [at + 1 for at, (source, _) in enumerate(routes) if source == 0]
    kinds = {"first": [0, *direct]}
    kinds["late"] = [piece for piece in range(len(masks)) if piece not in kinds["first"]]
    relayed = [piece for piece in direct if piece in {source for source, _ in routes}]

    groups = [([base], [rows]) for base, rows in zip(bases, sizes)]
    widths = w_query.shape[1], key_weight.shape[1]

    def add(kind, chunk, carried=()):
        pieces = [lines[chunk][piece] for piece in kinds[kind]]
        final = kind == "late"
        turned = turns[chunk] if final else ()
        offsets = [masks[piece] for piece in kinds[kind]]
        return project(final, shards, offsets, pieces, gain, weights, carried, turned)

    def from_chips(block):
        return [shift_chips(block, hop, chips) for hop in range(1, chips)]

    def all_blocks(block, arrived):
        return [leaf for piece in (block, *arrived) for leaf in (piece, swap_cores(piece, chips))]

    def start(line, group):
        for index, (source, distance) in enumerate(routes):
            if index + 1 in group:
                pairs = [(at, at ^ distance) for at in range(shards)]
                line[index + 1] = lax.ppermute(line[source], "tp", pairs)

    lines, own, sent = [], [], []
    last = len(sizes) - 1

    def finish(chunk):
        own.append(add("late", chunk, add("first", chunk))[0])
        sent.append(from_chips(own[-1]))

    def fence(chunk, block):
        passed, anchors = [], []
        if chunk:
            before = lines[chunk - 1]
            passed = [before[piece] for piece in relayed]
            anchors += [before[piece] for piece in direct if piece not in relayed]
        if chunk == 1:
            weights[0], token = load(w_query, lines[0][0])
            anchors.append(token)
        if 1 < chunk <= last:
            finish(chunk - 2)
            anchors.append(own[-1])
        if chunk > 2:
            anchors += sent[chunk - 3]
        if passed:
            passed = after([*passed, *block], anchors)
            before.update(zip(relayed, passed))
            block = passed[len(relayed) :]
        return block

    for chunk in range(last + 1):
        arrived = [shift_chips(aways[chunk][hop - 1], hop, chips) for hop in range(1, chips)]
        later = aways[chunk + 1 : chunk + 2]
        block, aways[chunk + 1 : chunk + 2] = merge(homes[chunk], arrived, later)
        lines.append({0: fence(chunk, [block])[0]})
        if chunk:
            start(lines[-2], kinds["late"])
        start(lines[-1], direct)
        if chunk == 1:
            turns = angles(groups, lengths, frequency, lines[1][0])
    fence(last + 1, [])
    start(lines[-1], kinds["late"])
    finish(last - 1)
    sums = list(add("first", last))
    blocks = []
    for at in range(last - 1):
        blocks += all_blocks(own[at], after(sent[at], own[at + 1 : at + 2]))
    sums[1:] = after(sums[1:], blocks[: 2 * chips])
    own.append(add("late", last, sums)[0])
    blocks += all_blocks(own[last - 1], after(sent[last - 1], own[last:]))
    sent.append(from_chips(own[last]))
    known = workers * sum(sizes[:-1])
    common = widths, slots, lengths, plan
    *outputs, token = attend(chips, groups[:-1], known, 0, *common, blocks, ())
    blocks += all_blocks(own[last], after(sent[last], [token]))
    return tuple(attend(chips, groups, workers * live, known, *common, blocks, outputs)[:2])


def solution(mesh):
    placed = (
        P(("groups", "req"), "tp"),
        P(),
        P(None, "tp"),
        P(None, "tp"),
        P(None, "tp"),
        P("groups"),
        P("groups"),
    )
    return jax.shard_map(
        functools.partial(local, mesh.shape["req"] // 2, mesh.shape["tp"]),
        mesh=mesh,
        in_specs=placed,
        out_specs=(P(("groups", "req"), "tp"), P(None, ("groups", "req"), "tp")),
        check_vma=False,
    )
```

```python
import functools
import math

import jax
import jax.numpy as jnp
import numpy as np
from jax import lax
from jax.experimental import pallas as pl
from jax.experimental.pallas import tpu as pltpu
from jax.sharding import PartitionSpec as P

HEAD_SIZE = 128
SPAN = 128
ALIGN = 16
TILE = 2 * SPAN
SHARES = (3, 5, 5, 3)
DEPTH = 1024
MEBI = 1024 * 1024
F32, BF16 = jnp.float32, jnp.bfloat16


def run_of(lengths_ref, request, count):
    start = jnp.int32(0)
    length = jnp.int32(0)
    for other in range(count):
        amount = lengths_ref[other]
        start = start + jnp.where(other < request, amount, 0)
        length = jnp.where(other == request, amount, length)
    return start, length


def iota(shape, dimension):
    return lax.broadcasted_iota(jnp.int32, shape, dimension)


def deal_kernel(chips, bases, sizes, twins, lengths_ref, *refs):
    me = lax.axis_index("req")
    chip, core = lax.div(me, 2), lax.rem(me, 2)
    sources, refs = refs[: len(twins)], refs[len(twins) :]
    count = 2 * len(sizes)
    priors, out_refs = refs[:-count], refs[-count:]
    requests = [me + 1 - 2 * core if twin else me for twin in twins]
    runs = [run_of(lengths_ref, request, 2 * chips) for request in requests]
    slots = sources[0].shape[0]
    total = None
    for (start, length), source in zip(runs, sources):
        hots = []
        for base, rows in zip(bases, sizes):
            for hop in range(chips):
                target = lax.rem(chip + hop, chips) * 2 + core
                number = base + target * rows + iota((rows, slots), 0)
                slot = iota((rows, slots), 1)
                hot = (number - start == slot) & (slot < length)
                hots.append(hot.astype(F32).astype(BF16))
        hot = jnp.concatenate(hots, axis=0) if len(hots) > 1 else hots[0]
        part = jnp.dot(hot, source[...], preferred_element_type=F32)
        total = part if total is None else total + part
    total = total.astype(BF16)
    at = 0
    for chunk, rows in enumerate(sizes):
        for hop in range(chips):
            picked = total[at : at + rows]
            at += rows
            if priors:
                prior = priors[2 * chunk + 1][hop - 1] if hop else priors[2 * chunk][...]
                picked = picked + prior
            if hop:
                out_refs[2 * chunk + 1][hop - 1] = picked
            else:
                out_refs[2 * chunk][...] = picked


def deal(chips, bases, sizes, lengths, sources, twins, priors=()):
    slots, width = sources[0].shape
    block = min(1024, width)
    out_specs, out_shape = [], []
    for rows in sizes:
        out_specs += [
            pl.BlockSpec((rows, block), lambda i: (0, i)),
            pl.BlockSpec((chips - 1, rows, block), lambda i: (0, 0, i)),
        ]
        out_shape += [
            jax.ShapeDtypeStruct((rows, width), BF16),
            jax.ShapeDtypeStruct((chips - 1, rows, width), BF16),
        ]
    return pl.pallas_call(
        functools.partial(deal_kernel, chips, bases, sizes, twins),
        grid=(width // block,),
        in_specs=[pl.BlockSpec(memory_space=pltpu.SMEM)]
        + [pl.BlockSpec((slots, block), lambda i: (0, i)) for _ in sources]
        + (out_specs if priors else []),
        out_specs=out_specs,
        out_shape=out_shape,
        compiler_params=pltpu.CompilerParams(vmem_limit_bytes=10 * MEBI),
        name="deal",
    )(lengths, *sources, *priors)


def merge_kernel(count, passed, home_ref, *refs):
    total = home_ref[...]
    for ref in refs[:count]:
        total = total + ref[...]
    refs[len(refs) - 1 - passed][...] = total


def merge(home, arrived, later):
    count = len(arrived)
    vmem, anywhere = pl.BlockSpec(memory_space=pltpu.VMEM), pl.BlockSpec(memory_space=pl.ANY)
    block, *later = pl.pallas_call(
        functools.partial(merge_kernel, count, len(later)),
        in_specs=[vmem] * (count + 1) + [anywhere] * len(later),
        out_specs=[vmem] + [anywhere] * len(later),
        out_shape=[jax.ShapeDtypeStruct(leaf.shape, leaf.dtype) for leaf in (home, *later)],
        input_output_aliases={count + 1 + at: 1 + at for at in range(len(later))},
        compiler_params=pltpu.CompilerParams(vmem_limit_bytes=4 * MEBI),
        name="merge",
    )(home, *arrived, *later)
    return block, later


def after(arrays, anchors):
    def kernel(*refs):
        pass

    anywhere = pl.BlockSpec(memory_space=pl.ANY)
    return pl.pallas_call(
        kernel,
        in_specs=[anywhere] * (len(arrays) + len(anchors)),
        out_specs=[anywhere] * len(arrays),
        out_shape=[jax.ShapeDtypeStruct(leaf.shape, leaf.dtype) for leaf in arrays],
        input_output_aliases={at: at for at in range(len(arrays))},
        compiler_params=pltpu.CompilerParams(vmem_limit_bytes=MEBI),
        name="after",
    )(*arrays, *anchors)


def routes_of(shards):
    routes, masks, distance = [], [0], shards // 2
    while distance:
        for source in range(len(masks)):
            routes.append((source, distance))
            masks.append(masks[source] ^ distance)
        distance //= 2
    return routes, masks


def angles_kernel(groups, members, lengths_ref, frequency_ref, anchor_ref, *out_refs):
    me = lax.axis_index("req")
    for group, (bases, sizes) in enumerate(groups):
        first = 0
        for base, rows in zip(bases, sizes):
            number = base + me * rows + iota((rows, HEAD_SIZE), 0)
            start = jnp.zeros((rows, HEAD_SIZE), jnp.int32)
            before = jnp.int32(0)
            for other in range(members):
                before = before + lengths_ref[other]
                start = jnp.where(number >= before, before, start)
            angle = (number - start).astype(F32) * frequency_ref[...]
            sine = jnp.sin(angle)
            lower = iota((rows, HEAD_SIZE), 1) < HEAD_SIZE // 2
            out_refs[2 * group][first : first + rows, :] = jnp.cos(angle)
            out_refs[2 * group + 1][first : first + rows, :] = jnp.where(lower, -sine, sine)
            first += rows


def angles(groups, lengths, frequency, anchor):
    shapes = [
        jax.ShapeDtypeStruct((sum(sizes), HEAD_SIZE), F32) for _, sizes in groups for _ in range(2)
    ]
    vmem = pl.BlockSpec(memory_space=pltpu.VMEM)
    tables = pl.pallas_call(
        functools.partial(angles_kernel, groups, lengths.shape[0]),
        in_specs=[
            pl.BlockSpec(memory_space=pltpu.SMEM),
            vmem,
            pl.BlockSpec(memory_space=pl.ANY),
        ],
        out_specs=[vmem] * len(shapes),
        out_shape=shapes,
        compiler_params=pltpu.CompilerParams(vmem_limit_bytes=4 * MEBI),
        name="angles",
    )(lengths, frequency, anchor)
    return [tables[at : at + 2] for at in range(0, len(tables), 2)]


def load(weight, anchor):
    parts = 8
    depth = weight.shape[0] // parts

    def kernel(weight_ref, anchor_ref, out_ref, token_ref, sems):
        copies = [
            pltpu.make_async_copy(
                weight_ref.at[pl.ds(part * depth, depth), :],
                out_ref.at[pl.ds(part * depth, depth), :],
                sems.at[part],
            )
            for part in range(parts)
        ]
        for copy in copies:
            copy.start()
        token_ref[...] = jnp.zeros_like(token_ref)
        for copy in copies:
            copy.wait()

    vmem, anywhere = pl.BlockSpec(memory_space=pltpu.VMEM), pl.BlockSpec(memory_space=pl.ANY)
    return pl.pallas_call(
        kernel,
        in_specs=[anywhere, anywhere],
        out_specs=[vmem, vmem],
        out_shape=[
            jax.ShapeDtypeStruct(weight.shape, weight.dtype),
            jax.ShapeDtypeStruct((8, 128), F32),
        ],
        scratch_shapes=[pltpu.SemaphoreType.DMA((parts,))],
        compiler_params=pltpu.CompilerParams(vmem_limit_bytes=2 * MEBI),
        name="load",
    )(pltpu.with_memory_space_constraint(weight, pltpu.HBM), anchor)


def project_kernel(masks, carries, final, shards, *refs):
    pieces, refs = refs[: len(masks)], refs[len(masks) :]
    (gain_ref, *weights), refs = refs[:4], refs[4:]
    if carries:
        sums_in, squares_in, *refs = refs
    if final:
        cosine_ref, sine_ref, out_ref, *refs = refs
    sums, squares = refs
    width = pieces[0].shape[1]
    depth = min(DEPTH, width)
    sums[...] = sums_in[...] if carries else jnp.zeros_like(sums)
    squares[...] = squares_in[...] if carries else jnp.zeros_like(squares)
    for piece, mask in zip(pieces, masks):
        shard = lax.bitwise_xor(lax.axis_index("tp"), jnp.int32(mask))

        def add_part(part, carry):
            at = pl.multiple_of(part * depth, depth)
            deep = pl.ds(pl.multiple_of(shard * width + at, depth), depth)
            wide = piece[:, pl.ds(at, depth)].astype(F32)
            square = wide * wide
            lanes = square[:, :128]
            for left in range(128, depth, 128):
                lanes = lanes + square[:, left : left + 128]
            squares[...] += lanes
            scaled = (wide * gain_ref[:, deep]).astype(BF16)
            left = 0
            for weight in weights:
                columns = slice(left, left + weight.shape[1])
                sums[:, columns] += jnp.dot(
                    scaled, weight[deep, :], preferred_element_type=F32
                )
                left += weight.shape[1]
            return carry

        lax.fori_loop(0, width // depth, add_part, 0)
    if final:
        mean = jnp.sum(squares[...], axis=1, keepdims=True) / (shards * width)
        scale = lax.rsqrt(mean + 1e-05)
        turned = sums.shape[1] - weights[-1].shape[1]
        for left in range(0, sums.shape[1], HEAD_SIZE):
            columns = slice(left, left + HEAD_SIZE)
            head = sums[:, columns] * scale
            if left < turned:
                head = head * cosine_ref[...] + pltpu.roll(
                    head, HEAD_SIZE // 2, 1
                ) * sine_ref[...]
            out_ref[:, columns] = head.astype(BF16)


def project(final, shards, masks, pieces, gain, weights, carried, tables):
    rows = pieces[0].shape[0]
    columns = sum(weight.shape[1] for weight in weights)
    operands = [*pieces, gain, *weights, *carried, *tables]
    sums = (rows, columns), (rows, 128)
    if final:
        out_shape = [jax.ShapeDtypeStruct((rows, columns), BF16)]
        scratch = [pltpu.VMEM(shape, F32) for shape in sums]
    else:
        out_shape = [jax.ShapeDtypeStruct(shape, F32) for shape in sums]
        scratch = []
    vmem = pl.BlockSpec(memory_space=pltpu.VMEM)
    return pl.pallas_call(
        functools.partial(project_kernel, masks, bool(carried), final, shards),
        in_specs=[vmem] * len(operands),
        out_specs=[vmem] * len(out_shape),
        out_shape=out_shape,
        scratch_shapes=scratch,
        compiler_params=pltpu.CompilerParams(vmem_limit_bytes=6 * MEBI),
        name="project",
    )(*operands)


def attend_kernel(
    chips, groups, known, prior, query_width, key_width, lengths_ref, plan_ref, *refs
):
    blocks, refs = refs[: -13 if prior else -11], refs[-11:]
    attended_out, cache_out, token_ref, attended_ref, cache_ref, rows_ref, queries_ref = refs[:7]
    scores_ref, top_ref, sems, out_sems = refs[7:]
    token_ref[...] = jnp.zeros_like(token_ref)
    workers = 2 * chips
    me = lax.axis_index("req")
    chip, core = lax.div(me, 2), lax.rem(me, 2)
    slots = cache_ref.shape[1]
    spans = slots // SPAN
    total = workers * sum(sum(sizes) for _, sizes in groups)
    end = needed = jnp.int32(0)
    for other in range(workers):
        end = end + lengths_ref[other]
        needed = jnp.where(end <= prior, end, needed)
    copies = []
    for group, (bases, sizes) in enumerate(groups):
        for hop in range(chips):
            source = lax.rem(chip - hop + chips, chips) * 2
            for twin in range(2):
                owner = source + (core if twin == 0 else 1 - core)
                block = blocks[(group * chips + hop) * 2 + twin]
                first = 0
                for base, rows in zip(bases, sizes):
                    at = pl.multiple_of(base + owner * rows, ALIGN)
                    for columns, least in (
                        (slice(query_width, None), needed),
                        (slice(0, query_width), prior - SPAN - ALIGN),
                    ):
                        copy = pltpu.make_async_copy(
                            block.at[pl.ds(first, rows), columns],
                            rows_ref.at[pl.ds(at, rows), columns],
                            sems.at[len(copies)],
                        )
                        copies.append((at + rows > least, copy))
                    first += rows
    for wanted, copy in copies:

        @pl.when(wanted)
        def _():
            copy.start()

    rows_ref[total:, :] = jnp.zeros((rows_ref.shape[0] - total, rows_ref.shape[1]), BF16)
    for wanted, copy in copies:

        @pl.when(wanted)
        def _():
            copy.wait()

    def window(row, columns):
        first = pl.multiple_of(lax.div(row, ALIGN) * ALIGN, ALIGN)
        shape = (SPAN, 2 * SPAN)
        hot = (iota(shape, 1) == iota(shape, 0) + (row - first)).astype(BF16)
        return jnp.dot(
            hot, rows_ref[pl.ds(first, 2 * SPAN), columns], preferred_element_type=F32
        )

    own_start, own_length = run_of(lengths_ref, me, workers)
    mine = (own_start + own_length <= known) & (own_start + own_length > prior)
    cache_copy = pltpu.make_async_copy(cache_ref, cache_out, out_sems.at[spans])

    @pl.when(mine)
    def _():
        def step(part, carry):
            at = pl.multiple_of(part * SPAN, SPAN)

            @pl.when(at < own_length)
            def _():
                picked = window(own_start + at, slice(query_width, query_width + 2 * key_width))
                live = at + iota(picked.shape, 0) < own_length
                picked = jnp.where(live, picked, 0.0).astype(BF16)
                cache_ref[0, pl.ds(at, SPAN), :] = picked[:, :key_width]
                cache_ref[1, pl.ds(at, SPAN), :] = picked[:, key_width:]

            @pl.when(at >= own_length)
            def _():
                empty = jnp.zeros((SPAN, key_width), BF16)
                cache_ref[0, pl.ds(at, SPAN), :] = empty
                cache_ref[1, pl.ds(at, SPAN), :] = empty

            return carry

        lax.fori_loop(0, spans, step, 0)
        cache_copy.start()

    heads, key_heads = query_width // HEAD_SIZE, key_width // HEAD_SIZE
    group = heads // key_heads
    factor = math.log2(math.e) / math.sqrt(HEAD_SIZE)
    tall = group * SPAN

    def span_of(slot):
        span = plan_ref[me * spans + slot]
        start, length = run_of(lengths_ref, lax.div(span, spans), workers)
        offset = lax.rem(span, spans) * SPAN
        dead = offset >= length
        needed = start + jnp.minimum(offset + SPAN, length)
        due = jnp.logical_not(dead) & (needed <= known) & (needed > prior)
        return start, length, offset, dead, due

    def result(slot):
        rows = pl.ds(pl.multiple_of(slot * SPAN, SPAN), SPAN)
        return pltpu.make_async_copy(
            attended_ref.at[rows, :], attended_out.at[rows, :], out_sems.at[slot]
        )

    def attend_slot(slot, carry):
        start, length, offset, dead, due = span_of(slot)
        out_rows = pl.ds(pl.multiple_of(slot * SPAN, SPAN), SPAN)

        if not prior:

            @pl.when(dead)
            def _():
                attended_ref[out_rows, :] = jnp.zeros((SPAN, query_width), BF16)
                result(slot).start()

        @pl.when(due)
        def _():
            queries = window(start + offset, slice(0, query_width)).astype(BF16)
            for head in range(heads):
                at = head % group * SPAN
                queries_ref[head // group, at : at + SPAN, :] = queries[
                    :, head * HEAD_SIZE : (head + 1) * HEAD_SIZE
                ]
            first = pl.multiple_of(lax.div(start, ALIGN) * ALIGN, ALIGN)
            shift = start - first
            reach = shift + jnp.minimum(offset + SPAN, length)
            tiles = lax.div(reach + TILE - 1, TILE)

            def columns(at, head):
                return slice(at + head * HEAD_SIZE, at + (head + 1) * HEAD_SIZE)

            def tile_rows(tile):
                return pl.ds(pl.multiple_of(first + tile * TILE, ALIGN), TILE)

            top_ref[...] = jnp.full(top_ref.shape, -1e30, F32)

            def score(tile, carry):
                key_pos = tile * TILE + iota((SPAN, TILE), 1) - shift
                query_pos = offset + iota((SPAN, TILE), 0)
                allowed = (key_pos >= 0) & (key_pos <= query_pos) & (key_pos < length)
                bias = jnp.where(allowed, 0.0, -1e30)
                bias = jnp.concatenate([bias] * group, axis=0)
                for head in range(key_heads):
                    scores = lax.dot_general(
                        queries_ref[head],
                        rows_ref[tile_rows(tile), columns(query_width, head)],
                        (((1,), (1,)), ((), ())),
                        preferred_element_type=F32,
                    )
                    scores = scores + bias
                    scores_ref[head, tile] = scores
                    halves = jnp.maximum(scores[:, :SPAN], scores[:, SPAN:])
                    top_ref[head] = jnp.maximum(top_ref[head], halves)
                return carry

            lax.fori_loop(0, tiles, score, 0)
            tops = [jnp.max(top_ref[head], axis=1, keepdims=True) for head in range(key_heads)]

            def mix(tile, carry):
                ones = jnp.ones((TILE, HEAD_SIZE), BF16)
                totals = []
                for head in range(key_heads):
                    weights = jnp.exp2((scores_ref[head, tile] - tops[head]) * factor)
                    values = rows_ref[tile_rows(tile), columns(query_width + key_width, head)]
                    values = jnp.concatenate([values, ones], axis=1)
                    totals.append(
                        carry[head]
                        + jnp.dot(weights.astype(BF16), values, preferred_element_type=F32)
                    )
                return tuple(totals)

            empty = jnp.zeros((tall, 2 * HEAD_SIZE), F32)
            mixed = lax.fori_loop(0, tiles, mix, (empty,) * key_heads)
            live = offset + iota((SPAN, HEAD_SIZE), 0) < length
            for head in range(heads):
                at = head % group * SPAN
                part = mixed[head // group][at : at + SPAN]
                part = part[:, :HEAD_SIZE] / part[:, HEAD_SIZE:]
                attended_ref[out_rows, columns(0, head)] = jnp.where(live, part, 0.0).astype(BF16)

            result(slot).start()

        return carry

    lax.fori_loop(0, spans, attend_slot, 0)

    def finish(slot, carry):
        _, _, _, dead, due = span_of(slot)

        @pl.when(due if prior else due | dead)
        def _():
            result(slot).wait()

        return carry

    lax.fori_loop(0, spans, finish, 0)

    @pl.when(mine)
    def _():
        cache_copy.wait()


def attend(chips, groups, known, prior, widths, slots, lengths, plan, blocks, outputs):
    query_width, key_width = widths
    width = query_width + 2 * key_width
    total = 2 * chips * sum(sum(sizes) for _, sizes in groups)
    copies = 4 * chips * sum(len(sizes) for _, sizes in groups)
    key_heads, tall = key_width // HEAD_SIZE, query_width // key_width * SPAN
    at = 2 + len(blocks)
    return pl.pallas_call(
        functools.partial(attend_kernel, chips, groups, known, prior, query_width, key_width),
        in_specs=[pl.BlockSpec(memory_space=pltpu.SMEM)] * 2
        + [pl.BlockSpec(memory_space=pl.ANY)] * (len(blocks) + len(outputs)),
        out_specs=[pl.BlockSpec(memory_space=pl.ANY)] * 2
        + [pl.BlockSpec(memory_space=pltpu.VMEM)],
        out_shape=[
            jax.ShapeDtypeStruct((slots, query_width), BF16),
            jax.ShapeDtypeStruct((2, slots, key_width), BF16),
            jax.ShapeDtypeStruct((8, 128), F32),
        ],
        input_output_aliases={at + index: index for index in range(len(outputs))},
        scratch_shapes=[
            pltpu.VMEM((slots, query_width), BF16),
            pltpu.VMEM((2, slots, key_width), BF16),
            pltpu.VMEM((total + TILE + ALIGN, width), BF16),
            pltpu.VMEM((key_heads, tall, HEAD_SIZE), BF16),
            pltpu.VMEM((key_heads, slots // TILE + 1, tall, TILE), F32),
            pltpu.VMEM((key_heads, tall, SPAN), F32),
            pltpu.SemaphoreType.DMA((copies,)),
            pltpu.SemaphoreType.DMA((slots // SPAN + 1,)),
        ],
        compiler_params=pltpu.CompilerParams(vmem_limit_bytes=16 * MEBI),
        name="attend",
    )(lengths, plan, *blocks, *outputs)


def shift_chips(value, hop, chips):
    pairs = [(2 * x + c, 2 * ((x + hop) % chips) + c) for x in range(chips) for c in range(2)]
    return lax.ppermute(value, "req", pairs)


def swap_cores(value, chips):
    return lax.ppermute(value, "req", [(d, d ^ 1) for d in range(2 * chips)])


def local(
    chips, shards, tokens, norm_gain, w_query, key_weight, value_weight, lengths, plan
):
    workers = 2 * chips
    slots = tokens.shape[0]
    live = slots // 2
    sizes = [live * share // sum(SHARES) // ALIGN * ALIGN for share in SHARES]
    sizes[-1] = live - sum(sizes[:-1])
    bases = [workers * sum(sizes[:chunk]) for chunk in range(len(sizes))]
    weights = [w_query, key_weight, value_weight]
    gain = norm_gain.astype(F32).reshape(1, -1)
    halfway = HEAD_SIZE // 2
    frequency = np.exp(-np.arange(halfway) * 2.0 / HEAD_SIZE * math.log(500000.0))
    frequency = jnp.asarray(np.tile(frequency, 2)[None, :], F32)

    twin = swap_cores(tokens, chips)
    first = deal(chips, bases[:1], sizes[:1], lengths, [tokens], [False])
    dealt = [
        *deal(chips, bases[:1], sizes[:1], lengths, [twin], [True], first),
        *deal(chips, bases[1:], sizes[1:], lengths, [tokens, twin], [False, True]),
    ]
    homes, aways = dealt[::2], dealt[1::2]
    routes, masks = routes_of(shards)
    direct = [at + 1 for at, (source, _) in enumerate(routes) if source == 0]
    kinds = {"first": [0, *direct]}
    kinds["late"] = [piece for piece in range(len(masks)) if piece not in kinds["first"]]
    relayed = [piece for piece in direct if piece in {source for source, _ in routes}]

    groups = [([base], [rows]) for base, rows in zip(bases, sizes)]
    widths = w_query.shape[1], key_weight.shape[1]

    def add(kind, chunk, carried=()):
        pieces = [lines[chunk][piece] for piece in kinds[kind]]
        final = kind == "late"
        turned = turns[chunk] if final else ()
        offsets = [masks[piece] for piece in kinds[kind]]
        return project(final, shards, offsets, pieces, gain, weights, carried, turned)

    def from_chips(block):
        return [shift_chips(block, hop, chips) for hop in range(1, chips)]

    def all_blocks(block, arrived):
        return [leaf for piece in (block, *arrived) for leaf in (piece, swap_cores(piece, chips))]

    def start(line, group):
        for index, (source, distance) in enumerate(routes):
            if index + 1 in group:
                pairs = [(at, at ^ distance) for at in range(shards)]
                line[index + 1] = lax.ppermute(line[source], "tp", pairs)

    lines, own, sent, blocks = [], [], [], []
    last = len(sizes) - 1

    def finish(chunk):
        own.append(add("late", chunk, add("first", chunk))[0])
        sent.append(from_chips(own[-1]))

    def fence(chunk, block, *anchors):
        passed, anchors = [], list(anchors)
        if chunk:
            before = lines[chunk - 1]
            passed = [before[piece] for piece in relayed]
            anchors += [before[piece] for piece in direct if piece not in relayed]
        if chunk == 1:
            weights[0], token = load(w_query, lines[0][0])
            anchors.append(token)
        if 1 < chunk <= last:
            finish(chunk - 2)
            anchors.append(own[-1])
        if 2 < chunk <= last:
            arrived = after(sent[chunk - 3], own[-1:])
            blocks.extend(all_blocks(own[chunk - 3], arrived))
            anchors += blocks[-2 * chips :]
        if passed:
            passed = after([*passed, *block], anchors)
            before.update(zip(relayed, passed))
            block = passed[len(relayed) :]
        return block

    for chunk in range(last + 1):
        arrived = [shift_chips(aways[chunk][hop - 1], hop, chips) for hop in range(1, chips)]
        later = aways[chunk + 1 : chunk + 2]
        block, aways[chunk + 1 : chunk + 2] = merge(homes[chunk], arrived, later)
        lines.append({0: fence(chunk, [block])[0]})
        if chunk:
            start(lines[-2], kinds["late"])
        start(lines[-1], direct)
        if chunk == 1:
            turns = angles(groups, lengths, frequency, lines[1][0])
    common = widths, slots, lengths, plan

    def attended(at, prior, blocks, outputs):
        known = workers * sum(sizes[: at + 1])
        return attend(chips, groups[: at + 1], known, prior, *common, blocks, outputs)

    sums = list(add("first", last - 1))
    for at in range(last - 2, last - 1):
        blocks += all_blocks(own[at], after(sent[at], own[at + 1 : at + 2] or [sums[1]]))
    *outputs, token = attended(last - 2, 0, blocks, ())
    sums[1:] = after(sums[1:], [token])
    fence(last + 1, [])
    start(lines[-1], kinds["late"])
    own.append(add("late", last - 1, sums)[0])
    sent.append(from_chips(own[-1]))
    finish(last)
    blocks += all_blocks(own[last - 1], after(sent[last - 1], own[last:]))
    prior = workers * sum(sizes[:-2])
    *outputs, token = attended(last - 1, prior, blocks, outputs)
    blocks += all_blocks(own[last], after(sent[last], [token]))
    prior = workers * sum(sizes[:-1])
    return tuple(attended(last, prior, blocks, outputs)[:2])


def solution(mesh):
    placed = (
        P(("groups", "req"), "tp"),
        P(),
        P(None, "tp"),
        P(None, "tp"),
        P(None, "tp"),
        P("groups"),
        P("groups"),
    )
    return jax.shard_map(
        functools.partial(local, mesh.shape["req"] // 2, mesh.shape["tp"]),
        mesh=mesh,
        in_specs=placed,
        out_specs=(P(("groups", "req"), "tp"), P(None, ("groups", "req"), "tp")),
        check_vma=False,
    )
```
